32 devices in a mesh: space: 8 (over z, x), basis: 4 (over y, core).
Axes of the slice: x: 2, y: 2, z: 4, core: 2. Of those that a mesh axis runs over, the one named last changes fastest.
Arguments:
- x_block: float32 [16, 3, 8, 32, 128], P(None, None, 'space', 'basis'), may hold values from -68 to 68
- basis: float32 [64, 3, 8, 32, 128], P('basis', None, 'space'), may hold values from -11 to 11
- material: int32 [8, 32, 128], P('space', 'basis'), may hold values from 0 to 7
- k0_blocks: float32 [8, 7, 3, 3], replicated, may hold values from -4 to 4
- k0_diag: float32 [8, 3], replicated, may hold values from 2 to 8
- ke_blocks: float32 [8, 7, 3, 3], replicated, may hold values from -6 to 6
- mass: float32 [8, 3], replicated, may hold values from 0.5 to 2
- velocities: float32 [1024], replicated, may hold values from 0.5 to 1
- shifts: float32 [1024], replicated, may hold values from 0.5 to 1.5
- sample: int32 [1], replicated, may hold values from 0 to 1023
Outputs:
- orthonormal: float32 [16, 3, 8, 32, 128], P(None, None, 'space', 'basis')
- coefficients: float32 [64, 16], P('basis')
- upper_factor: float32 [16, 16], replicated
The draws below stay inside these ranges and needn't reach their ends.
All inputs are finite; a program needn't handle non-finite values.
Results may differ from the reference program's by a relative error of at most 0.00015.
Values sent between devices are 32-bit elements; how exact they have to be, the bound alone decides.
No kernel may reach another device: no remote copies, remote signals or barrier semaphores. Data moves between devices by JAX's collectives and lax.ppermute only.
A program may use at most 64 MiB of HBM per device.

```python
import math
import jax
import jax.numpy as jnp
from jax import lax

BLOCK = 16
BASIS_COLS = 64
NMAT = 8
NSAMP = 1024
GX = 8
GY = 32
GZ = 128


def shared_fields(key):
    keys = [jax.random.fold_in(key, 100 + index) for index in range(8)]
    cell_shape = (GX, GY, GZ)
    basis_shape = (BASIS_COLS, 3, GX, GY, GZ)
    noise = jnp.clip(jax.random.normal(keys[0], basis_shape, jnp.float32), -4.0, 4.0)
    weight = 0.15
    common = jnp.clip(jax.random.normal(keys[1], (3, GX, GY, GZ), jnp.float32), -4.0, 4.0)
    signs = 2.0 * jax.random.randint(keys[2], (BASIS_COLS,), 0, 2).astype(jnp.float32) - 1.0
    spread = jax.random.uniform(keys[3], cell_shape, jnp.float32)
    position = (jnp.arange(GX).astype(jnp.float32) / GX)[:, None, None]
    row_scale = jnp.exp(jnp.log(10.0) * (0.5 * position + 0.5 * spread))
    basis = 0.22 * row_scale * (noise + weight * signs[:, None, None, None, None] * common)
    return (basis, keys, row_scale)


def draw_basis(key, part):
    return shared_fields(key)[0]


def draw_x_block(key, part):
    basis, keys, row_scale = shared_fields(key)
    groups = BASIS_COLS // BLOCK
    mix_signs = 2.0 * jax.random.randint(keys[4], (groups, 4, BLOCK), 0, 2).astype(jnp.float32) - 1.0
    mixing = jax.random.uniform(keys[5], (groups, 4, BLOCK), jnp.float32, 0.5, 1.5) * mix_signs
    extra = jnp.clip(jax.random.normal(keys[6], (BLOCK, 3, GX, GY, GZ), jnp.float32), -4.0, 4.0)
    result = 0.11 * row_scale * extra
    columns = jnp.arange(BLOCK)
    for group in range(groups):
        for band in range(4):
            chosen = group * BLOCK + (columns + band) % BLOCK
            result = result + 0.25 * mixing[group, band][:, None, None, None, None] * basis[chosen]
    return result


def place_ends(values, own_key, least, high):
    spot = [jax.random.randint(jax.random.fold_in(own_key, axis), (), 0, length) for axis, length in enumerate(values.shape)]
    main_axis = values.shape.index(max(values.shape))
    beside = spot[:main_axis] + [(spot[main_axis] + 1) % values.shape[main_axis]] + spot[main_axis + 1:]
    return values.at[tuple(spot)].set(least).at[tuple(beside)].set(high)


def normal_values(key, extent, scale, bound, kind=jnp.bfloat16):
    drawn = scale * jax.random.normal(key, extent, jnp.float32)
    return jnp.clip(drawn, min=-bound, max=bound).astype(kind)


def setup_inputs(seed: int = 0) -> dict:
    key_list = jax.random.split(jax.random.key(seed), 11)
    return {
        "x_block": draw_x_block(jax.random.fold_in(key_list[10], 71), 0),
        "basis": draw_basis(jax.random.fold_in(key_list[10], 71), 0),
        "material": place_ends(jax.random.randint(key_list[2], (GX, GY, GZ), 0, NMAT), jax.random.fold_in(key_list[2], 1), 0, NMAT - 1).astype(jnp.int32),
        "k0_blocks": normal_values(key_list[3], (NMAT, 7, 3, 3), 0.3, 4.0, jnp.float32),
        "k0_diag": jnp.clip(jnp.exp(jax.random.uniform(key_list[4], (NMAT, 3), jnp.float32, math.log(2.0), math.log(8.0))), 2.0, 8.0),
        "ke_blocks": normal_values(key_list[5], (NMAT, 7, 3, 3), 0.5, 6.0, jnp.float32),
        "mass": jnp.clip(jnp.exp(jax.random.uniform(key_list[6], (NMAT, 3), jnp.float32, math.log(0.5), math.log(2.0))), 0.5, 2.0),
        "velocities": jnp.clip(jax.random.uniform(key_list[7], (NSAMP,), jnp.float32, 0.5, 1.0), 0.5, 1.0),
        "shifts": jnp.clip(jax.random.uniform(key_list[8], (NSAMP,), jnp.float32, 0.5, 1.5), 0.5, 1.5),
        "sample": jax.random.randint(key_list[9], (1,), 0, NSAMP).astype(jnp.int32),
    }


exact_precision = lax.Precision.HIGHEST

def stencil_tables(k0_blocks, k0_diag, ke_blocks, mass, velocities, shifts, sample):
    velocity = jnp.take(velocities, sample, axis=0)[0]
    sigma_value = jnp.take(shifts, sample, axis=0)[0]
    center = (k0_diag - sigma_value * mass)[:, :, None] * jnp.eye(3, dtype=jnp.float32)
    tables = k0_blocks - velocity * velocity * ke_blocks
    return tables.at[:, 0].add(center)

def neighbour_views(padded):
    extent_x = padded.shape[2] - 2
    extent_y = padded.shape[3] - 2
    extent_z = padded.shape[4] - 2

    def window(step_x, step_y, step_z):
        return padded[:, :, 1 + step_x:1 + step_x + extent_x, 1 + step_y:1 + step_y + extent_y, 1 + step_z:1 + step_z + extent_z]
    return [window(0, 0, 0), window(-1, 0, 0), window(1, 0, 0), window(0, -1, 0), window(0, 1, 0), window(0, 0, -1), window(0, 0, 1)]

def reference(x_block, basis, material, k0_blocks, k0_diag, ke_blocks, mass, velocities, shifts, sample):
    tables = stencil_tables(k0_blocks, k0_diag, ke_blocks, mass, velocities, shifts, sample)
    cell_blocks = tables[material]
    padded = jnp.pad(x_block, ((0, 0), (0, 0), (1, 1), (1, 1), (1, 1)))
    stencil_views = neighbour_views(padded)
    applied = jnp.zeros(x_block.shape, jnp.float32)
    for offset in range(7):
        applied = applied + jnp.einsum('xyzij,njxyz->nixyz', cell_blocks[:, :, :, offset], stencil_views[offset], precision=exact_precision)
    row_count = 3.0 * GX * GY * GZ
    running = jnp.zeros((BASIS_COLS, BLOCK), jnp.float32)
    for repeat in range(2):
        coeffs = jnp.einsum('kcxyz,ncxyz->kn', basis, applied, precision=exact_precision) / row_count
        applied = applied - jnp.einsum('kcxyz,kn->ncxyz', basis, coeffs, precision=exact_precision)
        running = running + coeffs
    gram_matrix = jnp.einsum('ncxyz,mcxyz->nm', applied, applied, precision=exact_precision) / row_count
    lower_factor = jnp.linalg.cholesky(gram_matrix)
    inverse = jax.scipy.linalg.solve_triangular(lower_factor, jnp.eye(BLOCK, dtype=jnp.float32), lower=True).T
    orthonormal = jnp.einsum('mcxyz,mn->ncxyz', applied, inverse, precision=exact_precision)
    return (orthonormal, running, lower_factor.T)
```

```python
import jax
import jax.numpy as jnp
from jax import lax
from jax.sharding import PartitionSpec as P

exact_precision = lax.Precision.HIGHEST


def from_lower(values, axis):
    count = lax.axis_size(axis)
    return lax.ppermute(values, axis, [(i, i + 1) for i in range(count - 1)])


def from_upper(values, axis):
    count = lax.axis_size(axis)
    return lax.ppermute(values, axis, [(i + 1, i) for i in range(count - 1)])


def stencil_tables(k0_blocks, k0_diag, ke_blocks, mass, velocities, shifts, sample):
    velocity = jnp.take(velocities, sample, axis=0)[0]
    sigma_value = jnp.take(shifts, sample, axis=0)[0]
    center = (k0_diag - sigma_value * mass)[:, :, None] * jnp.eye(3, dtype=jnp.float32)
    tables = k0_blocks - velocity * velocity * ke_blocks
    return tables.at[:, 0].add(center)


def cell_fields(tables, material_cells):
    fields = jnp.zeros((7, 3, 3) + material_cells.shape, jnp.float32)
    for level in range(tables.shape[0]):
        chosen = (material_cells == level).astype(jnp.float32)
        fields = fields + tables[level][:, :, :, None, None, None] * chosen[None, None, None]
    return fields


def apply_fields(views, fields):
    sums = [None, None, None]
    for offset in range(7):
        view = views[offset]
        for row in range(3):
            term = fields[offset, row, 0][None] * view[:, 0]
            term = term + fields[offset, row, 1][None] * view[:, 1]
            term = term + fields[offset, row, 2][None] * view[:, 2]
            sums[row] = term if sums[row] is None else sums[row] + term
    return jnp.stack(sums, axis=1)


def neighbour_views(x_block):
    extent_x = x_block.shape[2]
    extent_y = x_block.shape[3]
    extent_z = x_block.shape[4]
    before_x = from_lower(x_block[:, :, extent_x - 1 :], "space")
    after_x = from_upper(x_block[:, :, :1], "space")
    before_y = from_lower(x_block[:, :, :, extent_y - 1 :], "basis")
    after_y = from_upper(x_block[:, :, :, :1], "basis")
    zero_col = jnp.zeros(x_block.shape[:4] + (1,), x_block.dtype)
    return [
        x_block,
        jnp.concatenate((before_x, x_block[:, :, : extent_x - 1]), axis=2),
        jnp.concatenate((x_block[:, :, 1:], after_x), axis=2),
        jnp.concatenate((before_y, x_block[:, :, :, : extent_y - 1]), axis=3),
        jnp.concatenate((x_block[:, :, :, 1:], after_y), axis=3),
        jnp.concatenate((zero_col, x_block[:, :, :, :, : extent_z - 1]), axis=4),
        jnp.concatenate((x_block[:, :, :, :, 1:], zero_col), axis=4),
    ]


def own_rows(basis):
    group_cols, comps, extent_x, full_y, extent_z = basis.shape
    count = lax.axis_size("basis")
    pieces = basis.reshape(group_cols, comps, extent_x, count, full_y // count, extent_z)
    pieces = jnp.moveaxis(pieces, 3, 0)
    pieces = lax.all_to_all(pieces, "basis", 0, 0)
    return pieces.reshape((count * group_cols,) + pieces.shape[2:])


def total_sum(part):
    for axis in ("basis", "space"):
        part = jnp.sum(lax.all_gather(part, axis, axis=0), axis=0)
    return part


def shards(
    x_block, basis, material, k0_blocks, k0_diag, ke_blocks, mass, velocities, shifts, sample
):
    tables = stencil_tables(k0_blocks, k0_diag, ke_blocks, mass, velocities, shifts, sample)
    block_cols, comps, extent_x, _, extent_z = x_block.shape
    group_cols = basis.shape[0]
    row_count = float(comps * extent_x * lax.axis_size("space") * basis.shape[3] * extent_z)

    views = neighbour_views(x_block)
    rows = own_rows(basis)
    basis_cols = rows.shape[0]
    applied = apply_fields(views, cell_fields(tables, material))
    joined = jnp.concatenate((rows, applied), axis=0)
    part = jnp.einsum("kcxyz,ncxyz->kn", joined, joined, precision=exact_precision)
    sums = total_sum(part) / row_count
    basis_gram = sums[:basis_cols, :basis_cols]
    first = sums[:basis_cols, basis_cols:]
    block_gram = sums[basis_cols:, basis_cols:]

    def times(left, right):
        return jnp.matmul(left, right, precision=exact_precision)

    gram_first = times(basis_gram, first)
    coeffs = first + (first - gram_first)
    cross = times(coeffs.T, first)
    gram_matrix = block_gram - cross - cross.T + times(coeffs.T, times(basis_gram, coeffs))
    lower_factor = jnp.linalg.cholesky(gram_matrix)
    inverse = lax.linalg.triangular_solve(
        lower_factor, jnp.eye(block_cols, dtype=jnp.float32), left_side=True, lower=True
    ).T
    weights = jnp.concatenate((-times(coeffs, inverse), inverse), axis=0)
    orthonormal = jnp.einsum("kcxyz,kn->ncxyz", joined, weights, precision=exact_precision)
    own_coeffs = lax.dynamic_slice_in_dim(
        coeffs, lax.axis_index("basis") * group_cols, group_cols, axis=0
    )
    return (orthonormal, own_coeffs, lower_factor.T)


def solution(mesh):
    in_specs = (
        P(None, None, "space", "basis", None),
        P("basis", None, "space", None, None),
        P("space", "basis", None),
        P(),
        P(),
        P(),
        P(),
        P(),
        P(),
        P(),
    )
    out_specs = (P(None, None, "space", "basis", None), P("basis", None), P())
    return jax.shard_map(shards, mesh=mesh, in_specs=in_specs, out_specs=out_specs, check_vma=False)
```

```python
import jax
import jax.numpy as jnp
from jax import lax
from jax.sharding import PartitionSpec as P

exact_precision = lax.Precision.HIGHEST


def from_lower(values, axis):
    count = lax.axis_size(axis)
    return lax.ppermute(values, axis, [(i, i + 1) for i in range(count - 1)])


def from_upper(values, axis):
    count = lax.axis_size(axis)
    return lax.ppermute(values, axis, [(i + 1, i) for i in range(count - 1)])


def stencil_tables(k0_blocks, k0_diag, ke_blocks, mass, velocities, shifts, sample):
    velocity = jnp.take(velocities, sample, axis=0)[0]
    sigma_value = jnp.take(shifts, sample, axis=0)[0]
    center = (k0_diag - sigma_value * mass)[:, :, None] * jnp.eye(3, dtype=jnp.float32)
    tables = k0_blocks - velocity * velocity * ke_blocks
    return tables.at[:, 0].add(center)


def cell_fields(tables, material_cells):
    fields = jnp.zeros((7, 3, 3) + material_cells.shape, jnp.float32)
    for level in range(tables.shape[0]):
        chosen = (material_cells == level).astype(jnp.float32)
        fields = fields + tables[level][:, :, :, None, None, None] * chosen[None, None, None]
    return fields


def apply_fields(views, fields):
    sums = [None, None, None]
    for offset in range(7):
        view = views[offset]
        for row in range(3):
            term = fields[offset, row, 0][None] * view[:, 0]
            term = term + fields[offset, row, 1][None] * view[:, 1]
            term = term + fields[offset, row, 2][None] * view[:, 2]
            sums[row] = term if sums[row] is None else sums[row] + term
    return jnp.stack(sums, axis=1)


def neighbour_views(x_block):
    extent_x = x_block.shape[2]
    extent_y = x_block.shape[3]
    extent_z = x_block.shape[4]
    before_x = from_lower(x_block[:, :, extent_x - 1 :], "space")
    after_x = from_upper(x_block[:, :, :1], "space")
    before_y = from_lower(x_block[:, :, :, extent_y - 1 :], "basis")
    after_y = from_upper(x_block[:, :, :, :1], "basis")
    zero_col = jnp.zeros(x_block.shape[:4] + (1,), x_block.dtype)
    return [
        x_block,
        jnp.concatenate((before_x, x_block[:, :, : extent_x - 1]), axis=2),
        jnp.concatenate((x_block[:, :, 1:], after_x), axis=2),
        jnp.concatenate((before_y, x_block[:, :, :, : extent_y - 1]), axis=3),
        jnp.concatenate((x_block[:, :, :, 1:], after_y), axis=3),
        jnp.concatenate((zero_col, x_block[:, :, :, :, : extent_z - 1]), axis=4),
        jnp.concatenate((x_block[:, :, :, :, 1:], zero_col), axis=4),
    ]


def own_rows(basis):
    group_cols, comps, extent_x, full_y, extent_z = basis.shape
    count = lax.axis_size("basis")
    pieces = basis.reshape(group_cols, comps, extent_x, count, full_y // count, extent_z)
    pieces = jnp.moveaxis(pieces, 3, 0)
    pieces = lax.all_to_all(pieces, "basis", 0, 0)
    return pieces.reshape((count * group_cols,) + pieces.shape[2:])


def total_sum(part):
    for axis in ("basis", "space"):
        count = lax.axis_size(axis)
        copies = jnp.broadcast_to(part[None], (count,) + part.shape)
        part = jnp.sum(lax.all_to_all(copies, axis, 0, 0), axis=0)
    return part


def shards(
    x_block, basis, material, k0_blocks, k0_diag, ke_blocks, mass, velocities, shifts, sample
):
    tables = stencil_tables(k0_blocks, k0_diag, ke_blocks, mass, velocities, shifts, sample)
    block_cols, comps, extent_x, _, extent_z = x_block.shape
    group_cols = basis.shape[0]
    row_count = float(comps * extent_x * lax.axis_size("space") * basis.shape[3] * extent_z)

    views = neighbour_views(x_block)
    rows = own_rows(basis)
    basis_cols = rows.shape[0]
    applied = apply_fields(views, cell_fields(tables, material))
    joined = jnp.concatenate((rows, applied), axis=0)
    part = jnp.einsum("kcxyz,ncxyz->kn", joined, joined, precision=exact_precision)
    sums = total_sum(part) / row_count
    basis_gram = sums[:basis_cols, :basis_cols]
    first = sums[:basis_cols, basis_cols:]
    block_gram = sums[basis_cols:, basis_cols:]

    def times(left, right):
        return jnp.matmul(left, right, precision=exact_precision)

    gram_first = times(basis_gram, first)
    coeffs = first + (first - gram_first)
    cross = times(coeffs.T, first)
    gram_matrix = block_gram - cross - cross.T + times(coeffs.T, times(basis_gram, coeffs))
    lower_factor = jnp.linalg.cholesky(gram_matrix)
    inverse = lax.linalg.triangular_solve(
        lower_factor, jnp.eye(block_cols, dtype=jnp.float32), left_side=True, lower=True
    ).T
    weights = jnp.concatenate((-times(coeffs, inverse), inverse), axis=0)
    orthonormal = jnp.einsum("kcxyz,kn->ncxyz", joined, weights, precision=exact_precision)
    own_coeffs = lax.dynamic_slice_in_dim(
        coeffs, lax.axis_index("basis") * group_cols, group_cols, axis=0
    )
    return (orthonormal, own_coeffs, lower_factor.T)


def solution(mesh):
    in_specs = (
        P(None, None, "space", "basis", None),
        P("basis", None, "space", None, None),
        P("space", "basis", None),
        P(),
        P(),
        P(),
        P(),
        P(),
        P(),
        P(),
    )
    out_specs = (P(None, None, "space", "basis", None), P("basis", None), P())
    return jax.shard_map(shards, mesh=mesh, in_specs=in_specs, out_specs=out_specs, check_vma=False)
```

```python
import functools

import jax
import jax.numpy as jnp
from jax import lax
from jax.experimental import pallas as pl
from jax.experimental.pallas import tpu as pltpu
from jax.sharding import PartitionSpec as P

exact_precision = lax.Precision.HIGHEST
VMEM = pl.BlockSpec(memory_space=pltpu.VMEM)
SMEM = pl.BlockSpec(memory_space=pltpu.SMEM)
ANY = pl.BlockSpec(memory_space=pl.ANY)


def f32(*shape):
    return jax.ShapeDtypeStruct(shape, jnp.float32)


def from_lower(values, axis):
    count = lax.axis_size(axis)
    return lax.ppermute(values, axis, [(i, i + 1) for i in range(count - 1)])


def from_upper(values, axis):
    count = lax.axis_size(axis)
    return lax.ppermute(values, axis, [(i + 1, i) for i in range(count - 1)])


def stencil_tables(k0_blocks, k0_diag, ke_blocks, mass, velocities, shifts, sample):
    velocity = jnp.take(velocities, sample, axis=0)[0]
    sigma_value = jnp.take(shifts, sample, axis=0)[0]
    center = (k0_diag - sigma_value * mass)[:, :, None] * jnp.eye(3, dtype=jnp.float32)
    tables = k0_blocks - velocity * velocity * ke_blocks
    return tables.at[:, 0].add(center)


def pack_kernel(basis_ref, x_ref, sent_ref, first_ref, last_ref, sems):
    count, cols, comps, rows, lanes = sent_ref.shape
    copies = [
        pltpu.make_async_copy(
            basis_ref.at[:, :, 0, pl.ds(rows * piece, rows), :], sent_ref.at[piece], sems.at[piece]
        )
        for piece in range(count)
    ]
    for copy in copies:
        copy.start()
    block_cols = x_ref.shape[0] // (comps * rows)
    for comp in range(comps):
        there = pl.ds(comp * block_cols, block_cols)
        for edge_ref, row in ((first_ref, 0), (last_ref, rows - 1)):
            edge_ref[there, :] = x_ref[pl.ds(comp * rows + row, block_cols, stride=comps * rows), :]
    for copy in copies:
        copy.wait()


def pack(basis, x_rows, block_cols):
    group_cols, comps, _, full_y, lanes = basis.shape
    count = lax.axis_size("basis")
    edge = f32(comps * block_cols, lanes)
    return pl.pallas_call(
        pack_kernel,
        out_shape=(f32(count, group_cols, comps, full_y // count, lanes), edge, edge),
        in_specs=[ANY, VMEM],
        out_specs=(ANY, VMEM, VMEM),
        scratch_shapes=[pltpu.SemaphoreType.DMA((count,))],
        name="pack",
    )(basis, x_rows)


def stencil_kernel(
    comps, x_ref, before_x_ref, after_x_ref, before_y_ref, after_y_ref, table_ref, material_ref,
    applied_ref,
):
    rows, lanes = material_ref.shape
    levels = table_ref.shape[1]
    block_cols = x_ref.shape[0] // (comps * rows)
    lane = lax.broadcasted_iota(jnp.int32, (block_cols, lanes), 1)
    level = lax.broadcasted_iota(jnp.int32, (levels, lanes), 0)

    def line(ref, comp, row):
        return ref[pl.ds(comp * rows + row, block_cols, stride=comps * rows), :]

    def edge(ref, comp):
        return ref[pl.ds(comp * block_cols, block_cols), :]

    for row in range(rows):
        chosen = (jnp.broadcast_to(material_ref[row : row + 1, :], (levels, lanes)) == level)
        fields = jnp.dot(
            table_ref[...], chosen.astype(jnp.float32),
            precision=exact_precision, preferred_element_type=jnp.float32,
        )
        sums = [None] * comps
        for comp in range(comps):
            centre = line(x_ref, comp, row)
            views = [
                centre,
                line(before_x_ref, comp, row),
                line(after_x_ref, comp, row),
                line(x_ref, comp, row - 1) if row > 0 else edge(before_y_ref, comp),
                line(x_ref, comp, row + 1) if row < rows - 1 else edge(after_y_ref, comp),
                jnp.where(lane == 0, 0.0, pltpu.roll(centre, 1, 1)),
                jnp.where(lane == lanes - 1, 0.0, pltpu.roll(centre, lanes - 1, 1)),
            ]
            for offset, view in enumerate(views):
                for out in range(comps):
                    entry = (offset * comps + out) * comps + comp
                    term = fields[entry : entry + 1, :] * view
                    sums[out] = term if sums[out] is None else sums[out] + term
        for out in range(comps):
            applied_ref[out * rows + row] = sums[out]


def stencil(x_rows, halos, table, material, comps):
    rows, lanes = material.shape
    block_cols = x_rows.shape[0] // (comps * rows)
    return pl.pallas_call(
        functools.partial(stencil_kernel, comps),
        out_shape=f32(comps * rows, block_cols, lanes),
        in_specs=[VMEM] * 7,
        out_specs=VMEM,
        name="stencil",
    )(x_rows, *halos, table, material)


def three_parts(values):
    high = values.astype(jnp.bfloat16)
    rest = values - high.astype(jnp.float32)
    middle = rest.astype(jnp.bfloat16)
    low = (rest - middle.astype(jnp.float32)).astype(jnp.bfloat16)
    return high, middle, low


def sums_kernel(basis_ref, applied_ref, stack_ref, sums_ref):
    lines, block_cols, lanes = applied_ref.shape
    basis_cols = basis_ref.shape[0] // lines
    joined = basis_cols + block_cols
    for line in range(lines):
        there = pl.ds(line * lanes, lanes)
        for place, values in (
            (0, basis_ref[pl.ds(line, basis_cols, stride=lines), :]),
            (basis_cols, applied_ref[line]),
        ):
            for index, part in enumerate(three_parts(values)):
                stack_ref[pl.ds(index * joined + place, values.shape[0]), there] = part
    stack = stack_ref[...]
    products = lax.dot_general(
        stack, stack, (((1,), (1,)), ((), ())), preferred_element_type=jnp.float32
    )
    wide = products[:joined] + products[joined : 2 * joined] + products[2 * joined :]
    total = wide[:, :joined] + wide[:, joined : 2 * joined] + wide[:, 2 * joined :]
    half = basis_cols // 2
    sums_ref[pl.ds(0, half), :] = jnp.concatenate(
        (total[:half, :basis_cols], total[half:basis_cols, :basis_cols]), axis=1
    )
    sums_ref[pl.ds(half, block_cols), :] = jnp.concatenate(
        (total[basis_cols:], jnp.zeros((block_cols, sums_ref.shape[1] - joined), jnp.float32)), axis=1
    )


def sums(basis_rows, applied):
    lines, block_cols, lanes = applied.shape
    basis_cols = basis_rows.shape[0] // lines
    joined = basis_cols + block_cols
    return pl.pallas_call(
        sums_kernel,
        out_shape=(
            jax.ShapeDtypeStruct((3 * joined, lines * lanes), jnp.bfloat16),
            f32(basis_cols // 2 + block_cols, 2 * basis_cols),
        ),
        in_specs=[VMEM] * 2,
        out_specs=(VMEM, VMEM),
        name="sums",
    )(basis_rows, applied)


def exchange_total(part):
    other = jnp.zeros_like(part)
    for axis in ("basis", "space"):
        count = lax.axis_size(axis)
        step = 1
        while step < count:
            part = part + other
            other = lax.ppermute(part, axis, [(i, i ^ step) for i in range(count)])
            step *= 2
    return part, other


def finish_kernel(
    row_count, place_ref, part_ref, other_ref, stack_ref, block_ref, coeffs_ref, upper_ref,
    coeffs_scratch,
):
    block_cols = upper_ref.shape[0]
    basis_cols = part_ref.shape[1] // 2
    half = basis_cols // 2
    joined = basis_cols + block_cols
    lines = block_ref.shape[0] // block_cols
    lanes = block_ref.shape[1]
    total = (part_ref[...] + other_ref[...]) / row_count
    gram = jnp.concatenate((total[:half, :basis_cols], total[:half, basis_cols:]), axis=0)
    first = total[half:, :basis_cols]
    block_gram = total[half:, basis_cols:joined]

    def times(left, right, right_dim=0):
        return lax.dot_general(
            left, right, (((1,), (right_dim,)), ((), ())),
            precision=exact_precision, preferred_element_type=jnp.float32,
        )

    coeffs = first + (first - times(first, gram))
    image = times(coeffs, gram)
    matrix = block_gram - times(coeffs, first, 1) - times(first - image, coeffs, 1)
    coeffs_scratch[...] = coeffs.T
    group_cols = coeffs_ref.shape[0]
    start = pl.multiple_of(place_ref[0] * group_cols, group_cols)
    coeffs_ref[...] = coeffs_scratch[pl.ds(start, group_cols), :]

    row = lax.broadcasted_iota(jnp.int32, (block_cols, block_cols), 0)
    column = lax.broadcasted_iota(jnp.int32, (block_cols, block_cols), 1)
    unit = jnp.where(row == column, 1.0, 0.0)
    pad = jnp.zeros((block_cols, 2 * basis_cols - joined - block_cols), jnp.float32)
    work = jnp.concatenate((-coeffs, unit, matrix, pad), axis=1)
    height = lax.broadcasted_iota(jnp.int32, work.shape, 0)
    for step in range(block_cols):
        pivots = jnp.broadcast_to(work[:, joined + step : joined + step + 1], work.shape)
        pivot = pivots[step : step + 1, :]
        pivot_row = work[step : step + 1, :]
        scaled = pivot_row / pivot
        new_row = pivot_row * lax.rsqrt(pivot)
        work = jnp.where(
            height > step, work - pivots * scaled, jnp.where(height == step, new_row, work)
        )
    upper_ref[...] = work[:, joined : joined + block_cols]
    weights = three_parts(work[:, :joined])
    wide = jnp.concatenate(
        [jnp.concatenate((part, part, part), axis=1) for part in weights], axis=0
    )
    result = jnp.dot(wide, stack_ref[...], preferred_element_type=jnp.float32)
    result = result[:block_cols] + result[block_cols : 2 * block_cols] + result[2 * block_cols :]
    for line in range(lines):
        block_ref[pl.ds(line, block_cols, stride=lines), :] = result[
            :, line * lanes : (line + 1) * lanes
        ]


def finish(place, part, other, stack, row_count, block_cols, group_cols, lines):
    lanes = stack.shape[1] // lines
    basis_cols = part.shape[1] // 2
    return pl.pallas_call(
        functools.partial(finish_kernel, row_count),
        out_shape=(
            f32(block_cols * lines, lanes), f32(group_cols, block_cols), f32(block_cols, block_cols),
        ),
        in_specs=[SMEM] + [VMEM] * 3,
        out_specs=(VMEM, VMEM, VMEM),
        scratch_shapes=[pltpu.VMEM((basis_cols, block_cols), jnp.float32)],
        name="finish",
    )(place, part, other, stack)


def shards(
    x_block, basis, material, k0_blocks, k0_diag, ke_blocks, mass, velocities, shifts, sample
):
    block_cols, comps, extent_x, rows, lanes = x_block.shape
    group_cols = basis.shape[0]
    lines = comps * rows
    row_count = float(comps * extent_x * lax.axis_size("space") * basis.shape[3] * lanes)

    x_rows = x_block.reshape(block_cols * lines, lanes)
    sent, first_row, last_row = pack(basis, x_rows, block_cols)
    basis_rows = lax.all_to_all(sent, "basis", 0, 0).reshape(-1, lanes)
    halos = (
        from_lower(x_rows, "space"),
        from_upper(x_rows, "space"),
        from_lower(last_row, "basis"),
        from_upper(first_row, "basis"),
    )
    tables = stencil_tables(k0_blocks, k0_diag, ke_blocks, mass, velocities, shifts, sample)
    table = tables.reshape(tables.shape[0], -1).T
    applied = stencil(x_rows, halos, table, material.reshape(rows, lanes), comps)
    stack, part = sums(basis_rows, applied)
    part, other = exchange_total(part)
    place = lax.axis_index("basis").astype(jnp.int32).reshape(1)
    block, coeffs, upper = finish(
        place, part, other, stack, row_count, block_cols, group_cols, lines
    )
    return (block.reshape(x_block.shape), coeffs, upper)


def solution(mesh):
    in_specs = (
        P(None, None, "space", "basis", None),
        P("basis", None, "space", None, None),
        P("space", "basis", None),
        P(),
        P(),
        P(),
        P(),
        P(),
        P(),
        P(),
    )
    out_specs = (P(None, None, "space", "basis", None), P("basis", None), P())
    return jax.shard_map(shards, mesh=mesh, in_specs=in_specs, out_specs=out_specs, check_vma=False)
```

```python
import functools

import jax
import jax.numpy as jnp
from jax import lax
from jax.experimental import pallas as pl
from jax.experimental.pallas import tpu as pltpu
from jax.sharding import PartitionSpec as P

exact_precision = lax.Precision.HIGHEST
VMEM = pl.BlockSpec(memory_space=pltpu.VMEM)
SMEM = pl.BlockSpec(memory_space=pltpu.SMEM)
HBM = pl.BlockSpec(memory_space=pltpu.HBM)


def f32(*shape):
    return jax.ShapeDtypeStruct(shape, jnp.float32)


def from_lower(values, axis):
    count = lax.axis_size(axis)
    return lax.ppermute(values, axis, [(i, i + 1) for i in range(count - 1)])


def from_upper(values, axis):
    count = lax.axis_size(axis)
    return lax.ppermute(values, axis, [(i + 1, i) for i in range(count - 1)])


def stencil_tables(k0_blocks, k0_diag, ke_blocks, mass, velocities, shifts, sample):
    velocity = jnp.take(velocities, sample, axis=0)[0]
    sigma_value = jnp.take(shifts, sample, axis=0)[0]
    center = (k0_diag - sigma_value * mass)[:, :, None] * jnp.eye(3, dtype=jnp.float32)
    tables = k0_blocks - velocity * velocity * ke_blocks
    return tables.at[:, 0].add(center)


def partners(count):
    return range(1, count), [k for k in range(1, count) if k & (k + 1) == 0]


def pack_kernel(comps, place_ref, basis_ref, x_ref, *refs):
    *piece_refs, x_out_ref, sems = refs
    group_cols = basis_ref.shape[0]
    rows, lanes = piece_refs[0].shape[2:]
    block_cols = x_ref.shape[0] // (comps * rows)
    place = place_ref[0]
    x_copy = pltpu.make_async_copy(x_ref, x_out_ref, sems.at[len(piece_refs)])
    x_copy.start()
    copies = []
    for k, piece_ref in enumerate(piece_refs):
        start = pl.multiple_of((place ^ k) * rows, rows)
        copies.append(
            pltpu.make_async_copy(
                basis_ref.at[:, :, 0, pl.ds(start, rows), :],
                piece_ref.at[pl.ds(0, group_cols)],
                sems.at[k],
            )
        )
        copies[-1].start()
    x_copy.wait()
    with_edge = [k for k in partners(len(piece_refs))[1]]
    for comp in range(comps):
        first, last = (
            x_out_ref[pl.ds(comp * rows + row, block_cols, stride=comps * rows), :]
            for row in (0, rows - 1)
        )
        for k in with_edge:
            edge = jnp.where((place ^ k) > place, last, first)
            for part in range(block_cols // rows):
                tile = comp * (block_cols // rows) + part
                piece_refs[k][group_cols + tile // comps, tile % comps] = edge[
                    part * rows : (part + 1) * rows
                ]
    for copy in copies:
        copy.wait()


def pack(place, basis, x_rows, block_cols):
    group_cols, comps, _, full_y, lanes = basis.shape
    count = lax.axis_size("basis")
    rows = full_y // count
    with_edge = partners(count)[1]
    more = block_cols // rows
    pieces = [
        f32(group_cols + (more if k in with_edge else 0), comps, rows, lanes) for k in range(count)
    ]
    return pl.pallas_call(
        functools.partial(pack_kernel, comps),
        out_shape=(*pieces, f32(*x_rows.shape)),
        in_specs=[SMEM, HBM, HBM],
        out_specs=(VMEM,) * (count + 1),
        scratch_shapes=[pltpu.SemaphoreType.DMA((count + 1,))],
        name="pack",
    )(place, basis, x_rows)


def stencil_kernel(
    comps, edge_ks, place_ref, x_ref, before_x_ref, after_x_ref, table_ref, material_ref, *refs
):
    *edge_refs, applied_ref = refs
    place = place_ref[0]
    rows, lanes = material_ref.shape
    levels = table_ref.shape[1]
    block_cols = x_ref.shape[0] // (comps * rows)
    lane = lax.broadcasted_iota(jnp.int32, (block_cols, lanes), 1)
    level = lax.broadcasted_iota(jnp.int32, (levels, lanes), 0)

    def line(ref, comp, row):
        return ref[pl.ds(comp * rows + row, block_cols, stride=comps * rows), :]

    def edge(comp, step):
        result = jnp.zeros((block_cols, lanes), jnp.float32)
        for k, ref in zip(edge_ks, edge_refs):
            begin = ref.shape[0] - comps * block_cols + comp * block_cols
            here = (place ^ k) == place + step
            result = jnp.where(here, ref[pl.ds(begin, block_cols), :], result)
        return result

    for row in range(rows):
        chosen = (jnp.broadcast_to(material_ref[row : row + 1, :], (levels, lanes)) == level)
        fields = jnp.dot(
            table_ref[...], chosen.astype(jnp.float32),
            precision=exact_precision, preferred_element_type=jnp.float32,
        )
        sums = [None] * comps
        for comp in range(comps):
            centre = line(x_ref, comp, row)
            views = [
                centre,
                line(before_x_ref, comp, row),
                line(after_x_ref, comp, row),
                line(x_ref, comp, row - 1) if row > 0 else edge(comp, -1),
                line(x_ref, comp, row + 1) if row < rows - 1 else edge(comp, 1),
                jnp.where(lane == 0, 0.0, pltpu.roll(centre, 1, 1)),
                jnp.where(lane == lanes - 1, 0.0, pltpu.roll(centre, lanes - 1, 1)),
            ]
            for offset, view in enumerate(views):
                for out in range(comps):
                    entry = (offset * comps + out) * comps + comp
                    term = fields[entry : entry + 1, :] * view
                    sums[out] = term if sums[out] is None else sums[out] + term
        for out in range(comps):
            applied_ref[out * rows + row] = sums[out]


def stencil(place, x_rows, halos, edges, table, material, comps):
    rows, lanes = material.shape
    block_cols = x_rows.shape[0] // (comps * rows)
    return pl.pallas_call(
        functools.partial(stencil_kernel, comps, tuple(edges)),
        out_shape=f32(comps * rows, block_cols, lanes),
        in_specs=[SMEM] + [VMEM] * (5 + len(edges)),
        out_specs=VMEM,
        name="stencil",
    )(place, x_rows, *halos, table, material, *edges.values())


def three_parts(values):
    high = values.astype(jnp.bfloat16)
    rest = values - high.astype(jnp.float32)
    middle = rest.astype(jnp.bfloat16)
    low = (rest - middle.astype(jnp.float32)).astype(jnp.bfloat16)
    return high, middle, low


def sums_kernel(group_cols, place_ref, applied_ref, *refs):
    *piece_refs, stack_ref, sums_ref = refs
    lines, block_cols, lanes = applied_ref.shape
    basis_cols = len(piece_refs) * group_cols
    joined = basis_cols + block_cols

    def store(begin, line, values):
        for index, part in enumerate(three_parts(values)):
            there = pl.ds(index * joined + begin, values.shape[0])
            stack_ref[there, pl.ds(line * lanes, lanes)] = part

    for k, piece_ref in enumerate(piece_refs):
        begin = pl.multiple_of((place_ref[0] ^ k) * group_cols, group_cols)
        for line in range(lines):
            store(begin, line, piece_ref[pl.ds(line, group_cols, stride=lines), :])
    for line in range(lines):
        store(basis_cols, line, applied_ref[line])
    stack = stack_ref[...]
    products = lax.dot_general(
        stack, stack, (((1,), (1,)), ((), ())), preferred_element_type=jnp.float32
    )
    wide = products[:joined] + products[joined : 2 * joined] + products[2 * joined :]
    total = wide[:, :joined] + wide[:, joined : 2 * joined] + wide[:, 2 * joined :]
    half = basis_cols // 2
    sums_ref[pl.ds(0, half), :] = jnp.concatenate(
        (total[:half, :basis_cols], total[half:basis_cols, :basis_cols]), axis=1
    )
    sums_ref[pl.ds(half, block_cols), :] = jnp.concatenate(
        (total[basis_cols:], jnp.zeros((block_cols, sums_ref.shape[1] - joined), jnp.float32)), axis=1
    )


def sums(place, applied, pieces, group_cols):
    lines, block_cols, lanes = applied.shape
    basis_cols = len(pieces) * group_cols
    joined = basis_cols + block_cols
    return pl.pallas_call(
        functools.partial(sums_kernel, group_cols),
        out_shape=(
            jax.ShapeDtypeStruct((3 * joined, lines * lanes), jnp.bfloat16),
            f32(basis_cols // 2 + block_cols, 2 * basis_cols),
        ),
        in_specs=[SMEM] + [VMEM] * (1 + len(pieces)),
        out_specs=(VMEM, VMEM),
        name="sums",
    )(place, applied, *pieces)


def exchange_sum(part, axis):
    count = lax.axis_size(axis)
    terms = [part] + [
        lax.ppermute(part, axis, [(i, i ^ k) for i in range(count)]) for k in range(1, count)
    ]
    while len(terms) > 1:
        terms = [a + b for a, b in zip(terms[::2], terms[1::2])]
    return terms[0]


def exchange(part, axis):
    count = lax.axis_size(axis)
    return lax.all_to_all(jnp.broadcast_to(part[None], (count,) + part.shape), axis, 0, 0)


def finish_kernel(
    row_count, place_ref, parts_ref, stack_ref, block_ref, coeffs_ref, upper_ref,
    coeffs_scratch,
):
    block_cols = upper_ref.shape[0]
    basis_cols = parts_ref.shape[2] // 2
    half = basis_cols // 2
    joined = basis_cols + block_cols
    lines = block_ref.shape[0] // block_cols
    lanes = block_ref.shape[1]
    total = jnp.sum(parts_ref[...], axis=0) / row_count
    gram = jnp.concatenate((total[:half, :basis_cols], total[:half, basis_cols:]), axis=0)
    first = total[half:, :basis_cols]
    block_gram = total[half:, basis_cols:joined]

    def times(left, right, right_dim=0):
        return lax.dot_general(
            left, right, (((1,), (right_dim,)), ((), ())),
            precision=exact_precision, preferred_element_type=jnp.float32,
        )

    coeffs = first + (first - times(first, gram))
    image = times(coeffs, gram)
    matrix = block_gram - times(coeffs, first, 1) - times(first - image, coeffs, 1)
    coeffs_scratch[...] = coeffs.T
    group_cols = coeffs_ref.shape[0]
    start = pl.multiple_of(place_ref[0] * group_cols, group_cols)
    coeffs_ref[...] = coeffs_scratch[pl.ds(start, group_cols), :]

    row = lax.broadcasted_iota(jnp.int32, (block_cols, block_cols), 0)
    column = lax.broadcasted_iota(jnp.int32, (block_cols, block_cols), 1)
    unit = jnp.where(row == column, 1.0, 0.0)
    pad = jnp.zeros((block_cols, 2 * basis_cols - joined - block_cols), jnp.float32)
    work = jnp.concatenate((-coeffs, unit, matrix, pad), axis=1)
    height = lax.broadcasted_iota(jnp.int32, work.shape, 0)
    for step in range(block_cols):
        pivots = jnp.broadcast_to(work[:, joined + step : joined + step + 1], work.shape)
        pivot = pivots[step : step + 1, :]
        pivot_row = work[step : step + 1, :]
        scaled = pivot_row / pivot
        new_row = pivot_row * lax.rsqrt(pivot)
        work = jnp.where(
            height > step, work - pivots * scaled, jnp.where(height == step, new_row, work)
        )
    upper_ref[...] = work[:, joined : joined + block_cols]
    weights = three_parts(work[:, :joined])
    wide = jnp.concatenate(
        [jnp.concatenate((part, part, part), axis=1) for part in weights], axis=0
    )
    result = jnp.dot(wide, stack_ref[...], preferred_element_type=jnp.float32)
    result = result[:block_cols] + result[block_cols : 2 * block_cols] + result[2 * block_cols :]
    for line in range(lines):
        block_ref[pl.ds(line, block_cols, stride=lines), :] = result[
            :, line * lanes : (line + 1) * lanes
        ]


def finish(place, parts, stack, row_count, block_cols, group_cols, lines):
    lanes = stack.shape[1] // lines
    basis_cols = parts.shape[2] // 2
    return pl.pallas_call(
        functools.partial(finish_kernel, row_count),
        out_shape=(
            f32(block_cols * lines, lanes), f32(group_cols, block_cols), f32(block_cols, block_cols),
        ),
        in_specs=[SMEM] + [VMEM] * 2,
        out_specs=(VMEM, VMEM, VMEM),
        scratch_shapes=[pltpu.VMEM((basis_cols, block_cols), jnp.float32)],
        name="finish",
    )(place, parts, stack)


def shards(
    x_block, basis, material, k0_blocks, k0_diag, ke_blocks, mass, velocities, shifts, sample
):
    block_cols, comps, extent_x, rows, lanes = x_block.shape
    group_cols = basis.shape[0]
    lines = comps * rows
    row_count = float(comps * extent_x * lax.axis_size("space") * basis.shape[3] * lanes)

    place = lax.axis_index("basis").astype(jnp.int32).reshape(1)
    count = lax.axis_size("basis")
    *pieces, x_rows = pack(place, basis, x_block.reshape(block_cols * lines, lanes), block_cols)
    for k in reversed(partners(count)[0]):
        pieces[k] = lax.ppermute(pieces[k], "basis", [(i, i ^ k) for i in range(count)])
    pieces = [piece.reshape(-1, lanes) for piece in pieces]
    halos = (from_lower(x_rows, "space"), from_upper(x_rows, "space"))
    tables = stencil_tables(k0_blocks, k0_diag, ke_blocks, mass, velocities, shifts, sample)
    table = tables.reshape(tables.shape[0], -1).T
    edges = {k: pieces[k] for k in partners(count)[1]}
    applied = stencil(place, x_rows, halos, edges, table, material.reshape(rows, lanes), comps)
    stack, part = sums(place, applied, pieces, group_cols)
    parts = exchange(exchange_sum(part, "basis"), "space")
    block, coeffs, upper = finish(place, parts, stack, row_count, block_cols, group_cols, lines)
    return (block.reshape(x_block.shape), coeffs, upper)


def solution(mesh):
    in_specs = (
        P(None, None, "space", "basis", None),
        P("basis", None, "space", None, None),
        P("space", "basis", None),
        P(),
        P(),
        P(),
        P(),
        P(),
        P(),
        P(),
    )
    out_specs = (P(None, None, "space", "basis", None), P("basis", None), P())
    return jax.shard_map(shards, mesh=mesh, in_specs=in_specs, out_specs=out_specs, check_vma=False)
```

```python
import functools

import jax
import jax.numpy as jnp
from jax import lax
from jax.experimental import pallas as pl
from jax.experimental.pallas import tpu as pltpu
from jax.sharding import PartitionSpec as P

exact_precision = lax.Precision.HIGHEST
VMEM = pl.BlockSpec(memory_space=pltpu.VMEM)
SMEM = pl.BlockSpec(memory_space=pltpu.SMEM)
HBM = pl.BlockSpec(memory_space=pltpu.HBM)


def f32(*shape):
    return jax.ShapeDtypeStruct(shape, jnp.float32)


def from_lower(values, axis):
    count = lax.axis_size(axis)
    return lax.ppermute(values, axis, [(i, i + 1) for i in range(count - 1)])


def from_upper(values, axis):
    count = lax.axis_size(axis)
    return lax.ppermute(values, axis, [(i + 1, i) for i in range(count - 1)])


def partners(count):
    return range(1, count), [k for k in range(1, count) if k & (k + 1) == 0]


def pack_kernel(comps, place_ref, basis_ref, x_ref, material_ref, *refs):
    *piece_refs, x_out_ref, material_out_ref, sems = refs
    count = len(piece_refs)
    tiles, _, rows, lanes = basis_ref.shape
    block_cols = x_ref.shape[0] // (comps * rows)
    place = place_ref[0]
    x_copy = pltpu.make_async_copy(x_ref, x_out_ref, sems.at[count])
    x_copy.start()
    copies = [pltpu.make_async_copy(material_ref, material_out_ref, sems.at[count + 1])]
    for k in reversed(range(count)):
        copies.append(
            pltpu.make_async_copy(
                basis_ref.at[:, place ^ k], piece_refs[k].at[pl.ds(0, tiles)], sems.at[k]
            )
        )
    for copy in copies:
        copy.start()
    x_copy.wait()
    for comp in range(comps):
        first, last = (
            x_out_ref[pl.ds(comp * rows + row, block_cols, stride=comps * rows), :]
            for row in (0, rows - 1)
        )
        for k in partners(count)[1]:
            edge = jnp.where((place ^ k) > place, last, first)
            for part in range(block_cols // rows):
                piece_refs[k][tiles + comp * (block_cols // rows) + part] = edge[
                    part * rows : (part + 1) * rows
                ]
    for copy in copies:
        copy.wait()


def pack(place, basis, x_rows, material, block_cols):
    group_cols, comps, _, full_y, lanes = basis.shape
    count = lax.axis_size("basis")
    rows = full_y // count
    tiles = group_cols * comps
    edge_tiles = block_cols * comps // rows
    pieces = [
        f32(tiles + (edge_tiles if k in partners(count)[1] else 0), rows, lanes)
        for k in range(count)
    ]
    return pl.pallas_call(
        functools.partial(pack_kernel, comps),
        out_shape=(*pieces, f32(*x_rows.shape), jax.ShapeDtypeStruct(material.shape, jnp.int32)),
        in_specs=[SMEM, HBM, HBM, HBM],
        out_specs=(VMEM,) * (count + 2),
        scratch_shapes=[pltpu.SemaphoreType.DMA((count + 2,))],
        name="pack",
    )(place, basis.reshape(tiles, count, rows, lanes), x_rows, material)


def three_parts(values):
    high = values.astype(jnp.bfloat16)
    rest = values - high.astype(jnp.float32)
    middle = rest.astype(jnp.bfloat16)
    low = (rest - middle.astype(jnp.float32)).astype(jnp.bfloat16)
    return high, middle, low


def line_of(ref, comp, row, comps, rows, block_cols):
    return ref[pl.ds(comp * rows + row, block_cols, stride=comps * rows), :]


def ahead_kernel(
    sample_ref, velocities_ref, shifts_ref, k0_ref, ke_ref, diag_ref, mass_ref, material_ref,
    x_ref, own_ref, fields_ref, applied_ref, stack_ref,
):
    comps, _, levels, offsets = k0_ref.shape
    rows, lanes = material_ref.shape
    lines = comps * rows
    block_cols = x_ref.shape[0] // lines
    velocity = velocities_ref[sample_ref[0]]
    sigma = shifts_ref[sample_ref[0]]
    entry_rows = fields_ref.shape[1]
    stride = entry_rows // (comps * comps)
    gap = jnp.zeros((levels, stride - offsets), jnp.float32)
    wide = []
    for out in range(comps):
        for comp in range(comps):
            wide += [k0_ref[out, comp] - velocity * velocity * ke_ref[out, comp], gap]
    wide.append(jnp.zeros((levels, lanes - entry_rows), jnp.float32))
    table = jnp.concatenate(wide, axis=1).T[:entry_rows]
    entry = lax.broadcasted_iota(jnp.int32, table.shape, 0)
    for comp in range(comps):
        centre = diag_ref[comp : comp + 1, :] - sigma * mass_ref[comp : comp + 1, :]
        table = table + jnp.where(entry == comp * (comps + 1) * stride, centre, 0.0)

    lane = lax.broadcasted_iota(jnp.int32, (block_cols, lanes), 1)
    level = lax.broadcasted_iota(jnp.int32, (levels, lanes), 0)
    for row in range(rows):
        chosen = jnp.broadcast_to(material_ref[row : row + 1, :], (levels, lanes)) == level
        fields = jnp.dot(
            table, chosen.astype(jnp.float32),
            precision=exact_precision, preferred_element_type=jnp.float32,
        )
        fields_ref[row] = fields
        sums = [None] * comps
        for comp in range(comps):
            centre = line_of(x_ref, comp, row, comps, rows, block_cols)
            views = {
                0: centre,
                5: jnp.where(lane == 0, 0.0, pltpu.roll(centre, 1, 1)),
                6: jnp.where(lane == lanes - 1, 0.0, pltpu.roll(centre, lanes - 1, 1)),
            }
            if row > 0:
                views[3] = line_of(x_ref, comp, row - 1, comps, rows, block_cols)
            if row < rows - 1:
                views[4] = line_of(x_ref, comp, row + 1, comps, rows, block_cols)
            for offset, view in views.items():
                for out in range(comps):
                    place = (out * comps + comp) * stride + offset
                    term = fields[place : place + 1, :] * view
                    sums[out] = term if sums[out] is None else sums[out] + term
        for out in range(comps):
            applied_ref[out * rows + row] = sums[out]

    group_cols = own_ref.shape[0] // lines
    for line in range(lines):
        values = own_ref[pl.ds(line, group_cols, stride=lines), :]
        for index, part in enumerate(three_parts(values)):
            stack_ref[pl.ds(index * group_cols, group_cols), pl.ds(line * lanes, lanes)] = part


def ahead(sample, velocities, shifts, k0, ke, diag, mass, material, x_rows, own, comps):
    rows, lanes = material.shape
    lines = comps * rows
    offsets = k0.shape[1]
    stride = -(-offsets // 8) * 8
    return pl.pallas_call(
        ahead_kernel,
        out_shape=(
            f32(rows, comps * comps * stride, lanes),
            f32(lines, x_rows.shape[0] // lines, lanes),
            jax.ShapeDtypeStruct((3 * own.shape[0] // lines, lines * lanes), jnp.bfloat16),
        ),
        in_specs=[SMEM] * 3 + [VMEM] * 7,
        out_specs=(VMEM,) * 3,
        name="ahead",
    )(
        sample, velocities, shifts,
        jnp.transpose(k0, (2, 3, 0, 1)), jnp.transpose(ke, (2, 3, 0, 1)), diag.T, mass.T,
        material, x_rows, own,
    )


def sums_kernel(
    comps, edge_ks, place_ref, fields_ref, applied_ref, own_ref, before_x_ref, after_x_ref, *refs
):
    *piece_refs, stack_ref, sums_ref = refs
    lines, block_cols, lanes = applied_ref.shape
    rows = lines // comps
    stride = fields_ref.shape[1] // (comps * comps)
    group_cols = own_ref.shape[0] // 3
    basis_cols = (1 + len(piece_refs)) * group_cols
    joined = basis_cols + block_cols
    place = place_ref[0]

    def store(begin, line, values):
        for index, part in enumerate(three_parts(values)):
            there = pl.ds(index * joined + begin, values.shape[0])
            stack_ref[there, pl.ds(line * lanes, lanes)] = part

    begin = pl.multiple_of(place * group_cols, group_cols)
    for index in range(3):
        stack_ref[pl.ds(index * joined + begin, group_cols), :] = own_ref[
            pl.ds(index * group_cols, group_cols), :
        ]
    for k, piece_ref in enumerate(piece_refs, 1):
        begin = pl.multiple_of((place ^ k) * group_cols, group_cols)
        for line in range(lines):
            store(begin, line, piece_ref[pl.ds(line, group_cols, stride=lines), :])

    def edge(comp, step):
        result = jnp.zeros((block_cols, lanes), jnp.float32)
        for k in edge_ks:
            ref = piece_refs[k - 1]
            begin = ref.shape[0] - (comps - comp) * block_cols
            here = (place ^ k) == place + step
            result = jnp.where(here, ref[pl.ds(begin, block_cols), :], result)
        return result

    for row in range(rows):
        totals = [applied_ref[out * rows + row] for out in range(comps)]
        for comp in range(comps):
            views = {
                1: line_of(before_x_ref, comp, row, comps, rows, block_cols),
                2: line_of(after_x_ref, comp, row, comps, rows, block_cols),
            }
            if row == 0:
                views[3] = edge(comp, -1)
            if row == rows - 1:
                views[4] = edge(comp, 1)
            for offset, view in views.items():
                for out in range(comps):
                    entry = (out * comps + comp) * stride + offset
                    totals[out] = totals[out] + fields_ref[row, entry : entry + 1, :] * view
        for out in range(comps):
            store(basis_cols, out * rows + row, totals[out])

    stack = stack_ref[...]
    products = lax.dot_general(
        stack, stack, (((1,), (1,)), ((), ())), preferred_element_type=jnp.float32
    )
    wide = products[:joined] + products[joined : 2 * joined] + products[2 * joined :]
    total = wide[:, :joined] + wide[:, joined : 2 * joined] + wide[:, 2 * joined :]
    half = basis_cols // 2
    sums_ref[pl.ds(0, half), :] = jnp.concatenate(
        (total[:half, :basis_cols], total[half:basis_cols, :basis_cols]), axis=1
    )
    sums_ref[pl.ds(half, block_cols), :] = jnp.concatenate(
        (total[basis_cols:], jnp.zeros((block_cols, sums_ref.shape[1] - joined), jnp.float32)), axis=1
    )


def sums(place, fields, applied, own, halos, pieces, comps):
    lines, block_cols, lanes = applied.shape
    basis_cols = (1 + len(pieces)) * (own.shape[0] // 3)
    joined = basis_cols + block_cols
    return pl.pallas_call(
        functools.partial(sums_kernel, comps, partners(1 + len(pieces))[1]),
        out_shape=(
            jax.ShapeDtypeStruct((3 * joined, lines * lanes), jnp.bfloat16),
            f32(basis_cols // 2 + block_cols, 2 * basis_cols),
        ),
        in_specs=[SMEM] + [VMEM] * (3 + len(halos) + len(pieces)),
        out_specs=(VMEM, VMEM),
        name="sums",
    )(place, fields, applied, own, *halos, *pieces)


def exchange_sum(part, axis):
    count = lax.axis_size(axis)
    terms = [part] + [
        lax.ppermute(part, axis, [(i, i ^ k) for i in range(count)]) for k in range(1, count)
    ]
    while len(terms) > 1:
        terms = [a + b for a, b in zip(terms[::2], terms[1::2])]
    return terms[0]


def exchange(part, axis):
    count = lax.axis_size(axis)
    return lax.all_to_all(jnp.broadcast_to(part[None], (count,) + part.shape), axis, 0, 0)


def finish_kernel(
    row_count, place_ref, parts_ref, stack_ref, block_ref, coeffs_ref, upper_ref,
    coeffs_scratch,
):
    block_cols = upper_ref.shape[0]
    basis_cols = parts_ref.shape[2] // 2
    half = basis_cols // 2
    joined = basis_cols + block_cols
    lines = block_ref.shape[0] // block_cols
    lanes = block_ref.shape[1]
    total = jnp.sum(parts_ref[...], axis=0) / row_count
    gram = jnp.concatenate((total[:half, :basis_cols], total[:half, basis_cols:]), axis=0)
    first = total[half:, :basis_cols]
    block_gram = total[half:, basis_cols:joined]

    def times(left, right, right_dim=0):
        return lax.dot_general(
            left, right, (((1,), (right_dim,)), ((), ())),
            precision=exact_precision, preferred_element_type=jnp.float32,
        )

    coeffs = first + (first - times(first, gram))
    image = times(coeffs, gram)
    matrix = block_gram - times(coeffs, first, 1) - times(first - image, coeffs, 1)
    coeffs_scratch[...] = coeffs.T
    group_cols = coeffs_ref.shape[0]
    start = pl.multiple_of(place_ref[0] * group_cols, group_cols)
    coeffs_ref[...] = coeffs_scratch[pl.ds(start, group_cols), :]

    row = lax.broadcasted_iota(jnp.int32, (block_cols, block_cols), 0)
    column = lax.broadcasted_iota(jnp.int32, (block_cols, block_cols), 1)
    unit = jnp.where(row == column, 1.0, 0.0)
    pad = jnp.zeros((block_cols, 2 * basis_cols - joined - block_cols), jnp.float32)
    work = jnp.concatenate((-coeffs, unit, matrix, pad), axis=1)
    height = lax.broadcasted_iota(jnp.int32, work.shape, 0)
    for step in range(block_cols):
        pivots = jnp.broadcast_to(work[:, joined + step : joined + step + 1], work.shape)
        pivot = pivots[step : step + 1, :]
        pivot_row = work[step : step + 1, :]
        scaled = pivot_row / pivot
        new_row = pivot_row * lax.rsqrt(pivot)
        work = jnp.where(
            height > step, work - pivots * scaled, jnp.where(height == step, new_row, work)
        )
    upper_ref[...] = work[:, joined : joined + block_cols]
    weights = three_parts(work[:, :joined])
    wide = jnp.concatenate(
        [jnp.concatenate((part, part, part), axis=1) for part in weights], axis=0
    )
    result = jnp.dot(wide, stack_ref[...], preferred_element_type=jnp.float32)
    result = result[:block_cols] + result[block_cols : 2 * block_cols] + result[2 * block_cols :]
    for line in range(lines):
        block_ref[pl.ds(line, block_cols, stride=lines), :] = result[
            :, line * lanes : (line + 1) * lanes
        ]


def finish(place, parts, stack, row_count, block_cols, group_cols, lines):
    lanes = stack.shape[1] // lines
    basis_cols = parts.shape[2] // 2
    return pl.pallas_call(
        functools.partial(finish_kernel, row_count),
        out_shape=(
            f32(block_cols * lines, lanes), f32(group_cols, block_cols), f32(block_cols, block_cols),
        ),
        in_specs=[SMEM] + [VMEM] * 2,
        out_specs=(VMEM, VMEM, VMEM),
        scratch_shapes=[pltpu.VMEM((basis_cols, block_cols), jnp.float32)],
        name="finish",
    )(place, parts, stack)


def shards(
    x_block, basis, material, k0_blocks, k0_diag, ke_blocks, mass, velocities, shifts, sample
):
    block_cols, comps, extent_x, rows, lanes = x_block.shape
    group_cols = basis.shape[0]
    lines = comps * rows
    row_count = float(comps * extent_x * lax.axis_size("space") * basis.shape[3] * lanes)

    place = lax.axis_index("basis").astype(jnp.int32).reshape(1)
    count = lax.axis_size("basis")
    own, *pieces, x_rows, material = pack(
        place, basis, x_block.reshape(block_cols * lines, lanes), material.reshape(rows, lanes), block_cols
    )
    halos = [None, None]
    order = (3, "upper", 2, "lower", 1)
    pieces = dict(enumerate(pieces, 1))
    for name in order:
        if name == "lower":
            halos[0] = from_lower(x_rows, "space")
        elif name == "upper":
            halos[1] = from_upper(x_rows, "space")
        else:
            pieces[name] = lax.ppermute(pieces[name], "basis", [(i, i ^ name) for i in range(count)])
    pieces = [pieces[k].reshape(-1, lanes) for k in partners(count)[0]]
    fields, applied, own = ahead(
        sample, velocities, shifts, k0_blocks, ke_blocks, k0_diag, mass, material, x_rows,
        own.reshape(-1, lanes), comps,
    )
    stack, part = sums(place, fields, applied, own, halos, pieces, comps)
    parts = exchange(exchange_sum(part, "basis"), "space")
    block, coeffs, upper = finish(place, parts, stack, row_count, block_cols, group_cols, lines)
    return (block.reshape(x_block.shape), coeffs, upper)


def solution(mesh):
    in_specs = (
        P(None, None, "space", "basis", None),
        P("basis", None, "space", None, None),
        P("space", "basis", None),
        P(),
        P(),
        P(),
        P(),
        P(),
        P(),
        P(),
    )
    out_specs = (P(None, None, "space", "basis", None), P("basis", None), P())
    return jax.shard_map(shards, mesh=mesh, in_specs=in_specs, out_specs=out_specs, check_vma=False)
```

```python
import functools

import jax
import jax.numpy as jnp
from jax import lax
from jax.experimental import pallas as pl
from jax.experimental.pallas import tpu as pltpu
from jax.sharding import PartitionSpec as P

exact_precision = lax.Precision.HIGHEST
VMEM = pl.BlockSpec(memory_space=pltpu.VMEM)
SMEM = pl.BlockSpec(memory_space=pltpu.SMEM)
HBM = pl.BlockSpec(memory_space=pltpu.HBM)
SCRATCH = pltpu.CompilerParams(vmem_limit_bytes=8 * 2**20)


def f32(*shape):
    return jax.ShapeDtypeStruct(shape, jnp.float32)


def near(*shape, dtype=jnp.float32):
    return pltpu.VMEM(shape, dtype)


def kept(*arrays):
    return [pltpu.with_memory_space_constraint(array, pltpu.VMEM) for array in arrays]


def far(*arrays):
    return [pltpu.with_memory_space_constraint(array, pltpu.HBM) for array in arrays]


def from_lower(values, axis):
    count = lax.axis_size(axis)
    return lax.ppermute(values, axis, [(i, i + 1) for i in range(count - 1)])


def from_upper(values, axis):
    count = lax.axis_size(axis)
    return lax.ppermute(values, axis, [(i + 1, i) for i in range(count - 1)])


def partners(count):
    return range(1, count), [k for k in range(1, count) if k & (k + 1) == 0]


def pack_kernel(comps, place_ref, basis_ref, x_ref, material_ref, *refs):
    *piece_refs, x_out_ref, material_out_ref, sems = refs
    count = len(piece_refs)
    tiles, _, rows, lanes = basis_ref.shape
    block_cols = x_ref.shape[0] // (comps * rows)
    place = place_ref[0]
    x_copy = pltpu.make_async_copy(x_ref, x_out_ref, sems.at[count])
    x_copy.start()
    copies = [pltpu.make_async_copy(material_ref, material_out_ref, sems.at[count + 1])]
    for k in reversed(range(count)):
        copies.append(
            pltpu.make_async_copy(
                basis_ref.at[:, place ^ k], piece_refs[k].at[pl.ds(0, tiles)], sems.at[k]
            )
        )
    for copy in copies:
        copy.start()
    x_copy.wait()
    for comp in range(comps):
        first, last = (
            x_out_ref[pl.ds(comp * rows + row, block_cols, stride=comps * rows), :]
            for row in (0, rows - 1)
        )
        for k in partners(count)[1]:
            edge = jnp.where((place ^ k) > place, last, first)
            for part in range(block_cols // rows):
                piece_refs[k][tiles + comp * (block_cols // rows) + part] = edge[
                    part * rows : (part + 1) * rows
                ]
    for copy in copies:
        copy.wait()


def pack(place, basis, x_rows, material, block_cols):
    group_cols, comps, _, full_y, lanes = basis.shape
    count = lax.axis_size("basis")
    rows = full_y // count
    tiles = group_cols * comps
    edge_tiles = block_cols * comps // rows
    pieces = [
        near(tiles + (edge_tiles if k in partners(count)[1] else 0), rows, lanes)
        for k in range(count)
    ]
    return pl.pallas_call(
        functools.partial(pack_kernel, comps),
        out_shape=(*pieces, near(*x_rows.shape), near(*material.shape, dtype=jnp.int32)),
        in_specs=[SMEM, HBM, HBM, HBM],
        out_specs=(VMEM,) * (count + 2),
        scratch_shapes=[pltpu.SemaphoreType.DMA((count + 2,))],
        compiler_params=SCRATCH,
        name="pack",
    )(place, *far(basis.reshape(tiles, count, rows, lanes), x_rows, material))


def three_parts(values):
    high = values.astype(jnp.bfloat16)
    rest = values - high.astype(jnp.float32)
    middle = rest.astype(jnp.bfloat16)
    low = (rest - middle.astype(jnp.float32)).astype(jnp.bfloat16)
    return high, middle, low


def line_of(ref, comp, row, comps, rows, block_cols):
    return ref[pl.ds(comp * rows + row, block_cols, stride=comps * rows), :]


def ahead_kernel(
    sample_ref, *refs
):
    far_refs, refs = refs[:6], refs[6:]
    material_ref, x_ref, own_ref, fields_ref, applied_ref, stack_ref, *near_refs, sems = refs
    velocities_ref, shifts_ref, k0_ref, ke_ref, diag_ref, mass_ref = near_refs
    copies = [
        pltpu.make_async_copy(source, target, sems.at[index])
        for index, (source, target) in enumerate(zip(far_refs, near_refs))
    ]
    for copy in copies:
        copy.start()
    group_cols = stack_ref.shape[0] // 3
    for line in range(applied_ref.shape[0]):
        values = own_ref[pl.ds(line, group_cols, stride=applied_ref.shape[0]), :]
        for index, part in enumerate(three_parts(values)):
            there = pl.ds(line * values.shape[1], values.shape[1])
            stack_ref[pl.ds(index * group_cols, group_cols), there] = part
    for copy in copies:
        copy.wait()
    comps, _, levels, offsets = k0_ref.shape
    rows, lanes = material_ref.shape
    lines = comps * rows
    block_cols = x_ref.shape[0] // lines
    velocity = velocities_ref[sample_ref[0]]
    sigma = shifts_ref[sample_ref[0]]
    entry_rows = fields_ref.shape[1]
    stride = entry_rows // (comps * comps)
    gap = jnp.zeros((levels, stride - offsets), jnp.float32)
    wide = []
    for out in range(comps):
        for comp in range(comps):
            wide += [k0_ref[out, comp] - velocity * velocity * ke_ref[out, comp], gap]
    wide.append(jnp.zeros((levels, lanes - entry_rows), jnp.float32))
    table = jnp.concatenate(wide, axis=1).T[:entry_rows]
    entry = lax.broadcasted_iota(jnp.int32, table.shape, 0)
    for comp in range(comps):
        centre = diag_ref[comp : comp + 1, :] - sigma * mass_ref[comp : comp + 1, :]
        table = table + jnp.where(entry == comp * (comps + 1) * stride, centre, 0.0)

    lane = lax.broadcasted_iota(jnp.int32, (block_cols, lanes), 1)
    level = lax.broadcasted_iota(jnp.int32, (levels, lanes), 0)
    for row in range(rows):
        chosen = jnp.broadcast_to(material_ref[row : row + 1, :], (levels, lanes)) == level
        fields = jnp.dot(
            table, chosen.astype(jnp.float32),
            precision=exact_precision, preferred_element_type=jnp.float32,
        )
        fields_ref[row] = fields
        sums = [None] * comps
        for comp in range(comps):
            centre = line_of(x_ref, comp, row, comps, rows, block_cols)
            views = {
                0: centre,
                5: jnp.where(lane == 0, 0.0, pltpu.roll(centre, 1, 1)),
                6: jnp.where(lane == lanes - 1, 0.0, pltpu.roll(centre, lanes - 1, 1)),
            }
            if row > 0:
                views[3] = line_of(x_ref, comp, row - 1, comps, rows, block_cols)
            if row < rows - 1:
                views[4] = line_of(x_ref, comp, row + 1, comps, rows, block_cols)
            for offset, view in views.items():
                for out in range(comps):
                    place = (out * comps + comp) * stride + offset
                    term = fields[place : place + 1, :] * view
                    sums[out] = term if sums[out] is None else sums[out] + term
        for out in range(comps):
            applied_ref[out * rows + row] = sums[out]


def ahead(sample, velocities, shifts, k0, ke, diag, mass, material, x_rows, own, comps):
    rows, lanes = material.shape
    lines = comps * rows
    stride = -(-k0.shape[1] // 8) * 8
    k0, ke = (jnp.transpose(blocks, (2, 3, 0, 1)) for blocks in (k0, ke))
    tables = far(velocities, shifts, k0, ke, diag.T, mass.T)
    return pl.pallas_call(
        ahead_kernel,
        out_shape=(
            near(rows, comps * comps * stride, lanes),
            near(lines, x_rows.shape[0] // lines, lanes),
            near(3 * own.shape[0] // lines, lines * lanes, dtype=jnp.bfloat16),
        ),
        in_specs=[SMEM] + [HBM] * 6 + [VMEM] * 3,
        out_specs=(VMEM,) * 3,
        scratch_shapes=[
            (pltpu.SMEM if array.ndim == 1 else pltpu.VMEM)(array.shape, jnp.float32)
            for array in tables
        ] + [pltpu.SemaphoreType.DMA((len(tables),))],
        compiler_params=SCRATCH,
        name="ahead",
    )(sample, *tables, *kept(material, x_rows, own))


def sums_kernel(
    comps, edge_ks, place_ref, fields_ref, applied_ref, own_ref, before_x_ref, after_x_ref, *refs
):
    *piece_refs, stack_ref, sums_ref = refs
    lines, block_cols, lanes = applied_ref.shape
    rows = lines // comps
    stride = fields_ref.shape[1] // (comps * comps)
    group_cols = own_ref.shape[0] // 3
    basis_cols = (1 + len(piece_refs)) * group_cols
    joined = basis_cols + block_cols
    place = place_ref[0]

    def store(begin, line, values):
        for index, part in enumerate(three_parts(values)):
            there = pl.ds(index * joined + begin, values.shape[0])
            stack_ref[there, pl.ds(line * lanes, lanes)] = part

    begin = pl.multiple_of(place * group_cols, group_cols)
    for index in range(3):
        stack_ref[pl.ds(index * joined + begin, group_cols), :] = own_ref[
            pl.ds(index * group_cols, group_cols), :
        ]
    for k, piece_ref in enumerate(piece_refs, 1):
        begin = pl.multiple_of((place ^ k) * group_cols, group_cols)
        for line in range(lines):
            store(begin, line, piece_ref[pl.ds(line, group_cols, stride=lines), :])

    def edge(comp, step):
        result = jnp.zeros((block_cols, lanes), jnp.float32)
        for k in edge_ks:
            ref = piece_refs[k - 1]
            begin = ref.shape[0] - (comps - comp) * block_cols
            here = (place ^ k) == place + step
            result = jnp.where(here, ref[pl.ds(begin, block_cols), :], result)
        return result

    for row in range(rows):
        totals = [applied_ref[out * rows + row] for out in range(comps)]
        for comp in range(comps):
            views = {
                1: line_of(before_x_ref, comp, row, comps, rows, block_cols),
                2: line_of(after_x_ref, comp, row, comps, rows, block_cols),
            }
            if row == 0:
                views[3] = edge(comp, -1)
            if row == rows - 1:
                views[4] = edge(comp, 1)
            for offset, view in views.items():
                for out in range(comps):
                    entry = (out * comps + comp) * stride + offset
                    totals[out] = totals[out] + fields_ref[row, entry : entry + 1, :] * view
        for out in range(comps):
            store(basis_cols, out * rows + row, totals[out])

    stack = stack_ref[...]
    products = lax.dot_general(
        stack, stack, (((1,), (1,)), ((), ())), preferred_element_type=jnp.float32
    )
    wide = products[:joined] + products[joined : 2 * joined] + products[2 * joined :]
    total = wide[:, :joined] + wide[:, joined : 2 * joined] + wide[:, 2 * joined :]
    half = basis_cols // 2
    sums_ref[pl.ds(0, half), :] = jnp.concatenate(
        (total[:half, :basis_cols], total[half:basis_cols, :basis_cols]), axis=1
    )
    sums_ref[pl.ds(half, block_cols), :] = jnp.concatenate(
        (total[basis_cols:], jnp.zeros((block_cols, sums_ref.shape[1] - joined), jnp.float32)), axis=1
    )


def sums(place, fields, applied, own, halos, pieces, comps):
    lines, block_cols, lanes = applied.shape
    basis_cols = (1 + len(pieces)) * (own.shape[0] // 3)
    joined = basis_cols + block_cols
    return pl.pallas_call(
        functools.partial(sums_kernel, comps, partners(1 + len(pieces))[1]),
        out_shape=(
            near(3 * joined, lines * lanes, dtype=jnp.bfloat16),
            near(basis_cols // 2 + block_cols, 2 * basis_cols),
        ),
        in_specs=[SMEM] + [VMEM] * (3 + len(halos) + len(pieces)),
        out_specs=(VMEM, VMEM),
        compiler_params=SCRATCH,
        name="sums",
    )(place, *kept(fields, applied, own, *halos, *pieces))


def exchange_sum(part, axis):
    count = lax.axis_size(axis)
    terms = [part] + [
        lax.ppermute(part, axis, [(i, i ^ k) for i in range(count)]) for k in range(1, count)
    ]
    while len(terms) > 1:
        terms = [a + b for a, b in zip(terms[::2], terms[1::2])]
    return terms[0]


def exchange(part, axis):
    count = lax.axis_size(axis)
    return lax.all_to_all(jnp.broadcast_to(part[None], (count,) + part.shape), axis, 0, 0)


def finish_kernel(
    row_count, place_ref, parts_ref, stack_ref, block_ref, coeffs_ref, upper_ref,
    coeffs_scratch,
):
    block_cols = upper_ref.shape[0]
    basis_cols = parts_ref.shape[2] // 2
    half = basis_cols // 2
    joined = basis_cols + block_cols
    lines = block_ref.shape[0] // block_cols
    lanes = block_ref.shape[1]
    total = jnp.sum(parts_ref[...], axis=0) / row_count
    gram = jnp.concatenate((total[:half, :basis_cols], total[:half, basis_cols:]), axis=0)
    first = total[half:, :basis_cols]
    block_gram = total[half:, basis_cols:joined]

    def times(left, right, right_dim=0):
        return lax.dot_general(
            left, right, (((1,), (right_dim,)), ((), ())),
            precision=exact_precision, preferred_element_type=jnp.float32,
        )

    coeffs = first + (first - times(first, gram))
    image = times(coeffs, gram)
    matrix = block_gram - times(coeffs, first, 1) - times(first - image, coeffs, 1)
    coeffs_scratch[...] = coeffs.T
    group_cols = coeffs_ref.shape[0]
    start = pl.multiple_of(place_ref[0] * group_cols, group_cols)
    coeffs_ref[...] = coeffs_scratch[pl.ds(start, group_cols), :]

    row = lax.broadcasted_iota(jnp.int32, (block_cols, block_cols), 0)
    column = lax.broadcasted_iota(jnp.int32, (block_cols, block_cols), 1)
    unit = jnp.where(row == column, 1.0, 0.0)
    pad = jnp.zeros((block_cols, 2 * basis_cols - joined - block_cols), jnp.float32)
    work = jnp.concatenate((-coeffs, unit, matrix, pad), axis=1)
    height = lax.broadcasted_iota(jnp.int32, work.shape, 0)
    for step in range(block_cols):
        pivots = jnp.broadcast_to(work[:, joined + step : joined + step + 1], work.shape)
        pivot = pivots[step : step + 1, :]
        pivot_row = work[step : step + 1, :]
        scaled = pivot_row / pivot
        new_row = pivot_row * lax.rsqrt(pivot)
        work = jnp.where(
            height > step, work - pivots * scaled, jnp.where(height == step, new_row, work)
        )
    upper_ref[...] = work[:, joined : joined + block_cols]
    weights = three_parts(work[:, :joined])
    wide = jnp.concatenate(
        [jnp.concatenate((part, part, part), axis=1) for part in weights], axis=0
    )
    result = jnp.dot(wide, stack_ref[...], preferred_element_type=jnp.float32)
    result = result[:block_cols] + result[block_cols : 2 * block_cols] + result[2 * block_cols :]
    for line in range(lines):
        block_ref[pl.ds(line, block_cols, stride=lines), :] = result[
            :, line * lanes : (line + 1) * lanes
        ]


def finish(place, parts, stack, row_count, block_cols, group_cols, lines):
    lanes = stack.shape[1] // lines
    basis_cols = parts.shape[2] // 2
    return pl.pallas_call(
        functools.partial(finish_kernel, row_count),
        out_shape=(
            f32(block_cols * lines, lanes), f32(group_cols, block_cols), f32(block_cols, block_cols),
        ),
        in_specs=[SMEM] + [VMEM] * 2,
        out_specs=(VMEM, VMEM, VMEM),
        scratch_shapes=[pltpu.VMEM((basis_cols, block_cols), jnp.float32)],
        compiler_params=SCRATCH,
        name="finish",
    )(place, *kept(parts, stack))


def shards(
    x_block, basis, material, k0_blocks, k0_diag, ke_blocks, mass, velocities, shifts, sample
):
    block_cols, comps, extent_x, rows, lanes = x_block.shape
    group_cols = basis.shape[0]
    lines = comps * rows
    row_count = float(comps * extent_x * lax.axis_size("space") * basis.shape[3] * lanes)

    place = lax.axis_index("basis").astype(jnp.int32).reshape(1)
    count = lax.axis_size("basis")
    own, *pieces, x_rows, material = pack(
        place, basis, x_block.reshape(block_cols * lines, lanes), material.reshape(rows, lanes), block_cols
    )
    halos = [None, None]
    order = (3, "upper", 2, "lower", 1)
    pieces = dict(enumerate(pieces, 1))
    for name in order:
        if name == "lower":
            halos[0] = from_lower(x_rows, "space")
        elif name == "upper":
            halos[1] = from_upper(x_rows, "space")
        else:
            pieces[name] = lax.ppermute(pieces[name], "basis", [(i, i ^ name) for i in range(count)])
    pieces = [pieces[k].reshape(-1, lanes) for k in partners(count)[0]]
    fields, applied, own = ahead(
        sample, velocities, shifts, k0_blocks, ke_blocks, k0_diag, mass, material, x_rows,
        own.reshape(-1, lanes), comps,
    )
    stack, part = sums(place, fields, applied, own, halos, pieces, comps)
    parts = exchange(exchange_sum(part, "basis"), "space")
    block, coeffs, upper = finish(place, parts, stack, row_count, block_cols, group_cols, lines)
    return (block.reshape(x_block.shape), coeffs, upper)


def solution(mesh):
    in_specs = (
        P(None, None, "space", "basis", None),
        P("basis", None, "space", None, None),
        P("space", "basis", None),
        P(),
        P(),
        P(),
        P(),
        P(),
        P(),
        P(),
    )
    out_specs = (P(None, None, "space", "basis", None), P("basis", None), P())
    return jax.shard_map(shards, mesh=mesh, in_specs=in_specs, out_specs=out_specs, check_vma=False)
```

```python
import functools

import jax
import jax.numpy as jnp
from jax import lax
from jax.experimental import pallas as pl
from jax.experimental.pallas import tpu as pltpu
from jax.sharding import PartitionSpec as P

exact_precision = lax.Precision.HIGHEST
VMEM = pl.BlockSpec(memory_space=pltpu.VMEM)
SMEM = pl.BlockSpec(memory_space=pltpu.SMEM)
HBM = pl.BlockSpec(memory_space=pltpu.HBM)
SCRATCH = pltpu.CompilerParams(vmem_limit_bytes=8 * 2**20)


def f32(*shape):
    return jax.ShapeDtypeStruct(shape, jnp.float32)


def near(*shape, dtype=jnp.float32):
    return pltpu.VMEM(shape, dtype)


def kept(*arrays):
    return [pltpu.with_memory_space_constraint(array, pltpu.VMEM) for array in arrays]


def far(*arrays):
    return [pltpu.with_memory_space_constraint(array, pltpu.HBM) for array in arrays]


def swap(values, axis, first):
    pairs = [(i, i + 1) for i in range(first, lax.axis_size(axis) - 1, 2)]
    return lax.ppermute(values, axis, pairs + [(j, i) for i, j in pairs])


def partners(count):
    return range(1, count), [k for k in range(1, count) if k & (k + 1) == 0]


def pack_kernel(comps, place_ref, basis_ref, x_ref, material_ref, *refs):
    *piece_refs, x_out_ref, material_out_ref, sems = refs
    count = len(piece_refs)
    tiles, _, rows, lanes = basis_ref.shape
    block_cols = x_ref.shape[0] // (comps * rows)
    place = place_ref[0]
    x_copy = pltpu.make_async_copy(x_ref, x_out_ref, sems.at[count])
    x_copy.start()
    copies = [pltpu.make_async_copy(material_ref, material_out_ref, sems.at[count + 1])]
    for k in reversed(range(count)):
        copies.append(
            pltpu.make_async_copy(
                basis_ref.at[:, place ^ k], piece_refs[k].at[pl.ds(0, tiles)], sems.at[k]
            )
        )
    for copy in copies:
        copy.start()
    x_copy.wait()
    for comp in range(comps):
        first, last = (
            x_out_ref[pl.ds(comp * rows + row, block_cols, stride=comps * rows), :]
            for row in (0, rows - 1)
        )
        for k in partners(count)[1]:
            edge = jnp.where((place ^ k) > place, last, first)
            for part in range(block_cols // rows):
                piece_refs[k][tiles + comp * (block_cols // rows) + part] = edge[
                    part * rows : (part + 1) * rows
                ]
    for copy in copies:
        copy.wait()


def pack(place, basis, x_rows, material, block_cols):
    group_cols, comps, _, full_y, lanes = basis.shape
    count = lax.axis_size("basis")
    rows = full_y // count
    tiles = group_cols * comps
    edge_tiles = block_cols * comps // rows
    pieces = [
        near(tiles + (edge_tiles if k in partners(count)[1] else 0), rows, lanes)
        for k in range(count)
    ]
    return pl.pallas_call(
        functools.partial(pack_kernel, comps),
        out_shape=(*pieces, near(*x_rows.shape), near(*material.shape, dtype=jnp.int32)),
        in_specs=[SMEM, HBM, HBM, HBM],
        out_specs=(VMEM,) * (count + 2),
        scratch_shapes=[pltpu.SemaphoreType.DMA((count + 2,))],
        compiler_params=SCRATCH,
        name="pack",
    )(place, *far(basis.reshape(tiles, count, rows, lanes), x_rows, material))


def three_parts(values):
    high = values.astype(jnp.bfloat16)
    rest = values - high.astype(jnp.float32)
    middle = rest.astype(jnp.bfloat16)
    low = (rest - middle.astype(jnp.float32)).astype(jnp.bfloat16)
    return high, middle, low


def line_of(ref, comp, row, comps, rows, block_cols):
    return ref[pl.ds(comp * rows + row, block_cols, stride=comps * rows), :]


def ahead_kernel(
    sample_ref, *refs
):
    far_refs, refs = refs[:6], refs[6:]
    material_ref, x_ref, own_ref, fields_ref, applied_ref, stack_ref, *near_refs, sems = refs
    velocities_ref, shifts_ref, k0_ref, ke_ref, diag_ref, mass_ref = near_refs
    copies = [
        pltpu.make_async_copy(source, target, sems.at[index])
        for index, (source, target) in enumerate(zip(far_refs, near_refs))
    ]
    for copy in copies:
        copy.start()
    group_cols = stack_ref.shape[0] // 3
    for line in range(applied_ref.shape[0]):
        values = own_ref[pl.ds(line, group_cols, stride=applied_ref.shape[0]), :]
        for index, part in enumerate(three_parts(values)):
            there = pl.ds(line * values.shape[1], values.shape[1])
            stack_ref[pl.ds(index * group_cols, group_cols), there] = part
    for copy in copies:
        copy.wait()
    comps, _, levels, offsets = k0_ref.shape
    rows, lanes = material_ref.shape
    lines = comps * rows
    block_cols = x_ref.shape[0] // lines
    velocity = velocities_ref[sample_ref[0]]
    sigma = shifts_ref[sample_ref[0]]
    entry_rows = fields_ref.shape[1]
    stride = entry_rows // (comps * comps)
    gap = jnp.zeros((levels, stride - offsets), jnp.float32)
    wide = []
    for out in range(comps):
        for comp in range(comps):
            wide += [k0_ref[out, comp] - velocity * velocity * ke_ref[out, comp], gap]
    wide.append(jnp.zeros((levels, lanes - entry_rows), jnp.float32))
    table = jnp.concatenate(wide, axis=1).T[:entry_rows]
    entry = lax.broadcasted_iota(jnp.int32, table.shape, 0)
    for comp in range(comps):
        centre = diag_ref[comp : comp + 1, :] - sigma * mass_ref[comp : comp + 1, :]
        table = table + jnp.where(entry == comp * (comps + 1) * stride, centre, 0.0)

    lane = lax.broadcasted_iota(jnp.int32, (block_cols, lanes), 1)
    level = lax.broadcasted_iota(jnp.int32, (levels, lanes), 0)
    for row in range(rows):
        chosen = jnp.broadcast_to(material_ref[row : row + 1, :], (levels, lanes)) == level
        fields = jnp.dot(
            table, chosen.astype(jnp.float32),
            precision=exact_precision, preferred_element_type=jnp.float32,
        )
        fields_ref[row] = fields
        sums = [None] * comps
        for comp in range(comps):
            centre = line_of(x_ref, comp, row, comps, rows, block_cols)
            views = {
                0: centre,
                5: jnp.where(lane == 0, 0.0, pltpu.roll(centre, 1, 1)),
                6: jnp.where(lane == lanes - 1, 0.0, pltpu.roll(centre, lanes - 1, 1)),
            }
            if row > 0:
                views[3] = line_of(x_ref, comp, row - 1, comps, rows, block_cols)
            if row < rows - 1:
                views[4] = line_of(x_ref, comp, row + 1, comps, rows, block_cols)
            for offset, view in views.items():
                for out in range(comps):
                    place = (out * comps + comp) * stride + offset
                    term = fields[place : place + 1, :] * view
                    sums[out] = term if sums[out] is None else sums[out] + term
        for out in range(comps):
            applied_ref[out * rows + row] = sums[out]


def ahead(sample, velocities, shifts, k0, ke, diag, mass, material, x_rows, own, comps):
    rows, lanes = material.shape
    lines = comps * rows
    stride = -(-k0.shape[1] // 8) * 8
    k0, ke = (jnp.transpose(blocks, (2, 3, 0, 1)) for blocks in (k0, ke))
    tables = far(velocities, shifts, k0, ke, diag.T, mass.T)
    return pl.pallas_call(
        ahead_kernel,
        out_shape=(
            near(rows, comps * comps * stride, lanes),
            near(lines, x_rows.shape[0] // lines, lanes),
            near(3 * own.shape[0] // lines, lines * lanes, dtype=jnp.bfloat16),
        ),
        in_specs=[SMEM] + [HBM] * 6 + [VMEM] * 3,
        out_specs=(VMEM,) * 3,
        scratch_shapes=[
            (pltpu.SMEM if array.ndim == 1 else pltpu.VMEM)(array.shape, jnp.float32)
            for array in tables
        ] + [pltpu.SemaphoreType.DMA((len(tables),))],
        compiler_params=SCRATCH,
        name="ahead",
    )(sample, *tables, *kept(material, x_rows, own))


def sums_kernel(comps, names, edge_ks, place_ref, slab_ref, fields_ref, applied_ref, own_ref, *refs):
    *refs, stack_ref, sums_ref = refs
    got = dict(zip(names, refs))
    piece_refs = [got[k] for k in range(1, len(got) - 1)]
    lines, block_cols, lanes = applied_ref.shape
    rows = lines // comps
    stride = fields_ref.shape[1] // (comps * comps)
    group_cols = own_ref.shape[0] // 3
    basis_cols = (1 + len(piece_refs)) * group_cols
    joined = basis_cols + block_cols
    place = place_ref[0]
    swapped = slab_ref[0] % 2 == 1

    def store(begin, line, values):
        for index, part in enumerate(three_parts(values)):
            there = pl.ds(index * joined + begin, values.shape[0])
            stack_ref[there, pl.ds(line * lanes, lanes)] = part

    begin = pl.multiple_of(place * group_cols, group_cols)
    for index in range(3):
        stack_ref[pl.ds(index * joined + begin, group_cols), :] = own_ref[
            pl.ds(index * group_cols, group_cols), :
        ]
    for k, piece_ref in enumerate(piece_refs, 1):
        begin = pl.multiple_of((place ^ k) * group_cols, group_cols)
        for line in range(lines):
            store(begin, line, piece_ref[pl.ds(line, group_cols, stride=lines), :])

    def edge(comp, step):
        result = jnp.zeros((block_cols, lanes), jnp.float32)
        for k in edge_ks:
            ref = piece_refs[k - 1]
            begin = ref.shape[0] - (comps - comp) * block_cols
            here = (place ^ k) == place + step
            result = jnp.where(here, ref[pl.ds(begin, block_cols), :], result)
        return result

    for row in range(rows):
        totals = [applied_ref[out * rows + row] for out in range(comps)]
        for comp in range(comps):
            views = {
                name: line_of(got[name], comp, row, comps, rows, block_cols)
                for name in ("even", "odd")
            }
            if row == 0:
                views[3] = edge(comp, -1)
            if row == rows - 1:
                views[4] = edge(comp, 1)
            for out in range(comps):
                entries = fields_ref[row, pl.ds((out * comps + comp) * stride, stride), :]
                below, above = entries[1:2], entries[2:3]
                chosen = {
                    "even": jnp.where(swapped, below, above),
                    "odd": jnp.where(swapped, above, below),
                    3: entries[3:4],
                    4: entries[4:5],
                }
                for name, view in views.items():
                    totals[out] = totals[out] + chosen[name] * view
        for out in range(comps):
            store(basis_cols, out * rows + row, totals[out])

    stack = stack_ref[...]
    products = lax.dot_general(
        stack, stack, (((1,), (1,)), ((), ())), preferred_element_type=jnp.float32
    )
    wide = products[:joined] + products[joined : 2 * joined] + products[2 * joined :]
    total = wide[:, :joined] + wide[:, joined : 2 * joined] + wide[:, 2 * joined :]
    half = basis_cols // 2
    sums_ref[pl.ds(0, half), :] = jnp.concatenate(
        (total[:half, :basis_cols], total[half:basis_cols, :basis_cols]), axis=1
    )
    sums_ref[pl.ds(half, block_cols), :] = jnp.concatenate(
        (total[basis_cols:], jnp.zeros((block_cols, sums_ref.shape[1] - joined), jnp.float32)), axis=1
    )


def sums(place, slab, fields, applied, own, got, comps):
    count = len(got) - 1
    lines, block_cols, lanes = applied.shape
    basis_cols = count * (own.shape[0] // 3)
    joined = basis_cols + block_cols
    return pl.pallas_call(
        functools.partial(sums_kernel, comps, tuple(got), partners(count)[1]),
        out_shape=(
            near(3 * joined, lines * lanes, dtype=jnp.bfloat16),
            near(basis_cols // 2 + block_cols, 2 * basis_cols),
        ),
        in_specs=[SMEM] * 2 + [VMEM] * (3 + len(got)),
        out_specs=(VMEM, VMEM),
        compiler_params=SCRATCH,
        name="sums",
    )(place, slab, *kept(fields, applied, own, *got.values()))


def exchange_sum(part, axis):
    count = lax.axis_size(axis)
    terms = [part] + [
        lax.ppermute(part, axis, [(i, i ^ k) for i in range(count)]) for k in range(1, count)
    ]
    while len(terms) > 1:
        terms = [a + b for a, b in zip(terms[::2], terms[1::2])]
    return terms[0]


def exchange(part, axis):
    count = lax.axis_size(axis)
    return lax.all_to_all(jnp.broadcast_to(part[None], (count,) + part.shape), axis, 0, 0)


def finish_kernel(
    row_count, place_ref, parts_ref, stack_ref, block_ref, coeffs_ref, upper_ref,
    coeffs_scratch,
):
    block_cols = upper_ref.shape[0]
    basis_cols = parts_ref.shape[2] // 2
    half = basis_cols // 2
    joined = basis_cols + block_cols
    lines = block_ref.shape[0] // block_cols
    lanes = block_ref.shape[1]
    total = jnp.sum(parts_ref[...], axis=0) / row_count
    gram = jnp.concatenate((total[:half, :basis_cols], total[:half, basis_cols:]), axis=0)
    first = total[half:, :basis_cols]
    block_gram = total[half:, basis_cols:joined]

    def times(left, right, right_dim=0):
        return lax.dot_general(
            left, right, (((1,), (right_dim,)), ((), ())),
            precision=exact_precision, preferred_element_type=jnp.float32,
        )

    coeffs = first + (first - times(first, gram))
    image = times(coeffs, gram)
    matrix = block_gram - times(coeffs, first, 1) - times(first - image, coeffs, 1)
    coeffs_scratch[...] = coeffs.T
    group_cols = coeffs_ref.shape[0]
    start = pl.multiple_of(place_ref[0] * group_cols, group_cols)
    coeffs_ref[...] = coeffs_scratch[pl.ds(start, group_cols), :]

    row = lax.broadcasted_iota(jnp.int32, (block_cols, block_cols), 0)
    column = lax.broadcasted_iota(jnp.int32, (block_cols, block_cols), 1)
    unit = jnp.where(row == column, 1.0, 0.0)
    pad = jnp.zeros((block_cols, 2 * basis_cols - joined - block_cols), jnp.float32)
    work = jnp.concatenate((-coeffs, unit, matrix, pad), axis=1)
    height = lax.broadcasted_iota(jnp.int32, work.shape, 0)
    for step in range(block_cols):
        pivots = jnp.broadcast_to(work[:, joined + step : joined + step + 1], work.shape)
        pivot = pivots[step : step + 1, :]
        pivot_row = work[step : step + 1, :]
        scaled = pivot_row / pivot
        new_row = pivot_row * lax.rsqrt(pivot)
        work = jnp.where(
            height > step, work - pivots * scaled, jnp.where(height == step, new_row, work)
        )
    upper_ref[...] = work[:, joined : joined + block_cols]
    weights = three_parts(work[:, :joined])
    wide = jnp.concatenate(
        [jnp.concatenate((part, part, part), axis=1) for part in weights], axis=0
    )
    result = jnp.dot(wide, stack_ref[...], preferred_element_type=jnp.float32)
    result = result[:block_cols] + result[block_cols : 2 * block_cols] + result[2 * block_cols :]
    for line in range(lines):
        block_ref[pl.ds(line, block_cols, stride=lines), :] = result[
            :, line * lanes : (line + 1) * lanes
        ]


def finish(place, parts, stack, row_count, block_cols, group_cols, lines):
    lanes = stack.shape[1] // lines
    basis_cols = parts.shape[2] // 2
    return pl.pallas_call(
        functools.partial(finish_kernel, row_count),
        out_shape=(
            f32(block_cols * lines, lanes), f32(group_cols, block_cols), f32(block_cols, block_cols),
        ),
        in_specs=[SMEM] + [VMEM] * 2,
        out_specs=(VMEM, VMEM, VMEM),
        scratch_shapes=[pltpu.VMEM((basis_cols, block_cols), jnp.float32)],
        compiler_params=SCRATCH,
        name="finish",
    )(place, *kept(parts, stack))


def shards(
    x_block, basis, material, k0_blocks, k0_diag, ke_blocks, mass, velocities, shifts, sample
):
    block_cols, comps, extent_x, rows, lanes = x_block.shape
    group_cols = basis.shape[0]
    lines = comps * rows
    row_count = float(comps * extent_x * lax.axis_size("space") * basis.shape[3] * lanes)

    place = lax.axis_index("basis").astype(jnp.int32).reshape(1)
    slab = lax.axis_index("space").astype(jnp.int32).reshape(1)
    count = lax.axis_size("basis")
    x_far = x_block.reshape(block_cols * lines, lanes)
    own, *pieces, x_rows, material = pack(place, basis, x_far, material.reshape(rows, lanes), block_cols)
    got = {}
    for name in (3, "even", 2, "odd", 1):
        if name == "even":
            got[name] = swap(x_far, "space", 0)
        elif name == "odd":
            got[name] = swap(x_far, "space", 1)
        else:
            piece = lax.ppermute(pieces[name - 1], "basis", [(i, i ^ name) for i in range(count)])
            got[name] = piece.reshape(-1, lanes)
    fields, applied, own = ahead(
        sample, velocities, shifts, k0_blocks, ke_blocks, k0_diag, mass, material, x_rows,
        own.reshape(-1, lanes), comps,
    )
    stack, part = sums(place, slab, fields, applied, own, got, comps)
    parts = exchange(exchange_sum(part, "basis"), "space")
    block, coeffs, upper = finish(place, parts, stack, row_count, block_cols, group_cols, lines)
    return (block.reshape(x_block.shape), coeffs, upper)


def solution(mesh):
    in_specs = (
        P(None, None, "space", "basis", None),
        P("basis", None, "space", None, None),
        P("space", "basis", None),
        P(),
        P(),
        P(),
        P(),
        P(),
        P(),
        P(),
    )
    out_specs = (P(None, None, "space", "basis", None), P("basis", None), P())
    return jax.shard_map(shards, mesh=mesh, in_specs=in_specs, out_specs=out_specs, check_vma=False)
```

```python
import functools

import jax
import jax.numpy as jnp
from jax import lax
from jax.experimental import pallas as pl
from jax.experimental.pallas import tpu as pltpu
from jax.sharding import PartitionSpec as P

exact_precision = lax.Precision.HIGHEST
VMEM = pl.BlockSpec(memory_space=pltpu.VMEM)
SMEM = pl.BlockSpec(memory_space=pltpu.SMEM)
HBM = pl.BlockSpec(memory_space=pltpu.HBM)
SCRATCH = pltpu.CompilerParams(vmem_limit_bytes=8 * 2**20)


def f32(*shape):
    return jax.ShapeDtypeStruct(shape, jnp.float32)


def near(*shape, dtype=jnp.float32):
    return pltpu.VMEM(shape, dtype)


def kept(*arrays):
    return [pltpu.with_memory_space_constraint(array, pltpu.VMEM) for array in arrays]


def far(*arrays):
    return [pltpu.with_memory_space_constraint(array, pltpu.HBM) for array in arrays]


def swap(values, axis, first):
    pairs = [(i, i + 1) for i in range(first, lax.axis_size(axis) - 1, 2)]
    return lax.ppermute(values, axis, pairs + [(j, i) for i, j in pairs])


def partners(count):
    return range(1, count), [k for k in range(1, count) if k & (k + 1) == 0]


def pack_kernel(comps, place_ref, basis_ref, x_ref, material_ref, *refs):
    *piece_refs, x_out_ref, material_out_ref, sems = refs
    count = len(piece_refs)
    tiles, _, rows, lanes = basis_ref.shape
    block_cols = x_ref.shape[0] // (comps * rows)
    place = place_ref[0]
    x_copy = pltpu.make_async_copy(x_ref, x_out_ref, sems.at[count])
    x_copy.start()
    copies = [pltpu.make_async_copy(material_ref, material_out_ref, sems.at[count + 1])]
    for k in reversed(range(count)):
        copies.append(
            pltpu.make_async_copy(
                basis_ref.at[:, place ^ k], piece_refs[k].at[pl.ds(0, tiles)], sems.at[k]
            )
        )
    for copy in copies:
        copy.start()
    x_copy.wait()
    for comp in range(comps):
        first, last = (
            x_out_ref[pl.ds(comp * rows + row, block_cols, stride=comps * rows), :]
            for row in (0, rows - 1)
        )
        for k in partners(count)[1]:
            edge = jnp.where((place ^ k) > place, last, first)
            for part in range(block_cols // rows):
                piece_refs[k][tiles + comp * (block_cols // rows) + part] = edge[
                    part * rows : (part + 1) * rows
                ]
    for copy in copies:
        copy.wait()


def pack(place, basis, x_rows, material, block_cols):
    group_cols, comps, _, full_y, lanes = basis.shape
    count = lax.axis_size("basis")
    rows = full_y // count
    tiles = group_cols * comps
    edge_tiles = block_cols * comps // rows
    pieces = [
        near(tiles + (edge_tiles if k in partners(count)[1] else 0), rows, lanes)
        for k in range(count)
    ]
    return pl.pallas_call(
        functools.partial(pack_kernel, comps),
        out_shape=(*pieces, near(*x_rows.shape), near(*material.shape, dtype=jnp.int32)),
        in_specs=[SMEM, HBM, HBM, HBM],
        out_specs=(VMEM,) * (count + 2),
        scratch_shapes=[pltpu.SemaphoreType.DMA((count + 2,))],
        compiler_params=SCRATCH,
        name="pack",
    )(place, *far(basis.reshape(tiles, count, rows, lanes), x_rows, material))


def three_parts(values):
    high = values.astype(jnp.bfloat16)
    rest = values - high.astype(jnp.float32)
    middle = rest.astype(jnp.bfloat16)
    low = (rest - middle.astype(jnp.float32)).astype(jnp.bfloat16)
    return high, middle, low


def line_of(ref, comp, row, comps, rows, block_cols):
    return ref[pl.ds(comp * rows + row, block_cols, stride=comps * rows), :]


def ahead_kernel(
    sample_ref, *refs
):
    far_refs, refs = refs[:6], refs[6:]
    material_ref, x_ref, own_ref, fields_ref, applied_ref, stack_ref, *near_refs, sems = refs
    velocities_ref, shifts_ref, k0_ref, ke_ref, diag_ref, mass_ref = near_refs
    copies = [
        pltpu.make_async_copy(source, target, sems.at[index])
        for index, (source, target) in enumerate(zip(far_refs, near_refs))
    ]
    for copy in copies:
        copy.start()
    group_cols = stack_ref.shape[0] // 3
    for line in range(applied_ref.shape[0]):
        values = own_ref[pl.ds(line, group_cols, stride=applied_ref.shape[0]), :]
        for index, part in enumerate(three_parts(values)):
            there = pl.ds(line * values.shape[1], values.shape[1])
            stack_ref[pl.ds(index * group_cols, group_cols), there] = part
    for copy in copies:
        copy.wait()
    comps, _, levels, offsets = k0_ref.shape
    rows, lanes = material_ref.shape
    lines = comps * rows
    block_cols = x_ref.shape[0] // lines
    velocity = velocities_ref[sample_ref[0]]
    sigma = shifts_ref[sample_ref[0]]
    entry_rows = fields_ref.shape[1]
    stride = entry_rows // (comps * comps)
    gap = jnp.zeros((levels, stride - offsets), jnp.float32)
    wide = []
    for out in range(comps):
        for comp in range(comps):
            wide += [k0_ref[out, comp] - velocity * velocity * ke_ref[out, comp], gap]
    wide.append(jnp.zeros((levels, lanes - entry_rows), jnp.float32))
    table = jnp.concatenate(wide, axis=1).T[:entry_rows]
    entry = lax.broadcasted_iota(jnp.int32, table.shape, 0)
    for comp in range(comps):
        centre = diag_ref[comp : comp + 1, :] - sigma * mass_ref[comp : comp + 1, :]
        table = table + jnp.where(entry == comp * (comps + 1) * stride, centre, 0.0)

    lane = lax.broadcasted_iota(jnp.int32, (block_cols, lanes), 1)
    level = lax.broadcasted_iota(jnp.int32, (levels, lanes), 0)
    for row in range(rows):
        chosen = jnp.broadcast_to(material_ref[row : row + 1, :], (levels, lanes)) == level
        fields = jnp.dot(
            table, chosen.astype(jnp.float32),
            precision=exact_precision, preferred_element_type=jnp.float32,
        )
        fields_ref[row] = fields
        sums = [None] * comps
        for comp in range(comps):
            centre = line_of(x_ref, comp, row, comps, rows, block_cols)
            views = {
                0: centre,
                5: jnp.where(lane == 0, 0.0, pltpu.roll(centre, 1, 1)),
                6: jnp.where(lane == lanes - 1, 0.0, pltpu.roll(centre, lanes - 1, 1)),
            }
            if row > 0:
                views[3] = line_of(x_ref, comp, row - 1, comps, rows, block_cols)
            if row < rows - 1:
                views[4] = line_of(x_ref, comp, row + 1, comps, rows, block_cols)
            for offset, view in views.items():
                for out in range(comps):
                    place = (out * comps + comp) * stride + offset
                    term = fields[place : place + 1, :] * view
                    sums[out] = term if sums[out] is None else sums[out] + term
        for out in range(comps):
            applied_ref[out * rows + row] = sums[out]


def ahead(sample, velocities, shifts, k0, ke, diag, mass, material, x_rows, own, comps):
    rows, lanes = material.shape
    lines = comps * rows
    stride = -(-k0.shape[1] // 8) * 8
    k0, ke = (jnp.transpose(blocks, (2, 3, 0, 1)) for blocks in (k0, ke))
    tables = far(velocities, shifts, k0, ke, diag.T, mass.T)
    return pl.pallas_call(
        ahead_kernel,
        out_shape=(
            near(rows, comps * comps * stride, lanes),
            near(lines, x_rows.shape[0] // lines, lanes),
            near(3 * own.shape[0] // lines, lines * lanes, dtype=jnp.bfloat16),
        ),
        in_specs=[SMEM] + [HBM] * 6 + [VMEM] * 3,
        out_specs=(VMEM,) * 3,
        scratch_shapes=[
            (pltpu.SMEM if array.ndim == 1 else pltpu.VMEM)(array.shape, jnp.float32)
            for array in tables
        ] + [pltpu.SemaphoreType.DMA((len(tables),))],
        compiler_params=SCRATCH,
        name="ahead",
    )(sample, *tables, *kept(material, x_rows, own))


def sums_kernel(comps, names, edge_ks, place_ref, slab_ref, fields_ref, applied_ref, own_ref, *refs):
    *refs, stack_ref, sums_ref = refs
    got = dict(zip(names, refs))
    piece_refs = [got[k] for k in range(1, len(got) - 1)]
    lines, block_cols, lanes = applied_ref.shape
    rows = lines // comps
    stride = fields_ref.shape[1] // (comps * comps)
    group_cols = own_ref.shape[0] // 3
    basis_cols = (1 + len(piece_refs)) * group_cols
    joined = basis_cols + block_cols
    place = place_ref[0]
    swapped = slab_ref[0] % 2 == 1

    def store(begin, line, values):
        for index, part in enumerate(three_parts(values)):
            there = pl.ds(index * joined + begin, values.shape[0])
            stack_ref[there, pl.ds(line * lanes, lanes)] = part

    begin = pl.multiple_of(place * group_cols, group_cols)
    for index in range(3):
        stack_ref[pl.ds(index * joined + begin, group_cols), :] = own_ref[
            pl.ds(index * group_cols, group_cols), :
        ]
    for k, piece_ref in enumerate(piece_refs, 1):
        begin = pl.multiple_of((place ^ k) * group_cols, group_cols)
        for line in range(lines):
            store(begin, line, piece_ref[pl.ds(line, group_cols, stride=lines), :])

    def edge(comp, step):
        result = jnp.zeros((block_cols, lanes), jnp.float32)
        for k in edge_ks:
            ref = piece_refs[k - 1]
            begin = ref.shape[0] - (comps - comp) * block_cols
            here = (place ^ k) == place + step
            result = jnp.where(here, ref[pl.ds(begin, block_cols), :], result)
        return result

    for row in range(rows):
        totals = [applied_ref[out * rows + row] for out in range(comps)]
        for comp in range(comps):
            views = {
                name: line_of(got[name], comp, row, comps, rows, block_cols)
                for name in ("even", "odd")
            }
            if row == 0:
                views[3] = edge(comp, -1)
            if row == rows - 1:
                views[4] = edge(comp, 1)
            for out in range(comps):
                entries = fields_ref[row, pl.ds((out * comps + comp) * stride, stride), :]
                below, above = entries[1:2], entries[2:3]
                chosen = {
                    "even": jnp.where(swapped, below, above),
                    "odd": jnp.where(swapped, above, below),
                    3: entries[3:4],
                    4: entries[4:5],
                }
                for name, view in views.items():
                    totals[out] = totals[out] + chosen[name] * view
        for out in range(comps):
            store(basis_cols, out * rows + row, totals[out])

    stack = stack_ref[...]
    products = lax.dot_general(
        stack, stack, (((1,), (1,)), ((), ())), preferred_element_type=jnp.float32
    )
    wide = products[:joined] + products[joined : 2 * joined] + products[2 * joined :]
    total = wide[:, :joined] + wide[:, joined : 2 * joined] + wide[:, 2 * joined :]
    half = basis_cols // 2
    sums_ref[pl.ds(0, half), :] = jnp.concatenate(
        (total[:half, :basis_cols], total[half:basis_cols, :basis_cols]), axis=1
    )
    sums_ref[pl.ds(half, block_cols), :] = jnp.concatenate(
        (total[basis_cols:], jnp.zeros((block_cols, sums_ref.shape[1] - joined), jnp.float32)), axis=1
    )


def sums(place, slab, fields, applied, own, got, comps):
    count = len(got) - 1
    lines, block_cols, lanes = applied.shape
    basis_cols = count * (own.shape[0] // 3)
    joined = basis_cols + block_cols
    return pl.pallas_call(
        functools.partial(sums_kernel, comps, tuple(got), partners(count)[1]),
        out_shape=(
            near(3 * joined, lines * lanes, dtype=jnp.bfloat16),
            near(basis_cols // 2 + block_cols, 2 * basis_cols),
        ),
        in_specs=[SMEM] * 2 + [VMEM] * (3 + len(got)),
        out_specs=(VMEM, VMEM),
        compiler_params=SCRATCH,
        name="sums",
    )(place, slab, *kept(fields, applied, own, *got.values()))


def exchange(part, axes, stride, radix):
    count = lax.axis_size(axes)
    masks = [stride * k for k in range(1, radix)]
    return [part] + [lax.ppermute(part, axes, [(i, i ^ m) for i in range(count)]) for m in masks]


def pair_sum(terms):
    while len(terms) > 1:
        terms = [a + b for a, b in zip(terms[::2], terms[1::2])]
    return terms[0]


def exchange_all(part, axes, widest=8):
    count = lax.axis_size(axes)
    stride, terms = 1, [part]
    while stride < count:
        radix = min(widest, count // stride)
        terms = exchange(pair_sum(terms), axes, stride, radix)
        stride *= radix
    return terms


def finish_kernel(
    row_count, place_ref, stack_ref, *refs
):
    *part_refs, block_ref, coeffs_ref, upper_ref, coeffs_scratch = refs
    block_cols = upper_ref.shape[0]
    basis_cols = part_refs[0].shape[1] // 2
    half = basis_cols // 2
    joined = basis_cols + block_cols
    lines = block_ref.shape[0] // block_cols
    lanes = block_ref.shape[1]
    total = pair_sum([ref[...] for ref in part_refs]) / row_count
    gram = jnp.concatenate((total[:half, :basis_cols], total[:half, basis_cols:]), axis=0)
    first = total[half:, :basis_cols]
    block_gram = total[half:, basis_cols:joined]

    def times(left, right, right_dim=0):
        return lax.dot_general(
            left, right, (((1,), (right_dim,)), ((), ())),
            precision=exact_precision, preferred_element_type=jnp.float32,
        )

    coeffs = first + (first - times(first, gram))
    image = times(coeffs, gram)
    matrix = block_gram - times(coeffs, first, 1) - times(first - image, coeffs, 1)
    coeffs_scratch[...] = coeffs.T
    group_cols = coeffs_ref.shape[0]
    start = pl.multiple_of(place_ref[0] * group_cols, group_cols)
    coeffs_ref[...] = coeffs_scratch[pl.ds(start, group_cols), :]

    row = lax.broadcasted_iota(jnp.int32, (block_cols, block_cols), 0)
    column = lax.broadcasted_iota(jnp.int32, (block_cols, block_cols), 1)
    unit = jnp.where(row == column, 1.0, 0.0)
    pad = jnp.zeros((block_cols, 2 * basis_cols - joined - block_cols), jnp.float32)
    work = jnp.concatenate((-coeffs, unit, matrix, pad), axis=1)
    height = lax.broadcasted_iota(jnp.int32, work.shape, 0)
    for step in range(block_cols):
        pivots = jnp.broadcast_to(work[:, joined + step : joined + step + 1], work.shape)
        pivot = pivots[step : step + 1, :]
        pivot_row = work[step : step + 1, :]
        scaled = pivot_row / pivot
        new_row = pivot_row * lax.rsqrt(pivot)
        work = jnp.where(
            height > step, work - pivots * scaled, jnp.where(height == step, new_row, work)
        )
    upper_ref[...] = work[:, joined : joined + block_cols]
    weights = three_parts(work[:, :joined])
    wide = jnp.concatenate(
        [jnp.concatenate((part, part, part), axis=1) for part in weights], axis=0
    )
    result = jnp.dot(wide, stack_ref[...], preferred_element_type=jnp.float32)
    result = result[:block_cols] + result[block_cols : 2 * block_cols] + result[2 * block_cols :]
    for line in range(lines):
        block_ref[pl.ds(line, block_cols, stride=lines), :] = result[
            :, line * lanes : (line + 1) * lanes
        ]


def finish(place, parts, stack, row_count, block_cols, group_cols, lines):
    lanes = stack.shape[1] // lines
    basis_cols = parts[0].shape[1] // 2
    return pl.pallas_call(
        functools.partial(finish_kernel, row_count),
        out_shape=(
            f32(block_cols * lines, lanes), f32(group_cols, block_cols), f32(block_cols, block_cols),
        ),
        in_specs=[SMEM] + [VMEM] * (1 + len(parts)),
        out_specs=(VMEM, VMEM, VMEM),
        scratch_shapes=[pltpu.VMEM((basis_cols, block_cols), jnp.float32)],
        compiler_params=SCRATCH,
        name="finish",
    )(place, *kept(stack, *parts))


def shards(
    x_block, basis, material, k0_blocks, k0_diag, ke_blocks, mass, velocities, shifts, sample
):
    block_cols, comps, extent_x, rows, lanes = x_block.shape
    group_cols = basis.shape[0]
    lines = comps * rows
    row_count = float(comps * extent_x * lax.axis_size("space") * basis.shape[3] * lanes)

    place = lax.axis_index("basis").astype(jnp.int32).reshape(1)
    slab = lax.axis_index("space").astype(jnp.int32).reshape(1)
    count = lax.axis_size("basis")
    x_far = x_block.reshape(block_cols * lines, lanes)
    own, *pieces, x_rows, material = pack(place, basis, x_far, material.reshape(rows, lanes), block_cols)
    got = {}
    for name in (3, "even", 2, "odd", 1):
        if name == "even":
            got[name] = swap(x_far, "space", 0)
        elif name == "odd":
            got[name] = swap(x_far, "space", 1)
        else:
            piece = lax.ppermute(pieces[name - 1], "basis", [(i, i ^ name) for i in range(count)])
            got[name] = piece.reshape(-1, lanes)
    fields, applied, own = ahead(
        sample, velocities, shifts, k0_blocks, ke_blocks, k0_diag, mass, material, x_rows,
        own.reshape(-1, lanes), comps,
    )
    stack, part = sums(place, slab, fields, applied, own, got, comps)
    parts = exchange_all(part, ("space", "basis"))
    block, coeffs, upper = finish(place, parts, stack, row_count, block_cols, group_cols, lines)
    return (block.reshape(x_block.shape), coeffs, upper)


def solution(mesh):
    in_specs = (
        P(None, None, "space", "basis", None),
        P("basis", None, "space", None, None),
        P("space", "basis", None),
        P(),
        P(),
        P(),
        P(),
        P(),
        P(),
        P(),
    )
    out_specs = (P(None, None, "space", "basis", None), P("basis", None), P())
    return jax.shard_map(shards, mesh=mesh, in_specs=in_specs, out_specs=out_specs, check_vma=False)
```

```python
import functools

import jax
import jax.numpy as jnp
from jax import lax
from jax.experimental import pallas as pl
from jax.experimental.pallas import tpu as pltpu
from jax.sharding import PartitionSpec as P

exact_precision = lax.Precision.HIGHEST
VMEM = pl.BlockSpec(memory_space=pltpu.VMEM)
SMEM = pl.BlockSpec(memory_space=pltpu.SMEM)
HBM = pl.BlockSpec(memory_space=pltpu.HBM)
EARLY = pl.CostEstimate(flops=10**9, bytes_accessed=10**6, transcendentals=0)
SCRATCH = pltpu.CompilerParams(vmem_limit_bytes=8 * 2**20)


def f32(*shape):
    return jax.ShapeDtypeStruct(shape, jnp.float32)


def near(*shape, dtype=jnp.float32):
    return pltpu.VMEM(shape, dtype)


def kept(*arrays):
    return [pltpu.with_memory_space_constraint(array, pltpu.VMEM) for array in arrays]


def far(*arrays):
    return [pltpu.with_memory_space_constraint(array, pltpu.HBM) for array in arrays]


def swap(values, axis, first):
    pairs = [(i, i + 1) for i in range(first, lax.axis_size(axis) - 1, 2)]
    return lax.ppermute(values, axis, pairs + [(j, i) for i, j in pairs])


def partners(count):
    return range(1, count), [k for k in range(1, count) if k & (k + 1) == 0]


def pack_kernel(comps, place_ref, basis_ref, x_ref, material_ref, *refs):
    *piece_refs, x_out_ref, material_out_ref, sems = refs
    count = len(piece_refs)
    tiles, _, rows, lanes = basis_ref.shape
    block_cols = x_ref.shape[0] // (comps * rows)
    place = place_ref[0]
    x_copy = pltpu.make_async_copy(x_ref, x_out_ref, sems.at[count])
    x_copy.start()
    copies = [pltpu.make_async_copy(material_ref, material_out_ref, sems.at[count + 1])]
    for k in reversed(range(count)):
        copies.append(
            pltpu.make_async_copy(
                basis_ref.at[:, place ^ k], piece_refs[k].at[pl.ds(0, tiles)], sems.at[k]
            )
        )
    for copy in copies:
        copy.start()
    x_copy.wait()
    for comp in range(comps):
        first, last = (
            x_out_ref[pl.ds(comp * rows + row, block_cols, stride=comps * rows), :]
            for row in (0, rows - 1)
        )
        for k in partners(count)[1]:
            edge = jnp.where((place ^ k) > place, last, first)
            for part in range(block_cols // rows):
                piece_refs[k][tiles + comp * (block_cols // rows) + part] = edge[
                    part * rows : (part + 1) * rows
                ]
    for copy in copies:
        copy.wait()


def pack(place, basis, x_rows, material, block_cols):
    group_cols, comps, _, full_y, lanes = basis.shape
    count = lax.axis_size("basis")
    rows = full_y // count
    tiles = group_cols * comps
    edge_tiles = block_cols * comps // rows
    pieces = [
        near(tiles + (edge_tiles if k in partners(count)[1] else 0), rows, lanes)
        for k in range(count)
    ]
    return pl.pallas_call(
        functools.partial(pack_kernel, comps),
        out_shape=(*pieces, near(*x_rows.shape), near(*material.shape, dtype=jnp.int32)),
        in_specs=[SMEM, HBM, HBM, HBM],
        out_specs=(VMEM,) * (count + 2),
        scratch_shapes=[pltpu.SemaphoreType.DMA((count + 2,))],
        compiler_params=SCRATCH,
        name="pack",
    )(place, *far(basis.reshape(tiles, count, rows, lanes), x_rows, material))


def three_parts(values):
    high = values.astype(jnp.bfloat16)
    rest = values - high.astype(jnp.float32)
    middle = rest.astype(jnp.bfloat16)
    low = (rest - middle.astype(jnp.float32)).astype(jnp.bfloat16)
    return high, middle, low


def line_of(ref, comp, row, comps, rows, block_cols):
    return ref[pl.ds(comp * rows + row, block_cols, stride=comps * rows), :]


def ahead_kernel(
    sample_ref, *refs
):
    far_refs, refs = refs[:6], refs[6:]
    material_ref, x_ref, own_ref, fields_ref, applied_ref, stack_ref, *near_refs, sems = refs
    velocities_ref, shifts_ref, k0_ref, ke_ref, diag_ref, mass_ref = near_refs
    copies = [
        pltpu.make_async_copy(source, target, sems.at[index])
        for index, (source, target) in enumerate(zip(far_refs, near_refs))
    ]
    for copy in copies:
        copy.start()
    group_cols = stack_ref.shape[0] // 3
    for line in range(applied_ref.shape[0]):
        values = own_ref[pl.ds(line, group_cols, stride=applied_ref.shape[0]), :]
        for index, part in enumerate(three_parts(values)):
            there = pl.ds(line * values.shape[1], values.shape[1])
            stack_ref[pl.ds(index * group_cols, group_cols), there] = part
    for copy in copies:
        copy.wait()
    comps, _, levels, offsets = k0_ref.shape
    rows, lanes = material_ref.shape
    lines = comps * rows
    block_cols = x_ref.shape[0] // lines
    velocity = velocities_ref[sample_ref[0]]
    sigma = shifts_ref[sample_ref[0]]
    entry_rows = fields_ref.shape[1]
    stride = entry_rows // (comps * comps)
    gap = jnp.zeros((levels, stride - offsets), jnp.float32)
    wide = []
    for out in range(comps):
        for comp in range(comps):
            wide += [k0_ref[out, comp] - velocity * velocity * ke_ref[out, comp], gap]
    wide.append(jnp.zeros((levels, lanes - entry_rows), jnp.float32))
    table = jnp.concatenate(wide, axis=1).T[:entry_rows]
    entry = lax.broadcasted_iota(jnp.int32, table.shape, 0)
    for comp in range(comps):
        centre = diag_ref[comp : comp + 1, :] - sigma * mass_ref[comp : comp + 1, :]
        table = table + jnp.where(entry == comp * (comps + 1) * stride, centre, 0.0)

    lane = lax.broadcasted_iota(jnp.int32, (block_cols, lanes), 1)
    level = lax.broadcasted_iota(jnp.int32, (levels, lanes), 0)
    for row in range(rows):
        chosen = jnp.broadcast_to(material_ref[row : row + 1, :], (levels, lanes)) == level
        fields = jnp.dot(
            table, chosen.astype(jnp.float32),
            precision=exact_precision, preferred_element_type=jnp.float32,
        )
        fields_ref[row] = fields
        sums = [None] * comps
        for comp in range(comps):
            centre = line_of(x_ref, comp, row, comps, rows, block_cols)
            views = {
                0: centre,
                5: jnp.where(lane == 0, 0.0, pltpu.roll(centre, 1, 1)),
                6: jnp.where(lane == lanes - 1, 0.0, pltpu.roll(centre, lanes - 1, 1)),
            }
            if row > 0:
                views[3] = line_of(x_ref, comp, row - 1, comps, rows, block_cols)
            if row < rows - 1:
                views[4] = line_of(x_ref, comp, row + 1, comps, rows, block_cols)
            for offset, view in views.items():
                for out in range(comps):
                    place = (out * comps + comp) * stride + offset
                    term = fields[place : place + 1, :] * view
                    sums[out] = term if sums[out] is None else sums[out] + term
        for out in range(comps):
            applied_ref[out * rows + row] = sums[out]


def ahead(sample, velocities, shifts, k0, ke, diag, mass, material, x_rows, own, comps):
    rows, lanes = material.shape
    lines = comps * rows
    stride = -(-k0.shape[1] // 8) * 8
    k0, ke = (jnp.transpose(blocks, (2, 3, 0, 1)) for blocks in (k0, ke))
    tables = far(velocities, shifts, k0, ke, diag.T, mass.T)
    return pl.pallas_call(
        ahead_kernel,
        out_shape=(
            near(rows, comps * comps * stride, lanes),
            near(lines, x_rows.shape[0] // lines, lanes),
            near(3 * own.shape[0] // lines, lines * lanes, dtype=jnp.bfloat16),
        ),
        in_specs=[SMEM] + [HBM] * 6 + [VMEM] * 3,
        out_specs=(VMEM,) * 3,
        scratch_shapes=[
            (pltpu.SMEM if array.ndim == 1 else pltpu.VMEM)(array.shape, jnp.float32)
            for array in tables
        ] + [pltpu.SemaphoreType.DMA((len(tables),))],
        compiler_params=SCRATCH,
        name="ahead",
    )(sample, *tables, *kept(material, x_rows, own))


def side_terms(field_row, swapped, side, out, comp, comps):
    stride = field_row.shape[0] // (comps * comps)
    begin = (out * comps + comp) * stride
    below, above = field_row[begin + 1 : begin + 2], field_row[begin + 2 : begin + 3]
    other = (below, above) if side == "even" else (above, below)
    return jnp.where(swapped, *other)


def side_kernel(comps, side, slab_ref, fields_ref, applied_ref, halo_ref, out_ref):
    lines, block_cols, _ = applied_ref.shape
    rows = lines // comps
    swapped = slab_ref[0] % 2 == 1
    for row in range(rows):
        field_row = fields_ref[row]
        views = [line_of(halo_ref, comp, row, comps, rows, block_cols) for comp in range(comps)]
        for out in range(comps):
            total = applied_ref[out * rows + row]
            for comp, view in enumerate(views):
                total = total + side_terms(field_row, swapped, side, out, comp, comps) * view
            out_ref[out * rows + row] = total


def add_side(slab, fields, applied, halo, comps, side):
    return pl.pallas_call(
        functools.partial(side_kernel, comps, side),
        out_shape=near(*applied.shape),
        in_specs=[SMEM] + [VMEM] * 3,
        out_specs=VMEM,
        compiler_params=SCRATCH,
        cost_estimate=EARLY,
        name="side",
    )(slab, *kept(fields, applied, halo))


def fold(total, basis_cols, block_cols, lanes):
    half = basis_cols // 2
    row = lax.broadcasted_iota(jnp.int32, (half, half), 0)
    column = lax.broadcasted_iota(jnp.int32, (half, half), 1)
    last = total[half:basis_cols, half:basis_cols]
    shared = jnp.where(row >= column, total[:half, :half], last)
    diagonal = jnp.sum(jnp.where(row == column, last, 0.0), axis=1, keepdims=True)
    below = total[basis_cols:]
    first = jnp.concatenate((below[:, :half], below[:, half:basis_cols]), axis=0)
    rest = jnp.zeros((half - block_cols, block_cols), jnp.float32)
    block = jnp.concatenate((below[:, basis_cols:], rest), axis=0)
    pad = jnp.zeros((half, lanes - 3 * half - block_cols - 1), jnp.float32)
    return jnp.concatenate(
        (shared, total[:half, half:basis_cols], first, block, diagonal, pad), axis=1
    )


def unfold(folded, block_cols):
    half = folded.shape[0]
    row = lax.broadcasted_iota(jnp.int32, (half, half), 0)
    column = lax.broadcasted_iota(jnp.int32, (half, half), 1)
    shared, across = folded[:, :half], folded[:, half : 2 * half]
    turned = shared.T
    start = jnp.where(row >= column, shared, turned)
    end = jnp.where(row < column, shared, turned)
    diagonal = folded[:, 3 * half + block_cols : 3 * half + block_cols + 1]
    end = jnp.where(row == column, diagonal, end)
    gram = jnp.concatenate(
        (jnp.concatenate((start, across), axis=1), jnp.concatenate((across.T, end), axis=1)), axis=0
    )
    first = folded[:, 2 * half : 3 * half]
    first = jnp.concatenate((first[:block_cols], first[block_cols : 2 * block_cols]), axis=1)
    return gram, first, folded[:block_cols, 3 * half : 3 * half + block_cols]


def sums_kernel(comps, names, edge_ks, place_ref, slab_ref, fields_ref, applied_ref, own_ref, *refs):
    *refs, stack_ref, sums_ref = refs
    got = dict(zip(names, refs))
    piece_refs = [got[k] for k in range(1, len(got))]
    lines, block_cols, lanes = applied_ref.shape
    rows = lines // comps
    stride = fields_ref.shape[1] // (comps * comps)
    group_cols = own_ref.shape[0] // 3
    basis_cols = (1 + len(piece_refs)) * group_cols
    joined = basis_cols + block_cols
    place = place_ref[0]
    swapped = slab_ref[0] % 2 == 1

    def store(begin, line, values):
        for index, part in enumerate(three_parts(values)):
            there = pl.ds(index * joined + begin, values.shape[0])
            stack_ref[there, pl.ds(line * lanes, lanes)] = part

    begin = pl.multiple_of(place * group_cols, group_cols)
    for index in range(3):
        stack_ref[pl.ds(index * joined + begin, group_cols), :] = own_ref[
            pl.ds(index * group_cols, group_cols), :
        ]
    for k, piece_ref in enumerate(piece_refs, 1):
        begin = pl.multiple_of((place ^ k) * group_cols, group_cols)
        for line in range(lines):
            store(begin, line, piece_ref[pl.ds(line, group_cols, stride=lines), :])

    def edge(comp, step):
        result = jnp.zeros((block_cols, lanes), jnp.float32)
        for k in edge_ks:
            ref = piece_refs[k - 1]
            begin = ref.shape[0] - (comps - comp) * block_cols
            here = (place ^ k) == place + step
            result = jnp.where(here, ref[pl.ds(begin, block_cols), :], result)
        return result

    for row in range(rows):
        field_row = fields_ref[row]
        totals = [applied_ref[out * rows + row] for out in range(comps)]
        for comp in range(comps):
            views = {}
            if row == 0:
                views[3] = edge(comp, -1)
            if row == rows - 1:
                views[4] = edge(comp, 1)
            side = line_of(got["even"], comp, row, comps, rows, block_cols)
            for out in range(comps):
                entry = (out * comps + comp) * stride
                totals[out] += side_terms(field_row, swapped, "even", out, comp, comps) * side
                for offset, view in views.items():
                    totals[out] += field_row[entry + offset : entry + offset + 1] * view
        for out in range(comps):
            store(basis_cols, out * rows + row, totals[out])

    stack = stack_ref[...]
    products = lax.dot_general(
        stack, stack, (((1,), (1,)), ((), ())), preferred_element_type=jnp.float32
    )
    wide = products[:joined] + products[joined : 2 * joined] + products[2 * joined :]
    total = wide[:, :joined] + wide[:, joined : 2 * joined] + wide[:, 2 * joined :]
    sums_ref[...] = fold(total, basis_cols, block_cols, sums_ref.shape[1])


def sums(place, slab, fields, applied, own, got, comps):
    count = len(got)
    lines, block_cols, lanes = applied.shape
    basis_cols = count * (own.shape[0] // 3)
    joined = basis_cols + block_cols
    return pl.pallas_call(
        functools.partial(sums_kernel, comps, tuple(got), partners(count)[1]),
        out_shape=(
            near(3 * joined, lines * lanes, dtype=jnp.bfloat16),
            near(basis_cols // 2, 2 * basis_cols),
        ),
        in_specs=[SMEM] * 2 + [VMEM] * (3 + len(got)),
        out_specs=(VMEM, VMEM),
        compiler_params=SCRATCH,
        name="sums",
    )(place, slab, *kept(fields, applied, own, *got.values()))


def exchange_sum(part, axis):
    count = lax.axis_size(axis)
    terms = [part] + [
        lax.ppermute(part, axis, [(i, i ^ k) for i in range(count)]) for k in range(1, count)
    ]
    while len(terms) > 1:
        terms = [a + b for a, b in zip(terms[::2], terms[1::2])]
    return terms[0]


def exchange(part, axis):
    count = lax.axis_size(axis)
    return lax.all_to_all(jnp.broadcast_to(part[None], (count,) + part.shape), axis, 0, 0)


def finish_kernel(
    row_count, place_ref, parts_ref, stack_ref, block_ref, coeffs_ref, upper_ref,
    coeffs_scratch,
):
    block_cols = upper_ref.shape[0]
    basis_cols = parts_ref.shape[2] // 2
    joined = basis_cols + block_cols
    lines = block_ref.shape[0] // block_cols
    lanes = block_ref.shape[1]
    total = jnp.sum(parts_ref[...], axis=0) / row_count
    gram, first, block_gram = unfold(total, block_cols)

    def times(left, right, right_dim=0):
        return lax.dot_general(
            left, right, (((1,), (right_dim,)), ((), ())),
            precision=exact_precision, preferred_element_type=jnp.float32,
        )

    coeffs = first + (first - times(first, gram))
    image = times(coeffs, gram)
    matrix = block_gram - times(coeffs, first, 1) - times(first - image, coeffs, 1)
    coeffs_scratch[...] = coeffs.T
    group_cols = coeffs_ref.shape[0]
    start = pl.multiple_of(place_ref[0] * group_cols, group_cols)
    coeffs_ref[...] = coeffs_scratch[pl.ds(start, group_cols), :]

    row = lax.broadcasted_iota(jnp.int32, (block_cols, block_cols), 0)
    column = lax.broadcasted_iota(jnp.int32, (block_cols, block_cols), 1)
    unit = jnp.where(row == column, 1.0, 0.0)
    pad = jnp.zeros((block_cols, 2 * basis_cols - joined - block_cols), jnp.float32)
    work = jnp.concatenate((-coeffs, unit, matrix, pad), axis=1)
    height = lax.broadcasted_iota(jnp.int32, work.shape, 0)
    for step in range(block_cols):
        pivots = jnp.broadcast_to(work[:, joined + step : joined + step + 1], work.shape)
        pivot = pivots[step : step + 1, :]
        pivot_row = work[step : step + 1, :]
        scaled = pivot_row / pivot
        new_row = pivot_row * lax.rsqrt(pivot)
        work = jnp.where(
            height > step, work - pivots * scaled, jnp.where(height == step, new_row, work)
        )
    upper_ref[...] = work[:, joined : joined + block_cols]
    weights = three_parts(work[:, :joined])
    wide = jnp.concatenate(
        [jnp.concatenate((part, part, part), axis=1) for part in weights], axis=0
    )
    result = jnp.dot(wide, stack_ref[...], preferred_element_type=jnp.float32)
    result = result[:block_cols] + result[block_cols : 2 * block_cols] + result[2 * block_cols :]
    for line in range(lines):
        block_ref[pl.ds(line, block_cols, stride=lines), :] = result[
            :, line * lanes : (line + 1) * lanes
        ]


def finish(place, parts, stack, row_count, block_cols, group_cols, lines):
    lanes = stack.shape[1] // lines
    basis_cols = parts.shape[2] // 2
    return pl.pallas_call(
        functools.partial(finish_kernel, row_count),
        out_shape=(
            f32(block_cols * lines, lanes), f32(group_cols, block_cols), f32(block_cols, block_cols),
        ),
        in_specs=[SMEM] + [VMEM] * 2,
        out_specs=(VMEM, VMEM, VMEM),
        scratch_shapes=[pltpu.VMEM((basis_cols, block_cols), jnp.float32)],
        compiler_params=SCRATCH,
        name="finish",
    )(place, *kept(parts, stack))


def shards(
    x_block, basis, material, k0_blocks, k0_diag, ke_blocks, mass, velocities, shifts, sample
):
    block_cols, comps, extent_x, rows, lanes = x_block.shape
    group_cols = basis.shape[0]
    lines = comps * rows
    row_count = float(comps * extent_x * lax.axis_size("space") * basis.shape[3] * lanes)

    place = lax.axis_index("basis").astype(jnp.int32).reshape(1)
    slab = lax.axis_index("space").astype(jnp.int32).reshape(1)
    count = lax.axis_size("basis")
    x_far = x_block.reshape(block_cols * lines, lanes)
    own, *pieces, x_rows, material = pack(place, basis, x_far, material.reshape(rows, lanes), block_cols)
    got = {}
    for name in ("odd", 3, "even", 2, 1):
        if name == "even":
            got[name] = swap(x_far, "space", 0)
        elif name == "odd":
            got[name] = swap(x_far, "space", 1)
        else:
            piece = lax.ppermute(pieces[name - 1], "basis", [(i, i ^ name) for i in range(count)])
            got[name] = piece.reshape(-1, lanes)
    fields, applied, own = ahead(
        sample, velocities, shifts, k0_blocks, ke_blocks, k0_diag, mass, material, x_rows,
        own.reshape(-1, lanes), comps,
    )
    applied = add_side(slab, fields, applied, got.pop("odd"), comps, "odd")
    stack, part = sums(place, slab, fields, applied, own, got, comps)
    parts = exchange(exchange_sum(part, "basis"), "space")
    block, coeffs, upper = finish(place, parts, stack, row_count, block_cols, group_cols, lines)
    return (block.reshape(x_block.shape), coeffs, upper)


def solution(mesh):
    in_specs = (
        P(None, None, "space", "basis", None),
        P("basis", None, "space", None, None),
        P("space", "basis", None),
        P(),
        P(),
        P(),
        P(),
        P(),
        P(),
        P(),
    )
    out_specs = (P(None, None, "space", "basis", None), P("basis", None), P())
    return jax.shard_map(shards, mesh=mesh, in_specs=in_specs, out_specs=out_specs, check_vma=False)
```

```python
import functools

import jax
import jax.numpy as jnp
from jax import lax
from jax.experimental import pallas as pl
from jax.experimental.pallas import tpu as pltpu
from jax.sharding import PartitionSpec as P

exact_precision = lax.Precision.HIGHEST
VMEM = pl.BlockSpec(memory_space=pltpu.VMEM)
SMEM = pl.BlockSpec(memory_space=pltpu.SMEM)
HBM = pl.BlockSpec(memory_space=pltpu.HBM)
EARLY = pl.CostEstimate(flops=10**9, bytes_accessed=10**6, transcendentals=0)
NEXT = pl.CostEstimate(flops=10**6, bytes_accessed=10**6, transcendentals=0)
SCRATCH = pltpu.CompilerParams(vmem_limit_bytes=8 * 2**20)


def f32(*shape):
    return jax.ShapeDtypeStruct(shape, jnp.float32)


def near(*shape, dtype=jnp.float32):
    return pltpu.VMEM(shape, dtype)


def kept(*arrays):
    return [pltpu.with_memory_space_constraint(array, pltpu.VMEM) for array in arrays]


def far(*arrays):
    return [pltpu.with_memory_space_constraint(array, pltpu.HBM) for array in arrays]


def swap(values, axis, first):
    pairs = [(i, i + 1) for i in range(first, lax.axis_size(axis) - 1, 2)]
    return lax.ppermute(values, axis, pairs + [(j, i) for i, j in pairs])


def partners(count):
    return range(1, count), [k for k in range(1, count) if k & (k + 1) == 0]


def pack_kernel(comps, place_ref, basis_ref, x_ref, material_ref, *refs):
    *piece_refs, x_out_ref, material_out_ref, sems = refs
    count = len(piece_refs)
    tiles, _, rows, lanes = basis_ref.shape
    block_cols = x_ref.shape[0] // (comps * rows)
    place = place_ref[0]
    x_copy = pltpu.make_async_copy(x_ref, x_out_ref, sems.at[count])
    x_copy.start()
    copies = [pltpu.make_async_copy(material_ref, material_out_ref, sems.at[count + 1])]
    for k in reversed(range(count)):
        copies.append(
            pltpu.make_async_copy(
                basis_ref.at[:, place ^ k], piece_refs[k].at[pl.ds(0, tiles)], sems.at[k]
            )
        )
    for copy in copies:
        copy.start()
    x_copy.wait()
    for comp in range(comps):
        first, last = (
            x_out_ref[pl.ds(comp * rows + row, block_cols, stride=comps * rows), :]
            for row in (0, rows - 1)
        )
        for k in partners(count)[1]:
            edge = jnp.where((place ^ k) > place, last, first)
            for part in range(block_cols // rows):
                piece_refs[k][tiles + comp * (block_cols // rows) + part] = edge[
                    part * rows : (part + 1) * rows
                ]
    for copy in copies:
        copy.wait()


def pack(place, basis, x_rows, material, block_cols):
    group_cols, comps, _, full_y, lanes = basis.shape
    count = lax.axis_size("basis")
    rows = full_y // count
    tiles = group_cols * comps
    edge_tiles = block_cols * comps // rows
    pieces = [
        near(tiles + (edge_tiles if k in partners(count)[1] else 0), rows, lanes)
        for k in range(count)
    ]
    return pl.pallas_call(
        functools.partial(pack_kernel, comps),
        out_shape=(*pieces, near(*x_rows.shape), near(*material.shape, dtype=jnp.int32)),
        in_specs=[SMEM, HBM, HBM, HBM],
        out_specs=(VMEM,) * (count + 2),
        scratch_shapes=[pltpu.SemaphoreType.DMA((count + 2,))],
        compiler_params=SCRATCH,
        name="pack",
    )(place, *far(basis.reshape(tiles, count, rows, lanes), x_rows, material))


def three_parts(values):
    high = values.astype(jnp.bfloat16)
    rest = values - high.astype(jnp.float32)
    middle = rest.astype(jnp.bfloat16)
    low = (rest - middle.astype(jnp.float32)).astype(jnp.bfloat16)
    return high, middle, low


def line_of(ref, comp, row, comps, rows, block_cols):
    return ref[pl.ds(comp * rows + row, block_cols, stride=comps * rows), :]


def ahead_kernel(
    sample_ref, *refs
):
    far_refs, refs = refs[:6], refs[6:]
    material_ref, x_ref, own_ref, fields_ref, applied_ref, stack_ref, *near_refs, sems = refs
    velocities_ref, shifts_ref, k0_ref, ke_ref, diag_ref, mass_ref = near_refs
    copies = [
        pltpu.make_async_copy(source, target, sems.at[index])
        for index, (source, target) in enumerate(zip(far_refs, near_refs))
    ]
    for copy in copies:
        copy.start()
    group_cols = stack_ref.shape[0] // 3
    split_lines(
        own_ref, stack_ref, applied_ref.shape[0], group_cols, [i * group_cols for i in range(3)]
    )
    for copy in copies:
        copy.wait()
    comps, _, levels, offsets = k0_ref.shape
    rows, lanes = material_ref.shape
    lines = comps * rows
    block_cols = x_ref.shape[0] // lines
    velocity = velocities_ref[sample_ref[0]]
    sigma = shifts_ref[sample_ref[0]]
    entry_rows = fields_ref.shape[1]
    stride = entry_rows // (comps * comps)
    gap = jnp.zeros((levels, stride - offsets), jnp.float32)
    wide = []
    for out in range(comps):
        for comp in range(comps):
            wide += [k0_ref[out, comp] - velocity * velocity * ke_ref[out, comp], gap]
    wide.append(jnp.zeros((levels, lanes - entry_rows), jnp.float32))
    table = jnp.concatenate(wide, axis=1).T[:entry_rows]
    entry = lax.broadcasted_iota(jnp.int32, table.shape, 0)
    for comp in range(comps):
        centre = diag_ref[comp : comp + 1, :] - sigma * mass_ref[comp : comp + 1, :]
        table = table + jnp.where(entry == comp * (comps + 1) * stride, centre, 0.0)

    lane = lax.broadcasted_iota(jnp.int32, (block_cols, lanes), 1)
    level = lax.broadcasted_iota(jnp.int32, (levels, lanes), 0)
    for row in range(rows):
        chosen = jnp.broadcast_to(material_ref[row : row + 1, :], (levels, lanes)) == level
        fields = jnp.dot(
            table, chosen.astype(jnp.float32),
            precision=exact_precision, preferred_element_type=jnp.float32,
        )
        fields_ref[row] = fields
        sums = [None] * comps
        for comp in range(comps):
            centre = line_of(x_ref, comp, row, comps, rows, block_cols)
            views = {
                0: centre,
                5: jnp.where(lane == 0, 0.0, pltpu.roll(centre, 1, 1)),
                6: jnp.where(lane == lanes - 1, 0.0, pltpu.roll(centre, lanes - 1, 1)),
            }
            if row > 0:
                views[3] = line_of(x_ref, comp, row - 1, comps, rows, block_cols)
            if row < rows - 1:
                views[4] = line_of(x_ref, comp, row + 1, comps, rows, block_cols)
            for offset, view in views.items():
                for out in range(comps):
                    place = (out * comps + comp) * stride + offset
                    term = fields[place : place + 1, :] * view
                    sums[out] = term if sums[out] is None else sums[out] + term
        for out in range(comps):
            applied_ref[out * rows + row] = sums[out]


def ahead(sample, velocities, shifts, k0, ke, diag, mass, material, x_rows, own, comps):
    rows, lanes = material.shape
    lines = comps * rows
    stride = -(-k0.shape[1] // 8) * 8
    k0, ke = (jnp.transpose(blocks, (2, 3, 0, 1)) for blocks in (k0, ke))
    tables = far(velocities, shifts, k0, ke, diag.T, mass.T)
    return pl.pallas_call(
        ahead_kernel,
        out_shape=(
            near(rows, comps * comps * stride, lanes),
            near(lines, x_rows.shape[0] // lines, lanes),
            near(3 * own.shape[0] // lines, lines * lanes, dtype=jnp.bfloat16),
        ),
        in_specs=[SMEM] + [HBM] * 6 + [VMEM] * 3,
        out_specs=(VMEM,) * 3,
        scratch_shapes=[
            (pltpu.SMEM if array.ndim == 1 else pltpu.VMEM)(array.shape, jnp.float32)
            for array in tables
        ] + [pltpu.SemaphoreType.DMA((len(tables),))],
        compiler_params=SCRATCH,
        name="ahead",
    )(sample, *tables, *kept(material, x_rows, own))


def side_terms(field_row, swapped, side, out, comp, comps):
    stride = field_row.shape[0] // (comps * comps)
    begin = (out * comps + comp) * stride
    below, above = field_row[begin + 1 : begin + 2], field_row[begin + 2 : begin + 3]
    other = (below, above) if side == "even" else (above, below)
    return jnp.where(swapped, *other)


def side_kernel(comps, side, slab_ref, fields_ref, applied_ref, halo_ref, out_ref):
    lines, block_cols, _ = applied_ref.shape
    rows = lines // comps
    swapped = slab_ref[0] % 2 == 1
    for row in range(rows):
        field_row = fields_ref[row]
        views = [line_of(halo_ref, comp, row, comps, rows, block_cols) for comp in range(comps)]
        for out in range(comps):
            total = applied_ref[out * rows + row]
            for comp, view in enumerate(views):
                total = total + side_terms(field_row, swapped, side, out, comp, comps) * view
            out_ref[out * rows + row] = total


def add_side(slab, fields, applied, halo, comps, side):
    return pl.pallas_call(
        functools.partial(side_kernel, comps, side),
        out_shape=near(*applied.shape),
        in_specs=[SMEM] + [VMEM] * 3,
        out_specs=VMEM,
        compiler_params=SCRATCH,
        cost_estimate=EARLY,
        name="side",
    )(slab, *kept(fields, applied, halo))


def split_lines(piece_ref, stack_ref, lines, group_cols, begins):
    lanes = piece_ref.shape[1]
    for line in range(lines):
        values = piece_ref[pl.ds(line, group_cols, stride=lines), :]
        for begin, part in zip(begins, three_parts(values)):
            stack_ref[pl.ds(begin, group_cols), pl.ds(line * lanes, lanes)] = part


def edges_kernel(comps, ks, group_cols, place_ref, fields_ref, applied_ref, *refs):
    piece_refs, out_ref, parts_refs = refs[: len(ks)], refs[len(ks)], refs[len(ks) + 1 :]
    lines, block_cols, lanes = applied_ref.shape
    rows = lines // comps
    stride = fields_ref.shape[1] // (comps * comps)
    place = place_ref[0]

    def edge(comp, step):
        result = jnp.zeros((block_cols, lanes), jnp.float32)
        for k, ref in zip(ks, piece_refs):
            begin = ref.shape[0] - (comps - comp) * block_cols
            here = (place ^ k) == place + step
            result = jnp.where(here, ref[pl.ds(begin, block_cols), :], result)
        return result

    out_ref[...] = applied_ref[...]
    for row, offset, step in ((0, 3, -1), (rows - 1, 4, 1)):
        field_row = fields_ref[row]
        views = [edge(comp, step) for comp in range(comps)]
        for out in range(comps):
            total = out_ref[out * rows + row]
            for comp, view in enumerate(views):
                entry = (out * comps + comp) * stride + offset
                total = total + field_row[entry : entry + 1] * view
            out_ref[out * rows + row] = total
    for piece_ref, parts_ref in zip(piece_refs, parts_refs):
        split_lines(piece_ref, parts_ref, lines, group_cols, [i * group_cols for i in range(3)])


def add_edges(place, fields, applied, pieces, comps, group_cols):
    lines, _, lanes = applied.shape
    parts = near(3 * group_cols, lines * lanes, dtype=jnp.bfloat16)
    return pl.pallas_call(
        functools.partial(edges_kernel, comps, tuple(pieces), group_cols),
        out_shape=(near(*applied.shape),) + (parts,) * len(pieces),
        in_specs=[SMEM] + [VMEM] * (2 + len(pieces)),
        out_specs=(VMEM,) * (1 + len(pieces)),
        compiler_params=SCRATCH,
        cost_estimate=NEXT,
        name="edges",
    )(place, *kept(fields, applied, *pieces.values()))


def fold(total, basis_cols, block_cols, lanes):
    half = basis_cols // 2
    row = lax.broadcasted_iota(jnp.int32, (half, half), 0)
    column = lax.broadcasted_iota(jnp.int32, (half, half), 1)
    last = total[half:basis_cols, half:basis_cols]
    shared = jnp.where(row >= column, total[:half, :half], last)
    diagonal = jnp.sum(jnp.where(row == column, last, 0.0), axis=1, keepdims=True)
    below = total[basis_cols:]
    first = jnp.concatenate((below[:, :half], below[:, half:basis_cols]), axis=0)
    rest = jnp.zeros((half - block_cols, block_cols), jnp.float32)
    block = jnp.concatenate((below[:, basis_cols:], rest), axis=0)
    pad = jnp.zeros((half, lanes - 3 * half - block_cols - 1), jnp.float32)
    return jnp.concatenate(
        (shared, total[:half, half:basis_cols], first, block, diagonal, pad), axis=1
    )


def unfold(folded, block_cols):
    half = folded.shape[0]
    row = lax.broadcasted_iota(jnp.int32, (half, half), 0)
    column = lax.broadcasted_iota(jnp.int32, (half, half), 1)
    shared, across = folded[:, :half], folded[:, half : 2 * half]
    turned = shared.T
    start = jnp.where(row >= column, shared, turned)
    end = jnp.where(row < column, shared, turned)
    diagonal = folded[:, 3 * half + block_cols : 3 * half + block_cols + 1]
    end = jnp.where(row == column, diagonal, end)
    gram = jnp.concatenate(
        (jnp.concatenate((start, across), axis=1), jnp.concatenate((across.T, end), axis=1)), axis=0
    )
    first = folded[:, 2 * half : 3 * half]
    first = jnp.concatenate((first[:block_cols], first[block_cols : 2 * block_cols]), axis=1)
    return gram, first, folded[:block_cols, 3 * half : 3 * half + block_cols]


def sums_kernel(
    comps, split, raw, place_ref, slab_ref, fields_ref, applied_ref, halo_ref, *refs
):
    *refs, stack_ref, sums_ref = refs
    lines, block_cols, lanes = applied_ref.shape
    rows = lines // comps
    group_cols = refs[0].shape[0] // 3
    basis_cols = (len(split) + len(raw)) * group_cols
    joined = basis_cols + block_cols
    place = place_ref[0]
    swapped = slab_ref[0] % 2 == 1
    for k, ref in zip(split + raw, refs):
        begin = pl.multiple_of((place ^ k) * group_cols, group_cols)
        begins = [index * joined + begin for index in range(3)]
        if k in split:
            for index in range(3):
                stack_ref[pl.ds(begins[index], group_cols), :] = ref[
                    pl.ds(index * group_cols, group_cols), :
                ]
        else:
            split_lines(ref, stack_ref, lines, group_cols, begins)
    for row in range(rows):
        field_row = fields_ref[row]
        views = [line_of(halo_ref, comp, row, comps, rows, block_cols) for comp in range(comps)]
        for out in range(comps):
            line = out * rows + row
            total = applied_ref[line]
            for comp, view in enumerate(views):
                total = total + side_terms(field_row, swapped, "odd", out, comp, comps) * view
            for index, part in enumerate(three_parts(total)):
                there = pl.ds(index * joined + basis_cols, block_cols)
                stack_ref[there, pl.ds(line * lanes, lanes)] = part

    stack = stack_ref[...]
    products = lax.dot_general(
        stack, stack, (((1,), (1,)), ((), ())), preferred_element_type=jnp.float32
    )
    wide = products[:joined] + products[joined : 2 * joined] + products[2 * joined :]
    total = wide[:, :joined] + wide[:, joined : 2 * joined] + wide[:, 2 * joined :]
    sums_ref[...] = fold(total, basis_cols, block_cols, sums_ref.shape[1])


def sums(place, slab, fields, applied, halo, split, raw, comps):
    lines, block_cols, lanes = applied.shape
    basis_cols = (len(split) + len(raw)) * (split[0].shape[0] // 3)
    joined = basis_cols + block_cols
    return pl.pallas_call(
        functools.partial(sums_kernel, comps, tuple(split), tuple(raw)),
        out_shape=(
            near(3 * joined, lines * lanes, dtype=jnp.bfloat16),
            near(basis_cols // 2, 2 * basis_cols),
        ),
        in_specs=[SMEM] * 2 + [VMEM] * (3 + len(split) + len(raw)),
        out_specs=(VMEM, VMEM),
        compiler_params=SCRATCH,
        name="sums",
    )(place, slab, *kept(fields, applied, halo, *split.values(), *raw.values()))


def exchange_sum(part, axis):
    count = lax.axis_size(axis)
    terms = [part] + [
        lax.ppermute(part, axis, [(i, i ^ k) for i in range(count)]) for k in range(1, count)
    ]
    while len(terms) > 1:
        terms = [a + b for a, b in zip(terms[::2], terms[1::2])]
    return terms[0]


def exchange(part, axis):
    count = lax.axis_size(axis)
    return lax.all_to_all(jnp.broadcast_to(part[None], (count,) + part.shape), axis, 0, 0)


def finish_kernel(
    row_count, place_ref, parts_ref, stack_ref, block_ref, coeffs_ref, upper_ref,
    coeffs_scratch,
):
    block_cols = upper_ref.shape[0]
    basis_cols = parts_ref.shape[2] // 2
    joined = basis_cols + block_cols
    lines = block_ref.shape[0] // block_cols
    lanes = block_ref.shape[1]
    total = jnp.sum(parts_ref[...], axis=0) / row_count
    gram, first, block_gram = unfold(total, block_cols)

    def times(left, right, right_dim=0):
        return lax.dot_general(
            left, right, (((1,), (right_dim,)), ((), ())),
            precision=exact_precision, preferred_element_type=jnp.float32,
        )

    coeffs = first + (first - times(first, gram))
    image = times(coeffs, gram)
    matrix = block_gram - times(coeffs, first, 1) - times(first - image, coeffs, 1)
    coeffs_scratch[...] = coeffs.T
    group_cols = coeffs_ref.shape[0]
    start = pl.multiple_of(place_ref[0] * group_cols, group_cols)
    coeffs_ref[...] = coeffs_scratch[pl.ds(start, group_cols), :]

    row = lax.broadcasted_iota(jnp.int32, (block_cols, block_cols), 0)
    column = lax.broadcasted_iota(jnp.int32, (block_cols, block_cols), 1)
    unit = jnp.where(row == column, 1.0, 0.0)
    pad = jnp.zeros((block_cols, 2 * basis_cols - joined - block_cols), jnp.float32)
    work = jnp.concatenate((-coeffs, unit, matrix, pad), axis=1)
    height = lax.broadcasted_iota(jnp.int32, work.shape, 0)
    for step in range(block_cols):
        pivots = jnp.broadcast_to(work[:, joined + step : joined + step + 1], work.shape)
        pivot = pivots[step : step + 1, :]
        pivot_row = work[step : step + 1, :]
        scaled = pivot_row / pivot
        new_row = pivot_row * lax.rsqrt(pivot)
        work = jnp.where(
            height > step, work - pivots * scaled, jnp.where(height == step, new_row, work)
        )
    upper_ref[...] = work[:, joined : joined + block_cols]
    weights = three_parts(work[:, :joined])
    wide = jnp.concatenate(
        [jnp.concatenate((part, part, part), axis=1) for part in weights], axis=0
    )
    result = jnp.dot(wide, stack_ref[...], preferred_element_type=jnp.float32)
    result = result[:block_cols] + result[block_cols : 2 * block_cols] + result[2 * block_cols :]
    for line in range(lines):
        block_ref[pl.ds(line, block_cols, stride=lines), :] = result[
            :, line * lanes : (line + 1) * lanes
        ]


def finish(place, parts, stack, row_count, block_cols, group_cols, lines):
    lanes = stack.shape[1] // lines
    basis_cols = parts.shape[2] // 2
    return pl.pallas_call(
        functools.partial(finish_kernel, row_count),
        out_shape=(
            f32(block_cols * lines, lanes), f32(group_cols, block_cols), f32(block_cols, block_cols),
        ),
        in_specs=[SMEM] + [VMEM] * 2,
        out_specs=(VMEM, VMEM, VMEM),
        scratch_shapes=[pltpu.VMEM((basis_cols, block_cols), jnp.float32)],
        compiler_params=SCRATCH,
        name="finish",
    )(place, *kept(parts, stack))


def shards(
    x_block, basis, material, k0_blocks, k0_diag, ke_blocks, mass, velocities, shifts, sample
):
    block_cols, comps, extent_x, rows, lanes = x_block.shape
    group_cols = basis.shape[0]
    lines = comps * rows
    row_count = float(comps * extent_x * lax.axis_size("space") * basis.shape[3] * lanes)

    place = lax.axis_index("basis").astype(jnp.int32).reshape(1)
    slab = lax.axis_index("space").astype(jnp.int32).reshape(1)
    count = lax.axis_size("basis")
    x_far = x_block.reshape(block_cols * lines, lanes)
    own, *pieces, x_rows, material = pack(place, basis, x_far, material.reshape(rows, lanes), block_cols)
    got = {}
    for name in ("even", 3, "odd", 2, 1):
        if name == "even":
            got[name] = swap(x_far, "space", 0)
        elif name == "odd":
            got[name] = swap(x_far, "space", 1)
        else:
            piece = lax.ppermute(pieces[name - 1], "basis", [(i, i ^ name) for i in range(count)])
            got[name] = piece.reshape(-1, lanes)
    fields, applied, own = ahead(
        sample, velocities, shifts, k0_blocks, ke_blocks, k0_diag, mass, material, x_rows,
        own.reshape(-1, lanes), comps,
    )
    applied = add_side(slab, fields, applied, got.pop("even"), comps, "even")
    pieces = {k: got.pop(k) for k in reversed(partners(count)[1])}
    applied, *parts = add_edges(place, fields, applied, pieces, comps, group_cols)
    split = {0: own, **dict(zip(pieces, parts))}
    stack, part = sums(place, slab, fields, applied, got.pop("odd"), split, got, comps)
    parts = exchange(exchange_sum(part, "basis"), "space")
    block, coeffs, upper = finish(place, parts, stack, row_count, block_cols, group_cols, lines)
    return (block.reshape(x_block.shape), coeffs, upper)


def solution(mesh):
    in_specs = (
        P(None, None, "space", "basis", None),
        P("basis", None, "space", None, None),
        P("space", "basis", None),
        P(),
        P(),
        P(),
        P(),
        P(),
        P(),
        P(),
    )
    out_specs = (P(None, None, "space", "basis", None), P("basis", None), P())
    return jax.shard_map(shards, mesh=mesh, in_specs=in_specs, out_specs=out_specs, check_vma=False)
```

```python
import functools

import jax
import jax.numpy as jnp
from jax import lax
from jax.experimental import pallas as pl
from jax.experimental.pallas import tpu as pltpu
from jax.sharding import PartitionSpec as P

exact_precision = lax.Precision.HIGHEST
VMEM = pl.BlockSpec(memory_space=pltpu.VMEM)
SMEM = pl.BlockSpec(memory_space=pltpu.SMEM)
HBM = pl.BlockSpec(memory_space=pltpu.HBM)
EARLY = pl.CostEstimate(flops=10**9, bytes_accessed=10**6, transcendentals=0)
NEXT = pl.CostEstimate(flops=10**6, bytes_accessed=10**6, transcendentals=0)
SCRATCH = pltpu.CompilerParams(vmem_limit_bytes=8 * 2**20)


def f32(*shape):
    return jax.ShapeDtypeStruct(shape, jnp.float32)


def near(*shape, dtype=jnp.float32):
    return pltpu.VMEM(shape, dtype)


def kept(*arrays):
    return [pltpu.with_memory_space_constraint(array, pltpu.VMEM) for array in arrays]


def far(*arrays):
    return [pltpu.with_memory_space_constraint(array, pltpu.HBM) for array in arrays]


def swap(values, axis, first):
    pairs = [(i, i + 1) for i in range(first, lax.axis_size(axis) - 1, 2)]
    return lax.ppermute(values, axis, pairs + [(j, i) for i, j in pairs])


def partners(count):
    return range(1, count), [k for k in range(1, count) if k & (k + 1) == 0]


def pack_kernel(comps, place_ref, basis_ref, x_ref, material_ref, *refs):
    *piece_refs, x_out_ref, material_out_ref, sems = refs
    count = len(piece_refs)
    tiles, _, rows, lanes = basis_ref.shape
    block_cols = x_ref.shape[0] // (comps * rows)
    place = place_ref[0]
    x_copy = pltpu.make_async_copy(x_ref, x_out_ref, sems.at[count])
    x_copy.start()
    copies = [pltpu.make_async_copy(material_ref, material_out_ref, sems.at[count + 1])]
    for k in reversed(range(count)):
        copies.append(
            pltpu.make_async_copy(
                basis_ref.at[:, place ^ k], piece_refs[k].at[pl.ds(0, tiles)], sems.at[k]
            )
        )
    for copy in copies:
        copy.start()
    x_copy.wait()
    for comp in range(comps):
        first, last = (
            x_out_ref[pl.ds(comp * rows + row, block_cols, stride=comps * rows), :]
            for row in (0, rows - 1)
        )
        for k in partners(count)[1]:
            edge = jnp.where((place ^ k) > place, last, first)
            for part in range(block_cols // rows):
                piece_refs[k][tiles + comp * (block_cols // rows) + part] = edge[
                    part * rows : (part + 1) * rows
                ]
    for copy in copies:
        copy.wait()


def pack(place, basis, x_rows, material, block_cols):
    group_cols, comps, _, full_y, lanes = basis.shape
    count = lax.axis_size("basis")
    rows = full_y // count
    tiles = group_cols * comps
    edge_tiles = block_cols * comps // rows
    pieces = [
        near(tiles + (edge_tiles if k in partners(count)[1] else 0), rows, lanes)
        for k in range(count)
    ]
    return pl.pallas_call(
        functools.partial(pack_kernel, comps),
        out_shape=(*pieces, near(*x_rows.shape), near(*material.shape, dtype=jnp.int32)),
        in_specs=[SMEM, HBM, HBM, HBM],
        out_specs=(VMEM,) * (count + 2),
        scratch_shapes=[pltpu.SemaphoreType.DMA((count + 2,))],
        compiler_params=SCRATCH,
        name="pack",
    )(place, *far(basis.reshape(tiles, count, rows, lanes), x_rows, material))


def three_parts(values):
    high = values.astype(jnp.bfloat16)
    rest = values - high.astype(jnp.float32)
    middle = rest.astype(jnp.bfloat16)
    low = (rest - middle.astype(jnp.float32)).astype(jnp.bfloat16)
    return high, middle, low


def line_of(ref, comp, row, comps, rows, block_cols):
    return ref[pl.ds(comp * rows + row, block_cols, stride=comps * rows), :]


def ahead_kernel(
    sample_ref, *refs
):
    far_refs, refs = refs[:6], refs[6:]
    material_ref, x_ref, own_ref, fields_ref, applied_ref, stack_ref, *near_refs, sems = refs
    velocities_ref, shifts_ref, k0_ref, ke_ref, diag_ref, mass_ref = near_refs
    copies = [
        pltpu.make_async_copy(source, target, sems.at[index])
        for index, (source, target) in enumerate(zip(far_refs, near_refs))
    ]
    for copy in copies:
        copy.start()
    group_cols = stack_ref.shape[0] // 3
    split_lines(
        own_ref, stack_ref, applied_ref.shape[0], group_cols, [i * group_cols for i in range(3)]
    )
    for copy in copies:
        copy.wait()
    comps, _, levels, offsets = k0_ref.shape
    rows, lanes = material_ref.shape
    lines = comps * rows
    block_cols = x_ref.shape[0] // lines
    velocity = velocities_ref[sample_ref[0]]
    sigma = shifts_ref[sample_ref[0]]
    entry_rows = fields_ref.shape[1]
    stride = entry_rows // (comps * comps)
    gap = jnp.zeros((levels, stride - offsets), jnp.float32)
    wide = []
    for out in range(comps):
        for comp in range(comps):
            wide += [k0_ref[out, comp] - velocity * velocity * ke_ref[out, comp], gap]
    wide.append(jnp.zeros((levels, lanes - entry_rows), jnp.float32))
    table = jnp.concatenate(wide, axis=1).T[:entry_rows]
    entry = lax.broadcasted_iota(jnp.int32, table.shape, 0)
    for comp in range(comps):
        centre = diag_ref[comp : comp + 1, :] - sigma * mass_ref[comp : comp + 1, :]
        table = table + jnp.where(entry == comp * (comps + 1) * stride, centre, 0.0)

    lane = lax.broadcasted_iota(jnp.int32, (block_cols, lanes), 1)
    level = lax.broadcasted_iota(jnp.int32, (levels, lanes), 0)
    for row in range(rows):
        chosen = jnp.broadcast_to(material_ref[row : row + 1, :], (levels, lanes)) == level
        fields = jnp.dot(
            table, chosen.astype(jnp.float32),
            precision=exact_precision, preferred_element_type=jnp.float32,
        )
        fields_ref[row] = fields
        sums = [None] * comps
        for comp in range(comps):
            centre = line_of(x_ref, comp, row, comps, rows, block_cols)
            views = {
                0: centre,
                5: jnp.where(lane == 0, 0.0, pltpu.roll(centre, 1, 1)),
                6: jnp.where(lane == lanes - 1, 0.0, pltpu.roll(centre, lanes - 1, 1)),
            }
            if row > 0:
                views[3] = line_of(x_ref, comp, row - 1, comps, rows, block_cols)
            if row < rows - 1:
                views[4] = line_of(x_ref, comp, row + 1, comps, rows, block_cols)
            for offset, view in views.items():
                for out in range(comps):
                    place = (out * comps + comp) * stride + offset
                    term = fields[place : place + 1, :] * view
                    sums[out] = term if sums[out] is None else sums[out] + term
        for out in range(comps):
            applied_ref[out * rows + row] = sums[out]


def ahead(sample, velocities, shifts, k0, ke, diag, mass, material, x_rows, own, comps):
    rows, lanes = material.shape
    lines = comps * rows
    stride = -(-k0.shape[1] // 8) * 8
    k0, ke = (jnp.transpose(blocks, (2, 3, 0, 1)) for blocks in (k0, ke))
    tables = far(velocities, shifts, k0, ke, diag.T, mass.T)
    return pl.pallas_call(
        ahead_kernel,
        out_shape=(
            near(rows, comps * comps * stride, lanes),
            near(lines, x_rows.shape[0] // lines, lanes),
            near(3 * own.shape[0] // lines, lines * lanes, dtype=jnp.bfloat16),
        ),
        in_specs=[SMEM] + [HBM] * 6 + [VMEM] * 3,
        out_specs=(VMEM,) * 3,
        scratch_shapes=[
            (pltpu.SMEM if array.ndim == 1 else pltpu.VMEM)(array.shape, jnp.float32)
            for array in tables
        ] + [pltpu.SemaphoreType.DMA((len(tables),))],
        compiler_params=SCRATCH,
        name="ahead",
    )(sample, *tables, *kept(material, x_rows, own))


def side_terms(field_row, swapped, side, out, comp, comps):
    stride = field_row.shape[0] // (comps * comps)
    begin = (out * comps + comp) * stride
    below, above = field_row[begin + 1 : begin + 2], field_row[begin + 2 : begin + 3]
    other = (below, above) if side == "even" else (above, below)
    return jnp.where(swapped, *other)


def side_kernel(comps, side, slab_ref, fields_ref, applied_ref, halo_ref, out_ref):
    lines, block_cols, _ = applied_ref.shape
    rows = lines // comps
    swapped = slab_ref[0] % 2 == 1
    for row in range(rows):
        field_row = fields_ref[row]
        views = [line_of(halo_ref, comp, row, comps, rows, block_cols) for comp in range(comps)]
        for out in range(comps):
            total = applied_ref[out * rows + row]
            for comp, view in enumerate(views):
                total = total + side_terms(field_row, swapped, side, out, comp, comps) * view
            out_ref[out * rows + row] = total


def add_side(slab, fields, applied, halo, comps, side):
    return pl.pallas_call(
        functools.partial(side_kernel, comps, side),
        out_shape=near(*applied.shape),
        in_specs=[SMEM] + [VMEM] * 3,
        out_specs=VMEM,
        compiler_params=SCRATCH,
        cost_estimate=EARLY,
        name="side",
    )(slab, *kept(fields, applied, halo))


def split_lines(piece_ref, stack_ref, lines, group_cols, begins):
    lanes = piece_ref.shape[1]
    for line in range(lines):
        values = piece_ref[pl.ds(line, group_cols, stride=lines), :]
        for begin, part in zip(begins, three_parts(values)):
            stack_ref[pl.ds(begin, group_cols), pl.ds(line * lanes, lanes)] = part


def edges_kernel(comps, ks, group_cols, place_ref, fields_ref, applied_ref, *refs):
    piece_refs, out_ref, parts_refs = refs[: len(ks)], refs[len(ks)], refs[len(ks) + 1 :]
    lines, block_cols, lanes = applied_ref.shape
    rows = lines // comps
    stride = fields_ref.shape[1] // (comps * comps)
    place = place_ref[0]

    def edge(comp, step):
        result = jnp.zeros((block_cols, lanes), jnp.float32)
        for k, ref in zip(ks, piece_refs):
            begin = ref.shape[0] - (comps - comp) * block_cols
            here = (place ^ k) == place + step
            result = jnp.where(here, ref[pl.ds(begin, block_cols), :], result)
        return result

    out_ref[...] = applied_ref[...]
    for row, offset, step in ((0, 3, -1), (rows - 1, 4, 1)):
        field_row = fields_ref[row]
        views = [edge(comp, step) for comp in range(comps)]
        for out in range(comps):
            total = out_ref[out * rows + row]
            for comp, view in enumerate(views):
                entry = (out * comps + comp) * stride + offset
                total = total + field_row[entry : entry + 1] * view
            out_ref[out * rows + row] = total
    for piece_ref, parts_ref in zip(piece_refs, parts_refs):
        split_lines(piece_ref, parts_ref, lines, group_cols, [i * group_cols for i in range(3)])


def add_edges(place, fields, applied, pieces, comps, group_cols):
    lines, _, lanes = applied.shape
    parts = near(3 * group_cols, lines * lanes, dtype=jnp.bfloat16)
    return pl.pallas_call(
        functools.partial(edges_kernel, comps, tuple(pieces), group_cols),
        out_shape=(near(*applied.shape),) + (parts,) * len(pieces),
        in_specs=[SMEM] + [VMEM] * (2 + len(pieces)),
        out_specs=(VMEM,) * (1 + len(pieces)),
        compiler_params=SCRATCH,
        cost_estimate=NEXT,
        name="edges",
    )(place, *kept(fields, applied, *pieces.values()))


def fold(total, basis_cols, block_cols, lanes):
    half = basis_cols // 2
    row = lax.broadcasted_iota(jnp.int32, (half, half), 0)
    column = lax.broadcasted_iota(jnp.int32, (half, half), 1)
    last = total[half:basis_cols, half:basis_cols]
    shared = jnp.where(row >= column, total[:half, :half], last)
    diagonal = jnp.sum(jnp.where(row == column, last, 0.0), axis=1, keepdims=True)
    below = total[basis_cols:]
    first = jnp.concatenate((below[:, :half], below[:, half:basis_cols]), axis=0)
    rest = jnp.zeros((half - block_cols, block_cols), jnp.float32)
    block = jnp.concatenate((below[:, basis_cols:], rest), axis=0)
    pad = jnp.zeros((half, lanes - 3 * half - block_cols - 1), jnp.float32)
    return jnp.concatenate(
        (shared, total[:half, half:basis_cols], first, block, diagonal, pad), axis=1
    )


def unfold(folded, block_cols):
    half = folded.shape[0]
    row = lax.broadcasted_iota(jnp.int32, (half, half), 0)
    column = lax.broadcasted_iota(jnp.int32, (half, half), 1)
    shared, across = folded[:, :half], folded[:, half : 2 * half]
    turned = shared.T
    start = jnp.where(row >= column, shared, turned)
    end = jnp.where(row < column, shared, turned)
    diagonal = folded[:, 3 * half + block_cols : 3 * half + block_cols + 1]
    end = jnp.where(row == column, diagonal, end)
    gram = jnp.concatenate(
        (jnp.concatenate((start, across), axis=1), jnp.concatenate((across.T, end), axis=1)), axis=0
    )
    first = folded[:, 2 * half : 3 * half]
    first = jnp.concatenate((first[:block_cols], first[block_cols : 2 * block_cols]), axis=1)
    return gram, first, folded[:block_cols, 3 * half : 3 * half + block_cols]


def sums_kernel(
    comps, split, raw, place_ref, slab_ref, fields_ref, applied_ref, halo_ref, *refs
):
    *refs, stack_ref, sums_ref = refs
    lines, block_cols, lanes = applied_ref.shape
    rows = lines // comps
    group_cols = refs[0].shape[0] // 3
    basis_cols = (len(split) + len(raw)) * group_cols
    joined = basis_cols + block_cols
    place = place_ref[0]
    swapped = slab_ref[0] % 2 == 1
    for k, ref in zip(split + raw, refs):
        begin = pl.multiple_of((place ^ k) * group_cols, group_cols)
        begins = [index * joined + begin for index in range(3)]
        if k in split:
            for index in range(3):
                stack_ref[pl.ds(begins[index], group_cols), :] = ref[
                    pl.ds(index * group_cols, group_cols), :
                ]
        else:
            split_lines(ref, stack_ref, lines, group_cols, begins)
    for row in range(rows):
        field_row = fields_ref[row]
        views = [line_of(halo_ref, comp, row, comps, rows, block_cols) for comp in range(comps)]
        for out in range(comps):
            line = out * rows + row
            total = applied_ref[line]
            for comp, view in enumerate(views):
                total = total + side_terms(field_row, swapped, "odd", out, comp, comps) * view
            for index, part in enumerate(three_parts(total)):
                there = pl.ds(index * joined + basis_cols, block_cols)
                stack_ref[there, pl.ds(line * lanes, lanes)] = part

    stack = stack_ref[...]
    products = lax.dot_general(
        stack, stack, (((1,), (1,)), ((), ())), preferred_element_type=jnp.float32
    )
    wide = products[:joined] + products[joined : 2 * joined] + products[2 * joined :]
    total = wide[:, :joined] + wide[:, joined : 2 * joined] + wide[:, 2 * joined :]
    sums_ref[...] = fold(total, basis_cols, block_cols, sums_ref.shape[1])


def sums(place, slab, fields, applied, halo, split, raw, comps):
    lines, block_cols, lanes = applied.shape
    basis_cols = (len(split) + len(raw)) * (split[0].shape[0] // 3)
    joined = basis_cols + block_cols
    return pl.pallas_call(
        functools.partial(sums_kernel, comps, tuple(split), tuple(raw)),
        out_shape=(
            near(3 * joined, lines * lanes, dtype=jnp.bfloat16),
            near(basis_cols // 2, 2 * basis_cols),
        ),
        in_specs=[SMEM] * 2 + [VMEM] * (3 + len(split) + len(raw)),
        out_specs=(VMEM, VMEM),
        compiler_params=SCRATCH,
        name="sums",
    )(place, slab, *kept(fields, applied, halo, *split.values(), *raw.values()))


def exchange_sum(part, axis):
    count = lax.axis_size(axis)
    terms = [part] + [
        lax.ppermute(part, axis, [(i, i ^ k) for i in range(count)]) for k in range(1, count)
    ]
    while len(terms) > 1:
        terms = [a + b for a, b in zip(terms[::2], terms[1::2])]
    return terms[0]


def exchange(part, axis):
    count = lax.axis_size(axis)
    return lax.all_to_all(jnp.broadcast_to(part[None], (count,) + part.shape), axis, 0, 0)


def finish_kernel(
    row_count, comps, place_ref, parts_ref, stack_ref, block_ref, coeffs_ref, upper_ref,
    coeffs_scratch, block_scratch, sems,
):
    block_cols = upper_ref.shape[0]
    basis_cols = parts_ref.shape[2] // 2
    joined = basis_cols + block_cols
    lines, lanes = block_ref.shape[1:]
    total = jnp.sum(parts_ref[...], axis=0) / row_count
    gram, first, block_gram = unfold(total, block_cols)

    def times(left, right, right_dim=0):
        return lax.dot_general(
            left, right, (((1,), (right_dim,)), ((), ())),
            precision=exact_precision, preferred_element_type=jnp.float32,
        )

    coeffs = first + (first - times(first, gram))
    image = times(coeffs, gram)
    matrix = block_gram - times(
        jnp.concatenate((coeffs, first - image), axis=1), jnp.concatenate((first, coeffs), axis=1), 1
    )
    coeffs_scratch[...] = coeffs.T
    group_cols = coeffs_ref.shape[0]
    start = pl.multiple_of(place_ref[0] * group_cols, group_cols)
    coeffs_ref[...] = coeffs_scratch[pl.ds(start, group_cols), :]

    row = lax.broadcasted_iota(jnp.int32, (block_cols, block_cols), 0)
    column = lax.broadcasted_iota(jnp.int32, (block_cols, block_cols), 1)
    unit = jnp.where(row == column, 1.0, 0.0)
    pad = jnp.zeros((block_cols, 2 * basis_cols - joined - block_cols), jnp.float32)
    work = jnp.concatenate((-coeffs, unit, matrix, pad), axis=1)
    height = lax.broadcasted_iota(jnp.int32, work.shape, 0)
    width = 4
    for begin in range(0, block_cols, width):
        done, new_rows = [], []
        for step in range(begin, begin + width):
            column_here = jnp.broadcast_to(work[:, joined + step : joined + step + 1], work.shape)
            pivot_row = work[step : step + 1]
            for other_column, other_row, inverse in done:
                entry = other_column[step : step + 1]
                pivot_row = pivot_row - entry * other_row
                column_here = column_here - other_column * (entry * inverse)
            pivot = column_here[step : step + 1]
            inverse = 1.0 / pivot
            done.append((column_here, pivot_row * inverse, inverse))
            new_rows.append(pivot_row * lax.rsqrt(pivot))
        rest = work
        for column_here, scaled, _ in done:
            rest = rest - column_here * scaled
        work = jnp.where(height >= begin + width, rest, work)
        for step, new_row in enumerate(new_rows, begin):
            work = jnp.where(height == step, new_row, work)
    upper_ref[...] = jnp.where(row <= column, work[:, joined : joined + block_cols], 0.0)
    weights = three_parts(work[:, :joined])
    wide = jnp.concatenate(
        [jnp.concatenate((part, part, part), axis=1) for part in weights], axis=0
    )
    rows = lines // comps
    copies = []
    for comp in range(comps):
        there = pl.ds(comp * rows * lanes, rows * lanes)
        result = jnp.dot(wide, stack_ref[:, there], preferred_element_type=jnp.float32)
        result = result[:block_cols] + result[block_cols : 2 * block_cols] + result[2 * block_cols :]
        for index in range(rows):
            block_scratch[pl.ds(comp * rows + index, block_cols, stride=lines), :] = result[
                :, index * lanes : (index + 1) * lanes
            ]
        part = pl.ds(comp * rows, rows)
        copies.append(
            pltpu.make_async_copy(
                block_scratch.reshape(block_cols, lines, lanes).at[:, part, :],
                block_ref.at[:, part, :],
                sems.at[comp],
            )
        )
        copies[-1].start()
    for copy in copies:
        copy.wait()


def finish(place, parts, stack, row_count, block_cols, group_cols, lines, comps):
    lanes = stack.shape[1] // lines
    basis_cols = parts.shape[2] // 2
    return pl.pallas_call(
        functools.partial(finish_kernel, row_count, comps),
        out_shape=(
            f32(block_cols, lines, lanes), f32(group_cols, block_cols), f32(block_cols, block_cols),
        ),
        in_specs=[SMEM] + [VMEM] * 2,
        out_specs=(HBM, VMEM, VMEM),
        scratch_shapes=[
            pltpu.VMEM((basis_cols, block_cols), jnp.float32),
            pltpu.VMEM((block_cols * lines, lanes), jnp.float32),
            pltpu.SemaphoreType.DMA((comps,)),
        ],
        compiler_params=SCRATCH,
        name="finish",
    )(place, *kept(parts, stack))


def shards(
    x_block, basis, material, k0_blocks, k0_diag, ke_blocks, mass, velocities, shifts, sample
):
    block_cols, comps, extent_x, rows, lanes = x_block.shape
    group_cols = basis.shape[0]
    lines = comps * rows
    row_count = float(comps * extent_x * lax.axis_size("space") * basis.shape[3] * lanes)

    place = lax.axis_index("basis").astype(jnp.int32).reshape(1)
    slab = lax.axis_index("space").astype(jnp.int32).reshape(1)
    count = lax.axis_size("basis")
    x_far = x_block.reshape(block_cols * lines, lanes)
    own, *pieces, x_rows, material = pack(place, basis, x_far, material.reshape(rows, lanes), block_cols)
    got = {}
    for name in ("even", 3, "odd", 2, 1):
        if name == "even":
            got[name] = swap(x_far, "space", 0)
        elif name == "odd":
            got[name] = swap(x_far, "space", 1)
        else:
            piece = lax.ppermute(pieces[name - 1], "basis", [(i, i ^ name) for i in range(count)])
            got[name] = piece.reshape(-1, lanes)
    fields, applied, own = ahead(
        sample, velocities, shifts, k0_blocks, ke_blocks, k0_diag, mass, material, x_rows,
        own.reshape(-1, lanes), comps,
    )
    applied = add_side(slab, fields, applied, got.pop("even"), comps, "even")
    pieces = {k: got.pop(k) for k in reversed(partners(count)[1])}
    applied, *parts = add_edges(place, fields, applied, pieces, comps, group_cols)
    split = {0: own, **dict(zip(pieces, parts))}
    stack, part = sums(place, slab, fields, applied, got.pop("odd"), split, got, comps)
    parts = exchange(exchange_sum(part, "basis"), "space")
    block, coeffs, upper = finish(
        place, parts, stack, row_count, block_cols, group_cols, lines, comps
    )
    return (block.reshape(x_block.shape), coeffs, upper)


def solution(mesh):
    in_specs = (
        P(None, None, "space", "basis", None),
        P("basis", None, "space", None, None),
        P("space", "basis", None),
        P(),
        P(),
        P(),
        P(),
        P(),
        P(),
        P(),
    )
    out_specs = (P(None, None, "space", "basis", None), P("basis", None), P())
    return jax.shard_map(shards, mesh=mesh, in_specs=in_specs, out_specs=out_specs, check_vma=False)
```

```python
import functools

import jax
import jax.numpy as jnp
from jax import lax
from jax.experimental import pallas as pl
from jax.experimental.pallas import tpu as pltpu
from jax.sharding import PartitionSpec as P

exact_precision = lax.Precision.HIGHEST
VMEM = pl.BlockSpec(memory_space=pltpu.VMEM)
SMEM = pl.BlockSpec(memory_space=pltpu.SMEM)
HBM = pl.BlockSpec(memory_space=pltpu.HBM)
EARLY = pl.CostEstimate(flops=10**9, bytes_accessed=10**6, transcendentals=0)
NEXT = pl.CostEstimate(flops=10**6, bytes_accessed=10**6, transcendentals=0)
SCRATCH = pltpu.CompilerParams(vmem_limit_bytes=8 * 2**20)


def f32(*shape):
    return jax.ShapeDtypeStruct(shape, jnp.float32)


def near(*shape, dtype=jnp.float32):
    return pltpu.VMEM(shape, dtype)


def kept(*arrays):
    return [pltpu.with_memory_space_constraint(array, pltpu.VMEM) for array in arrays]


def far(*arrays):
    return [pltpu.with_memory_space_constraint(array, pltpu.HBM) for array in arrays]


def swap(values, axis, first):
    pairs = [(i, i + 1) for i in range(first, lax.axis_size(axis) - 1, 2)]
    return lax.ppermute(values, axis, pairs + [(j, i) for i, j in pairs])


def partners(count):
    return range(1, count), [k for k in range(1, count) if k & (k + 1) == 0]


def pack_kernel(comps, place_ref, basis_ref, x_ref, material_ref, *refs):
    *piece_refs, x_out_ref, material_out_ref, sems = refs
    count = len(piece_refs)
    tiles, _, rows, lanes = basis_ref.shape
    block_cols = x_ref.shape[0] // (comps * rows)
    place = place_ref[0]
    x_copy = pltpu.make_async_copy(x_ref, x_out_ref, sems.at[count])
    x_copy.start()
    copies = [pltpu.make_async_copy(material_ref, material_out_ref, sems.at[count + 1])]
    for k in reversed(range(count)):
        copies.append(
            pltpu.make_async_copy(
                basis_ref.at[:, place ^ k], piece_refs[k].at[pl.ds(0, tiles)], sems.at[k]
            )
        )
    for copy in copies:
        copy.start()
    x_copy.wait()
    for comp in range(comps):
        first, last = (
            x_out_ref[pl.ds(comp * rows + row, block_cols, stride=comps * rows), :]
            for row in (0, rows - 1)
        )
        for k in partners(count)[1]:
            edge = jnp.where((place ^ k) > place, last, first)
            for part in range(block_cols // rows):
                piece_refs[k][tiles + comp * (block_cols // rows) + part] = edge[
                    part * rows : (part + 1) * rows
                ]
    for copy in copies:
        copy.wait()


def pack(place, basis, x_rows, material, block_cols):
    group_cols, comps, _, full_y, lanes = basis.shape
    count = lax.axis_size("basis")
    rows = full_y // count
    tiles = group_cols * comps
    edge_tiles = block_cols * comps // rows
    pieces = [
        near(tiles + (edge_tiles if k in partners(count)[1] else 0), rows, lanes)
        for k in range(count)
    ]
    return pl.pallas_call(
        functools.partial(pack_kernel, comps),
        out_shape=(*pieces, near(*x_rows.shape), near(*material.shape, dtype=jnp.int32)),
        in_specs=[SMEM, HBM, HBM, HBM],
        out_specs=(VMEM,) * (count + 2),
        scratch_shapes=[pltpu.SemaphoreType.DMA((count + 2,))],
        compiler_params=SCRATCH,
        name="pack",
    )(place, *far(basis.reshape(tiles, count, rows, lanes), x_rows, material))


def three_parts(values):
    high = values.astype(jnp.bfloat16)
    rest = values - high.astype(jnp.float32)
    middle = rest.astype(jnp.bfloat16)
    low = (rest - middle.astype(jnp.float32)).astype(jnp.bfloat16)
    return high, middle, low


def line_of(ref, comp, row, comps, rows, block_cols):
    return ref[pl.ds(comp * rows + row, block_cols, stride=comps * rows), :]


def ahead_kernel(
    sample_ref, *refs
):
    far_refs, refs = refs[:6], refs[6:]
    material_ref, x_ref, own_ref, fields_ref, applied_ref, stack_ref, *near_refs, sems = refs
    velocities_ref, shifts_ref, k0_ref, ke_ref, diag_ref, mass_ref = near_refs
    copies = [
        pltpu.make_async_copy(source, target, sems.at[index])
        for index, (source, target) in enumerate(zip(far_refs, near_refs))
    ]
    for copy in copies:
        copy.start()
    group_cols = stack_ref.shape[0] // 3
    split_lines(
        own_ref, stack_ref, applied_ref.shape[0], group_cols, [i * group_cols for i in range(3)]
    )
    for copy in copies:
        copy.wait()
    comps, _, levels, offsets = k0_ref.shape
    rows, lanes = material_ref.shape
    lines = comps * rows
    block_cols = x_ref.shape[0] // lines
    velocity = velocities_ref[sample_ref[0]]
    sigma = shifts_ref[sample_ref[0]]
    entry_rows = fields_ref.shape[1]
    stride = entry_rows // (comps * comps)
    gap = jnp.zeros((levels, stride - offsets), jnp.float32)
    wide = []
    for out in range(comps):
        for comp in range(comps):
            wide += [k0_ref[out, comp] - velocity * velocity * ke_ref[out, comp], gap]
    wide.append(jnp.zeros((levels, lanes - entry_rows), jnp.float32))
    table = jnp.concatenate(wide, axis=1).T[:entry_rows]
    entry = lax.broadcasted_iota(jnp.int32, table.shape, 0)
    for comp in range(comps):
        centre = diag_ref[comp : comp + 1, :] - sigma * mass_ref[comp : comp + 1, :]
        table = table + jnp.where(entry == comp * (comps + 1) * stride, centre, 0.0)

    lane = lax.broadcasted_iota(jnp.int32, (block_cols, lanes), 1)
    level = lax.broadcasted_iota(jnp.int32, (levels, lanes), 0)
    for row in range(rows):
        chosen = jnp.broadcast_to(material_ref[row : row + 1, :], (levels, lanes)) == level
        fields = jnp.dot(
            table, chosen.astype(jnp.float32),
            precision=exact_precision, preferred_element_type=jnp.float32,
        )
        fields_ref[row] = fields
        sums = [None] * comps
        for comp in range(comps):
            centre = line_of(x_ref, comp, row, comps, rows, block_cols)
            views = {
                0: centre,
                5: jnp.where(lane == 0, 0.0, pltpu.roll(centre, 1, 1)),
                6: jnp.where(lane == lanes - 1, 0.0, pltpu.roll(centre, lanes - 1, 1)),
            }
            if row > 0:
                views[3] = line_of(x_ref, comp, row - 1, comps, rows, block_cols)
            if row < rows - 1:
                views[4] = line_of(x_ref, comp, row + 1, comps, rows, block_cols)
            for offset, view in views.items():
                for out in range(comps):
                    place = (out * comps + comp) * stride + offset
                    term = fields[place : place + 1, :] * view
                    sums[out] = term if sums[out] is None else sums[out] + term
        for out in range(comps):
            applied_ref[out * rows + row] = sums[out]


def ahead(sample, velocities, shifts, k0, ke, diag, mass, material, x_rows, own, comps):
    rows, lanes = material.shape
    lines = comps * rows
    stride = -(-k0.shape[1] // 8) * 8
    k0, ke = (jnp.transpose(blocks, (2, 3, 0, 1)) for blocks in (k0, ke))
    tables = far(velocities, shifts, k0, ke, diag.T, mass.T)
    return pl.pallas_call(
        ahead_kernel,
        out_shape=(
            near(rows, comps * comps * stride, lanes),
            near(lines, x_rows.shape[0] // lines, lanes),
            near(3 * own.shape[0] // lines, lines * lanes, dtype=jnp.bfloat16),
        ),
        in_specs=[SMEM] + [HBM] * 6 + [VMEM] * 3,
        out_specs=(VMEM,) * 3,
        scratch_shapes=[
            (pltpu.SMEM if array.ndim == 1 else pltpu.VMEM)(array.shape, jnp.float32)
            for array in tables
        ] + [pltpu.SemaphoreType.DMA((len(tables),))],
        compiler_params=SCRATCH,
        name="ahead",
    )(sample, *tables, *kept(material, x_rows, own))


def side_terms(field_row, swapped, side, out, comp, comps):
    stride = field_row.shape[0] // (comps * comps)
    begin = (out * comps + comp) * stride
    below, above = field_row[begin + 1 : begin + 2], field_row[begin + 2 : begin + 3]
    other = (below, above) if side == "even" else (above, below)
    return jnp.where(swapped, *other)


def side_kernel(comps, side, slab_ref, fields_ref, applied_ref, halo_ref, out_ref):
    lines, block_cols, _ = applied_ref.shape
    rows = lines // comps
    swapped = slab_ref[0] % 2 == 1
    for row in range(rows):
        field_row = fields_ref[row]
        views = [line_of(halo_ref, comp, row, comps, rows, block_cols) for comp in range(comps)]
        for out in range(comps):
            total = applied_ref[out * rows + row]
            for comp, view in enumerate(views):
                total = total + side_terms(field_row, swapped, side, out, comp, comps) * view
            out_ref[out * rows + row] = total


def add_side(slab, fields, applied, halo, comps, side):
    return pl.pallas_call(
        functools.partial(side_kernel, comps, side),
        out_shape=near(*applied.shape),
        in_specs=[SMEM] + [VMEM] * 3,
        out_specs=VMEM,
        compiler_params=SCRATCH,
        cost_estimate=EARLY,
        name="side",
    )(slab, *kept(fields, applied, halo))


def split_lines(piece_ref, stack_ref, lines, group_cols, begins):
    lanes = piece_ref.shape[1]
    for line in range(lines):
        values = piece_ref[pl.ds(line, group_cols, stride=lines), :]
        for begin, part in zip(begins, three_parts(values)):
            stack_ref[pl.ds(begin, group_cols), pl.ds(line * lanes, lanes)] = part


def edges_kernel(comps, ks, group_cols, place_ref, fields_ref, applied_ref, *refs):
    piece_refs, out_ref, parts_refs = refs[: len(ks)], refs[len(ks)], refs[len(ks) + 1 :]
    lines, block_cols, lanes = applied_ref.shape
    rows = lines // comps
    stride = fields_ref.shape[1] // (comps * comps)
    place = place_ref[0]

    def edge(comp, step):
        result = jnp.zeros((block_cols, lanes), jnp.float32)
        for k, ref in zip(ks, piece_refs):
            begin = ref.shape[0] - (comps - comp) * block_cols
            here = (place ^ k) == place + step
            result = jnp.where(here, ref[pl.ds(begin, block_cols), :], result)
        return result

    out_ref[...] = applied_ref[...]
    for row, offset, step in ((0, 3, -1), (rows - 1, 4, 1)):
        field_row = fields_ref[row]
        views = [edge(comp, step) for comp in range(comps)]
        for out in range(comps):
            total = out_ref[out * rows + row]
            for comp, view in enumerate(views):
                entry = (out * comps + comp) * stride + offset
                total = total + field_row[entry : entry + 1] * view
            out_ref[out * rows + row] = total
    for piece_ref, parts_ref in zip(piece_refs, parts_refs):
        split_lines(piece_ref, parts_ref, lines, group_cols, [i * group_cols for i in range(3)])


def add_edges(place, fields, applied, pieces, comps, group_cols):
    lines, _, lanes = applied.shape
    parts = near(3 * group_cols, lines * lanes, dtype=jnp.bfloat16)
    return pl.pallas_call(
        functools.partial(edges_kernel, comps, tuple(pieces), group_cols),
        out_shape=(near(*applied.shape),) + (parts,) * len(pieces),
        in_specs=[SMEM] + [VMEM] * (2 + len(pieces)),
        out_specs=(VMEM,) * (1 + len(pieces)),
        compiler_params=SCRATCH,
        cost_estimate=NEXT,
        name="edges",
    )(place, *kept(fields, applied, *pieces.values()))


def fold(total, basis_cols, block_cols, lanes):
    half = basis_cols // 2
    row = lax.broadcasted_iota(jnp.int32, (half, half), 0)
    column = lax.broadcasted_iota(jnp.int32, (half, half), 1)
    last = total[half:basis_cols, half:basis_cols]
    shared = jnp.where(row >= column, total[:half, :half], last)
    diagonal = jnp.sum(jnp.where(row == column, last, 0.0), axis=1, keepdims=True)
    below = total[basis_cols:]
    first = jnp.concatenate((below[:, :half], below[:, half:basis_cols]), axis=0)
    rest = jnp.zeros((half - block_cols, block_cols), jnp.float32)
    block = jnp.concatenate((below[:, basis_cols:], rest), axis=0)
    pad = jnp.zeros((half, lanes - 3 * half - block_cols - 1), jnp.float32)
    return jnp.concatenate(
        (shared, total[:half, half:basis_cols], first, block, diagonal, pad), axis=1
    )


def unfold(folded, block_cols):
    half = folded.shape[0]
    row = lax.broadcasted_iota(jnp.int32, (half, half), 0)
    column = lax.broadcasted_iota(jnp.int32, (half, half), 1)
    shared, across = folded[:, :half], folded[:, half : 2 * half]
    turned = shared.T
    start = jnp.where(row >= column, shared, turned)
    end = jnp.where(row < column, shared, turned)
    diagonal = folded[:, 3 * half + block_cols : 3 * half + block_cols + 1]
    end = jnp.where(row == column, diagonal, end)
    gram = jnp.concatenate(
        (jnp.concatenate((start, across), axis=1), jnp.concatenate((across.T, end), axis=1)), axis=0
    )
    first = folded[:, 2 * half : 3 * half]
    first = jnp.concatenate((first[:block_cols], first[block_cols : 2 * block_cols]), axis=1)
    return gram, first, folded[:block_cols, 3 * half : 3 * half + block_cols]


def sums_kernel(
    comps, split, raw, place_ref, slab_ref, fields_ref, applied_ref, halo_ref, *refs
):
    *refs, stack_ref, sums_ref = refs
    lines, block_cols, lanes = applied_ref.shape
    rows = lines // comps
    group_cols = refs[0].shape[0] // 3
    basis_cols = (len(split) + len(raw)) * group_cols
    joined = basis_cols + block_cols
    place = place_ref[0]
    swapped = slab_ref[0] % 2 == 1
    for k, ref in zip(split + raw, refs):
        begin = pl.multiple_of((place ^ k) * group_cols, group_cols)
        begins = [index * joined + begin for index in range(3)]
        if k in split:
            for index in range(3):
                stack_ref[pl.ds(begins[index], group_cols), :] = ref[
                    pl.ds(index * group_cols, group_cols), :
                ]
        else:
            split_lines(ref, stack_ref, lines, group_cols, begins)
    for row in range(rows):
        field_row = fields_ref[row]
        views = [line_of(halo_ref, comp, row, comps, rows, block_cols) for comp in range(comps)]
        for out in range(comps):
            line = out * rows + row
            total = applied_ref[line]
            for comp, view in enumerate(views):
                total = total + side_terms(field_row, swapped, "odd", out, comp, comps) * view
            for index, part in enumerate(three_parts(total)):
                there = pl.ds(index * joined + basis_cols, block_cols)
                stack_ref[there, pl.ds(line * lanes, lanes)] = part

    stack = stack_ref[...]
    products = lax.dot_general(
        stack, stack, (((1,), (1,)), ((), ())), preferred_element_type=jnp.float32
    )
    wide = products[:joined] + products[joined : 2 * joined] + products[2 * joined :]
    total = wide[:, :joined] + wide[:, joined : 2 * joined] + wide[:, 2 * joined :]
    sums_ref[...] = fold(total, basis_cols, block_cols, sums_ref.shape[1])


def sums(place, slab, fields, applied, halo, split, raw, comps):
    lines, block_cols, lanes = applied.shape
    basis_cols = (len(split) + len(raw)) * (split[0].shape[0] // 3)
    joined = basis_cols + block_cols
    return pl.pallas_call(
        functools.partial(sums_kernel, comps, tuple(split), tuple(raw)),
        out_shape=(
            near(3 * joined, lines * lanes, dtype=jnp.bfloat16),
            near(basis_cols // 2, 2 * basis_cols),
        ),
        in_specs=[SMEM] * 2 + [VMEM] * (3 + len(split) + len(raw)),
        out_specs=(VMEM, VMEM),
        compiler_params=SCRATCH,
        name="sums",
    )(place, slab, *kept(fields, applied, halo, *split.values(), *raw.values()))


def exchange_sum(part, axis):
    count = lax.axis_size(axis)
    mask = 1
    while mask < count:
        part = part + lax.ppermute(part, axis, [(i, i ^ mask) for i in range(count)])
        mask *= 2
    return part


def exchange(part, axis):
    count = lax.axis_size(axis)
    return lax.all_to_all(jnp.broadcast_to(part[None], (count,) + part.shape), axis, 0, 0)


def finish_kernel(
    row_count, comps, place_ref, parts_ref, stack_ref, block_ref, coeffs_ref, upper_ref,
    coeffs_scratch, upper_scratch, block_scratch, sems,
):
    block_cols = upper_ref.shape[0]
    basis_cols = parts_ref.shape[2] // 2
    joined = basis_cols + block_cols
    lines, lanes = block_ref.shape[1:]
    total = jnp.sum(parts_ref[...], axis=0) / row_count
    gram, first, block_gram = unfold(total, block_cols)

    def times(left, right, right_dim=0):
        return lax.dot_general(
            left, right, (((1,), (right_dim,)), ((), ())),
            precision=exact_precision, preferred_element_type=jnp.float32,
        )

    coeffs = first + (first - times(first, gram))
    image = times(coeffs, gram)
    matrix = block_gram - times(
        jnp.concatenate((coeffs, first - image), axis=1), jnp.concatenate((first, coeffs), axis=1), 1
    )
    coeffs_scratch[...] = coeffs.T
    group_cols = coeffs_ref.shape[0]
    start = pl.multiple_of(place_ref[0] * group_cols, group_cols)
    copies = [
        pltpu.make_async_copy(
            coeffs_scratch.at[pl.ds(start, group_cols)], coeffs_ref, sems.at[comps]
        )
    ]
    copies[0].start()

    row = lax.broadcasted_iota(jnp.int32, (block_cols, block_cols), 0)
    column = lax.broadcasted_iota(jnp.int32, (block_cols, block_cols), 1)
    unit = jnp.where(row == column, 1.0, 0.0)
    pad = jnp.zeros((block_cols, 2 * basis_cols - joined - block_cols), jnp.float32)
    work = jnp.concatenate((-coeffs, unit, matrix, pad), axis=1)
    height = lax.broadcasted_iota(jnp.int32, work.shape, 0)
    width = 4
    for begin in range(0, block_cols, width):
        done, new_rows = [], []
        for step in range(begin, begin + width):
            column_here = jnp.broadcast_to(work[:, joined + step : joined + step + 1], work.shape)
            pivot_row = work[step : step + 1]
            for other_column, other_row, inverse in done:
                entry = other_column[step : step + 1]
                pivot_row = pivot_row - entry * other_row
                column_here = column_here - other_column * (entry * inverse)
            pivot = column_here[step : step + 1]
            inverse = 1.0 / pivot
            done.append((column_here, pivot_row * inverse, inverse))
            new_rows.append(pivot_row * lax.rsqrt(pivot))
        rest = work
        for column_here, scaled, _ in done:
            rest = rest - column_here * scaled
        work = jnp.where(height >= begin + width, rest, work)
        for step, new_row in enumerate(new_rows, begin):
            work = jnp.where(height == step, new_row, work)
    upper_scratch[...] = jnp.where(row <= column, work[:, joined : joined + block_cols], 0.0)
    copies.append(pltpu.make_async_copy(upper_scratch, upper_ref, sems.at[comps + 1]))
    copies[1].start()
    weights = three_parts(work[:, :joined])
    wide = jnp.concatenate(
        [jnp.concatenate((part, part, part), axis=1) for part in weights], axis=0
    )
    rows = lines // comps
    for comp in range(comps):
        there = pl.ds(comp * rows * lanes, rows * lanes)
        result = jnp.dot(wide, stack_ref[:, there], preferred_element_type=jnp.float32)
        result = result[:block_cols] + result[block_cols : 2 * block_cols] + result[2 * block_cols :]
        for index in range(rows):
            block_scratch[pl.ds(comp * rows + index, block_cols, stride=lines), :] = result[
                :, index * lanes : (index + 1) * lanes
            ]
        part = pl.ds(comp * rows, rows)
        copies.append(
            pltpu.make_async_copy(
                block_scratch.reshape(block_cols, lines, lanes).at[:, part, :],
                block_ref.at[:, part, :],
                sems.at[comp],
            )
        )
        copies[-1].start()
    for copy in copies:
        copy.wait()


def finish(place, parts, stack, row_count, block_cols, group_cols, lines, comps):
    lanes = stack.shape[1] // lines
    basis_cols = parts.shape[2] // 2
    return pl.pallas_call(
        functools.partial(finish_kernel, row_count, comps),
        out_shape=(
            f32(block_cols, lines, lanes), f32(group_cols, block_cols), f32(block_cols, block_cols),
        ),
        in_specs=[SMEM] + [VMEM] * 2,
        out_specs=(HBM,) * 3,
        scratch_shapes=[
            pltpu.VMEM((basis_cols, block_cols), jnp.float32),
            pltpu.VMEM((block_cols, block_cols), jnp.float32),
            pltpu.VMEM((block_cols * lines, lanes), jnp.float32),
            pltpu.SemaphoreType.DMA((comps + 2,)),
        ],
        compiler_params=SCRATCH,
        name="finish",
    )(place, *kept(parts, stack))


def shards(
    x_block, basis, material, k0_blocks, k0_diag, ke_blocks, mass, velocities, shifts, sample
):
    block_cols, comps, extent_x, rows, lanes = x_block.shape
    group_cols = basis.shape[0]
    lines = comps * rows
    row_count = float(comps * extent_x * lax.axis_size("space") * basis.shape[3] * lanes)

    place = lax.axis_index("basis").astype(jnp.int32).reshape(1)
    slab = lax.axis_index("space").astype(jnp.int32).reshape(1)
    count = lax.axis_size("basis")
    x_far = x_block.reshape(block_cols * lines, lanes)
    own, *pieces, x_rows, material = pack(place, basis, x_far, material.reshape(rows, lanes), block_cols)
    got = {}
    for name in ("even", 3, "odd", 2, 1):
        if name == "even":
            got[name] = swap(x_far, "space", 0)
        elif name == "odd":
            got[name] = swap(x_far, "space", 1)
        else:
            piece = lax.ppermute(pieces[name - 1], "basis", [(i, i ^ name) for i in range(count)])
            got[name] = piece.reshape(-1, lanes)
    fields, applied, own = ahead(
        sample, velocities, shifts, k0_blocks, ke_blocks, k0_diag, mass, material, x_rows,
        own.reshape(-1, lanes), comps,
    )
    applied = add_side(slab, fields, applied, got.pop("even"), comps, "even")
    pieces = {k: got.pop(k) for k in reversed(partners(count)[1])}
    applied, *parts = add_edges(place, fields, applied, pieces, comps, group_cols)
    split = {0: own, **dict(zip(pieces, parts))}
    stack, part = sums(place, slab, fields, applied, got.pop("odd"), split, got, comps)
    parts = exchange(exchange_sum(part, "basis"), "space")
    block, coeffs, upper = finish(
        place, parts, stack, row_count, block_cols, group_cols, lines, comps
    )
    return (block.reshape(x_block.shape), coeffs, upper)


def solution(mesh):
    in_specs = (
        P(None, None, "space", "basis", None),
        P("basis", None, "space", None, None),
        P("space", "basis", None),
        P(),
        P(),
        P(),
        P(),
        P(),
        P(),
        P(),
    )
    out_specs = (P(None, None, "space", "basis", None), P("basis", None), P())
    return jax.shard_map(shards, mesh=mesh, in_specs=in_specs, out_specs=out_specs, check_vma=False)
```

```python
import functools

import jax
import jax.numpy as jnp
from jax import lax
from jax.experimental import pallas as pl
from jax.experimental.pallas import tpu as pltpu
from jax.sharding import PartitionSpec as P

exact_precision = lax.Precision.HIGHEST
VMEM = pl.BlockSpec(memory_space=pltpu.VMEM)
SMEM = pl.BlockSpec(memory_space=pltpu.SMEM)
HBM = pl.BlockSpec(memory_space=pltpu.HBM)
EARLY = pl.CostEstimate(flops=10**9, bytes_accessed=10**6, transcendentals=0)
NEXT = pl.CostEstimate(flops=10**6, bytes_accessed=10**6, transcendentals=0)
SCRATCH = pltpu.CompilerParams(vmem_limit_bytes=8 * 2**20)


def f32(*shape):
    return jax.ShapeDtypeStruct(shape, jnp.float32)


def near(*shape, dtype=jnp.float32):
    return pltpu.VMEM(shape, dtype)


def kept(*arrays):
    return [pltpu.with_memory_space_constraint(array, pltpu.VMEM) for array in arrays]


def far(*arrays):
    return [pltpu.with_memory_space_constraint(array, pltpu.HBM) for array in arrays]


def swap(values, axis, first):
    pairs = [(i, i + 1) for i in range(first, lax.axis_size(axis) - 1, 2)]
    return lax.ppermute(values, axis, pairs + [(j, i) for i, j in pairs])


def partners(count):
    return range(1, count), [k for k in range(1, count) if k & (k + 1) == 0]


def pack_kernel(comps, place_ref, basis_ref, x_ref, material_ref, *refs):
    *piece_refs, x_out_ref, material_out_ref, sems = refs
    count = len(piece_refs)
    tiles, _, rows, lanes = basis_ref.shape
    block_cols = x_ref.shape[0] // (comps * rows)
    place = place_ref[0]
    x_copy = pltpu.make_async_copy(x_ref, x_out_ref, sems.at[count])
    x_copy.start()
    copies = [pltpu.make_async_copy(material_ref, material_out_ref, sems.at[count + 1])]
    for k in reversed(range(count)):
        copies.append(
            pltpu.make_async_copy(
                basis_ref.at[:, place ^ k], piece_refs[k].at[pl.ds(0, tiles)], sems.at[k]
            )
        )
    for copy in copies:
        copy.start()
    x_copy.wait()
    for comp in range(comps):
        first, last = (
            x_out_ref[pl.ds(comp * rows + row, block_cols, stride=comps * rows), :]
            for row in (0, rows - 1)
        )
        for k in partners(count)[1]:
            edge = jnp.where((place ^ k) > place, last, first)
            for part in range(block_cols // rows):
                piece_refs[k][tiles + comp * (block_cols // rows) + part] = edge[
                    part * rows : (part + 1) * rows
                ]
    for copy in copies:
        copy.wait()


def pack(place, basis, x_rows, material, block_cols):
    group_cols, comps, _, full_y, lanes = basis.shape
    count = lax.axis_size("basis")
    rows = full_y // count
    tiles = group_cols * comps
    edge_tiles = block_cols * comps // rows
    pieces = [
        near(tiles + (edge_tiles if k in partners(count)[1] else 0), rows, lanes)
        for k in range(count)
    ]
    return pl.pallas_call(
        functools.partial(pack_kernel, comps),
        out_shape=(*pieces, near(*x_rows.shape), near(*material.shape, dtype=jnp.int32)),
        in_specs=[SMEM, HBM, HBM, HBM],
        out_specs=(VMEM,) * (count + 2),
        scratch_shapes=[pltpu.SemaphoreType.DMA((count + 2,))],
        compiler_params=SCRATCH,
        name="pack",
    )(place, *far(basis.reshape(tiles, count, rows, lanes), x_rows, material))


def three_parts(values):
    high = values.astype(jnp.bfloat16)
    rest = values - high.astype(jnp.float32)
    middle = rest.astype(jnp.bfloat16)
    low = (rest - middle.astype(jnp.float32)).astype(jnp.bfloat16)
    return high, middle, low


def line_of(ref, comp, row, comps, rows, block_cols):
    return ref[pl.ds(comp * rows + row, block_cols, stride=comps * rows), :]


def ahead_kernel(
    sample_ref, *refs
):
    far_refs, refs = refs[:6], refs[6:]
    material_ref, x_ref, own_ref, fields_ref, applied_ref, stack_ref, *near_refs, sems = refs
    velocities_ref, shifts_ref, k0_ref, ke_ref, diag_ref, mass_ref = near_refs
    copies = [
        pltpu.make_async_copy(source, target, sems.at[index])
        for index, (source, target) in enumerate(zip(far_refs, near_refs))
    ]
    for copy in copies:
        copy.start()
    group_cols = stack_ref.shape[0] // 3
    split_lines(
        own_ref, stack_ref, applied_ref.shape[0], group_cols, [i * group_cols for i in range(3)]
    )
    for copy in copies:
        copy.wait()
    comps, _, levels, offsets = k0_ref.shape
    rows, lanes = material_ref.shape
    lines = comps * rows
    block_cols = x_ref.shape[0] // lines
    velocity = velocities_ref[sample_ref[0]]
    sigma = shifts_ref[sample_ref[0]]
    entry_rows = fields_ref.shape[1]
    stride = entry_rows // (comps * comps)
    gap = jnp.zeros((levels, stride - offsets), jnp.float32)
    wide = []
    for out in range(comps):
        for comp in range(comps):
            wide += [k0_ref[out, comp] - velocity * velocity * ke_ref[out, comp], gap]
    wide.append(jnp.zeros((levels, lanes - entry_rows), jnp.float32))
    table = jnp.concatenate(wide, axis=1).T[:entry_rows]
    entry = lax.broadcasted_iota(jnp.int32, table.shape, 0)
    for comp in range(comps):
        centre = diag_ref[comp : comp + 1, :] - sigma * mass_ref[comp : comp + 1, :]
        table = table + jnp.where(entry == comp * (comps + 1) * stride, centre, 0.0)

    lane = lax.broadcasted_iota(jnp.int32, (block_cols, lanes), 1)
    level = lax.broadcasted_iota(jnp.int32, (levels, lanes), 0)
    for row in range(rows):
        chosen = jnp.broadcast_to(material_ref[row : row + 1, :], (levels, lanes)) == level
        fields = jnp.dot(
            table, chosen.astype(jnp.float32),
            precision=exact_precision, preferred_element_type=jnp.float32,
        )
        fields_ref[row] = fields
        sums = [None] * comps
        for comp in range(comps):
            centre = line_of(x_ref, comp, row, comps, rows, block_cols)
            views = {
                0: centre,
                5: jnp.where(lane == 0, 0.0, pltpu.roll(centre, 1, 1)),
                6: jnp.where(lane == lanes - 1, 0.0, pltpu.roll(centre, lanes - 1, 1)),
            }
            if row > 0:
                views[3] = line_of(x_ref, comp, row - 1, comps, rows, block_cols)
            if row < rows - 1:
                views[4] = line_of(x_ref, comp, row + 1, comps, rows, block_cols)
            for offset, view in views.items():
                for out in range(comps):
                    place = (out * comps + comp) * stride + offset
                    term = fields[place : place + 1, :] * view
                    sums[out] = term if sums[out] is None else sums[out] + term
        for out in range(comps):
            applied_ref[out * rows + row] = sums[out]


def ahead(sample, velocities, shifts, k0, ke, diag, mass, material, x_rows, own, comps):
    rows, lanes = material.shape
    lines = comps * rows
    stride = -(-k0.shape[1] // 8) * 8
    k0, ke = (jnp.transpose(blocks, (2, 3, 0, 1)) for blocks in (k0, ke))
    tables = far(velocities, shifts, k0, ke, diag.T, mass.T)
    return pl.pallas_call(
        ahead_kernel,
        out_shape=(
            near(rows, comps * comps * stride, lanes),
            near(lines, x_rows.shape[0] // lines, lanes),
            near(3 * own.shape[0] // lines, lines * lanes, dtype=jnp.bfloat16),
        ),
        in_specs=[SMEM] + [HBM] * 6 + [VMEM] * 3,
        out_specs=(VMEM,) * 3,
        scratch_shapes=[
            (pltpu.SMEM if array.ndim == 1 else pltpu.VMEM)(array.shape, jnp.float32)
            for array in tables
        ] + [pltpu.SemaphoreType.DMA((len(tables),))],
        compiler_params=SCRATCH,
        name="ahead",
    )(sample, *tables, *kept(material, x_rows, own))


def side_terms(field_row, swapped, side, out, comp, comps):
    stride = field_row.shape[0] // (comps * comps)
    begin = (out * comps + comp) * stride
    below, above = field_row[begin + 1 : begin + 2], field_row[begin + 2 : begin + 3]
    other = (below, above) if side == "even" else (above, below)
    return jnp.where(swapped, *other)


def side_kernel(comps, side, slab_ref, fields_ref, applied_ref, halo_ref, out_ref):
    lines, block_cols, _ = applied_ref.shape
    rows = lines // comps
    swapped = slab_ref[0] % 2 == 1
    for row in range(rows):
        field_row = fields_ref[row]
        views = [line_of(halo_ref, comp, row, comps, rows, block_cols) for comp in range(comps)]
        for out in range(comps):
            total = applied_ref[out * rows + row]
            for comp, view in enumerate(views):
                total = total + side_terms(field_row, swapped, side, out, comp, comps) * view
            out_ref[out * rows + row] = total


def add_side(slab, fields, applied, halo, comps, side):
    return pl.pallas_call(
        functools.partial(side_kernel, comps, side),
        out_shape=near(*applied.shape),
        in_specs=[SMEM] + [VMEM] * 3,
        out_specs=VMEM,
        compiler_params=SCRATCH,
        cost_estimate=EARLY,
        name="side",
    )(slab, *kept(fields, applied, halo))


def split_lines(piece_ref, stack_ref, lines, group_cols, begins):
    lanes = piece_ref.shape[1]
    for line in range(lines):
        values = piece_ref[pl.ds(line, group_cols, stride=lines), :]
        for begin, part in zip(begins, three_parts(values)):
            stack_ref[pl.ds(begin, group_cols), pl.ds(line * lanes, lanes)] = part


def edges_kernel(comps, ks, group_cols, place_ref, fields_ref, applied_ref, *refs):
    piece_refs, out_ref, parts_refs = refs[: len(ks)], refs[len(ks)], refs[len(ks) + 1 :]
    lines, block_cols, lanes = applied_ref.shape
    rows = lines // comps
    stride = fields_ref.shape[1] // (comps * comps)
    place = place_ref[0]

    def edge(comp, step):
        result = jnp.zeros((block_cols, lanes), jnp.float32)
        for k, ref in zip(ks, piece_refs):
            begin = ref.shape[0] - (comps - comp) * block_cols
            here = (place ^ k) == place + step
            result = jnp.where(here, ref[pl.ds(begin, block_cols), :], result)
        return result

    out_ref[...] = applied_ref[...]
    for row, offset, step in ((0, 3, -1), (rows - 1, 4, 1)):
        field_row = fields_ref[row]
        views = [edge(comp, step) for comp in range(comps)]
        for out in range(comps):
            total = out_ref[out * rows + row]
            for comp, view in enumerate(views):
                entry = (out * comps + comp) * stride + offset
                total = total + field_row[entry : entry + 1] * view
            out_ref[out * rows + row] = total
    for piece_ref, parts_ref in zip(piece_refs, parts_refs):
        split_lines(piece_ref, parts_ref, lines, group_cols, [i * group_cols for i in range(3)])


def add_edges(place, fields, applied, pieces, comps, group_cols):
    lines, _, lanes = applied.shape
    parts = near(3 * group_cols, lines * lanes, dtype=jnp.bfloat16)
    return pl.pallas_call(
        functools.partial(edges_kernel, comps, tuple(pieces), group_cols),
        out_shape=(near(*applied.shape),) + (parts,) * len(pieces),
        in_specs=[SMEM] + [VMEM] * (2 + len(pieces)),
        out_specs=(VMEM,) * (1 + len(pieces)),
        compiler_params=SCRATCH,
        cost_estimate=NEXT,
        name="edges",
    )(place, *kept(fields, applied, *pieces.values()))


def fold(total, basis_cols, block_cols, lanes):
    half = basis_cols // 2
    row = lax.broadcasted_iota(jnp.int32, (half, half), 0)
    column = lax.broadcasted_iota(jnp.int32, (half, half), 1)
    last = total[half:basis_cols, half:basis_cols]
    shared = jnp.where(row >= column, total[:half, :half], last)
    diagonal = jnp.sum(jnp.where(row == column, last, 0.0), axis=1, keepdims=True)
    below = total[basis_cols:]
    first = jnp.concatenate((below[:, :half], below[:, half:basis_cols]), axis=0)
    rest = jnp.zeros((half - block_cols, block_cols), jnp.float32)
    block = jnp.concatenate((below[:, basis_cols:], rest), axis=0)
    pad = jnp.zeros((half, lanes - 3 * half - block_cols - 1), jnp.float32)
    return jnp.concatenate(
        (shared, total[:half, half:basis_cols], first, block, diagonal, pad), axis=1
    )


def unfold(folded, block_cols):
    half = folded.shape[0]
    row = lax.broadcasted_iota(jnp.int32, (half, half), 0)
    column = lax.broadcasted_iota(jnp.int32, (half, half), 1)
    shared, across = folded[:, :half], folded[:, half : 2 * half]
    turned = shared.T
    start = jnp.where(row >= column, shared, turned)
    end = jnp.where(row < column, shared, turned)
    diagonal = folded[:, 3 * half + block_cols : 3 * half + block_cols + 1]
    end = jnp.where(row == column, diagonal, end)
    gram = jnp.concatenate(
        (jnp.concatenate((start, across), axis=1), jnp.concatenate((across.T, end), axis=1)), axis=0
    )
    first = folded[:, 2 * half : 3 * half]
    first = jnp.concatenate((first[:block_cols], first[block_cols : 2 * block_cols]), axis=1)
    return gram, first, folded[:block_cols, 3 * half : 3 * half + block_cols]


def sums_kernel(
    comps, split, raw, place_ref, slab_ref, fields_ref, applied_ref, halo_ref, *refs
):
    *refs, stack_ref, sums_ref = refs
    lines, block_cols, lanes = applied_ref.shape
    rows = lines // comps
    group_cols = refs[0].shape[0] // 3
    basis_cols = (len(split) + len(raw)) * group_cols
    joined = basis_cols + block_cols
    place = place_ref[0]
    swapped = slab_ref[0] % 2 == 1
    for k, ref in zip(split + raw, refs):
        begin = pl.multiple_of((place ^ k) * group_cols, group_cols)
        begins = [index * joined + begin for index in range(3)]
        if k in split:
            for index in range(3):
                stack_ref[pl.ds(begins[index], group_cols), :] = ref[
                    pl.ds(index * group_cols, group_cols), :
                ]
        else:
            split_lines(ref, stack_ref, lines, group_cols, begins)
    for row in range(rows):
        field_row = fields_ref[row]
        views = [line_of(halo_ref, comp, row, comps, rows, block_cols) for comp in range(comps)]
        for out in range(comps):
            line = out * rows + row
            total = applied_ref[line]
            for comp, view in enumerate(views):
                total = total + side_terms(field_row, swapped, "odd", out, comp, comps) * view
            for index, part in enumerate(three_parts(total)):
                there = pl.ds(index * joined + basis_cols, block_cols)
                stack_ref[there, pl.ds(line * lanes, lanes)] = part

    stack = stack_ref[...]
    products = lax.dot_general(
        stack, stack, (((1,), (1,)), ((), ())), preferred_element_type=jnp.float32
    )
    wide = products[:joined] + products[joined : 2 * joined] + products[2 * joined :]
    total = wide[:, :joined] + wide[:, joined : 2 * joined] + wide[:, 2 * joined :]
    sums_ref[...] = fold(total, basis_cols, block_cols, sums_ref.shape[1])


def sums(place, slab, fields, applied, halo, split, raw, comps):
    lines, block_cols, lanes = applied.shape
    basis_cols = (len(split) + len(raw)) * (split[0].shape[0] // 3)
    joined = basis_cols + block_cols
    return pl.pallas_call(
        functools.partial(sums_kernel, comps, tuple(split), tuple(raw)),
        out_shape=(
            near(3 * joined, lines * lanes, dtype=jnp.bfloat16),
            near(basis_cols // 2, 2 * basis_cols),
        ),
        in_specs=[SMEM] * 2 + [VMEM] * (3 + len(split) + len(raw)),
        out_specs=(VMEM, VMEM),
        compiler_params=SCRATCH,
        name="sums",
    )(place, slab, *kept(fields, applied, halo, *split.values(), *raw.values()))


def pair_sum(part, axis, mask):
    count = lax.axis_size(axis)
    return part + lax.ppermute(part, axis, [(i, i ^ mask) for i in range(count)])


def exchange_all(part):
    mask = 1
    while mask < lax.axis_size("basis"):
        part = pair_sum(part, "basis", mask)
        mask *= 2
    part = pair_sum(part, "space", 1)
    count = lax.axis_size("space")
    groups = [list(range(first, count, 2)) for first in range(2)]
    copies = jnp.broadcast_to(part[None], (count // 2,) + part.shape)
    return lax.all_to_all(copies, "space", 0, 0, axis_index_groups=groups)


def finish_kernel(
    row_count, comps, place_ref, parts_ref, stack_ref, block_ref, coeffs_ref, upper_ref,
    coeffs_scratch, upper_scratch, block_scratch, sems,
):
    block_cols = upper_ref.shape[0]
    basis_cols = parts_ref.shape[2] // 2
    joined = basis_cols + block_cols
    lines, lanes = block_ref.shape[1:]
    total = jnp.sum(parts_ref[...], axis=0) / row_count
    gram, first, block_gram = unfold(total, block_cols)

    def times(left, right, right_dim=0):
        return lax.dot_general(
            left, right, (((1,), (right_dim,)), ((), ())),
            precision=exact_precision, preferred_element_type=jnp.float32,
        )

    coeffs = first + (first - times(first, gram))
    image = times(coeffs, gram)
    matrix = block_gram - times(
        jnp.concatenate((coeffs, first - image), axis=1), jnp.concatenate((first, coeffs), axis=1), 1
    )
    coeffs_scratch[...] = coeffs.T
    group_cols = coeffs_ref.shape[0]
    start = pl.multiple_of(place_ref[0] * group_cols, group_cols)
    copies = [
        pltpu.make_async_copy(
            coeffs_scratch.at[pl.ds(start, group_cols)], coeffs_ref, sems.at[comps]
        )
    ]
    copies[0].start()

    row = lax.broadcasted_iota(jnp.int32, (block_cols, block_cols), 0)
    column = lax.broadcasted_iota(jnp.int32, (block_cols, block_cols), 1)
    unit = jnp.where(row == column, 1.0, 0.0)
    pad = jnp.zeros((block_cols, 2 * basis_cols - joined - block_cols), jnp.float32)
    work = jnp.concatenate((-coeffs, unit, matrix, pad), axis=1)
    height = lax.broadcasted_iota(jnp.int32, work.shape, 0)
    width = 4
    for begin in range(0, block_cols, width):
        done, new_rows = [], []
        for step in range(begin, begin + width):
            column_here = jnp.broadcast_to(work[:, joined + step : joined + step + 1], work.shape)
            pivot_row = work[step : step + 1]
            for other_column, other_row, inverse in done:
                entry = other_column[step : step + 1]
                pivot_row = pivot_row - entry * other_row
                column_here = column_here - other_column * (entry * inverse)
            pivot = column_here[step : step + 1]
            inverse = 1.0 / pivot
            done.append((column_here, pivot_row * inverse, inverse))
            new_rows.append(pivot_row * lax.rsqrt(pivot))
        rest = work
        for column_here, scaled, _ in done:
            rest = rest - column_here * scaled
        work = jnp.where(height >= begin + width, rest, work)
        for step, new_row in enumerate(new_rows, begin):
            work = jnp.where(height == step, new_row, work)
    upper_scratch[...] = jnp.where(row <= column, work[:, joined : joined + block_cols], 0.0)
    copies.append(pltpu.make_async_copy(upper_scratch, upper_ref, sems.at[comps + 1]))
    copies[1].start()
    weights = three_parts(work[:, :joined])
    wide = jnp.concatenate(
        [jnp.concatenate((part, part, part), axis=1) for part in weights], axis=0
    )
    rows = lines // comps
    for comp in range(comps):
        there = pl.ds(comp * rows * lanes, rows * lanes)
        result = jnp.dot(wide, stack_ref[:, there], preferred_element_type=jnp.float32)
        result = result[:block_cols] + result[block_cols : 2 * block_cols] + result[2 * block_cols :]
        for index in range(rows):
            block_scratch[pl.ds(comp * rows + index, block_cols, stride=lines), :] = result[
                :, index * lanes : (index + 1) * lanes
            ]
        part = pl.ds(comp * rows, rows)
        copies.append(
            pltpu.make_async_copy(
                block_scratch.reshape(block_cols, lines, lanes).at[:, part, :],
                block_ref.at[:, part, :],
                sems.at[comp],
            )
        )
        copies[-1].start()
    for copy in copies:
        copy.wait()


def finish(place, parts, stack, row_count, block_cols, group_cols, lines, comps):
    lanes = stack.shape[1] // lines
    basis_cols = parts.shape[2] // 2
    return pl.pallas_call(
        functools.partial(finish_kernel, row_count, comps),
        out_shape=(
            f32(block_cols, lines, lanes), f32(group_cols, block_cols), f32(block_cols, block_cols),
        ),
        in_specs=[SMEM] + [VMEM] * 2,
        out_specs=(HBM,) * 3,
        scratch_shapes=[
            pltpu.VMEM((basis_cols, block_cols), jnp.float32),
            pltpu.VMEM((block_cols, block_cols), jnp.float32),
            pltpu.VMEM((block_cols * lines, lanes), jnp.float32),
            pltpu.SemaphoreType.DMA((comps + 2,)),
        ],
        compiler_params=SCRATCH,
        name="finish",
    )(place, *kept(parts, stack))


def shards(
    x_block, basis, material, k0_blocks, k0_diag, ke_blocks, mass, velocities, shifts, sample
):
    block_cols, comps, extent_x, rows, lanes = x_block.shape
    group_cols = basis.shape[0]
    lines = comps * rows
    row_count = float(comps * extent_x * lax.axis_size("space") * basis.shape[3] * lanes)

    place = lax.axis_index("basis").astype(jnp.int32).reshape(1)
    slab = lax.axis_index("space").astype(jnp.int32).reshape(1)
    count = lax.axis_size("basis")
    x_far = x_block.reshape(block_cols * lines, lanes)
    own, *pieces, x_rows, material = pack(place, basis, x_far, material.reshape(rows, lanes), block_cols)
    got = {}
    for name in ("even", 3, "odd", 2, 1):
        if name == "even":
            got[name] = swap(x_far, "space", 0)
        elif name == "odd":
            got[name] = swap(x_far, "space", 1)
        else:
            piece = lax.ppermute(pieces[name - 1], "basis", [(i, i ^ name) for i in range(count)])
            got[name] = piece.reshape(-1, lanes)
    fields, applied, own = ahead(
        sample, velocities, shifts, k0_blocks, ke_blocks, k0_diag, mass, material, x_rows,
        own.reshape(-1, lanes), comps,
    )
    applied = add_side(slab, fields, applied, got.pop("even"), comps, "even")
    pieces = {k: got.pop(k) for k in reversed(partners(count)[1])}
    applied, *parts = add_edges(place, fields, applied, pieces, comps, group_cols)
    split = {0: own, **dict(zip(pieces, parts))}
    stack, part = sums(place, slab, fields, applied, got.pop("odd"), split, got, comps)
    parts = exchange_all(part)
    block, coeffs, upper = finish(
        place, parts, stack, row_count, block_cols, group_cols, lines, comps
    )
    return (block.reshape(x_block.shape), coeffs, upper)


def solution(mesh):
    in_specs = (
        P(None, None, "space", "basis", None),
        P("basis", None, "space", None, None),
        P("space", "basis", None),
        P(),
        P(),
        P(),
        P(),
        P(),
        P(),
        P(),
    )
    out_specs = (P(None, None, "space", "basis", None), P("basis", None), P())
    return jax.shard_map(shards, mesh=mesh, in_specs=in_specs, out_specs=out_specs, check_vma=False)
```

```python
import functools

import jax
import jax.numpy as jnp
from jax import lax
from jax.experimental import pallas as pl
from jax.experimental.pallas import tpu as pltpu
from jax.sharding import PartitionSpec as P

exact_precision = lax.Precision.HIGHEST
VMEM = pl.BlockSpec(memory_space=pltpu.VMEM)
SMEM = pl.BlockSpec(memory_space=pltpu.SMEM)
HBM = pl.BlockSpec(memory_space=pltpu.HBM)
LOSS = 64.0
EARLY = pl.CostEstimate(flops=10**9, bytes_accessed=10**6, transcendentals=0)
NEXT = pl.CostEstimate(flops=10**6, bytes_accessed=10**6, transcendentals=0)
SCRATCH = pltpu.CompilerParams(vmem_limit_bytes=8 * 2**20)


def f32(*shape):
    return jax.ShapeDtypeStruct(shape, jnp.float32)


def near(*shape, dtype=jnp.float32):
    return pltpu.VMEM(shape, dtype)


def kept(*arrays):
    return [pltpu.with_memory_space_constraint(array, pltpu.VMEM) for array in arrays]


def far(*arrays):
    return [pltpu.with_memory_space_constraint(array, pltpu.HBM) for array in arrays]


def swap(values, axis, first):
    pairs = [(i, i + 1) for i in range(first, lax.axis_size(axis) - 1, 2)]
    return lax.ppermute(values, axis, pairs + [(j, i) for i, j in pairs])


def partners(count):
    return range(1, count), [k for k in range(1, count) if k & (k + 1) == 0]


def pack_kernel(comps, place_ref, basis_ref, x_ref, material_ref, *refs):
    *piece_refs, x_out_ref, material_out_ref, sems = refs
    count = len(piece_refs)
    tiles, _, rows, lanes = basis_ref.shape
    block_cols = x_ref.shape[0] // (comps * rows)
    place = place_ref[0]
    x_copy = pltpu.make_async_copy(x_ref, x_out_ref, sems.at[count])
    x_copy.start()
    copies = [pltpu.make_async_copy(material_ref, material_out_ref, sems.at[count + 1])]
    for k in reversed(range(count)):
        copies.append(
            pltpu.make_async_copy(
                basis_ref.at[:, place ^ k], piece_refs[k].at[pl.ds(0, tiles)], sems.at[k]
            )
        )
    for copy in copies:
        copy.start()
    x_copy.wait()
    for comp in range(comps):
        first, last = (
            x_out_ref[pl.ds(comp * rows + row, block_cols, stride=comps * rows), :]
            for row in (0, rows - 1)
        )
        for k in partners(count)[1]:
            edge = jnp.where((place ^ k) > place, last, first)
            for part in range(block_cols // rows):
                piece_refs[k][tiles + comp * (block_cols // rows) + part] = edge[
                    part * rows : (part + 1) * rows
                ]
    for copy in copies:
        copy.wait()


def pack(place, basis, x_rows, material, block_cols):
    group_cols, comps, _, full_y, lanes = basis.shape
    count = lax.axis_size("basis")
    rows = full_y // count
    tiles = group_cols * comps
    edge_tiles = block_cols * comps // rows
    pieces = [
        near(tiles + (edge_tiles if k in partners(count)[1] else 0), rows, lanes)
        for k in range(count)
    ]
    return pl.pallas_call(
        functools.partial(pack_kernel, comps),
        out_shape=(*pieces, near(*x_rows.shape), near(*material.shape, dtype=jnp.int32)),
        in_specs=[SMEM, HBM, HBM, HBM],
        out_specs=(VMEM,) * (count + 2),
        scratch_shapes=[pltpu.SemaphoreType.DMA((count + 2,))],
        compiler_params=SCRATCH,
        name="pack",
    )(place, *far(basis.reshape(tiles, count, rows, lanes), x_rows, material))


def three_parts(values):
    high = values.astype(jnp.bfloat16)
    rest = values - high.astype(jnp.float32)
    middle = rest.astype(jnp.bfloat16)
    low = (rest - middle.astype(jnp.float32)).astype(jnp.bfloat16)
    return high, middle, low


def line_of(ref, comp, row, comps, rows, block_cols):
    return ref[pl.ds(comp * rows + row, block_cols, stride=comps * rows), :]


def ahead_kernel(
    sample_ref, *refs
):
    far_refs, refs = refs[:6], refs[6:]
    material_ref, x_ref, own_ref, fields_ref, applied_ref, stack_ref, *near_refs, sems = refs
    velocities_ref, shifts_ref, k0_ref, ke_ref, diag_ref, mass_ref = near_refs
    copies = [
        pltpu.make_async_copy(source, target, sems.at[index])
        for index, (source, target) in enumerate(zip(far_refs, near_refs))
    ]
    for copy in copies:
        copy.start()
    group_cols = stack_ref.shape[0] // 3
    split_lines(
        own_ref, stack_ref, applied_ref.shape[0], group_cols, [i * group_cols for i in range(3)]
    )
    for copy in copies:
        copy.wait()
    comps, _, levels, offsets = k0_ref.shape
    rows, lanes = material_ref.shape
    lines = comps * rows
    block_cols = x_ref.shape[0] // lines
    velocity = velocities_ref[sample_ref[0]]
    sigma = shifts_ref[sample_ref[0]]
    entry_rows = fields_ref.shape[1]
    stride = entry_rows // (comps * comps)
    gap = jnp.zeros((levels, stride - offsets), jnp.float32)
    wide = []
    for out in range(comps):
        for comp in range(comps):
            wide += [k0_ref[out, comp] - velocity * velocity * ke_ref[out, comp], gap]
    wide.append(jnp.zeros((levels, lanes - entry_rows), jnp.float32))
    table = jnp.concatenate(wide, axis=1).T[:entry_rows]
    entry = lax.broadcasted_iota(jnp.int32, table.shape, 0)
    for comp in range(comps):
        centre = diag_ref[comp : comp + 1, :] - sigma * mass_ref[comp : comp + 1, :]
        table = table + jnp.where(entry == comp * (comps + 1) * stride, centre, 0.0)

    lane = lax.broadcasted_iota(jnp.int32, (block_cols, lanes), 1)
    level = lax.broadcasted_iota(jnp.int32, (levels, lanes), 0)
    for row in range(rows):
        chosen = jnp.broadcast_to(material_ref[row : row + 1, :], (levels, lanes)) == level
        fields = jnp.dot(
            table, chosen.astype(jnp.float32),
            precision=exact_precision, preferred_element_type=jnp.float32,
        )
        fields_ref[row] = fields
        sums = [None] * comps
        for comp in range(comps):
            centre = line_of(x_ref, comp, row, comps, rows, block_cols)
            views = {
                0: centre,
                5: jnp.where(lane == 0, 0.0, pltpu.roll(centre, 1, 1)),
                6: jnp.where(lane == lanes - 1, 0.0, pltpu.roll(centre, lanes - 1, 1)),
            }
            if row > 0:
                views[3] = line_of(x_ref, comp, row - 1, comps, rows, block_cols)
            if row < rows - 1:
                views[4] = line_of(x_ref, comp, row + 1, comps, rows, block_cols)
            for offset, view in views.items():
                for out in range(comps):
                    place = (out * comps + comp) * stride + offset
                    term = fields[place : place + 1, :] * view
                    sums[out] = term if sums[out] is None else sums[out] + term
        for out in range(comps):
            applied_ref[out * rows + row] = sums[out]


def ahead(sample, velocities, shifts, k0, ke, diag, mass, material, x_rows, own, comps):
    rows, lanes = material.shape
    lines = comps * rows
    stride = -(-k0.shape[1] // 8) * 8
    k0, ke = (jnp.transpose(blocks, (2, 3, 0, 1)) for blocks in (k0, ke))
    tables = far(velocities, shifts, k0, ke, diag.T, mass.T)
    return pl.pallas_call(
        ahead_kernel,
        out_shape=(
            near(rows, comps * comps * stride, lanes),
            near(lines, x_rows.shape[0] // lines, lanes),
            near(3 * own.shape[0] // lines, lines * lanes, dtype=jnp.bfloat16),
        ),
        in_specs=[SMEM] + [HBM] * 6 + [VMEM] * 3,
        out_specs=(VMEM,) * 3,
        scratch_shapes=[
            (pltpu.SMEM if array.ndim == 1 else pltpu.VMEM)(array.shape, jnp.float32)
            for array in tables
        ] + [pltpu.SemaphoreType.DMA((len(tables),))],
        compiler_params=SCRATCH,
        name="ahead",
    )(sample, *tables, *kept(material, x_rows, own))


def side_terms(field_row, swapped, side, out, comp, comps):
    stride = field_row.shape[0] // (comps * comps)
    begin = (out * comps + comp) * stride
    below, above = field_row[begin + 1 : begin + 2], field_row[begin + 2 : begin + 3]
    other = (below, above) if side == "even" else (above, below)
    return jnp.where(swapped, *other)


def side_kernel(comps, side, slab_ref, fields_ref, applied_ref, halo_ref, out_ref):
    lines, block_cols, _ = applied_ref.shape
    rows = lines // comps
    swapped = slab_ref[0] % 2 == 1
    for row in range(rows):
        field_row = fields_ref[row]
        views = [line_of(halo_ref, comp, row, comps, rows, block_cols) for comp in range(comps)]
        for out in range(comps):
            total = applied_ref[out * rows + row]
            for comp, view in enumerate(views):
                total = total + side_terms(field_row, swapped, side, out, comp, comps) * view
            out_ref[out * rows + row] = total


def add_side(slab, fields, applied, halo, comps, side):
    return pl.pallas_call(
        functools.partial(side_kernel, comps, side),
        out_shape=near(*applied.shape),
        in_specs=[SMEM] + [VMEM] * 3,
        out_specs=VMEM,
        compiler_params=SCRATCH,
        cost_estimate=EARLY,
        name="side",
    )(slab, *kept(fields, applied, halo))


def split_lines(piece_ref, stack_ref, lines, group_cols, begins):
    lanes = piece_ref.shape[1]
    for line in range(lines):
        values = piece_ref[pl.ds(line, group_cols, stride=lines), :]
        for begin, part in zip(begins, three_parts(values)):
            stack_ref[pl.ds(begin, group_cols), pl.ds(line * lanes, lanes)] = part


def edges_kernel(comps, ks, group_cols, place_ref, fields_ref, applied_ref, *refs):
    piece_refs, out_ref, parts_refs = refs[: len(ks)], refs[len(ks)], refs[len(ks) + 1 :]
    lines, block_cols, lanes = applied_ref.shape
    rows = lines // comps
    stride = fields_ref.shape[1] // (comps * comps)
    place = place_ref[0]

    def edge(comp, step):
        result = jnp.zeros((block_cols, lanes), jnp.float32)
        for k, ref in zip(ks, piece_refs):
            begin = ref.shape[0] - (comps - comp) * block_cols
            here = (place ^ k) == place + step
            result = jnp.where(here, ref[pl.ds(begin, block_cols), :], result)
        return result

    out_ref[...] = applied_ref[...]
    for row, offset, step in ((0, 3, -1), (rows - 1, 4, 1)):
        field_row = fields_ref[row]
        views = [edge(comp, step) for comp in range(comps)]
        for out in range(comps):
            total = out_ref[out * rows + row]
            for comp, view in enumerate(views):
                entry = (out * comps + comp) * stride + offset
                total = total + field_row[entry : entry + 1] * view
            out_ref[out * rows + row] = total
    for piece_ref, parts_ref in zip(piece_refs, parts_refs):
        split_lines(piece_ref, parts_ref, lines, group_cols, [i * group_cols for i in range(3)])


def add_edges(place, fields, applied, pieces, comps, group_cols):
    lines, _, lanes = applied.shape
    parts = near(3 * group_cols, lines * lanes, dtype=jnp.bfloat16)
    return pl.pallas_call(
        functools.partial(edges_kernel, comps, tuple(pieces), group_cols),
        out_shape=(near(*applied.shape),) + (parts,) * len(pieces),
        in_specs=[SMEM] + [VMEM] * (2 + len(pieces)),
        out_specs=(VMEM,) * (1 + len(pieces)),
        compiler_params=SCRATCH,
        cost_estimate=NEXT,
        name="edges",
    )(place, *kept(fields, applied, *pieces.values()))


def fold(total, basis_cols, block_cols, lanes):
    half = basis_cols // 2
    row = lax.broadcasted_iota(jnp.int32, (half, half), 0)
    column = lax.broadcasted_iota(jnp.int32, (half, half), 1)
    last = total[half:basis_cols, half:basis_cols]
    shared = jnp.where(row >= column, total[:half, :half], last)
    diagonal = jnp.sum(jnp.where(row == column, last, 0.0), axis=1, keepdims=True)
    below = total[basis_cols:]
    first = jnp.concatenate((below[:, :half], below[:, half:basis_cols]), axis=0)
    rest = jnp.zeros((half - block_cols, block_cols), jnp.float32)
    block = jnp.concatenate((below[:, basis_cols:], rest), axis=0)
    pad = jnp.zeros((half, lanes - 3 * half - block_cols - 1), jnp.float32)
    return jnp.concatenate(
        (shared, total[:half, half:basis_cols], first, block, diagonal, pad), axis=1
    )


def unfold(folded, block_cols):
    half = folded.shape[0]
    row = lax.broadcasted_iota(jnp.int32, (half, half), 0)
    column = lax.broadcasted_iota(jnp.int32, (half, half), 1)
    shared, across = folded[:, :half], folded[:, half : 2 * half]
    turned = shared.T
    start = jnp.where(row >= column, shared, turned)
    end = jnp.where(row < column, shared, turned)
    diagonal = folded[:, 3 * half + block_cols : 3 * half + block_cols + 1]
    end = jnp.where(row == column, diagonal, end)
    gram = jnp.concatenate(
        (jnp.concatenate((start, across), axis=1), jnp.concatenate((across.T, end), axis=1)), axis=0
    )
    first = folded[:, 2 * half : 3 * half]
    first = jnp.concatenate((first[:block_cols], first[block_cols : 2 * block_cols]), axis=1)
    return gram, first, folded[:block_cols, 3 * half : 3 * half + block_cols]


def sums_kernel(
    comps, split, raw, place_ref, slab_ref, fields_ref, applied_ref, halo_ref, *refs
):
    *refs, stack_ref, sums_ref = refs
    lines, block_cols, lanes = applied_ref.shape
    rows = lines // comps
    group_cols = refs[0].shape[0] // 3
    basis_cols = (len(split) + len(raw)) * group_cols
    joined = basis_cols + block_cols
    place = place_ref[0]
    swapped = slab_ref[0] % 2 == 1
    for k, ref in zip(split + raw, refs):
        begin = pl.multiple_of((place ^ k) * group_cols, group_cols)
        begins = [index * joined + begin for index in range(3)]
        if k in split:
            for index in range(3):
                stack_ref[pl.ds(begins[index], group_cols), :] = ref[
                    pl.ds(index * group_cols, group_cols), :
                ]
        else:
            split_lines(ref, stack_ref, lines, group_cols, begins)
    for row in range(rows):
        field_row = fields_ref[row]
        views = [line_of(halo_ref, comp, row, comps, rows, block_cols) for comp in range(comps)]
        for out in range(comps):
            line = out * rows + row
            total = applied_ref[line]
            for comp, view in enumerate(views):
                total = total + side_terms(field_row, swapped, "odd", out, comp, comps) * view
            for index, part in enumerate(three_parts(total)):
                there = pl.ds(index * joined + basis_cols, block_cols)
                stack_ref[there, pl.ds(line * lanes, lanes)] = part

    stack = stack_ref[...]
    products = lax.dot_general(
        stack, stack, (((1,), (1,)), ((), ())), preferred_element_type=jnp.float32
    )
    wide = products[:joined] + products[joined : 2 * joined] + products[2 * joined :]
    total = wide[:, :joined] + wide[:, joined : 2 * joined] + wide[:, 2 * joined :]
    sums_ref[...] = fold(total, basis_cols, block_cols, sums_ref.shape[1])


def sums(place, slab, fields, applied, halo, split, raw, comps):
    lines, block_cols, lanes = applied.shape
    basis_cols = (len(split) + len(raw)) * (split[0].shape[0] // 3)
    joined = basis_cols + block_cols
    return pl.pallas_call(
        functools.partial(sums_kernel, comps, tuple(split), tuple(raw)),
        out_shape=(
            near(3 * joined, lines * lanes, dtype=jnp.bfloat16),
            near(basis_cols // 2, 2 * basis_cols),
        ),
        in_specs=[SMEM] * 2 + [VMEM] * (3 + len(split) + len(raw)),
        out_specs=(VMEM, VMEM),
        compiler_params=SCRATCH,
        name="sums",
    )(place, slab, *kept(fields, applied, halo, *split.values(), *raw.values()))


def exchange_sum(part, axis):
    count = lax.axis_size(axis)
    mask = 1
    while mask < count:
        part = part + lax.ppermute(part, axis, [(i, i ^ mask) for i in range(count)])
        mask *= 2
    return part


def exchange(part, axis):
    count = lax.axis_size(axis)
    return lax.all_to_all(jnp.broadcast_to(part[None], (count,) + part.shape), axis, 0, 0)


def finish_kernel(
    row_count, comps, place_ref, parts_ref, stack_ref, block_ref, coeffs_ref, upper_ref, bad_ref,
    coeffs_scratch, upper_scratch, block_scratch, sems,
):
    block_cols = upper_ref.shape[0]
    basis_cols = parts_ref.shape[2] // 2
    joined = basis_cols + block_cols
    lines, lanes = block_ref.shape[1:]
    total = jnp.sum(parts_ref[...], axis=0) / row_count
    gram, first, block_gram = unfold(total, block_cols)

    def times(left, right, right_dim=0):
        return lax.dot_general(
            left, right, (((1,), (right_dim,)), ((), ())),
            precision=exact_precision, preferred_element_type=jnp.float32,
        )

    coeffs = first + (first - times(first, gram))
    image = times(coeffs, gram)
    matrix = block_gram - times(
        jnp.concatenate((coeffs, first - image), axis=1), jnp.concatenate((first, coeffs), axis=1), 1
    )
    coeffs_scratch[...] = coeffs.T
    group_cols = coeffs_ref.shape[0]
    start = pl.multiple_of(place_ref[0] * group_cols, group_cols)
    copies = [
        pltpu.make_async_copy(
            coeffs_scratch.at[pl.ds(start, group_cols)], coeffs_ref, sems.at[comps]
        )
    ]
    copies[0].start()

    row = lax.broadcasted_iota(jnp.int32, (block_cols, block_cols), 0)
    column = lax.broadcasted_iota(jnp.int32, (block_cols, block_cols), 1)
    unit = jnp.where(row == column, 1.0, 0.0)
    pad = jnp.zeros((block_cols, 2 * basis_cols - joined - block_cols), jnp.float32)
    work = jnp.concatenate((-coeffs, unit, matrix, pad), axis=1)
    height = lax.broadcasted_iota(jnp.int32, work.shape, 0)
    width = 4
    for begin in range(0, block_cols, width):
        done, new_rows = [], []
        for step in range(begin, begin + width):
            column_here = jnp.broadcast_to(work[:, joined + step : joined + step + 1], work.shape)
            pivot_row = work[step : step + 1]
            for other_column, other_row, inverse in done:
                entry = other_column[step : step + 1]
                pivot_row = pivot_row - entry * other_row
                column_here = column_here - other_column * (entry * inverse)
            pivot = column_here[step : step + 1]
            inverse = 1.0 / pivot
            done.append((column_here, pivot_row * inverse, inverse))
            new_rows.append(pivot_row * lax.rsqrt(pivot))
        rest = work
        for column_here, scaled, _ in done:
            rest = rest - column_here * scaled
        work = jnp.where(height >= begin + width, rest, work)
        for step, new_row in enumerate(new_rows, begin):
            work = jnp.where(height == step, new_row, work)
    upper = jnp.where(row <= column, work[:, joined : joined + block_cols], 0.0)
    upper_scratch[...] = upper
    kept_enough = jnp.where(row == column, upper * upper * LOSS, block_gram) >= block_gram
    bad_ref[0] = 1 - jnp.min(jnp.where(kept_enough, 1, 0))
    copies.append(pltpu.make_async_copy(upper_scratch, upper_ref, sems.at[comps + 1]))
    copies[1].start()
    weights = three_parts(work[:, :joined])
    wide = jnp.concatenate(
        [jnp.concatenate((part, part, part), axis=1) for part in weights], axis=0
    )
    rows = lines // comps
    for comp in range(comps):
        there = pl.ds(comp * rows * lanes, rows * lanes)
        result = jnp.dot(wide, stack_ref[:, there], preferred_element_type=jnp.float32)
        result = result[:block_cols] + result[block_cols : 2 * block_cols] + result[2 * block_cols :]
        for index in range(rows):
            block_scratch[pl.ds(comp * rows + index, block_cols, stride=lines), :] = result[
                :, index * lanes : (index + 1) * lanes
            ]
        part = pl.ds(comp * rows, rows)
        copies.append(
            pltpu.make_async_copy(
                block_scratch.reshape(block_cols, lines, lanes).at[:, part, :],
                block_ref.at[:, part, :],
                sems.at[comp],
            )
        )
        copies[-1].start()
    for copy in copies:
        copy.wait()


def finish(place, parts, stack, row_count, block_cols, group_cols, lines, comps):
    lanes = stack.shape[1] // lines
    basis_cols = parts.shape[2] // 2
    return pl.pallas_call(
        functools.partial(finish_kernel, row_count, comps),
        out_shape=(
            f32(block_cols, lines, lanes), f32(group_cols, block_cols), f32(block_cols, block_cols),
            jax.ShapeDtypeStruct((1,), jnp.int32),
        ),
        in_specs=[SMEM] + [VMEM] * 2,
        out_specs=(HBM,) * 3 + (SMEM,),
        scratch_shapes=[
            pltpu.VMEM((basis_cols, block_cols), jnp.float32),
            pltpu.VMEM((block_cols, block_cols), jnp.float32),
            pltpu.VMEM((block_cols * lines, lanes), jnp.float32),
            pltpu.SemaphoreType.DMA((comps + 2,)),
        ],
        compiler_params=SCRATCH,
        name="finish",
    )(place, *kept(parts, stack))


def stencil_tables(k0_blocks, k0_diag, ke_blocks, mass, velocities, shifts, sample):
    velocity = jnp.take(velocities, sample, axis=0)[0]
    sigma_value = jnp.take(shifts, sample, axis=0)[0]
    center = (k0_diag - sigma_value * mass)[:, :, None] * jnp.eye(3, dtype=jnp.float32)
    tables = k0_blocks - velocity * velocity * ke_blocks
    return tables.at[:, 0].add(center)


def shifted(cells, dim, axis, up):
    extent = cells.shape[dim]
    edge = lax.slice_in_dim(cells, 0, 1, axis=dim) if up else (
        lax.slice_in_dim(cells, extent - 1, extent, axis=dim)
    )
    if axis is None:
        edge = jnp.zeros_like(edge)
    else:
        ends = [(i, i + 1) for i in range(lax.axis_size(axis) - 1)]
        edge = lax.ppermute(edge, axis, [(j, i) for i, j in ends] if up else ends)
    if up:
        return jnp.concatenate((lax.slice_in_dim(cells, 1, extent, axis=dim), edge), axis=dim)
    return jnp.concatenate((edge, lax.slice_in_dim(cells, 0, extent - 1, axis=dim)), axis=dim)


def hold_kernel(*refs):
    *refs, sems = refs
    half = len(refs) // 2
    copies = [
        pltpu.make_async_copy(source, target, sems.at[index])
        for index, (source, target) in enumerate(zip(refs[:half], refs[half:]))
    ]
    for copy in copies:
        copy.start()
    for copy in copies:
        copy.wait()


def hold(*arrays):
    return pl.pallas_call(
        hold_kernel,
        out_shape=[jax.ShapeDtypeStruct(array.shape, array.dtype) for array in arrays],
        in_specs=[HBM] * len(arrays),
        out_specs=[HBM] * len(arrays),
        scratch_shapes=[pltpu.SemaphoreType.DMA((len(arrays),))],
        compiler_params=SCRATCH,
        name="hold",
    )(*far(*arrays))


def careful(arguments):
    x_block, basis, material, k0_blocks, k0_diag, ke_blocks, mass, velocities, shifts, sample = arguments
    x_block, basis, material, k0_blocks, k0_diag, ke_blocks, mass, velocities, shifts = hold(
        x_block, basis, material, jnp.transpose(k0_blocks, (2, 3, 0, 1)), k0_diag.T,
        jnp.transpose(ke_blocks, (2, 3, 0, 1)), mass.T, velocities, shifts,
    )
    k0_blocks, ke_blocks = (jnp.transpose(blocks, (2, 3, 0, 1)) for blocks in (k0_blocks, ke_blocks))
    k0_diag, mass = k0_diag.T, mass.T
    tables = stencil_tables(k0_blocks, k0_diag, ke_blocks, mass, velocities, shifts, sample)
    block_cols, comps, extent_x, _, lanes = x_block.shape
    group_cols = basis.shape[0]
    row_count = float(comps * extent_x * lax.axis_size("space") * basis.shape[3] * lanes)
    fields = jnp.zeros((7, comps, comps) + material.shape, jnp.float32)
    for level in range(tables.shape[0]):
        chosen = (material == level).astype(jnp.float32)
        fields = fields + tables[level][:, :, :, None, None, None] * chosen
    views = [x_block]
    for dim, axis in ((2, "space"), (3, "basis"), (4, None)):
        views += [shifted(x_block, dim, axis, False), shifted(x_block, dim, axis, True)]
    applied = jnp.zeros_like(x_block)
    for offset, view in enumerate(views):
        for comp in range(comps):
            applied = applied + fields[offset, :, comp][None] * view[:, comp : comp + 1]

    count = lax.axis_size("basis")
    place = lax.axis_index("basis")
    pieces = jnp.moveaxis(basis.reshape(basis.shape[:3] + (count, -1, lanes)), 3, 0)
    rows = jnp.zeros((count,) + pieces.shape[1:], jnp.float32)
    for k in range(count):
        piece = lax.dynamic_index_in_dim(pieces, place ^ k, 0, keepdims=False)
        if k:
            piece = lax.ppermute(piece, "basis", [(i, i ^ k) for i in range(count)])
        rows = lax.dynamic_update_index_in_dim(rows, piece, place ^ k, 0)
    rows = rows.reshape((count * group_cols,) + pieces.shape[2:])

    def total(part):
        for axis in ("basis", "space"):
            mask = 1
            while mask < lax.axis_size(axis):
                pairs = [(i, i ^ mask) for i in range(lax.axis_size(axis))]
                part = part + lax.ppermute(part, axis, pairs)
                mask *= 2
        return part / row_count

    running = jnp.zeros((count * group_cols, block_cols), jnp.float32)
    for repeat in range(2):
        coeffs = total(
            jnp.einsum("kcxyz,ncxyz->kn", rows, applied, precision=exact_precision)
        )
        applied = applied - jnp.einsum("kcxyz,kn->ncxyz", rows, coeffs, precision=exact_precision)
        running = running + coeffs
    gram = total(jnp.einsum("ncxyz,mcxyz->nm", applied, applied, precision=exact_precision))
    lower = jnp.linalg.cholesky(gram)
    inverse = lax.linalg.triangular_solve(
        lower, jnp.eye(block_cols, dtype=jnp.float32), left_side=True, lower=True
    )
    block = jnp.einsum("mcxyz,nm->ncxyz", applied, inverse, precision=exact_precision)
    own = lax.dynamic_slice_in_dim(running, place * group_cols, group_cols, axis=0)
    return tuple(hold(block.reshape(block_cols, -1, lanes), own, lower.T))


def shards(
    x_block, basis, material, k0_blocks, k0_diag, ke_blocks, mass, velocities, shifts, sample
):
    arguments = (
        x_block, basis, material, k0_blocks, k0_diag, ke_blocks, mass, velocities, shifts, sample
    )
    block_cols, comps, extent_x, rows, lanes = x_block.shape
    group_cols = basis.shape[0]
    lines = comps * rows
    row_count = float(comps * extent_x * lax.axis_size("space") * basis.shape[3] * lanes)

    place = lax.axis_index("basis").astype(jnp.int32).reshape(1)
    slab = lax.axis_index("space").astype(jnp.int32).reshape(1)
    count = lax.axis_size("basis")
    x_far = x_block.reshape(block_cols * lines, lanes)
    own, *pieces, x_rows, material = pack(place, basis, x_far, material.reshape(rows, lanes), block_cols)
    got = {}
    for name in ("even", 3, "odd", 2, 1):
        if name == "even":
            got[name] = swap(x_far, "space", 0)
        elif name == "odd":
            got[name] = swap(x_far, "space", 1)
        else:
            piece = lax.ppermute(pieces[name - 1], "basis", [(i, i ^ name) for i in range(count)])
            got[name] = piece.reshape(-1, lanes)
    fields, applied, own = ahead(
        sample, velocities, shifts, k0_blocks, ke_blocks, k0_diag, mass, material, x_rows,
        own.reshape(-1, lanes), comps,
    )
    applied = add_side(slab, fields, applied, got.pop("even"), comps, "even")
    pieces = {k: got.pop(k) for k in reversed(partners(count)[1])}
    applied, *parts = add_edges(place, fields, applied, pieces, comps, group_cols)
    split = {0: own, **dict(zip(pieces, parts))}
    stack, part = sums(place, slab, fields, applied, got.pop("odd"), split, got, comps)
    parts = exchange(exchange_sum(part, "basis"), "space")
    block, coeffs, upper, bad = finish(
        place, parts, stack, row_count, block_cols, group_cols, lines, comps
    )
    block, coeffs, upper = lax.while_loop(
        lambda state: state[0] > 0,
        lambda state: (jnp.zeros_like(state[0]), careful(arguments)),
        (bad[0], (block, coeffs, upper)),
    )[1]
    return block.reshape(x_block.shape), coeffs, upper


def solution(mesh):
    in_specs = (
        P(None, None, "space", "basis", None),
        P("basis", None, "space", None, None),
        P("space", "basis", None),
        P(),
        P(),
        P(),
        P(),
        P(),
        P(),
        P(),
    )
    out_specs = (P(None, None, "space", "basis", None), P("basis", None), P())
    return jax.shard_map(shards, mesh=mesh, in_specs=in_specs, out_specs=out_specs, check_vma=False)
```

```python
import functools

import jax
import jax.numpy as jnp
from jax import lax
from jax.experimental import pallas as pl
from jax.experimental.pallas import tpu as pltpu
from jax.sharding import PartitionSpec as P

exact_precision = lax.Precision.HIGHEST
VMEM = pl.BlockSpec(memory_space=pltpu.VMEM)
SMEM = pl.BlockSpec(memory_space=pltpu.SMEM)
HBM = pl.BlockSpec(memory_space=pltpu.HBM)
LOSS = 256.0
EARLY = pl.CostEstimate(flops=10**9, bytes_accessed=10**6, transcendentals=0)
NEXT = pl.CostEstimate(flops=10**6, bytes_accessed=10**6, transcendentals=0)
SCRATCH = pltpu.CompilerParams(vmem_limit_bytes=8 * 2**20)


def f32(*shape):
    return jax.ShapeDtypeStruct(shape, jnp.float32)


def near(*shape, dtype=jnp.float32):
    return pltpu.VMEM(shape, dtype)


def kept(*arrays):
    return [pltpu.with_memory_space_constraint(array, pltpu.VMEM) for array in arrays]


def far(*arrays):
    return [pltpu.with_memory_space_constraint(array, pltpu.HBM) for array in arrays]


def swap(values, axis, first):
    pairs = [(i, i + 1) for i in range(first, lax.axis_size(axis) - 1, 2)]
    return lax.ppermute(values, axis, pairs + [(j, i) for i, j in pairs])


def partners(count):
    return range(1, count), [k for k in range(1, count) if k & (k + 1) == 0]


def pack_kernel(comps, place_ref, basis_ref, x_ref, material_ref, *refs):
    *piece_refs, x_out_ref, material_out_ref, sems = refs
    count = len(piece_refs)
    tiles, _, rows, lanes = basis_ref.shape
    block_cols = x_ref.shape[0] // (comps * rows)
    place = place_ref[0]
    x_copy = pltpu.make_async_copy(x_ref, x_out_ref, sems.at[count])
    x_copy.start()
    copies = [pltpu.make_async_copy(material_ref, material_out_ref, sems.at[count + 1])]
    for k in reversed(range(count)):
        copies.append(
            pltpu.make_async_copy(
                basis_ref.at[:, place ^ k], piece_refs[k].at[pl.ds(0, tiles)], sems.at[k]
            )
        )
    for copy in copies:
        copy.start()
    x_copy.wait()
    for comp in range(comps):
        first, last = (
            x_out_ref[pl.ds(comp * rows + row, block_cols, stride=comps * rows), :]
            for row in (0, rows - 1)
        )
        for k in partners(count)[1]:
            edge = jnp.where((place ^ k) > place, last, first)
            for part in range(block_cols // rows):
                piece_refs[k][tiles + comp * (block_cols // rows) + part] = edge[
                    part * rows : (part + 1) * rows
                ]
    for copy in copies:
        copy.wait()


def pack(place, basis, x_rows, material, block_cols):
    group_cols, comps, _, full_y, lanes = basis.shape
    count = lax.axis_size("basis")
    rows = full_y // count
    tiles = group_cols * comps
    edge_tiles = block_cols * comps // rows
    pieces = [
        near(tiles + (edge_tiles if k in partners(count)[1] else 0), rows, lanes)
        for k in range(count)
    ]
    return pl.pallas_call(
        functools.partial(pack_kernel, comps),
        out_shape=(*pieces, near(*x_rows.shape), near(*material.shape, dtype=jnp.int32)),
        in_specs=[SMEM, HBM, HBM, HBM],
        out_specs=(VMEM,) * (count + 2),
        scratch_shapes=[pltpu.SemaphoreType.DMA((count + 2,))],
        compiler_params=SCRATCH,
        name="pack",
    )(place, *far(basis.reshape(tiles, count, rows, lanes), x_rows, material))


def three_parts(values):
    high = values.astype(jnp.bfloat16)
    rest = values - high.astype(jnp.float32)
    middle = rest.astype(jnp.bfloat16)
    low = (rest - middle.astype(jnp.float32)).astype(jnp.bfloat16)
    return high, middle, low


def line_of(ref, comp, row, comps, rows, block_cols):
    return ref[pl.ds(comp * rows + row, block_cols, stride=comps * rows), :]


def ahead_kernel(
    sample_ref, *refs
):
    far_refs, refs = refs[:6], refs[6:]
    material_ref, x_ref, own_ref, fields_ref, applied_ref, stack_ref, *near_refs, sems = refs
    velocities_ref, shifts_ref, k0_ref, ke_ref, diag_ref, mass_ref = near_refs
    copies = [
        pltpu.make_async_copy(source, target, sems.at[index])
        for index, (source, target) in enumerate(zip(far_refs, near_refs))
    ]
    for copy in copies:
        copy.start()
    group_cols = stack_ref.shape[0] // 3
    split_lines(
        own_ref, stack_ref, applied_ref.shape[0], group_cols, [i * group_cols for i in range(3)]
    )
    for copy in copies:
        copy.wait()
    comps, _, levels, offsets = k0_ref.shape
    rows, lanes = material_ref.shape
    lines = comps * rows
    block_cols = x_ref.shape[0] // lines
    velocity = velocities_ref[sample_ref[0]]
    sigma = shifts_ref[sample_ref[0]]
    entry_rows = fields_ref.shape[1]
    stride = entry_rows // (comps * comps)
    gap = jnp.zeros((levels, stride - offsets), jnp.float32)
    wide = []
    for out in range(comps):
        for comp in range(comps):
            wide += [k0_ref[out, comp] - velocity * velocity * ke_ref[out, comp], gap]
    wide.append(jnp.zeros((levels, lanes - entry_rows), jnp.float32))
    table = jnp.concatenate(wide, axis=1).T[:entry_rows]
    entry = lax.broadcasted_iota(jnp.int32, table.shape, 0)
    for comp in range(comps):
        centre = diag_ref[comp : comp + 1, :] - sigma * mass_ref[comp : comp + 1, :]
        table = table + jnp.where(entry == comp * (comps + 1) * stride, centre, 0.0)

    lane = lax.broadcasted_iota(jnp.int32, (block_cols, lanes), 1)
    level = lax.broadcasted_iota(jnp.int32, (levels, lanes), 0)
    for row in range(rows):
        chosen = jnp.broadcast_to(material_ref[row : row + 1, :], (levels, lanes)) == level
        fields = jnp.dot(
            table, chosen.astype(jnp.float32),
            precision=exact_precision, preferred_element_type=jnp.float32,
        )
        fields_ref[row] = fields
        sums = [None] * comps
        for comp in range(comps):
            centre = line_of(x_ref, comp, row, comps, rows, block_cols)
            views = {
                0: centre,
                5: jnp.where(lane == 0, 0.0, pltpu.roll(centre, 1, 1)),
                6: jnp.where(lane == lanes - 1, 0.0, pltpu.roll(centre, lanes - 1, 1)),
            }
            if row > 0:
                views[3] = line_of(x_ref, comp, row - 1, comps, rows, block_cols)
            if row < rows - 1:
                views[4] = line_of(x_ref, comp, row + 1, comps, rows, block_cols)
            for offset, view in views.items():
                for out in range(comps):
                    place = (out * comps + comp) * stride + offset
                    term = fields[place : place + 1, :] * view
                    sums[out] = term if sums[out] is None else sums[out] + term
        for out in range(comps):
            applied_ref[out * rows + row] = sums[out]


def ahead(sample, velocities, shifts, k0, ke, diag, mass, material, x_rows, own, comps):
    rows, lanes = material.shape
    lines = comps * rows
    stride = -(-k0.shape[1] // 8) * 8
    k0, ke = (jnp.transpose(blocks, (2, 3, 0, 1)) for blocks in (k0, ke))
    tables = far(velocities, shifts, k0, ke, diag.T, mass.T)
    return pl.pallas_call(
        ahead_kernel,
        out_shape=(
            near(rows, comps * comps * stride, lanes),
            near(lines, x_rows.shape[0] // lines, lanes),
            near(3 * own.shape[0] // lines, lines * lanes, dtype=jnp.bfloat16),
        ),
        in_specs=[SMEM] + [HBM] * 6 + [VMEM] * 3,
        out_specs=(VMEM,) * 3,
        scratch_shapes=[
            (pltpu.SMEM if array.ndim == 1 else pltpu.VMEM)(array.shape, jnp.float32)
            for array in tables
        ] + [pltpu.SemaphoreType.DMA((len(tables),))],
        compiler_params=SCRATCH,
        name="ahead",
    )(sample, *tables, *kept(material, x_rows, own))


def side_terms(field_row, swapped, side, out, comp, comps):
    stride = field_row.shape[0] // (comps * comps)
    begin = (out * comps + comp) * stride
    below, above = field_row[begin + 1 : begin + 2], field_row[begin + 2 : begin + 3]
    other = (below, above) if side == "even" else (above, below)
    return jnp.where(swapped, *other)


def side_kernel(comps, side, slab_ref, fields_ref, applied_ref, halo_ref, out_ref):
    lines, block_cols, _ = applied_ref.shape
    rows = lines // comps
    swapped = slab_ref[0] % 2 == 1
    for row in range(rows):
        field_row = fields_ref[row]
        views = [line_of(halo_ref, comp, row, comps, rows, block_cols) for comp in range(comps)]
        for out in range(comps):
            total = applied_ref[out * rows + row]
            for comp, view in enumerate(views):
                total = total + side_terms(field_row, swapped, side, out, comp, comps) * view
            out_ref[out * rows + row] = total


def add_side(slab, fields, applied, halo, comps, side):
    return pl.pallas_call(
        functools.partial(side_kernel, comps, side),
        out_shape=near(*applied.shape),
        in_specs=[SMEM] + [VMEM] * 3,
        out_specs=VMEM,
        compiler_params=SCRATCH,
        cost_estimate=EARLY,
        name="side",
    )(slab, *kept(fields, applied, halo))


def split_lines(piece_ref, stack_ref, lines, group_cols, begins):
    lanes = piece_ref.shape[1]
    for line in range(lines):
        values = piece_ref[pl.ds(line, group_cols, stride=lines), :]
        for begin, part in zip(begins, three_parts(values)):
            stack_ref[pl.ds(begin, group_cols), pl.ds(line * lanes, lanes)] = part


def edges_kernel(comps, ks, group_cols, place_ref, fields_ref, applied_ref, *refs):
    piece_refs, out_ref, parts_refs = refs[: len(ks)], refs[len(ks)], refs[len(ks) + 1 :]
    lines, block_cols, lanes = applied_ref.shape
    rows = lines // comps
    stride = fields_ref.shape[1] // (comps * comps)
    place = place_ref[0]

    def edge(comp, step):
        result = jnp.zeros((block_cols, lanes), jnp.float32)
        for k, ref in zip(ks, piece_refs):
            begin = ref.shape[0] - (comps - comp) * block_cols
            here = (place ^ k) == place + step
            result = jnp.where(here, ref[pl.ds(begin, block_cols), :], result)
        return result

    out_ref[...] = applied_ref[...]
    for row, offset, step in ((0, 3, -1), (rows - 1, 4, 1)):
        field_row = fields_ref[row]
        views = [edge(comp, step) for comp in range(comps)]
        for out in range(comps):
            total = out_ref[out * rows + row]
            for comp, view in enumerate(views):
                entry = (out * comps + comp) * stride + offset
                total = total + field_row[entry : entry + 1] * view
            out_ref[out * rows + row] = total
    for piece_ref, parts_ref in zip(piece_refs, parts_refs):
        split_lines(piece_ref, parts_ref, lines, group_cols, [i * group_cols for i in range(3)])


def add_edges(place, fields, applied, pieces, comps, group_cols):
    lines, _, lanes = applied.shape
    parts = near(3 * group_cols, lines * lanes, dtype=jnp.bfloat16)
    return pl.pallas_call(
        functools.partial(edges_kernel, comps, tuple(pieces), group_cols),
        out_shape=(near(*applied.shape),) + (parts,) * len(pieces),
        in_specs=[SMEM] + [VMEM] * (2 + len(pieces)),
        out_specs=(VMEM,) * (1 + len(pieces)),
        compiler_params=SCRATCH,
        cost_estimate=NEXT,
        name="edges",
    )(place, *kept(fields, applied, *pieces.values()))


def fold(total, basis_cols, block_cols, lanes):
    half = basis_cols // 2
    row = lax.broadcasted_iota(jnp.int32, (half, half), 0)
    column = lax.broadcasted_iota(jnp.int32, (half, half), 1)
    last = total[half:basis_cols, half:basis_cols]
    shared = jnp.where(row >= column, total[:half, :half], last)
    diagonal = jnp.sum(jnp.where(row == column, last, 0.0), axis=1, keepdims=True)
    below = total[basis_cols:]
    first = jnp.concatenate((below[:, :half], below[:, half:basis_cols]), axis=0)
    rest = jnp.zeros((half - block_cols, block_cols), jnp.float32)
    block = jnp.concatenate((below[:, basis_cols:], rest), axis=0)
    pad = jnp.zeros((half, lanes - 3 * half - block_cols - 1), jnp.float32)
    return jnp.concatenate(
        (shared, total[:half, half:basis_cols], first, block, diagonal, pad), axis=1
    )


def unfold(folded, block_cols):
    half = folded.shape[0]
    row = lax.broadcasted_iota(jnp.int32, (half, half), 0)
    column = lax.broadcasted_iota(jnp.int32, (half, half), 1)
    shared, across = folded[:, :half], folded[:, half : 2 * half]
    turned = shared.T
    start = jnp.where(row >= column, shared, turned)
    end = jnp.where(row < column, shared, turned)
    diagonal = folded[:, 3 * half + block_cols : 3 * half + block_cols + 1]
    end = jnp.where(row == column, diagonal, end)
    gram = jnp.concatenate(
        (jnp.concatenate((start, across), axis=1), jnp.concatenate((across.T, end), axis=1)), axis=0
    )
    first = folded[:, 2 * half : 3 * half]
    first = jnp.concatenate((first[:block_cols], first[block_cols : 2 * block_cols]), axis=1)
    return gram, first, folded[:block_cols, 3 * half : 3 * half + block_cols]


def sums_kernel(
    comps, split, raw, place_ref, slab_ref, fields_ref, applied_ref, *refs
):
    *refs, halo_ref, stack_ref, sums_ref = refs
    lines, block_cols, lanes = applied_ref.shape
    rows = lines // comps
    group_cols = refs[0].shape[0] // 3
    basis_cols = (len(split) + len(raw)) * group_cols
    joined = basis_cols + block_cols
    place = place_ref[0]
    swapped = slab_ref[0] % 2 == 1
    for k, ref in zip(split + raw, refs):
        begin = pl.multiple_of((place ^ k) * group_cols, group_cols)
        begins = [index * joined + begin for index in range(3)]
        if k in split:
            for index in range(3):
                stack_ref[pl.ds(begins[index], group_cols), :] = ref[
                    pl.ds(index * group_cols, group_cols), :
                ]
        else:
            split_lines(ref, stack_ref, lines, group_cols, begins)
    for row in range(rows):
        field_row = fields_ref[row]
        views = [line_of(halo_ref, comp, row, comps, rows, block_cols) for comp in range(comps)]
        for out in range(comps):
            line = out * rows + row
            total = applied_ref[line]
            for comp, view in enumerate(views):
                total = total + side_terms(field_row, swapped, "odd", out, comp, comps) * view
            for index, part in enumerate(three_parts(total)):
                there = pl.ds(index * joined + basis_cols, block_cols)
                stack_ref[there, pl.ds(line * lanes, lanes)] = part

    stack = stack_ref[...]
    products = lax.dot_general(
        stack, stack, (((1,), (1,)), ((), ())), preferred_element_type=jnp.float32
    )
    wide = products[:joined] + products[joined : 2 * joined] + products[2 * joined :]
    total = wide[:, :joined] + wide[:, joined : 2 * joined] + wide[:, 2 * joined :]
    sums_ref[...] = fold(total, basis_cols, block_cols, sums_ref.shape[1])


def sums(place, slab, fields, applied, halo, split, raw, comps):
    lines, block_cols, lanes = applied.shape
    basis_cols = (len(split) + len(raw)) * (split[0].shape[0] // 3)
    joined = basis_cols + block_cols
    return pl.pallas_call(
        functools.partial(sums_kernel, comps, tuple(split), tuple(raw)),
        out_shape=(
            near(3 * joined, lines * lanes, dtype=jnp.bfloat16),
            near(basis_cols // 2, 2 * basis_cols),
        ),
        in_specs=[SMEM] * 2 + [VMEM] * (3 + len(split) + len(raw)),
        out_specs=(VMEM, VMEM),
        compiler_params=SCRATCH,
        name="sums",
    )(place, slab, *kept(fields, applied, *split.values(), *raw.values(), halo))


def exchange_sum(part, axis):
    count = lax.axis_size(axis)
    mask = 1
    while mask < count:
        part = part + lax.ppermute(part, axis, [(i, i ^ mask) for i in range(count)])
        mask *= 2
    return part


def exchange(part, axis):
    count = lax.axis_size(axis)
    return lax.all_to_all(jnp.broadcast_to(part[None], (count,) + part.shape), axis, 0, 0)


def finish_kernel(
    row_count, comps, place_ref, parts_ref, stack_ref, block_ref, coeffs_ref, upper_ref, bad_ref,
    coeffs_scratch, upper_scratch, bad_scratch, block_scratch, sems,
):
    block_cols = upper_ref.shape[0]
    basis_cols = parts_ref.shape[2] // 2
    joined = basis_cols + block_cols
    lines, lanes = block_ref.shape[1:]
    total = jnp.sum(parts_ref[...], axis=0) / row_count
    gram, first, block_gram = unfold(total, block_cols)

    def times(left, right, right_dim=0):
        return lax.dot_general(
            left, right, (((1,), (right_dim,)), ((), ())),
            precision=exact_precision, preferred_element_type=jnp.float32,
        )

    coeffs = first + (first - times(first, gram))
    image = times(coeffs, gram)
    matrix = block_gram - times(
        jnp.concatenate((coeffs, first - image), axis=1), jnp.concatenate((first, coeffs), axis=1), 1
    )
    coeffs_scratch[...] = coeffs.T
    group_cols = coeffs_ref.shape[0]
    start = pl.multiple_of(place_ref[0] * group_cols, group_cols)
    copies = [
        pltpu.make_async_copy(
            coeffs_scratch.at[pl.ds(start, group_cols)], coeffs_ref, sems.at[comps]
        )
    ]
    copies[0].start()

    row = lax.broadcasted_iota(jnp.int32, (block_cols, block_cols), 0)
    column = lax.broadcasted_iota(jnp.int32, (block_cols, block_cols), 1)
    unit = jnp.where(row == column, 1.0, 0.0)
    pad = jnp.zeros((block_cols, 2 * basis_cols - joined - block_cols), jnp.float32)
    work = jnp.concatenate((-coeffs, unit, matrix, pad), axis=1)
    height = lax.broadcasted_iota(jnp.int32, work.shape, 0)
    width = 4
    for begin in range(0, block_cols, width):
        done, new_rows = [], []
        for step in range(begin, begin + width):
            column_here = jnp.broadcast_to(work[:, joined + step : joined + step + 1], work.shape)
            pivot_row = work[step : step + 1]
            for other_column, other_row, inverse in done:
                entry = other_column[step : step + 1]
                pivot_row = pivot_row - entry * other_row
                column_here = column_here - other_column * (entry * inverse)
            pivot = column_here[step : step + 1]
            inverse = 1.0 / pivot
            done.append((column_here, pivot_row * inverse, inverse))
            new_rows.append(pivot_row * lax.rsqrt(pivot))
        rest = work
        for column_here, scaled, _ in done:
            rest = rest - column_here * scaled
        work = jnp.where(height >= begin + width, rest, work)
        for step, new_row in enumerate(new_rows, begin):
            work = jnp.where(height == step, new_row, work)
    upper = jnp.where(row <= column, work[:, joined : joined + block_cols], 0.0)
    upper_scratch[...] = upper
    kept_enough = jnp.where(row == column, upper * upper * LOSS, block_gram) >= block_gram
    kept_enough = jnp.min(jnp.where(kept_enough, 1.0, 0.0), axis=0, keepdims=True)
    kept_enough = jnp.min(kept_enough, axis=1, keepdims=True)
    bad_scratch[...] = jnp.where(kept_enough > 0.0, 0, 1)
    copies.append(pltpu.make_async_copy(bad_scratch, bad_ref, sems.at[comps + 2]))
    copies[-1].start()
    copies.append(pltpu.make_async_copy(upper_scratch, upper_ref, sems.at[comps + 1]))
    copies[-1].start()
    weights = three_parts(work[:, :joined])
    wide = jnp.concatenate(
        [jnp.concatenate((part, part, part), axis=1) for part in weights], axis=0
    )
    rows = lines // comps
    for comp in range(comps):
        there = pl.ds(comp * rows * lanes, rows * lanes)
        result = jnp.dot(wide, stack_ref[:, there], preferred_element_type=jnp.float32)
        result = result[:block_cols] + result[block_cols : 2 * block_cols] + result[2 * block_cols :]
        for index in range(rows):
            block_scratch[pl.ds(comp * rows + index, block_cols, stride=lines), :] = result[
                :, index * lanes : (index + 1) * lanes
            ]
        part = pl.ds(comp * rows, rows)
        copies.append(
            pltpu.make_async_copy(
                block_scratch.reshape(block_cols, lines, lanes).at[:, part, :],
                block_ref.at[:, part, :],
                sems.at[comp],
            )
        )
        copies[-1].start()
    for copy in copies:
        copy.wait()


def finish(place, parts, stack, row_count, block_cols, group_cols, lines, comps):
    lanes = stack.shape[1] // lines
    basis_cols = parts.shape[2] // 2
    return pl.pallas_call(
        functools.partial(finish_kernel, row_count, comps),
        out_shape=(
            f32(block_cols, lines, lanes), f32(group_cols, block_cols), f32(block_cols, block_cols),
            jax.ShapeDtypeStruct((1, 1), jnp.int32),
        ),
        in_specs=[SMEM] + [VMEM] * 2,
        out_specs=(HBM,) * 4,
        scratch_shapes=[
            pltpu.VMEM((basis_cols, block_cols), jnp.float32),
            pltpu.VMEM((block_cols, block_cols), jnp.float32),
            pltpu.VMEM((1, 1), jnp.int32),
            pltpu.VMEM((block_cols * lines, lanes), jnp.float32),
            pltpu.SemaphoreType.DMA((comps + 3,)),
        ],
        compiler_params=SCRATCH,
        name="finish",
    )(place, *kept(parts, stack))


def stencil_tables(k0_blocks, k0_diag, ke_blocks, mass, velocities, shifts, sample):
    velocity = jnp.take(velocities, sample, axis=0)[0]
    sigma_value = jnp.take(shifts, sample, axis=0)[0]
    center = (k0_diag - sigma_value * mass)[:, :, None] * jnp.eye(3, dtype=jnp.float32)
    tables = k0_blocks - velocity * velocity * ke_blocks
    return tables.at[:, 0].add(center)


def shifted(cells, dim, axis, up):
    extent = cells.shape[dim]
    edge = lax.slice_in_dim(cells, 0, 1, axis=dim) if up else (
        lax.slice_in_dim(cells, extent - 1, extent, axis=dim)
    )
    if axis is None:
        edge = jnp.zeros_like(edge)
    else:
        ends = [(i, i + 1) for i in range(lax.axis_size(axis) - 1)]
        edge = lax.ppermute(edge, axis, [(j, i) for i, j in ends] if up else ends)
    if up:
        return jnp.concatenate((lax.slice_in_dim(cells, 1, extent, axis=dim), edge), axis=dim)
    return jnp.concatenate((edge, lax.slice_in_dim(cells, 0, extent - 1, axis=dim)), axis=dim)


def hold_kernel(*refs):
    *refs, sems = refs
    half = len(refs) // 2
    copies = [
        pltpu.make_async_copy(source, target, sems.at[index])
        for index, (source, target) in enumerate(zip(refs[:half], refs[half:]))
    ]
    for copy in copies:
        copy.start()
    for copy in copies:
        copy.wait()


def hold(*arrays):
    return pl.pallas_call(
        hold_kernel,
        out_shape=[jax.ShapeDtypeStruct(array.shape, array.dtype) for array in arrays],
        in_specs=[HBM] * len(arrays),
        out_specs=[HBM] * len(arrays),
        scratch_shapes=[pltpu.SemaphoreType.DMA((len(arrays),))],
        compiler_params=SCRATCH,
        name="hold",
    )(*far(*arrays))


def careful(arguments):
    x_block, basis, material, k0_blocks, k0_diag, ke_blocks, mass, velocities, shifts, sample = arguments
    x_block, basis, material, k0_blocks, k0_diag, ke_blocks, mass, velocities, shifts = hold(
        x_block, basis, material, jnp.transpose(k0_blocks, (2, 3, 0, 1)), k0_diag.T,
        jnp.transpose(ke_blocks, (2, 3, 0, 1)), mass.T, velocities, shifts,
    )
    k0_blocks, ke_blocks = (jnp.transpose(blocks, (2, 3, 0, 1)) for blocks in (k0_blocks, ke_blocks))
    k0_diag, mass = k0_diag.T, mass.T
    tables = stencil_tables(k0_blocks, k0_diag, ke_blocks, mass, velocities, shifts, sample)
    block_cols, comps, extent_x, _, lanes = x_block.shape
    group_cols = basis.shape[0]
    row_count = float(comps * extent_x * lax.axis_size("space") * basis.shape[3] * lanes)
    fields = jnp.zeros((7, comps, comps) + material.shape, jnp.float32)
    for level in range(tables.shape[0]):
        chosen = (material == level).astype(jnp.float32)
        fields = fields + tables[level][:, :, :, None, None, None] * chosen
    views = [x_block]
    for dim, axis in ((2, "space"), (3, "basis"), (4, None)):
        views += [shifted(x_block, dim, axis, False), shifted(x_block, dim, axis, True)]
    applied = jnp.zeros_like(x_block)
    for offset, view in enumerate(views):
        for comp in range(comps):
            applied = applied + fields[offset, :, comp][None] * view[:, comp : comp + 1]

    count = lax.axis_size("basis")
    place = lax.axis_index("basis")
    pieces = jnp.moveaxis(basis.reshape(basis.shape[:3] + (count, -1, lanes)), 3, 0)
    rows = jnp.zeros((count,) + pieces.shape[1:], jnp.float32)
    for k in range(count):
        piece = lax.dynamic_index_in_dim(pieces, place ^ k, 0, keepdims=False)
        if k:
            piece = lax.ppermute(piece, "basis", [(i, i ^ k) for i in range(count)])
        rows = lax.dynamic_update_index_in_dim(rows, piece, place ^ k, 0)
    rows = rows.reshape((count * group_cols,) + pieces.shape[2:])

    def total(part):
        for axis in ("basis", "space"):
            mask = 1
            while mask < lax.axis_size(axis):
                pairs = [(i, i ^ mask) for i in range(lax.axis_size(axis))]
                part = part + lax.ppermute(part, axis, pairs)
                mask *= 2
        return part / row_count

    running = jnp.zeros((count * group_cols, block_cols), jnp.float32)
    for repeat in range(2):
        coeffs = total(
            jnp.einsum("kcxyz,ncxyz->kn", rows, applied, precision=exact_precision)
        )
        applied = applied - jnp.einsum("kcxyz,kn->ncxyz", rows, coeffs, precision=exact_precision)
        running = running + coeffs
    gram = total(jnp.einsum("ncxyz,mcxyz->nm", applied, applied, precision=exact_precision))
    lower = jnp.linalg.cholesky(gram)
    inverse = lax.linalg.triangular_solve(
        lower, jnp.eye(block_cols, dtype=jnp.float32), left_side=True, lower=True
    )
    block = jnp.einsum("mcxyz,nm->ncxyz", applied, inverse, precision=exact_precision)
    own = lax.dynamic_slice_in_dim(running, place * group_cols, group_cols, axis=0)
    return tuple(hold(block.reshape(block_cols, -1, lanes), own, lower.T))


def shards(
    x_block, basis, material, k0_blocks, k0_diag, ke_blocks, mass, velocities, shifts, sample
):
    arguments = (
        x_block, basis, material, k0_blocks, k0_diag, ke_blocks, mass, velocities, shifts, sample
    )
    block_cols, comps, extent_x, rows, lanes = x_block.shape
    group_cols = basis.shape[0]
    lines = comps * rows
    row_count = float(comps * extent_x * lax.axis_size("space") * basis.shape[3] * lanes)

    place = lax.axis_index("basis").astype(jnp.int32).reshape(1)
    slab = lax.axis_index("space").astype(jnp.int32).reshape(1)
    count = lax.axis_size("basis")
    x_far = x_block.reshape(block_cols * lines, lanes)
    own, *pieces, x_rows, material = pack(place, basis, x_far, material.reshape(rows, lanes), block_cols)
    got = {}
    for name in ("even", 3, "odd", 2, 1):
        if name == "even":
            got[name] = swap(x_far, "space", 0)
        elif name == "odd":
            got[name] = swap(x_far, "space", 1)
        else:
            piece = lax.ppermute(pieces[name - 1], "basis", [(i, i ^ name) for i in range(count)])
            got[name] = piece.reshape(-1, lanes)
    fields, applied, own = ahead(
        sample, velocities, shifts, k0_blocks, ke_blocks, k0_diag, mass, material, x_rows,
        own.reshape(-1, lanes), comps,
    )
    applied = add_side(slab, fields, applied, got.pop("even"), comps, "even")
    pieces = {k: got.pop(k) for k in reversed(partners(count)[1])}
    applied, *parts = add_edges(place, fields, applied, pieces, comps, group_cols)
    split = {0: own, **dict(zip(pieces, parts))}
    stack, part = sums(place, slab, fields, applied, got.pop("odd"), split, got, comps)
    parts = exchange(exchange_sum(part, "basis"), "space")
    block, coeffs, upper, bad = finish(
        place, parts, stack, row_count, block_cols, group_cols, lines, comps
    )
    block, coeffs, upper = lax.while_loop(
        lambda state: state[0] > 0,
        lambda state: (jnp.zeros_like(state[0]), careful(arguments)),
        (bad[0, 0], (block, coeffs, upper)),
    )[1]
    return block.reshape(x_block.shape), coeffs, upper


def solution(mesh):
    in_specs = (
        P(None, None, "space", "basis", None),
        P("basis", None, "space", None, None),
        P("space", "basis", None),
        P(),
        P(),
        P(),
        P(),
        P(),
        P(),
        P(),
    )
    out_specs = (P(None, None, "space", "basis", None), P("basis", None), P())
    return jax.shard_map(shards, mesh=mesh, in_specs=in_specs, out_specs=out_specs, check_vma=False)
```

```python
import functools

import jax
import jax.numpy as jnp
from jax import lax
from jax.experimental import pallas as pl
from jax.experimental.pallas import tpu as pltpu
from jax.sharding import PartitionSpec as P

exact_precision = lax.Precision.HIGHEST
VMEM = pl.BlockSpec(memory_space=pltpu.VMEM)
SMEM = pl.BlockSpec(memory_space=pltpu.SMEM)
HBM = pl.BlockSpec(memory_space=pltpu.HBM)
LOSS = 256.0
EARLY = pl.CostEstimate(flops=10**9, bytes_accessed=10**6, transcendentals=0)
NEXT = pl.CostEstimate(flops=10**6, bytes_accessed=10**6, transcendentals=0)
SCRATCH = pltpu.CompilerParams(vmem_limit_bytes=8 * 2**20)


def f32(*shape):
    return jax.ShapeDtypeStruct(shape, jnp.float32)


def near(*shape, dtype=jnp.float32):
    return pltpu.VMEM(shape, dtype)


def kept(*arrays):
    return [pltpu.with_memory_space_constraint(array, pltpu.VMEM) for array in arrays]


def far(*arrays):
    return [pltpu.with_memory_space_constraint(array, pltpu.HBM) for array in arrays]


def swap(values, axis, first):
    pairs = [(i, i + 1) for i in range(first, lax.axis_size(axis) - 1, 2)]
    return lax.ppermute(values, axis, pairs + [(j, i) for i, j in pairs])


def partners(count):
    return range(1, count), [k for k in range(1, count) if k & (k + 1) == 0]


def pack_kernel(comps, place_ref, basis_ref, x_ref, material_ref, *refs):
    *piece_refs, x_out_ref, material_out_ref, sems = refs
    count = len(piece_refs)
    tiles, _, rows, lanes = basis_ref.shape
    block_cols = x_ref.shape[0] // (comps * rows)
    place = place_ref[0]
    x_copy = pltpu.make_async_copy(x_ref, x_out_ref, sems.at[count])
    x_copy.start()
    copies = [pltpu.make_async_copy(material_ref, material_out_ref, sems.at[count + 1])]
    for k in reversed(range(count)):
        copies.append(
            pltpu.make_async_copy(
                basis_ref.at[:, place ^ k], piece_refs[k].at[pl.ds(0, tiles)], sems.at[k]
            )
        )
    for copy in copies:
        copy.start()
    x_copy.wait()
    for comp in range(comps):
        first, last = (
            x_out_ref[pl.ds(comp * rows + row, block_cols, stride=comps * rows), :]
            for row in (0, rows - 1)
        )
        for k in partners(count)[1]:
            edge = jnp.where((place ^ k) > place, last, first)
            for part in range(block_cols // rows):
                piece_refs[k][tiles + comp * (block_cols // rows) + part] = edge[
                    part * rows : (part + 1) * rows
                ]
    for copy in copies:
        copy.wait()


def pack(place, basis, x_rows, material, block_cols):
    group_cols, comps, _, full_y, lanes = basis.shape
    count = lax.axis_size("basis")
    rows = full_y // count
    tiles = group_cols * comps
    edge_tiles = block_cols * comps // rows
    pieces = [
        near(tiles + (edge_tiles if k in partners(count)[1] else 0), rows, lanes)
        for k in range(count)
    ]
    return pl.pallas_call(
        functools.partial(pack_kernel, comps),
        out_shape=(*pieces, near(*x_rows.shape), near(*material.shape, dtype=jnp.int32)),
        in_specs=[SMEM, HBM, HBM, HBM],
        out_specs=(VMEM,) * (count + 2),
        scratch_shapes=[pltpu.SemaphoreType.DMA((count + 2,))],
        compiler_params=SCRATCH,
        name="pack",
    )(place, *far(basis.reshape(tiles, count, rows, lanes), x_rows, material))


def three_parts(values):
    high = values.astype(jnp.bfloat16)
    rest = values - high.astype(jnp.float32)
    middle = rest.astype(jnp.bfloat16)
    low = (rest - middle.astype(jnp.float32)).astype(jnp.bfloat16)
    return high, middle, low


def line_of(ref, comp, row, comps, rows, block_cols):
    return ref[pl.ds(comp * rows + row, block_cols, stride=comps * rows), :]


def ahead_kernel(
    sample_ref, *refs
):
    far_refs, refs = refs[:6], refs[6:]
    material_ref, x_ref, own_ref, fields_ref, applied_ref, stack_ref, *near_refs, sems = refs
    velocities_ref, shifts_ref, k0_ref, ke_ref, diag_ref, mass_ref = near_refs
    copies = [
        pltpu.make_async_copy(source, target, sems.at[index])
        for index, (source, target) in enumerate(zip(far_refs, near_refs))
    ]
    for copy in copies:
        copy.start()
    group_cols = stack_ref.shape[0] // 3
    split_lines(
        own_ref, stack_ref, applied_ref.shape[0], group_cols, [i * group_cols for i in range(3)]
    )
    for copy in copies:
        copy.wait()
    comps, _, levels, offsets = k0_ref.shape
    rows, lanes = material_ref.shape
    lines = comps * rows
    block_cols = x_ref.shape[0] // lines
    velocity = velocities_ref[sample_ref[0]]
    sigma = shifts_ref[sample_ref[0]]
    entry_rows = fields_ref.shape[1]
    stride = entry_rows // (comps * comps)
    gap = jnp.zeros((levels, stride - offsets), jnp.float32)
    wide = []
    for out in range(comps):
        for comp in range(comps):
            wide += [k0_ref[out, comp] - velocity * velocity * ke_ref[out, comp], gap]
    wide.append(jnp.zeros((levels, lanes - entry_rows), jnp.float32))
    table = jnp.concatenate(wide, axis=1).T[:entry_rows]
    entry = lax.broadcasted_iota(jnp.int32, table.shape, 0)
    for comp in range(comps):
        centre = diag_ref[comp : comp + 1, :] - sigma * mass_ref[comp : comp + 1, :]
        table = table + jnp.where(entry == comp * (comps + 1) * stride, centre, 0.0)

    lane = lax.broadcasted_iota(jnp.int32, (block_cols, lanes), 1)
    level = lax.broadcasted_iota(jnp.int32, (levels, lanes), 0)
    for row in range(rows):
        chosen = jnp.broadcast_to(material_ref[row : row + 1, :], (levels, lanes)) == level
        fields = jnp.dot(
            table, chosen.astype(jnp.float32),
            precision=exact_precision, preferred_element_type=jnp.float32,
        )
        fields_ref[row] = fields
        sums = [None] * comps
        for comp in range(comps):
            centre = line_of(x_ref, comp, row, comps, rows, block_cols)
            views = {
                0: centre,
                5: jnp.where(lane == 0, 0.0, pltpu.roll(centre, 1, 1)),
                6: jnp.where(lane == lanes - 1, 0.0, pltpu.roll(centre, lanes - 1, 1)),
            }
            if row > 0:
                views[3] = line_of(x_ref, comp, row - 1, comps, rows, block_cols)
            if row < rows - 1:
                views[4] = line_of(x_ref, comp, row + 1, comps, rows, block_cols)
            for offset, view in views.items():
                for out in range(comps):
                    place = (out * comps + comp) * stride + offset
                    term = fields[place : place + 1, :] * view
                    sums[out] = term if sums[out] is None else sums[out] + term
        for out in range(comps):
            applied_ref[out * rows + row] = sums[out]


def ahead(sample, velocities, shifts, k0, ke, diag, mass, material, x_rows, own, comps):
    rows, lanes = material.shape
    lines = comps * rows
    stride = -(-k0.shape[1] // 8) * 8
    k0, ke = (jnp.transpose(blocks, (2, 3, 0, 1)) for blocks in (k0, ke))
    tables = far(velocities, shifts, k0, ke, diag.T, mass.T)
    return pl.pallas_call(
        ahead_kernel,
        out_shape=(
            near(rows, comps * comps * stride, lanes),
            near(lines, x_rows.shape[0] // lines, lanes),
            near(3 * own.shape[0] // lines, lines * lanes, dtype=jnp.bfloat16),
        ),
        in_specs=[SMEM] + [HBM] * 6 + [VMEM] * 3,
        out_specs=(VMEM,) * 3,
        scratch_shapes=[
            (pltpu.SMEM if array.ndim == 1 else pltpu.VMEM)(array.shape, jnp.float32)
            for array in tables
        ] + [pltpu.SemaphoreType.DMA((len(tables),))],
        compiler_params=SCRATCH,
        name="ahead",
    )(sample, *tables, *kept(material, x_rows, own))


def side_terms(field_row, swapped, side, out, comp, comps):
    stride = field_row.shape[0] // (comps * comps)
    begin = (out * comps + comp) * stride
    below, above = field_row[begin + 1 : begin + 2], field_row[begin + 2 : begin + 3]
    other = (below, above) if side == "even" else (above, below)
    return jnp.where(swapped, *other)


def side_kernel(comps, side, slab_ref, fields_ref, applied_ref, halo_ref, out_ref):
    lines, block_cols, _ = applied_ref.shape
    rows = lines // comps
    swapped = slab_ref[0] % 2 == 1
    for row in range(rows):
        field_row = fields_ref[row]
        views = [line_of(halo_ref, comp, row, comps, rows, block_cols) for comp in range(comps)]
        for out in range(comps):
            total = applied_ref[out * rows + row]
            for comp, view in enumerate(views):
                total = total + side_terms(field_row, swapped, side, out, comp, comps) * view
            out_ref[out * rows + row] = total


def add_side(slab, fields, applied, halo, comps, side):
    return pl.pallas_call(
        functools.partial(side_kernel, comps, side),
        out_shape=near(*applied.shape),
        in_specs=[SMEM] + [VMEM] * 3,
        out_specs=VMEM,
        compiler_params=SCRATCH,
        cost_estimate=EARLY,
        name="side",
    )(slab, *kept(fields, applied, halo))


def split_lines(piece_ref, stack_ref, lines, group_cols, begins):
    lanes = piece_ref.shape[1]
    for line in range(lines):
        values = piece_ref[pl.ds(line, group_cols, stride=lines), :]
        for begin, part in zip(begins, three_parts(values)):
            stack_ref[pl.ds(begin, group_cols), pl.ds(line * lanes, lanes)] = part


def edges_kernel(comps, ks, group_cols, place_ref, fields_ref, applied_ref, *refs):
    piece_refs, out_ref, parts_refs = refs[: len(ks)], refs[len(ks)], refs[len(ks) + 1 :]
    lines, block_cols, lanes = applied_ref.shape
    rows = lines // comps
    stride = fields_ref.shape[1] // (comps * comps)
    place = place_ref[0]

    def edge(comp, step):
        result = jnp.zeros((block_cols, lanes), jnp.float32)
        for k, ref in zip(ks, piece_refs):
            begin = ref.shape[0] - (comps - comp) * block_cols
            here = (place ^ k) == place + step
            result = jnp.where(here, ref[pl.ds(begin, block_cols), :], result)
        return result

    out_ref[...] = applied_ref[...]
    for row, offset, step in ((0, 3, -1), (rows - 1, 4, 1)):
        field_row = fields_ref[row]
        views = [edge(comp, step) for comp in range(comps)]
        for out in range(comps):
            total = out_ref[out * rows + row]
            for comp, view in enumerate(views):
                entry = (out * comps + comp) * stride + offset
                total = total + field_row[entry : entry + 1] * view
            out_ref[out * rows + row] = total
    for piece_ref, parts_ref in zip(piece_refs, parts_refs):
        split_lines(piece_ref, parts_ref, lines, group_cols, [i * group_cols for i in range(3)])


def add_edges(place, fields, applied, pieces, comps, group_cols):
    lines, _, lanes = applied.shape
    parts = near(3 * group_cols, lines * lanes, dtype=jnp.bfloat16)
    return pl.pallas_call(
        functools.partial(edges_kernel, comps, tuple(pieces), group_cols),
        out_shape=(near(*applied.shape),) + (parts,) * len(pieces),
        in_specs=[SMEM] + [VMEM] * (2 + len(pieces)),
        out_specs=(VMEM,) * (1 + len(pieces)),
        compiler_params=SCRATCH,
        cost_estimate=NEXT,
        name="edges",
    )(place, *kept(fields, applied, *pieces.values()))


def fold(total, basis_cols, block_cols, lanes):
    half = basis_cols // 2
    row = lax.broadcasted_iota(jnp.int32, (half, half), 0)
    column = lax.broadcasted_iota(jnp.int32, (half, half), 1)
    last = total[half:basis_cols, half:basis_cols]
    shared = jnp.where(row >= column, total[:half, :half], last)
    diagonal = jnp.sum(jnp.where(row == column, last, 0.0), axis=1, keepdims=True)
    below = total[basis_cols:]
    first = jnp.concatenate((below[:, :half], below[:, half:basis_cols]), axis=0)
    rest = jnp.zeros((half - block_cols, block_cols), jnp.float32)
    block = jnp.concatenate((below[:, basis_cols:], rest), axis=0)
    pad = jnp.zeros((half, lanes - 3 * half - block_cols - 1), jnp.float32)
    return jnp.concatenate(
        (shared, total[:half, half:basis_cols], first, block, diagonal, pad), axis=1
    )


def unfold(folded, block_cols):
    half = folded.shape[0]
    row = lax.broadcasted_iota(jnp.int32, (half, half), 0)
    column = lax.broadcasted_iota(jnp.int32, (half, half), 1)
    shared, across = folded[:, :half], folded[:, half : 2 * half]
    turned = shared.T
    start = jnp.where(row >= column, shared, turned)
    end = jnp.where(row < column, shared, turned)
    diagonal = folded[:, 3 * half + block_cols : 3 * half + block_cols + 1]
    end = jnp.where(row == column, diagonal, end)
    gram = jnp.concatenate(
        (jnp.concatenate((start, across), axis=1), jnp.concatenate((across.T, end), axis=1)), axis=0
    )
    first = folded[:, 2 * half : 3 * half]
    first = jnp.concatenate((first[:block_cols], first[block_cols : 2 * block_cols]), axis=1)
    return gram, first, folded[:block_cols, 3 * half : 3 * half + block_cols]


def sums_kernel(
    comps, split, raw, place_ref, slab_ref, fields_ref, applied_ref, *refs
):
    *refs, halo_ref, stack_ref, sums_ref = refs
    lines, block_cols, lanes = applied_ref.shape
    rows = lines // comps
    group_cols = refs[0].shape[0] // 3
    basis_cols = (len(split) + len(raw)) * group_cols
    joined = basis_cols + block_cols
    place = place_ref[0]
    swapped = slab_ref[0] % 2 == 1
    for k, ref in zip(split + raw, refs):
        begin = pl.multiple_of((place ^ k) * group_cols, group_cols)
        begins = [index * joined + begin for index in range(3)]
        if k in split:
            for index in range(3):
                stack_ref[pl.ds(begins[index], group_cols), :] = ref[
                    pl.ds(index * group_cols, group_cols), :
                ]
        else:
            split_lines(ref, stack_ref, lines, group_cols, begins)
    for row in range(rows):
        field_row = fields_ref[row]
        views = [line_of(halo_ref, comp, row, comps, rows, block_cols) for comp in range(comps)]
        for out in range(comps):
            line = out * rows + row
            total = applied_ref[line]
            for comp, view in enumerate(views):
                total = total + side_terms(field_row, swapped, "odd", out, comp, comps) * view
            for index, part in enumerate(three_parts(total)):
                there = pl.ds(index * joined + basis_cols, block_cols)
                stack_ref[there, pl.ds(line * lanes, lanes)] = part

    stack = stack_ref[...]
    products = lax.dot_general(
        stack, stack, (((1,), (1,)), ((), ())), preferred_element_type=jnp.float32
    )
    wide = products[:joined] + products[joined : 2 * joined] + products[2 * joined :]
    total = wide[:, :joined] + wide[:, joined : 2 * joined] + wide[:, 2 * joined :]
    sums_ref[...] = fold(total, basis_cols, block_cols, sums_ref.shape[1])


def sums(place, slab, fields, applied, halo, split, raw, comps):
    lines, block_cols, lanes = applied.shape
    basis_cols = (len(split) + len(raw)) * (split[0].shape[0] // 3)
    joined = basis_cols + block_cols
    return pl.pallas_call(
        functools.partial(sums_kernel, comps, tuple(split), tuple(raw)),
        out_shape=(
            near(3 * joined, lines * lanes, dtype=jnp.bfloat16),
            near(basis_cols // 2, 2 * basis_cols),
        ),
        in_specs=[SMEM] * 2 + [VMEM] * (3 + len(split) + len(raw)),
        out_specs=(VMEM, VMEM),
        compiler_params=SCRATCH,
        name="sums",
    )(place, slab, *kept(fields, applied, *split.values(), *raw.values(), halo))


def exchange_all(part):
    sizes = [lax.axis_size(axis) for axis in ("space", "basis")]
    part = part + lax.ppermute(part, "basis", [(i, i ^ 1) for i in range(sizes[1])])
    mask = 2
    while mask < sizes[1]:
        part = part + lax.ppermute(part, "basis", [(i, i ^ mask) for i in range(1, sizes[1], 2)])
        mask *= 2
    index = [[i * sizes[1] + j for j in range(sizes[1])] for i in range(sizes[0])]
    groups = [[row[j] for row in index] for j in range(1, sizes[1], 2)]
    others = [row[j] for row in index for j in range(0, sizes[1], 2)]
    groups += [others[i : i + sizes[0]] for i in range(0, len(others), sizes[0])]
    copies = jnp.broadcast_to(part[None], (sizes[0],) + part.shape)
    parts = lax.all_to_all(copies, ("space", "basis"), 0, 0, axis_index_groups=groups)
    own = jnp.sum(parts, axis=0)
    return own, lax.ppermute(own, "basis", [(i, i - 1) for i in range(1, sizes[1], 2)])


def finish_kernel(
    row_count, comps, place_ref, own_ref, given_ref, stack_ref, block_ref, coeffs_ref, upper_ref, bad_ref,
    coeffs_scratch, upper_scratch, bad_scratch, block_scratch, sems,
):
    block_cols = upper_ref.shape[0]
    basis_cols = own_ref.shape[1] // 2
    joined = basis_cols + block_cols
    lines, lanes = block_ref.shape[1:]
    total = jnp.where(place_ref[0] % 2 == 0, given_ref[...], own_ref[...]) / row_count
    gram, first, block_gram = unfold(total, block_cols)

    def times(left, right, right_dim=0):
        return lax.dot_general(
            left, right, (((1,), (right_dim,)), ((), ())),
            precision=exact_precision, preferred_element_type=jnp.float32,
        )

    coeffs = first + (first - times(first, gram))
    image = times(coeffs, gram)
    matrix = block_gram - times(
        jnp.concatenate((coeffs, first - image), axis=1), jnp.concatenate((first, coeffs), axis=1), 1
    )
    coeffs_scratch[...] = coeffs.T
    group_cols = coeffs_ref.shape[0]
    start = pl.multiple_of(place_ref[0] * group_cols, group_cols)
    copies = [
        pltpu.make_async_copy(
            coeffs_scratch.at[pl.ds(start, group_cols)], coeffs_ref, sems.at[comps]
        )
    ]
    copies[0].start()

    row = lax.broadcasted_iota(jnp.int32, (block_cols, block_cols), 0)
    column = lax.broadcasted_iota(jnp.int32, (block_cols, block_cols), 1)
    unit = jnp.where(row == column, 1.0, 0.0)
    pad = jnp.zeros((block_cols, 2 * basis_cols - joined - block_cols), jnp.float32)
    work = jnp.concatenate((-coeffs, unit, matrix, pad), axis=1)
    height = lax.broadcasted_iota(jnp.int32, work.shape, 0)
    width = 4
    for begin in range(0, block_cols, width):
        done, new_rows = [], []
        for step in range(begin, begin + width):
            column_here = jnp.broadcast_to(work[:, joined + step : joined + step + 1], work.shape)
            pivot_row = work[step : step + 1]
            for other_column, other_row, inverse in done:
                entry = other_column[step : step + 1]
                pivot_row = pivot_row - entry * other_row
                column_here = column_here - other_column * (entry * inverse)
            pivot = column_here[step : step + 1]
            inverse = 1.0 / pivot
            done.append((column_here, pivot_row * inverse, inverse))
            new_rows.append(pivot_row * lax.rsqrt(pivot))
        rest = work
        for column_here, scaled, _ in done:
            rest = rest - column_here * scaled
        work = jnp.where(height >= begin + width, rest, work)
        for step, new_row in enumerate(new_rows, begin):
            work = jnp.where(height == step, new_row, work)
    upper = jnp.where(row <= column, work[:, joined : joined + block_cols], 0.0)
    upper_scratch[...] = upper
    kept_enough = jnp.where(row == column, upper * upper * LOSS, block_gram) >= block_gram
    kept_enough = jnp.min(jnp.where(kept_enough, 1.0, 0.0), axis=0, keepdims=True)
    kept_enough = jnp.min(kept_enough, axis=1, keepdims=True)
    bad_scratch[...] = jnp.where(kept_enough > 0.0, 0, 1)
    copies.append(pltpu.make_async_copy(bad_scratch, bad_ref, sems.at[comps + 2]))
    copies[-1].start()
    copies.append(pltpu.make_async_copy(upper_scratch, upper_ref, sems.at[comps + 1]))
    copies[-1].start()
    weights = three_parts(work[:, :joined])
    wide = jnp.concatenate(
        [jnp.concatenate((part, part, part), axis=1) for part in weights], axis=0
    )
    rows = lines // comps
    for comp in range(comps):
        there = pl.ds(comp * rows * lanes, rows * lanes)
        result = jnp.dot(wide, stack_ref[:, there], preferred_element_type=jnp.float32)
        result = result[:block_cols] + result[block_cols : 2 * block_cols] + result[2 * block_cols :]
        for index in range(rows):
            block_scratch[pl.ds(comp * rows + index, block_cols, stride=lines), :] = result[
                :, index * lanes : (index + 1) * lanes
            ]
        part = pl.ds(comp * rows, rows)
        copies.append(
            pltpu.make_async_copy(
                block_scratch.reshape(block_cols, lines, lanes).at[:, part, :],
                block_ref.at[:, part, :],
                sems.at[comp],
            )
        )
        copies[-1].start()
    for copy in copies:
        copy.wait()


def finish(place, totals, stack, row_count, block_cols, group_cols, lines, comps):
    lanes = stack.shape[1] // lines
    basis_cols = totals[0].shape[1] // 2
    return pl.pallas_call(
        functools.partial(finish_kernel, row_count, comps),
        out_shape=(
            f32(block_cols, lines, lanes), f32(group_cols, block_cols), f32(block_cols, block_cols),
            jax.ShapeDtypeStruct((1, 1), jnp.int32),
        ),
        in_specs=[SMEM] + [VMEM] * 3,
        out_specs=(HBM,) * 4,
        scratch_shapes=[
            pltpu.VMEM((basis_cols, block_cols), jnp.float32),
            pltpu.VMEM((block_cols, block_cols), jnp.float32),
            pltpu.VMEM((1, 1), jnp.int32),
            pltpu.VMEM((block_cols * lines, lanes), jnp.float32),
            pltpu.SemaphoreType.DMA((comps + 3,)),
        ],
        compiler_params=SCRATCH,
        name="finish",
    )(place, *kept(*totals, stack))


def stencil_tables(k0_blocks, k0_diag, ke_blocks, mass, velocities, shifts, sample):
    velocity = jnp.take(velocities, sample, axis=0)[0]
    sigma_value = jnp.take(shifts, sample, axis=0)[0]
    center = (k0_diag - sigma_value * mass)[:, :, None] * jnp.eye(3, dtype=jnp.float32)
    tables = k0_blocks - velocity * velocity * ke_blocks
    return tables.at[:, 0].add(center)


def shifted(cells, dim, axis, up):
    extent = cells.shape[dim]
    edge = lax.slice_in_dim(cells, 0, 1, axis=dim) if up else (
        lax.slice_in_dim(cells, extent - 1, extent, axis=dim)
    )
    if axis is None:
        edge = jnp.zeros_like(edge)
    else:
        ends = [(i, i + 1) for i in range(lax.axis_size(axis) - 1)]
        edge = lax.ppermute(edge, axis, [(j, i) for i, j in ends] if up else ends)
    if up:
        return jnp.concatenate((lax.slice_in_dim(cells, 1, extent, axis=dim), edge), axis=dim)
    return jnp.concatenate((edge, lax.slice_in_dim(cells, 0, extent - 1, axis=dim)), axis=dim)


def hold_kernel(*refs):
    *refs, sems = refs
    half = len(refs) // 2
    copies = [
        pltpu.make_async_copy(source, target, sems.at[index])
        for index, (source, target) in enumerate(zip(refs[:half], refs[half:]))
    ]
    for copy in copies:
        copy.start()
    for copy in copies:
        copy.wait()


def hold(*arrays):
    return pl.pallas_call(
        hold_kernel,
        out_shape=[jax.ShapeDtypeStruct(array.shape, array.dtype) for array in arrays],
        in_specs=[HBM] * len(arrays),
        out_specs=[HBM] * len(arrays),
        scratch_shapes=[pltpu.SemaphoreType.DMA((len(arrays),))],
        compiler_params=SCRATCH,
        name="hold",
    )(*far(*arrays))


def careful(arguments):
    x_block, basis, material, k0_blocks, k0_diag, ke_blocks, mass, velocities, shifts, sample = arguments
    x_block, basis, material, k0_blocks, k0_diag, ke_blocks, mass, velocities, shifts = hold(
        x_block, basis, material, jnp.transpose(k0_blocks, (2, 3, 0, 1)), k0_diag.T,
        jnp.transpose(ke_blocks, (2, 3, 0, 1)), mass.T, velocities, shifts,
    )
    k0_blocks, ke_blocks = (jnp.transpose(blocks, (2, 3, 0, 1)) for blocks in (k0_blocks, ke_blocks))
    k0_diag, mass = k0_diag.T, mass.T
    tables = stencil_tables(k0_blocks, k0_diag, ke_blocks, mass, velocities, shifts, sample)
    block_cols, comps, extent_x, _, lanes = x_block.shape
    group_cols = basis.shape[0]
    row_count = float(comps * extent_x * lax.axis_size("space") * basis.shape[3] * lanes)
    fields = jnp.zeros((7, comps, comps) + material.shape, jnp.float32)
    for level in range(tables.shape[0]):
        chosen = (material == level).astype(jnp.float32)
        fields = fields + tables[level][:, :, :, None, None, None] * chosen
    views = [x_block]
    for dim, axis in ((2, "space"), (3, "basis"), (4, None)):
        views += [shifted(x_block, dim, axis, False), shifted(x_block, dim, axis, True)]
    applied = jnp.zeros_like(x_block)
    for offset, view in enumerate(views):
        for comp in range(comps):
            applied = applied + fields[offset, :, comp][None] * view[:, comp : comp + 1]

    count = lax.axis_size("basis")
    place = lax.axis_index("basis")
    pieces = jnp.moveaxis(basis.reshape(basis.shape[:3] + (count, -1, lanes)), 3, 0)
    rows = jnp.zeros((count,) + pieces.shape[1:], jnp.float32)
    for k in range(count):
        piece = lax.dynamic_index_in_dim(pieces, place ^ k, 0, keepdims=False)
        if k:
            piece = lax.ppermute(piece, "basis", [(i, i ^ k) for i in range(count)])
        rows = lax.dynamic_update_index_in_dim(rows, piece, place ^ k, 0)
    rows = rows.reshape((count * group_cols,) + pieces.shape[2:])

    def total(part):
        for axis in ("basis", "space"):
            mask = 1
            while mask < lax.axis_size(axis):
                pairs = [(i, i ^ mask) for i in range(lax.axis_size(axis))]
                part = part + lax.ppermute(part, axis, pairs)
                mask *= 2
        return part / row_count

    running = jnp.zeros((count * group_cols, block_cols), jnp.float32)
    for repeat in range(2):
        coeffs = total(
            jnp.einsum("kcxyz,ncxyz->kn", rows, applied, precision=exact_precision)
        )
        applied = applied - jnp.einsum("kcxyz,kn->ncxyz", rows, coeffs, precision=exact_precision)
        running = running + coeffs
    gram = total(jnp.einsum("ncxyz,mcxyz->nm", applied, applied, precision=exact_precision))
    lower = jnp.linalg.cholesky(gram)
    inverse = lax.linalg.triangular_solve(
        lower, jnp.eye(block_cols, dtype=jnp.float32), left_side=True, lower=True
    )
    block = jnp.einsum("mcxyz,nm->ncxyz", applied, inverse, precision=exact_precision)
    own = lax.dynamic_slice_in_dim(running, place * group_cols, group_cols, axis=0)
    return tuple(hold(block.reshape(block_cols, -1, lanes), own, lower.T))


def shards(
    x_block, basis, material, k0_blocks, k0_diag, ke_blocks, mass, velocities, shifts, sample
):
    arguments = (
        x_block, basis, material, k0_blocks, k0_diag, ke_blocks, mass, velocities, shifts, sample
    )
    block_cols, comps, extent_x, rows, lanes = x_block.shape
    group_cols = basis.shape[0]
    lines = comps * rows
    row_count = float(comps * extent_x * lax.axis_size("space") * basis.shape[3] * lanes)

    place = lax.axis_index("basis").astype(jnp.int32).reshape(1)
    slab = lax.axis_index("space").astype(jnp.int32).reshape(1)
    count = lax.axis_size("basis")
    x_far = x_block.reshape(block_cols * lines, lanes)
    own, *pieces, x_rows, material = pack(place, basis, x_far, material.reshape(rows, lanes), block_cols)
    got = {}
    for name in ("even", 3, "odd", 2, 1):
        if name == "even":
            got[name] = swap(x_far, "space", 0)
        elif name == "odd":
            got[name] = swap(x_far, "space", 1)
        else:
            piece = lax.ppermute(pieces[name - 1], "basis", [(i, i ^ name) for i in range(count)])
            got[name] = piece.reshape(-1, lanes)
    fields, applied, own = ahead(
        sample, velocities, shifts, k0_blocks, ke_blocks, k0_diag, mass, material, x_rows,
        own.reshape(-1, lanes), comps,
    )
    applied = add_side(slab, fields, applied, got.pop("even"), comps, "even")
    pieces = {k: got.pop(k) for k in reversed(partners(count)[1])}
    applied, *parts = add_edges(place, fields, applied, pieces, comps, group_cols)
    split = {0: own, **dict(zip(pieces, parts))}
    stack, part = sums(place, slab, fields, applied, got.pop("odd"), split, got, comps)
    totals = exchange_all(part)
    block, coeffs, upper, bad = finish(
        place, totals, stack, row_count, block_cols, group_cols, lines, comps
    )
    block, coeffs, upper = lax.while_loop(
        lambda state: state[0] > 0,
        lambda state: (jnp.zeros_like(state[0]), careful(arguments)),
        (bad[0, 0], (block, coeffs, upper)),
    )[1]
    return block.reshape(x_block.shape), coeffs, upper


def solution(mesh):
    in_specs = (
        P(None, None, "space", "basis", None),
        P("basis", None, "space", None, None),
        P("space", "basis", None),
        P(),
        P(),
        P(),
        P(),
        P(),
        P(),
        P(),
    )
    out_specs = (P(None, None, "space", "basis", None), P("basis", None), P())
    return jax.shard_map(shards, mesh=mesh, in_specs=in_specs, out_specs=out_specs, check_vma=False)
```

```python
import functools

import jax
import jax.numpy as jnp
from jax import lax
from jax.experimental import pallas as pl
from jax.experimental.pallas import tpu as pltpu
from jax.sharding import PartitionSpec as P

exact_precision = lax.Precision.HIGHEST
VMEM = pl.BlockSpec(memory_space=pltpu.VMEM)
SMEM = pl.BlockSpec(memory_space=pltpu.SMEM)
HBM = pl.BlockSpec(memory_space=pltpu.HBM)
LOSS = 256.0
EARLY = pl.CostEstimate(flops=10**9, bytes_accessed=10**6, transcendentals=0)
NEXT = pl.CostEstimate(flops=10**6, bytes_accessed=10**6, transcendentals=0)
SCRATCH = pltpu.CompilerParams(vmem_limit_bytes=8 * 2**20)


def f32(*shape):
    return jax.ShapeDtypeStruct(shape, jnp.float32)


def near(*shape, dtype=jnp.float32):
    return pltpu.VMEM(shape, dtype)


def kept(*arrays):
    return [pltpu.with_memory_space_constraint(array, pltpu.VMEM) for array in arrays]


def far(*arrays):
    return [pltpu.with_memory_space_constraint(array, pltpu.HBM) for array in arrays]


def swap(values, axis, first):
    pairs = [(i, i + 1) for i in range(first, lax.axis_size(axis) - 1, 2)]
    return lax.ppermute(values, axis, pairs + [(j, i) for i, j in pairs])


def partners(count):
    return range(1, count), [k for k in range(1, count) if k & (k + 1) == 0]


def pack_kernel(comps, place_ref, basis_ref, x_ref, material_ref, *refs):
    *piece_refs, x_out_ref, material_out_ref, sems = refs
    count = len(piece_refs)
    tiles, _, rows, lanes = basis_ref.shape
    block_cols = x_ref.shape[0] // (comps * rows)
    place = place_ref[0]
    x_copy = pltpu.make_async_copy(x_ref, x_out_ref, sems.at[count])
    x_copy.start()
    copies = [pltpu.make_async_copy(material_ref, material_out_ref, sems.at[count + 1])]
    for k in reversed(range(count)):
        copies.append(
            pltpu.make_async_copy(
                basis_ref.at[:, place ^ k], piece_refs[k].at[pl.ds(0, tiles)], sems.at[k]
            )
        )
    for copy in copies:
        copy.start()
    x_copy.wait()
    for comp in range(comps):
        first, last = (
            x_out_ref[pl.ds(comp * rows + row, block_cols, stride=comps * rows), :]
            for row in (0, rows - 1)
        )
        for k in partners(count)[1]:
            edge = jnp.where((place ^ k) > place, last, first)
            for part in range(block_cols // rows):
                piece_refs[k][tiles + comp * (block_cols // rows) + part] = edge[
                    part * rows : (part + 1) * rows
                ]
    for copy in copies:
        copy.wait()


def pack(place, basis, x_rows, material, block_cols):
    group_cols, comps, _, full_y, lanes = basis.shape
    count = lax.axis_size("basis")
    rows = full_y // count
    tiles = group_cols * comps
    edge_tiles = block_cols * comps // rows
    pieces = [
        near(tiles + (edge_tiles if k in partners(count)[1] else 0), rows, lanes)
        for k in range(count)
    ]
    return pl.pallas_call(
        functools.partial(pack_kernel, comps),
        out_shape=(*pieces, near(*x_rows.shape), near(*material.shape, dtype=jnp.int32)),
        in_specs=[SMEM, HBM, HBM, HBM],
        out_specs=(VMEM,) * (count + 2),
        scratch_shapes=[pltpu.SemaphoreType.DMA((count + 2,))],
        compiler_params=SCRATCH,
        name="pack",
    )(place, *far(basis.reshape(tiles, count, rows, lanes), x_rows, material))


def three_parts(values):
    high = values.astype(jnp.bfloat16)
    rest = values - high.astype(jnp.float32)
    middle = rest.astype(jnp.bfloat16)
    low = (rest - middle.astype(jnp.float32)).astype(jnp.bfloat16)
    return high, middle, low


def line_of(ref, comp, row, comps, rows, block_cols):
    return ref[pl.ds(comp * rows + row, block_cols, stride=comps * rows), :]


def ahead_kernel(
    sample_ref, *refs
):
    far_refs, refs = refs[:6], refs[6:]
    material_ref, x_ref, own_ref, fields_ref, applied_ref, stack_ref, *near_refs, sems = refs
    velocities_ref, shifts_ref, k0_ref, ke_ref, diag_ref, mass_ref = near_refs
    copies = [
        pltpu.make_async_copy(source, target, sems.at[index])
        for index, (source, target) in enumerate(zip(far_refs, near_refs))
    ]
    for copy in copies:
        copy.start()
    group_cols = stack_ref.shape[0] // 3
    split_lines(
        own_ref, stack_ref, applied_ref.shape[0], group_cols, [i * group_cols for i in range(3)]
    )
    for copy in copies:
        copy.wait()
    comps, _, levels, offsets = k0_ref.shape
    rows, lanes = material_ref.shape
    lines = comps * rows
    block_cols = x_ref.shape[0] // lines
    velocity = velocities_ref[sample_ref[0]]
    sigma = shifts_ref[sample_ref[0]]
    entry_rows = fields_ref.shape[1]
    stride = entry_rows // (comps * comps)
    gap = jnp.zeros((levels, stride - offsets), jnp.float32)
    wide = []
    for out in range(comps):
        for comp in range(comps):
            wide += [k0_ref[out, comp] - velocity * velocity * ke_ref[out, comp], gap]
    wide.append(jnp.zeros((levels, lanes - entry_rows), jnp.float32))
    table = jnp.concatenate(wide, axis=1).T[:entry_rows]
    entry = lax.broadcasted_iota(jnp.int32, table.shape, 0)
    for comp in range(comps):
        centre = diag_ref[comp : comp + 1, :] - sigma * mass_ref[comp : comp + 1, :]
        table = table + jnp.where(entry == comp * (comps + 1) * stride, centre, 0.0)

    lane = lax.broadcasted_iota(jnp.int32, (block_cols, lanes), 1)
    level = lax.broadcasted_iota(jnp.int32, (levels, lanes), 0)
    for row in range(rows):
        chosen = jnp.broadcast_to(material_ref[row : row + 1, :], (levels, lanes)) == level
        fields = jnp.dot(
            table, chosen.astype(jnp.float32),
            precision=exact_precision, preferred_element_type=jnp.float32,
        )
        fields_ref[row] = fields
        sums = [None] * comps
        for comp in range(comps):
            centre = line_of(x_ref, comp, row, comps, rows, block_cols)
            views = {
                0: centre,
                5: jnp.where(lane == 0, 0.0, pltpu.roll(centre, 1, 1)),
                6: jnp.where(lane == lanes - 1, 0.0, pltpu.roll(centre, lanes - 1, 1)),
            }
            if row > 0:
                views[3] = line_of(x_ref, comp, row - 1, comps, rows, block_cols)
            if row < rows - 1:
                views[4] = line_of(x_ref, comp, row + 1, comps, rows, block_cols)
            for offset, view in views.items():
                for out in range(comps):
                    place = (out * comps + comp) * stride + offset
                    term = fields[place : place + 1, :] * view
                    sums[out] = term if sums[out] is None else sums[out] + term
        for out in range(comps):
            applied_ref[out * rows + row] = sums[out]


def ahead(sample, velocities, shifts, k0, ke, diag, mass, material, x_rows, own, comps):
    rows, lanes = material.shape
    lines = comps * rows
    stride = -(-k0.shape[1] // 8) * 8
    k0, ke = (jnp.transpose(blocks, (2, 3, 0, 1)) for blocks in (k0, ke))
    tables = far(velocities, shifts, k0, ke, diag.T, mass.T)
    return pl.pallas_call(
        ahead_kernel,
        out_shape=(
            near(rows, comps * comps * stride, lanes),
            near(lines, x_rows.shape[0] // lines, lanes),
            near(3 * own.shape[0] // lines, lines * lanes, dtype=jnp.bfloat16),
        ),
        in_specs=[SMEM] + [HBM] * 6 + [VMEM] * 3,
        out_specs=(VMEM,) * 3,
        scratch_shapes=[
            (pltpu.SMEM if array.ndim == 1 else pltpu.VMEM)(array.shape, jnp.float32)
            for array in tables
        ] + [pltpu.SemaphoreType.DMA((len(tables),))],
        compiler_params=SCRATCH,
        name="ahead",
    )(sample, *tables, *kept(material, x_rows, own))


def side_terms(field_row, swapped, side, out, comp, comps):
    stride = field_row.shape[0] // (comps * comps)
    begin = (out * comps + comp) * stride
    below, above = field_row[begin + 1 : begin + 2], field_row[begin + 2 : begin + 3]
    other = (below, above) if side == "even" else (above, below)
    return jnp.where(swapped, *other)


def side_kernel(comps, side, slab_ref, fields_ref, applied_ref, halo_ref, out_ref):
    lines, block_cols, _ = applied_ref.shape
    rows = lines // comps
    swapped = slab_ref[0] % 2 == 1
    for row in range(rows):
        field_row = fields_ref[row]
        views = [line_of(halo_ref, comp, row, comps, rows, block_cols) for comp in range(comps)]
        for out in range(comps):
            total = applied_ref[out * rows + row]
            for comp, view in enumerate(views):
                total = total + side_terms(field_row, swapped, side, out, comp, comps) * view
            out_ref[out * rows + row] = total


def add_side(slab, fields, applied, halo, comps, side):
    return pl.pallas_call(
        functools.partial(side_kernel, comps, side),
        out_shape=near(*applied.shape),
        in_specs=[SMEM] + [VMEM] * 3,
        out_specs=VMEM,
        compiler_params=SCRATCH,
        cost_estimate=EARLY,
        name="side",
    )(slab, *kept(fields, applied, halo))


def split_lines(piece_ref, stack_ref, lines, group_cols, begins):
    lanes = piece_ref.shape[1]
    for line in range(lines):
        values = piece_ref[pl.ds(line, group_cols, stride=lines), :]
        for begin, part in zip(begins, three_parts(values)):
            stack_ref[pl.ds(begin, group_cols), pl.ds(line * lanes, lanes)] = part


def edges_kernel(comps, ks, group_cols, place_ref, fields_ref, applied_ref, *refs):
    piece_refs, out_ref, parts_refs = refs[: len(ks)], refs[len(ks)], refs[len(ks) + 1 :]
    lines, block_cols, lanes = applied_ref.shape
    rows = lines // comps
    stride = fields_ref.shape[1] // (comps * comps)
    place = place_ref[0]

    def edge(comp, step):
        result = jnp.zeros((block_cols, lanes), jnp.float32)
        for k, ref in zip(ks, piece_refs):
            begin = ref.shape[0] - (comps - comp) * block_cols
            here = (place ^ k) == place + step
            result = jnp.where(here, ref[pl.ds(begin, block_cols), :], result)
        return result

    out_ref[...] = applied_ref[...]
    for row, offset, step in ((0, 3, -1), (rows - 1, 4, 1)):
        field_row = fields_ref[row]
        views = [edge(comp, step) for comp in range(comps)]
        for out in range(comps):
            total = out_ref[out * rows + row]
            for comp, view in enumerate(views):
                entry = (out * comps + comp) * stride + offset
                total = total + field_row[entry : entry + 1] * view
            out_ref[out * rows + row] = total
    for piece_ref, parts_ref in zip(piece_refs, parts_refs):
        split_lines(piece_ref, parts_ref, lines, group_cols, [i * group_cols for i in range(3)])


def add_edges(place, fields, applied, pieces, comps, group_cols):
    lines, _, lanes = applied.shape
    parts = near(3 * group_cols, lines * lanes, dtype=jnp.bfloat16)
    return pl.pallas_call(
        functools.partial(edges_kernel, comps, tuple(pieces), group_cols),
        out_shape=(near(*applied.shape),) + (parts,) * len(pieces),
        in_specs=[SMEM] + [VMEM] * (2 + len(pieces)),
        out_specs=(VMEM,) * (1 + len(pieces)),
        compiler_params=SCRATCH,
        cost_estimate=NEXT,
        name="edges",
    )(place, *kept(fields, applied, *pieces.values()))


def fold(total, basis_cols, block_cols, lanes):
    half = basis_cols // 2
    row = lax.broadcasted_iota(jnp.int32, (half, half), 0)
    column = lax.broadcasted_iota(jnp.int32, (half, half), 1)
    last = total[half:basis_cols, half:basis_cols]
    shared = jnp.where(row >= column, total[:half, :half], last)
    diagonal = jnp.sum(jnp.where(row == column, last, 0.0), axis=1, keepdims=True)
    below = total[basis_cols:]
    first = jnp.concatenate((below[:, :half], below[:, half:basis_cols]), axis=0)
    rest = jnp.zeros((half - block_cols, block_cols), jnp.float32)
    block = jnp.concatenate((below[:, basis_cols:], rest), axis=0)
    pad = jnp.zeros((half, lanes - 3 * half - block_cols - 1), jnp.float32)
    return jnp.concatenate(
        (shared, total[:half, half:basis_cols], first, block, diagonal, pad), axis=1
    )


def unfold(folded, block_cols):
    half = folded.shape[0]
    row = lax.broadcasted_iota(jnp.int32, (half, half), 0)
    column = lax.broadcasted_iota(jnp.int32, (half, half), 1)
    shared, across = folded[:, :half], folded[:, half : 2 * half]
    turned = shared.T
    start = jnp.where(row >= column, shared, turned)
    end = jnp.where(row < column, shared, turned)
    diagonal = folded[:, 3 * half + block_cols : 3 * half + block_cols + 1]
    end = jnp.where(row == column, diagonal, end)
    gram = jnp.concatenate(
        (jnp.concatenate((start, across), axis=1), jnp.concatenate((across.T, end), axis=1)), axis=0
    )
    first = folded[:, 2 * half : 3 * half]
    first = jnp.concatenate((first[:block_cols], first[block_cols : 2 * block_cols]), axis=1)
    return gram, first, folded[:block_cols, 3 * half : 3 * half + block_cols]


def sums_kernel(
    comps, split, raw, place_ref, slab_ref, fields_ref, applied_ref, *refs
):
    *refs, halo_ref, stack_ref, keep_ref, give_ref = refs
    lines, block_cols, lanes = applied_ref.shape
    rows = lines // comps
    group_cols = refs[0].shape[0] // 3
    basis_cols = (len(split) + len(raw)) * group_cols
    joined = basis_cols + block_cols
    place = place_ref[0]
    swapped = slab_ref[0] % 2 == 1
    for k, ref in zip(split + raw, refs):
        begin = pl.multiple_of((place ^ k) * group_cols, group_cols)
        begins = [index * joined + begin for index in range(3)]
        if k in split:
            for index in range(3):
                stack_ref[pl.ds(begins[index], group_cols), :] = ref[
                    pl.ds(index * group_cols, group_cols), :
                ]
        else:
            split_lines(ref, stack_ref, lines, group_cols, begins)
    for row in range(rows):
        field_row = fields_ref[row]
        views = [line_of(halo_ref, comp, row, comps, rows, block_cols) for comp in range(comps)]
        for out in range(comps):
            line = out * rows + row
            total = applied_ref[line]
            for comp, view in enumerate(views):
                total = total + side_terms(field_row, swapped, "odd", out, comp, comps) * view
            for index, part in enumerate(three_parts(total)):
                there = pl.ds(index * joined + basis_cols, block_cols)
                stack_ref[there, pl.ds(line * lanes, lanes)] = part

    stack = stack_ref[...]
    products = lax.dot_general(
        stack, stack, (((1,), (1,)), ((), ())), preferred_element_type=jnp.float32
    )
    wide = products[:joined] + products[joined : 2 * joined] + products[2 * joined :]
    total = wide[:, :joined] + wide[:, joined : 2 * joined] + wide[:, 2 * joined :]
    folded = fold(total, basis_cols, block_cols, keep_ref.shape[1])
    half = keep_ref.shape[0]
    odd = place % 2 == 1
    keep_ref[...] = jnp.where(odd, folded[half:], folded[:half])
    give_ref[...] = jnp.where(odd, folded[:half], folded[half:])


def sums(place, slab, fields, applied, halo, split, raw, comps):
    lines, block_cols, lanes = applied.shape
    basis_cols = (len(split) + len(raw)) * (split[0].shape[0] // 3)
    joined = basis_cols + block_cols
    return pl.pallas_call(
        functools.partial(sums_kernel, comps, tuple(split), tuple(raw)),
        out_shape=(
            near(3 * joined, lines * lanes, dtype=jnp.bfloat16),
            near(basis_cols // 4, 2 * basis_cols),
            near(basis_cols // 4, 2 * basis_cols),
        ),
        in_specs=[SMEM] * 2 + [VMEM] * (3 + len(split) + len(raw)),
        out_specs=(VMEM,) * 3,
        compiler_params=SCRATCH,
        name="sums",
    )(place, slab, *kept(fields, applied, *split.values(), *raw.values(), halo))


def exchange_all(keep, give):
    sizes = [lax.axis_size(axis) for axis in ("space", "basis")]
    pairs = [(i, i ^ 1) for i in range(sizes[1])]
    part = keep + lax.ppermute(give, "basis", pairs)
    groups = [
        [i * sizes[1] + j for i in range(sizes[0]) for j in range(first, sizes[1], 2)]
        for first in range(2)
    ]
    copies = jnp.broadcast_to(part[None], (len(groups[0]),) + part.shape)
    parts = lax.all_to_all(copies, ("space", "basis"), 0, 0, axis_index_groups=groups)
    own = jnp.sum(parts, axis=0)
    return own, lax.ppermute(own, "basis", pairs)


def finish_kernel(
    row_count, comps, place_ref, own_ref, given_ref, stack_ref, block_ref, coeffs_ref, upper_ref, bad_ref,
    coeffs_scratch, upper_scratch, bad_scratch, block_scratch, sems,
):
    block_cols = upper_ref.shape[0]
    basis_cols = own_ref.shape[1] // 2
    joined = basis_cols + block_cols
    lines, lanes = block_ref.shape[1:]
    odd = place_ref[0] % 2 == 1
    own, given = own_ref[...], given_ref[...]
    total = jnp.concatenate((jnp.where(odd, given, own), jnp.where(odd, own, given)), axis=0)
    total = total / row_count
    gram, first, block_gram = unfold(total, block_cols)

    def times(left, right, right_dim=0):
        return lax.dot_general(
            left, right, (((1,), (right_dim,)), ((), ())),
            precision=exact_precision, preferred_element_type=jnp.float32,
        )

    coeffs = first + (first - times(first, gram))
    image = times(coeffs, gram)
    matrix = block_gram - times(
        jnp.concatenate((coeffs, first - image), axis=1), jnp.concatenate((first, coeffs), axis=1), 1
    )
    coeffs_scratch[...] = coeffs.T
    group_cols = coeffs_ref.shape[0]
    start = pl.multiple_of(place_ref[0] * group_cols, group_cols)
    copies = [
        pltpu.make_async_copy(
            coeffs_scratch.at[pl.ds(start, group_cols)], coeffs_ref, sems.at[comps]
        )
    ]
    copies[0].start()

    row = lax.broadcasted_iota(jnp.int32, (block_cols, block_cols), 0)
    column = lax.broadcasted_iota(jnp.int32, (block_cols, block_cols), 1)
    unit = jnp.where(row == column, 1.0, 0.0)
    pad = jnp.zeros((block_cols, 2 * basis_cols - joined - block_cols), jnp.float32)
    work = jnp.concatenate((-coeffs, unit, matrix, pad), axis=1)
    height = lax.broadcasted_iota(jnp.int32, work.shape, 0)
    width = 4
    for begin in range(0, block_cols, width):
        done, new_rows = [], []
        for step in range(begin, begin + width):
            column_here = jnp.broadcast_to(work[:, joined + step : joined + step + 1], work.shape)
            pivot_row = work[step : step + 1]
            for other_column, other_row, inverse in done:
                entry = other_column[step : step + 1]
                pivot_row = pivot_row - entry * other_row
                column_here = column_here - other_column * (entry * inverse)
            pivot = column_here[step : step + 1]
            inverse = 1.0 / pivot
            done.append((column_here, pivot_row * inverse, inverse))
            new_rows.append(pivot_row * lax.rsqrt(pivot))
        rest = work
        for column_here, scaled, _ in done:
            rest = rest - column_here * scaled
        work = jnp.where(height >= begin + width, rest, work)
        for step, new_row in enumerate(new_rows, begin):
            work = jnp.where(height == step, new_row, work)
    upper = jnp.where(row <= column, work[:, joined : joined + block_cols], 0.0)
    upper_scratch[...] = upper
    kept_enough = jnp.where(row == column, upper * upper * LOSS, block_gram) >= block_gram
    kept_enough = jnp.min(jnp.where(kept_enough, 1.0, 0.0), axis=0, keepdims=True)
    kept_enough = jnp.min(kept_enough, axis=1, keepdims=True)
    bad_scratch[...] = jnp.where(kept_enough > 0.0, 0, 1)
    copies.append(pltpu.make_async_copy(bad_scratch, bad_ref, sems.at[comps + 2]))
    copies[-1].start()
    copies.append(pltpu.make_async_copy(upper_scratch, upper_ref, sems.at[comps + 1]))
    copies[-1].start()
    weights = three_parts(work[:, :joined])
    wide = jnp.concatenate(
        [jnp.concatenate((part, part, part), axis=1) for part in weights], axis=0
    )
    rows = lines // comps
    for comp in range(comps):
        there = pl.ds(comp * rows * lanes, rows * lanes)
        result = jnp.dot(wide, stack_ref[:, there], preferred_element_type=jnp.float32)
        result = result[:block_cols] + result[block_cols : 2 * block_cols] + result[2 * block_cols :]
        for index in range(rows):
            block_scratch[pl.ds(comp * rows + index, block_cols, stride=lines), :] = result[
                :, index * lanes : (index + 1) * lanes
            ]
        part = pl.ds(comp * rows, rows)
        copies.append(
            pltpu.make_async_copy(
                block_scratch.reshape(block_cols, lines, lanes).at[:, part, :],
                block_ref.at[:, part, :],
                sems.at[comp],
            )
        )
        copies[-1].start()
    for copy in copies:
        copy.wait()


def finish(place, halves, stack, row_count, block_cols, group_cols, lines, comps):
    lanes = stack.shape[1] // lines
    basis_cols = halves[0].shape[1] // 2
    return pl.pallas_call(
        functools.partial(finish_kernel, row_count, comps),
        out_shape=(
            f32(block_cols, lines, lanes), f32(group_cols, block_cols), f32(block_cols, block_cols),
            jax.ShapeDtypeStruct((1, 1), jnp.int32),
        ),
        in_specs=[SMEM] + [VMEM] * 3,
        out_specs=(HBM,) * 4,
        scratch_shapes=[
            pltpu.VMEM((basis_cols, block_cols), jnp.float32),
            pltpu.VMEM((block_cols, block_cols), jnp.float32),
            pltpu.VMEM((1, 1), jnp.int32),
            pltpu.VMEM((block_cols * lines, lanes), jnp.float32),
            pltpu.SemaphoreType.DMA((comps + 3,)),
        ],
        compiler_params=SCRATCH,
        name="finish",
    )(place, *kept(*halves, stack))


def stencil_tables(k0_blocks, k0_diag, ke_blocks, mass, velocities, shifts, sample):
    velocity = jnp.take(velocities, sample, axis=0)[0]
    sigma_value = jnp.take(shifts, sample, axis=0)[0]
    center = (k0_diag - sigma_value * mass)[:, :, None] * jnp.eye(3, dtype=jnp.float32)
    tables = k0_blocks - velocity * velocity * ke_blocks
    return tables.at[:, 0].add(center)


def shifted(cells, dim, axis, up):
    extent = cells.shape[dim]
    edge = lax.slice_in_dim(cells, 0, 1, axis=dim) if up else (
        lax.slice_in_dim(cells, extent - 1, extent, axis=dim)
    )
    if axis is None:
        edge = jnp.zeros_like(edge)
    else:
        ends = [(i, i + 1) for i in range(lax.axis_size(axis) - 1)]
        edge = lax.ppermute(edge, axis, [(j, i) for i, j in ends] if up else ends)
    if up:
        return jnp.concatenate((lax.slice_in_dim(cells, 1, extent, axis=dim), edge), axis=dim)
    return jnp.concatenate((edge, lax.slice_in_dim(cells, 0, extent - 1, axis=dim)), axis=dim)


def hold_kernel(*refs):
    *refs, sems = refs
    half = len(refs) // 2
    copies = [
        pltpu.make_async_copy(source, target, sems.at[index])
        for index, (source, target) in enumerate(zip(refs[:half], refs[half:]))
    ]
    for copy in copies:
        copy.start()
    for copy in copies:
        copy.wait()


def hold(*arrays):
    return pl.pallas_call(
        hold_kernel,
        out_shape=[jax.ShapeDtypeStruct(array.shape, array.dtype) for array in arrays],
        in_specs=[HBM] * len(arrays),
        out_specs=[HBM] * len(arrays),
        scratch_shapes=[pltpu.SemaphoreType.DMA((len(arrays),))],
        compiler_params=SCRATCH,
        name="hold",
    )(*far(*arrays))


def careful(arguments):
    x_block, basis, material, k0_blocks, k0_diag, ke_blocks, mass, velocities, shifts, sample = arguments
    x_block, basis, material, k0_blocks, k0_diag, ke_blocks, mass, velocities, shifts = hold(
        x_block, basis, material, jnp.transpose(k0_blocks, (2, 3, 0, 1)), k0_diag.T,
        jnp.transpose(ke_blocks, (2, 3, 0, 1)), mass.T, velocities, shifts,
    )
    k0_blocks, ke_blocks = (jnp.transpose(blocks, (2, 3, 0, 1)) for blocks in (k0_blocks, ke_blocks))
    k0_diag, mass = k0_diag.T, mass.T
    tables = stencil_tables(k0_blocks, k0_diag, ke_blocks, mass, velocities, shifts, sample)
    block_cols, comps, extent_x, _, lanes = x_block.shape
    group_cols = basis.shape[0]
    row_count = float(comps * extent_x * lax.axis_size("space") * basis.shape[3] * lanes)
    fields = jnp.zeros((7, comps, comps) + material.shape, jnp.float32)
    for level in range(tables.shape[0]):
        chosen = (material == level).astype(jnp.float32)
        fields = fields + tables[level][:, :, :, None, None, None] * chosen
    views = [x_block]
    for dim, axis in ((2, "space"), (3, "basis"), (4, None)):
        views += [shifted(x_block, dim, axis, False), shifted(x_block, dim, axis, True)]
    applied = jnp.zeros_like(x_block)
    for offset, view in enumerate(views):
        for comp in range(comps):
            applied = applied + fields[offset, :, comp][None] * view[:, comp : comp + 1]

    count = lax.axis_size("basis")
    place = lax.axis_index("basis")
    pieces = jnp.moveaxis(basis.reshape(basis.shape[:3] + (count, -1, lanes)), 3, 0)
    rows = jnp.zeros((count,) + pieces.shape[1:], jnp.float32)
    for k in range(count):
        piece = lax.dynamic_index_in_dim(pieces, place ^ k, 0, keepdims=False)
        if k:
            piece = lax.ppermute(piece, "basis", [(i, i ^ k) for i in range(count)])
        rows = lax.dynamic_update_index_in_dim(rows, piece, place ^ k, 0)
    rows = rows.reshape((count * group_cols,) + pieces.shape[2:])

    def total(part):
        for axis in ("basis", "space"):
            mask = 1
            while mask < lax.axis_size(axis):
                pairs = [(i, i ^ mask) for i in range(lax.axis_size(axis))]
                part = part + lax.ppermute(part, axis, pairs)
                mask *= 2
        return part / row_count

    running = jnp.zeros((count * group_cols, block_cols), jnp.float32)
    for repeat in range(2):
        coeffs = total(
            jnp.einsum("kcxyz,ncxyz->kn", rows, applied, precision=exact_precision)
        )
        applied = applied - jnp.einsum("kcxyz,kn->ncxyz", rows, coeffs, precision=exact_precision)
        running = running + coeffs
    gram = total(jnp.einsum("ncxyz,mcxyz->nm", applied, applied, precision=exact_precision))
    lower = jnp.linalg.cholesky(gram)
    inverse = lax.linalg.triangular_solve(
        lower, jnp.eye(block_cols, dtype=jnp.float32), left_side=True, lower=True
    )
    block = jnp.einsum("mcxyz,nm->ncxyz", applied, inverse, precision=exact_precision)
    own = lax.dynamic_slice_in_dim(running, place * group_cols, group_cols, axis=0)
    return tuple(hold(block.reshape(block_cols, -1, lanes), own, lower.T))


def shards(
    x_block, basis, material, k0_blocks, k0_diag, ke_blocks, mass, velocities, shifts, sample
):
    arguments = (
        x_block, basis, material, k0_blocks, k0_diag, ke_blocks, mass, velocities, shifts, sample
    )
    block_cols, comps, extent_x, rows, lanes = x_block.shape
    group_cols = basis.shape[0]
    lines = comps * rows
    row_count = float(comps * extent_x * lax.axis_size("space") * basis.shape[3] * lanes)

    place = lax.axis_index("basis").astype(jnp.int32).reshape(1)
    slab = lax.axis_index("space").astype(jnp.int32).reshape(1)
    count = lax.axis_size("basis")
    x_far = x_block.reshape(block_cols * lines, lanes)
    own, *pieces, x_rows, material = pack(place, basis, x_far, material.reshape(rows, lanes), block_cols)
    got = {}
    for name in ("even", 3, "odd", 2, 1):
        if name == "even":
            got[name] = swap(x_far, "space", 0)
        elif name == "odd":
            got[name] = swap(x_far, "space", 1)
        else:
            piece = lax.ppermute(pieces[name - 1], "basis", [(i, i ^ name) for i in range(count)])
            got[name] = piece.reshape(-1, lanes)
    fields, applied, own = ahead(
        sample, velocities, shifts, k0_blocks, ke_blocks, k0_diag, mass, material, x_rows,
        own.reshape(-1, lanes), comps,
    )
    applied = add_side(slab, fields, applied, got.pop("even"), comps, "even")
    pieces = {k: got.pop(k) for k in reversed(partners(count)[1])}
    applied, *parts = add_edges(place, fields, applied, pieces, comps, group_cols)
    split = {0: own, **dict(zip(pieces, parts))}
    stack, keep, give = sums(place, slab, fields, applied, got.pop("odd"), split, got, comps)
    halves = exchange_all(keep, give)
    block, coeffs, upper, bad = finish(
        place, halves, stack, row_count, block_cols, group_cols, lines, comps
    )
    block, coeffs, upper = lax.while_loop(
        lambda state: state[0] > 0,
        lambda state: (jnp.zeros_like(state[0]), careful(arguments)),
        (bad[0, 0], (block, coeffs, upper)),
    )[1]
    return block.reshape(x_block.shape), coeffs, upper


def solution(mesh):
    in_specs = (
        P(None, None, "space", "basis", None),
        P("basis", None, "space", None, None),
        P("space", "basis", None),
        P(),
        P(),
        P(),
        P(),
        P(),
        P(),
        P(),
    )
    out_specs = (P(None, None, "space", "basis", None), P("basis", None), P())
    return jax.shard_map(shards, mesh=mesh, in_specs=in_specs, out_specs=out_specs, check_vma=False)
```

```python
import functools

import jax
import jax.numpy as jnp
from jax import lax
from jax.experimental import pallas as pl
from jax.experimental.pallas import tpu as pltpu
from jax.sharding import PartitionSpec as P

exact_precision = lax.Precision.HIGHEST
VMEM = pl.BlockSpec(memory_space=pltpu.VMEM)
SMEM = pl.BlockSpec(memory_space=pltpu.SMEM)
HBM = pl.BlockSpec(memory_space=pltpu.HBM)
LOSS = 256.0
EARLY = pl.CostEstimate(flops=10**9, bytes_accessed=10**6, transcendentals=0)
NEXT = pl.CostEstimate(flops=3 * 10**8, bytes_accessed=10**6, transcendentals=0)
SCRATCH = pltpu.CompilerParams(vmem_limit_bytes=8 * 2**20)


def f32(*shape):
    return jax.ShapeDtypeStruct(shape, jnp.float32)


def near(*shape, dtype=jnp.float32):
    return pltpu.VMEM(shape, dtype)


def kept(*arrays):
    return [pltpu.with_memory_space_constraint(array, pltpu.VMEM) for array in arrays]


def far(*arrays):
    return [pltpu.with_memory_space_constraint(array, pltpu.HBM) for array in arrays]


def swap(values, axis, first):
    pairs = [(i, i + 1) for i in range(first, lax.axis_size(axis) - 1, 2)]
    return lax.ppermute(values, axis, pairs + [(j, i) for i, j in pairs])


def partners(count):
    return range(1, count), [k for k in range(1, count) if k & (k + 1) == 0]


def pack_kernel(comps, place_ref, basis_ref, x_ref, material_ref, *refs):
    *piece_refs, x_out_ref, material_out_ref, sems = refs
    count = len(piece_refs)
    tiles, _, rows, lanes = basis_ref.shape
    block_cols = x_ref.shape[0] // (comps * rows)
    place = place_ref[0]
    x_copy = pltpu.make_async_copy(x_ref, x_out_ref, sems.at[count])
    x_copy.start()
    copies = [pltpu.make_async_copy(material_ref, material_out_ref, sems.at[count + 1])]
    for k in reversed(range(count)):
        copies.append(
            pltpu.make_async_copy(
                basis_ref.at[:, place ^ k], piece_refs[k].at[pl.ds(0, tiles)], sems.at[k]
            )
        )
    for copy in copies:
        copy.start()
    x_copy.wait()
    for comp in range(comps):
        first, last = (
            x_out_ref[pl.ds(comp * rows + row, block_cols, stride=comps * rows), :]
            for row in (0, rows - 1)
        )
        for k in partners(count)[1]:
            edge = jnp.where((place ^ k) > place, last, first)
            for part in range(block_cols // rows):
                piece_refs[k][tiles + comp * (block_cols // rows) + part] = edge[
                    part * rows : (part + 1) * rows
                ]
    for copy in copies:
        copy.wait()


def pack(place, basis, x_rows, material, block_cols):
    group_cols, comps, _, full_y, lanes = basis.shape
    count = lax.axis_size("basis")
    rows = full_y // count
    tiles = group_cols * comps
    edge_tiles = block_cols * comps // rows
    pieces = [
        near(tiles + (edge_tiles if k in partners(count)[1] else 0), rows, lanes)
        for k in range(count)
    ]
    return pl.pallas_call(
        functools.partial(pack_kernel, comps),
        out_shape=(*pieces, near(*x_rows.shape), near(*material.shape, dtype=jnp.int32)),
        in_specs=[SMEM, HBM, HBM, HBM],
        out_specs=(VMEM,) * (count + 2),
        scratch_shapes=[pltpu.SemaphoreType.DMA((count + 2,))],
        compiler_params=SCRATCH,
        name="pack",
    )(place, *far(basis.reshape(tiles, count, rows, lanes), x_rows, material))


def three_parts(values):
    high = values.astype(jnp.bfloat16)
    rest = values - high.astype(jnp.float32)
    middle = rest.astype(jnp.bfloat16)
    low = (rest - middle.astype(jnp.float32)).astype(jnp.bfloat16)
    return high, middle, low


def line_of(ref, comp, row, comps, rows, block_cols):
    return ref[pl.ds(comp * rows + row, block_cols, stride=comps * rows), :]


def ahead_kernel(
    sample_ref, *refs
):
    far_refs, refs = refs[:6], refs[6:]
    material_ref, x_ref, own_ref, fields_ref, applied_ref, stack_ref, *near_refs, sems = refs
    velocities_ref, shifts_ref, k0_ref, ke_ref, diag_ref, mass_ref = near_refs
    copies = [
        pltpu.make_async_copy(source, target, sems.at[index])
        for index, (source, target) in enumerate(zip(far_refs, near_refs))
    ]
    for copy in copies:
        copy.start()
    group_cols = stack_ref.shape[0] // 3
    split_lines(
        own_ref, stack_ref, applied_ref.shape[0], group_cols, [i * group_cols for i in range(3)]
    )
    for copy in copies:
        copy.wait()
    comps, _, levels, offsets = k0_ref.shape
    rows, lanes = material_ref.shape
    lines = comps * rows
    block_cols = x_ref.shape[0] // lines
    velocity = velocities_ref[sample_ref[0]]
    sigma = shifts_ref[sample_ref[0]]
    entry_rows = fields_ref.shape[1]
    stride = entry_rows // (comps * comps)
    gap = jnp.zeros((levels, stride - offsets), jnp.float32)
    wide = []
    for out in range(comps):
        for comp in range(comps):
            wide += [k0_ref[out, comp] - velocity * velocity * ke_ref[out, comp], gap]
    wide.append(jnp.zeros((levels, lanes - entry_rows), jnp.float32))
    table = jnp.concatenate(wide, axis=1).T[:entry_rows]
    entry = lax.broadcasted_iota(jnp.int32, table.shape, 0)
    for comp in range(comps):
        centre = diag_ref[comp : comp + 1, :] - sigma * mass_ref[comp : comp + 1, :]
        table = table + jnp.where(entry == comp * (comps + 1) * stride, centre, 0.0)

    lane = lax.broadcasted_iota(jnp.int32, (block_cols, lanes), 1)
    level = lax.broadcasted_iota(jnp.int32, (levels, lanes), 0)
    for row in range(rows):
        chosen = jnp.broadcast_to(material_ref[row : row + 1, :], (levels, lanes)) == level
        fields = jnp.dot(
            table, chosen.astype(jnp.float32),
            precision=exact_precision, preferred_element_type=jnp.float32,
        )
        fields_ref[row] = fields
        sums = [None] * comps
        for comp in range(comps):
            centre = line_of(x_ref, comp, row, comps, rows, block_cols)
            views = {
                0: centre,
                5: jnp.where(lane == 0, 0.0, pltpu.roll(centre, 1, 1)),
                6: jnp.where(lane == lanes - 1, 0.0, pltpu.roll(centre, lanes - 1, 1)),
            }
            if row > 0:
                views[3] = line_of(x_ref, comp, row - 1, comps, rows, block_cols)
            if row < rows - 1:
                views[4] = line_of(x_ref, comp, row + 1, comps, rows, block_cols)
            for offset, view in views.items():
                for out in range(comps):
                    place = (out * comps + comp) * stride + offset
                    term = fields[place : place + 1, :] * view
                    sums[out] = term if sums[out] is None else sums[out] + term
        for out in range(comps):
            applied_ref[out * rows + row] = sums[out]


def ahead(sample, velocities, shifts, k0, ke, diag, mass, material, x_rows, own, comps):
    rows, lanes = material.shape
    lines = comps * rows
    stride = -(-k0.shape[1] // 8) * 8
    k0, ke = (jnp.transpose(blocks, (2, 3, 0, 1)) for blocks in (k0, ke))
    tables = far(velocities, shifts, k0, ke, diag.T, mass.T)
    return pl.pallas_call(
        ahead_kernel,
        out_shape=(
            near(rows, comps * comps * stride, lanes),
            near(lines, x_rows.shape[0] // lines, lanes),
            near(3 * own.shape[0] // lines, lines * lanes, dtype=jnp.bfloat16),
        ),
        in_specs=[SMEM] + [HBM] * 6 + [VMEM] * 3,
        out_specs=(VMEM,) * 3,
        scratch_shapes=[
            (pltpu.SMEM if array.ndim == 1 else pltpu.VMEM)(array.shape, jnp.float32)
            for array in tables
        ] + [pltpu.SemaphoreType.DMA((len(tables),))],
        compiler_params=SCRATCH,
        name="ahead",
    )(sample, *tables, *kept(material, x_rows, own))


def side_terms(field_row, swapped, side, out, comp, comps):
    stride = field_row.shape[0] // (comps * comps)
    begin = (out * comps + comp) * stride
    below, above = field_row[begin + 1 : begin + 2], field_row[begin + 2 : begin + 3]
    other = (below, above) if side == "even" else (above, below)
    return jnp.where(swapped, *other)


def side_kernel(comps, side, slab_ref, fields_ref, applied_ref, halo_ref, out_ref):
    lines, block_cols, _ = applied_ref.shape
    rows = lines // comps
    swapped = slab_ref[0] % 2 == 1
    for row in range(rows):
        field_row = fields_ref[row]
        views = [line_of(halo_ref, comp, row, comps, rows, block_cols) for comp in range(comps)]
        for out in range(comps):
            total = applied_ref[out * rows + row]
            for comp, view in enumerate(views):
                total = total + side_terms(field_row, swapped, side, out, comp, comps) * view
            out_ref[out * rows + row] = total


def add_side(slab, fields, applied, halo, comps, side):
    return pl.pallas_call(
        functools.partial(side_kernel, comps, side),
        out_shape=near(*applied.shape),
        in_specs=[SMEM] + [VMEM] * 3,
        out_specs=VMEM,
        compiler_params=SCRATCH,
        cost_estimate=NEXT,
        name="side",
    )(slab, *kept(fields, applied, halo))


def split_lines(piece_ref, stack_ref, lines, group_cols, begins):
    lanes = piece_ref.shape[1]
    for line in range(lines):
        values = piece_ref[pl.ds(line, group_cols, stride=lines), :]
        for begin, part in zip(begins, three_parts(values)):
            stack_ref[pl.ds(begin, group_cols), pl.ds(line * lanes, lanes)] = part


def edges_kernel(comps, ks, group_cols, place_ref, fields_ref, applied_ref, *refs):
    piece_refs, out_ref, parts_refs = refs[: len(ks)], refs[len(ks)], refs[len(ks) + 1 :]
    lines, block_cols, lanes = applied_ref.shape
    rows = lines // comps
    stride = fields_ref.shape[1] // (comps * comps)
    place = place_ref[0]

    def edge(comp, step):
        result = jnp.zeros((block_cols, lanes), jnp.float32)
        for k, ref in zip(ks, piece_refs):
            begin = ref.shape[0] - (comps - comp) * block_cols
            here = (place ^ k) == place + step
            result = jnp.where(here, ref[pl.ds(begin, block_cols), :], result)
        return result

    out_ref[...] = applied_ref[...]
    for row, offset, step in ((0, 3, -1), (rows - 1, 4, 1)):
        field_row = fields_ref[row]
        views = [edge(comp, step) for comp in range(comps)]
        for out in range(comps):
            total = out_ref[out * rows + row]
            for comp, view in enumerate(views):
                entry = (out * comps + comp) * stride + offset
                total = total + field_row[entry : entry + 1] * view
            out_ref[out * rows + row] = total
    for piece_ref, parts_ref in zip(piece_refs, parts_refs):
        split_lines(piece_ref, parts_ref, lines, group_cols, [i * group_cols for i in range(3)])


def add_edges(place, fields, applied, pieces, comps, group_cols, weight):
    lines, _, lanes = applied.shape
    parts = near(3 * group_cols, lines * lanes, dtype=jnp.bfloat16)
    return pl.pallas_call(
        functools.partial(edges_kernel, comps, tuple(pieces), group_cols),
        out_shape=(near(*applied.shape),) + (parts,) * len(pieces),
        in_specs=[SMEM] + [VMEM] * (2 + len(pieces)),
        out_specs=(VMEM,) * (1 + len(pieces)),
        compiler_params=SCRATCH,
        cost_estimate=weight,
        name="edges",
    )(place, *kept(fields, applied, *pieces.values()))


def fold(total, basis_cols, block_cols, lanes):
    half = basis_cols // 2
    row = lax.broadcasted_iota(jnp.int32, (half, half), 0)
    column = lax.broadcasted_iota(jnp.int32, (half, half), 1)
    last = total[half:basis_cols, half:basis_cols]
    shared = jnp.where(row >= column, total[:half, :half], last)
    diagonal = jnp.sum(jnp.where(row == column, last, 0.0), axis=1, keepdims=True)
    below = total[basis_cols:]
    first = jnp.concatenate((below[:, :half], below[:, half:basis_cols]), axis=0)
    rest = jnp.zeros((half - block_cols, block_cols), jnp.float32)
    block = jnp.concatenate((below[:, basis_cols:], rest), axis=0)
    pad = jnp.zeros((half, lanes - 3 * half - block_cols - 1), jnp.float32)
    return jnp.concatenate(
        (shared, total[:half, half:basis_cols], first, block, diagonal, pad), axis=1
    )


def unfold(folded, block_cols):
    half = folded.shape[0]
    row = lax.broadcasted_iota(jnp.int32, (half, half), 0)
    column = lax.broadcasted_iota(jnp.int32, (half, half), 1)
    shared, across = folded[:, :half], folded[:, half : 2 * half]
    turned = shared.T
    start = jnp.where(row >= column, shared, turned)
    end = jnp.where(row < column, shared, turned)
    diagonal = folded[:, 3 * half + block_cols : 3 * half + block_cols + 1]
    end = jnp.where(row == column, diagonal, end)
    gram = jnp.concatenate(
        (jnp.concatenate((start, across), axis=1), jnp.concatenate((across.T, end), axis=1)), axis=0
    )
    first = folded[:, 2 * half : 3 * half]
    first = jnp.concatenate((first[:block_cols], first[block_cols : 2 * block_cols]), axis=1)
    return gram, first, folded[:block_cols, 3 * half : 3 * half + block_cols]


def sums_kernel(
    comps, split, raw, place_ref, slab_ref, fields_ref, applied_ref, *refs
):
    *refs, halo_ref, stack_ref, keep_ref, give_ref = refs
    lines, block_cols, lanes = applied_ref.shape
    rows = lines // comps
    group_cols = refs[0].shape[0] // 3
    basis_cols = (len(split) + len(raw)) * group_cols
    joined = basis_cols + block_cols
    place = place_ref[0]
    swapped = slab_ref[0] % 2 == 1
    for k, ref in zip(split + raw, refs):
        begin = pl.multiple_of((place ^ k) * group_cols, group_cols)
        begins = [index * joined + begin for index in range(3)]
        if k in split:
            for index in range(3):
                stack_ref[pl.ds(begins[index], group_cols), :] = ref[
                    pl.ds(index * group_cols, group_cols), :
                ]
        else:
            split_lines(ref, stack_ref, lines, group_cols, begins)
    for row in range(rows):
        field_row = fields_ref[row]
        views = [line_of(halo_ref, comp, row, comps, rows, block_cols) for comp in range(comps)]
        for out in range(comps):
            line = out * rows + row
            total = applied_ref[line]
            for comp, view in enumerate(views):
                total = total + side_terms(field_row, swapped, "odd", out, comp, comps) * view
            for index, part in enumerate(three_parts(total)):
                there = pl.ds(index * joined + basis_cols, block_cols)
                stack_ref[there, pl.ds(line * lanes, lanes)] = part

    stack = stack_ref[...]
    products = lax.dot_general(
        stack, stack, (((1,), (1,)), ((), ())), preferred_element_type=jnp.float32
    )
    wide = products[:joined] + products[joined : 2 * joined] + products[2 * joined :]
    total = wide[:, :joined] + wide[:, joined : 2 * joined] + wide[:, 2 * joined :]
    folded = fold(total, basis_cols, block_cols, keep_ref.shape[1])
    half = keep_ref.shape[0]
    odd = place % 2 == 1
    keep_ref[...] = jnp.where(odd, folded[half:], folded[:half])
    give_ref[...] = jnp.where(odd, folded[:half], folded[half:])


def sums(place, slab, fields, applied, halo, split, raw, comps):
    lines, block_cols, lanes = applied.shape
    basis_cols = (len(split) + len(raw)) * (split[0].shape[0] // 3)
    joined = basis_cols + block_cols
    return pl.pallas_call(
        functools.partial(sums_kernel, comps, tuple(split), tuple(raw)),
        out_shape=(
            near(3 * joined, lines * lanes, dtype=jnp.bfloat16),
            near(basis_cols // 4, 2 * basis_cols),
            near(basis_cols // 4, 2 * basis_cols),
        ),
        in_specs=[SMEM] * 2 + [VMEM] * (3 + len(split) + len(raw)),
        out_specs=(VMEM,) * 3,
        compiler_params=SCRATCH,
        name="sums",
    )(place, slab, *kept(fields, applied, *split.values(), *raw.values(), halo))


def exchange_all(keep, give):
    sizes = [lax.axis_size(axis) for axis in ("space", "basis")]
    pairs = [(i, i ^ 1) for i in range(sizes[1])]
    part = keep + lax.ppermute(give, "basis", pairs)
    groups = [
        [i * sizes[1] + j for i in range(sizes[0]) for j in range(first, sizes[1], 2)]
        for first in range(2)
    ]
    copies = jnp.broadcast_to(part[None], (len(groups[0]),) + part.shape)
    parts = lax.all_to_all(copies, ("space", "basis"), 0, 0, axis_index_groups=groups)
    own = jnp.sum(parts, axis=0)
    return own, lax.ppermute(own, "basis", pairs)


def finish_kernel(
    row_count, comps, place_ref, own_ref, given_ref, stack_ref, block_ref, coeffs_ref, upper_ref, bad_ref,
    coeffs_scratch, upper_scratch, bad_scratch, block_scratch, sems,
):
    block_cols = upper_ref.shape[0]
    basis_cols = own_ref.shape[1] // 2
    joined = basis_cols + block_cols
    lines, lanes = block_ref.shape[1:]
    odd = place_ref[0] % 2 == 1
    own, given = own_ref[...], given_ref[...]
    total = jnp.concatenate((jnp.where(odd, given, own), jnp.where(odd, own, given)), axis=0)
    total = total / row_count
    gram, first, block_gram = unfold(total, block_cols)

    def times(left, right, right_dim=0):
        return lax.dot_general(
            left, right, (((1,), (right_dim,)), ((), ())),
            precision=exact_precision, preferred_element_type=jnp.float32,
        )

    coeffs = first + (first - times(first, gram))
    image = times(coeffs, gram)
    matrix = block_gram - times(
        jnp.concatenate((coeffs, first - image), axis=1), jnp.concatenate((first, coeffs), axis=1), 1
    )
    coeffs_scratch[...] = coeffs.T
    group_cols = coeffs_ref.shape[0]
    start = pl.multiple_of(place_ref[0] * group_cols, group_cols)
    copies = [
        pltpu.make_async_copy(
            coeffs_scratch.at[pl.ds(start, group_cols)], coeffs_ref, sems.at[comps]
        )
    ]
    copies[0].start()

    row = lax.broadcasted_iota(jnp.int32, (block_cols, block_cols), 0)
    column = lax.broadcasted_iota(jnp.int32, (block_cols, block_cols), 1)
    unit = jnp.where(row == column, 1.0, 0.0)
    pad = jnp.zeros((block_cols, 2 * basis_cols - joined - block_cols), jnp.float32)
    work = jnp.concatenate((-coeffs, unit, matrix, pad), axis=1)
    height = lax.broadcasted_iota(jnp.int32, work.shape, 0)
    width = 4
    for begin in range(0, block_cols, width):
        done, new_rows = [], []
        for step in range(begin, begin + width):
            column_here = jnp.broadcast_to(work[:, joined + step : joined + step + 1], work.shape)
            pivot_row = work[step : step + 1]
            for other_column, other_row, inverse in done:
                entry = other_column[step : step + 1]
                pivot_row = pivot_row - entry * other_row
                column_here = column_here - other_column * (entry * inverse)
            pivot = column_here[step : step + 1]
            inverse = 1.0 / pivot
            done.append((column_here, pivot_row * inverse, inverse))
            new_rows.append(pivot_row * lax.rsqrt(pivot))
        rest = work
        for column_here, scaled, _ in done:
            rest = rest - column_here * scaled
        work = jnp.where(height >= begin + width, rest, work)
        for step, new_row in enumerate(new_rows, begin):
            work = jnp.where(height == step, new_row, work)
    upper = jnp.where(row <= column, work[:, joined : joined + block_cols], 0.0)
    upper_scratch[...] = upper
    kept_enough = jnp.where(row == column, upper * upper * LOSS, block_gram) >= block_gram
    kept_enough = jnp.min(jnp.where(kept_enough, 1.0, 0.0), axis=0, keepdims=True)
    kept_enough = jnp.min(kept_enough, axis=1, keepdims=True)
    bad_scratch[...] = jnp.where(kept_enough > 0.0, 0, 1)
    copies.append(pltpu.make_async_copy(bad_scratch, bad_ref, sems.at[comps + 2]))
    copies[-1].start()
    copies.append(pltpu.make_async_copy(upper_scratch, upper_ref, sems.at[comps + 1]))
    copies[-1].start()
    weights = three_parts(work[:, :joined])
    wide = jnp.concatenate(
        [jnp.concatenate((part, part, part), axis=1) for part in weights], axis=0
    )
    rows = lines // comps
    for comp in range(comps):
        there = pl.ds(comp * rows * lanes, rows * lanes)
        result = jnp.dot(wide, stack_ref[:, there], preferred_element_type=jnp.float32)
        result = result[:block_cols] + result[block_cols : 2 * block_cols] + result[2 * block_cols :]
        for index in range(rows):
            block_scratch[pl.ds(comp * rows + index, block_cols, stride=lines), :] = result[
                :, index * lanes : (index + 1) * lanes
            ]
        part = pl.ds(comp * rows, rows)
        copies.append(
            pltpu.make_async_copy(
                block_scratch.reshape(block_cols, lines, lanes).at[:, part, :],
                block_ref.at[:, part, :],
                sems.at[comp],
            )
        )
        copies[-1].start()
    for copy in copies:
        copy.wait()


def finish(place, halves, stack, row_count, block_cols, group_cols, lines, comps):
    lanes = stack.shape[1] // lines
    basis_cols = halves[0].shape[1] // 2
    return pl.pallas_call(
        functools.partial(finish_kernel, row_count, comps),
        out_shape=(
            f32(block_cols, lines, lanes), f32(group_cols, block_cols), f32(block_cols, block_cols),
            jax.ShapeDtypeStruct((1, 1), jnp.int32),
        ),
        in_specs=[SMEM] + [VMEM] * 3,
        out_specs=(HBM,) * 4,
        scratch_shapes=[
            pltpu.VMEM((basis_cols, block_cols), jnp.float32),
            pltpu.VMEM((block_cols, block_cols), jnp.float32),
            pltpu.VMEM((1, 1), jnp.int32),
            pltpu.VMEM((block_cols * lines, lanes), jnp.float32),
            pltpu.SemaphoreType.DMA((comps + 3,)),
        ],
        compiler_params=SCRATCH,
        name="finish",
    )(place, *kept(*halves, stack))


def stencil_tables(k0_blocks, k0_diag, ke_blocks, mass, velocities, shifts, sample):
    velocity = jnp.take(velocities, sample, axis=0)[0]
    sigma_value = jnp.take(shifts, sample, axis=0)[0]
    center = (k0_diag - sigma_value * mass)[:, :, None] * jnp.eye(3, dtype=jnp.float32)
    tables = k0_blocks - velocity * velocity * ke_blocks
    return tables.at[:, 0].add(center)


def shifted(cells, dim, axis, up):
    extent = cells.shape[dim]
    edge = lax.slice_in_dim(cells, 0, 1, axis=dim) if up else (
        lax.slice_in_dim(cells, extent - 1, extent, axis=dim)
    )
    if axis is None:
        edge = jnp.zeros_like(edge)
    else:
        ends = [(i, i + 1) for i in range(lax.axis_size(axis) - 1)]
        edge = lax.ppermute(edge, axis, [(j, i) for i, j in ends] if up else ends)
    if up:
        return jnp.concatenate((lax.slice_in_dim(cells, 1, extent, axis=dim), edge), axis=dim)
    return jnp.concatenate((edge, lax.slice_in_dim(cells, 0, extent - 1, axis=dim)), axis=dim)


def hold_kernel(*refs):
    *refs, sems = refs
    half = len(refs) // 2
    copies = [
        pltpu.make_async_copy(source, target, sems.at[index])
        for index, (source, target) in enumerate(zip(refs[:half], refs[half:]))
    ]
    for copy in copies:
        copy.start()
    for copy in copies:
        copy.wait()


def hold(*arrays):
    return pl.pallas_call(
        hold_kernel,
        out_shape=[jax.ShapeDtypeStruct(array.shape, array.dtype) for array in arrays],
        in_specs=[HBM] * len(arrays),
        out_specs=[HBM] * len(arrays),
        scratch_shapes=[pltpu.SemaphoreType.DMA((len(arrays),))],
        compiler_params=SCRATCH,
        name="hold",
    )(*far(*arrays))


def careful(arguments):
    x_block, basis, material, k0_blocks, k0_diag, ke_blocks, mass, velocities, shifts, sample = arguments
    x_block, basis, material, k0_blocks, k0_diag, ke_blocks, mass, velocities, shifts = hold(
        x_block, basis, material, jnp.transpose(k0_blocks, (2, 3, 0, 1)), k0_diag.T,
        jnp.transpose(ke_blocks, (2, 3, 0, 1)), mass.T, velocities, shifts,
    )
    k0_blocks, ke_blocks = (jnp.transpose(blocks, (2, 3, 0, 1)) for blocks in (k0_blocks, ke_blocks))
    k0_diag, mass = k0_diag.T, mass.T
    tables = stencil_tables(k0_blocks, k0_diag, ke_blocks, mass, velocities, shifts, sample)
    block_cols, comps, extent_x, _, lanes = x_block.shape
    group_cols = basis.shape[0]
    row_count = float(comps * extent_x * lax.axis_size("space") * basis.shape[3] * lanes)
    fields = jnp.zeros((7, comps, comps) + material.shape, jnp.float32)
    for level in range(tables.shape[0]):
        chosen = (material == level).astype(jnp.float32)
        fields = fields + tables[level][:, :, :, None, None, None] * chosen
    views = [x_block]
    for dim, axis in ((2, "space"), (3, "basis"), (4, None)):
        views += [shifted(x_block, dim, axis, False), shifted(x_block, dim, axis, True)]
    applied = jnp.zeros_like(x_block)
    for offset, view in enumerate(views):
        for comp in range(comps):
            applied = applied + fields[offset, :, comp][None] * view[:, comp : comp + 1]

    count = lax.axis_size("basis")
    place = lax.axis_index("basis")
    pieces = jnp.moveaxis(basis.reshape(basis.shape[:3] + (count, -1, lanes)), 3, 0)
    rows = jnp.zeros((count,) + pieces.shape[1:], jnp.float32)
    for k in range(count):
        piece = lax.dynamic_index_in_dim(pieces, place ^ k, 0, keepdims=False)
        if k:
            piece = lax.ppermute(piece, "basis", [(i, i ^ k) for i in range(count)])
        rows = lax.dynamic_update_index_in_dim(rows, piece, place ^ k, 0)
    rows = rows.reshape((count * group_cols,) + pieces.shape[2:])

    def total(part):
        for axis in ("basis", "space"):
            mask = 1
            while mask < lax.axis_size(axis):
                pairs = [(i, i ^ mask) for i in range(lax.axis_size(axis))]
                part = part + lax.ppermute(part, axis, pairs)
                mask *= 2
        return part / row_count

    running = jnp.zeros((count * group_cols, block_cols), jnp.float32)
    for repeat in range(2):
        coeffs = total(
            jnp.einsum("kcxyz,ncxyz->kn", rows, applied, precision=exact_precision)
        )
        applied = applied - jnp.einsum("kcxyz,kn->ncxyz", rows, coeffs, precision=exact_precision)
        running = running + coeffs
    gram = total(jnp.einsum("ncxyz,mcxyz->nm", applied, applied, precision=exact_precision))
    lower = jnp.linalg.cholesky(gram)
    inverse = lax.linalg.triangular_solve(
        lower, jnp.eye(block_cols, dtype=jnp.float32), left_side=True, lower=True
    )
    block = jnp.einsum("mcxyz,nm->ncxyz", applied, inverse, precision=exact_precision)
    own = lax.dynamic_slice_in_dim(running, place * group_cols, group_cols, axis=0)
    return tuple(hold(block.reshape(block_cols, -1, lanes), own, lower.T))


def shards(
    x_block, basis, material, k0_blocks, k0_diag, ke_blocks, mass, velocities, shifts, sample
):
    arguments = (
        x_block, basis, material, k0_blocks, k0_diag, ke_blocks, mass, velocities, shifts, sample
    )
    block_cols, comps, extent_x, rows, lanes = x_block.shape
    group_cols = basis.shape[0]
    lines = comps * rows
    row_count = float(comps * extent_x * lax.axis_size("space") * basis.shape[3] * lanes)

    place = lax.axis_index("basis").astype(jnp.int32).reshape(1)
    slab = lax.axis_index("space").astype(jnp.int32).reshape(1)
    count = lax.axis_size("basis")
    x_far = x_block.reshape(block_cols * lines, lanes)
    own, *pieces, x_rows, material = pack(place, basis, x_far, material.reshape(rows, lanes), block_cols)
    got = {}
    for name in ("even", 3, "odd", 2, 1):
        if name == "even":
            got[name] = swap(x_far, "space", 0)
        elif name == "odd":
            got[name] = swap(x_far, "space", 1)
        else:
            piece = lax.ppermute(pieces[name - 1], "basis", [(i, i ^ name) for i in range(count)])
            got[name] = piece.reshape(-1, lanes)
    fields, applied, own = ahead(
        sample, velocities, shifts, k0_blocks, ke_blocks, k0_diag, mass, material, x_rows,
        own.reshape(-1, lanes), comps,
    )
    split = {0: own}
    first, *rest = reversed(partners(count)[1])
    applied, split[first] = add_edges(
        place, fields, applied, {first: got.pop(first)}, comps, group_cols, EARLY
    )
    applied = add_side(slab, fields, applied, got.pop("even"), comps, "even")
    for k in rest:
        applied, split[k] = add_edges(
            place, fields, applied, {k: got.pop(k)}, comps, group_cols, None
        )
    stack, keep, give = sums(place, slab, fields, applied, got.pop("odd"), split, got, comps)
    halves = exchange_all(keep, give)
    block, coeffs, upper, bad = finish(
        place, halves, stack, row_count, block_cols, group_cols, lines, comps
    )
    block, coeffs, upper = lax.while_loop(
        lambda state: state[0] > 0,
        lambda state: (jnp.zeros_like(state[0]), careful(arguments)),
        (bad[0, 0], (block, coeffs, upper)),
    )[1]
    return block.reshape(x_block.shape), coeffs, upper


def solution(mesh):
    in_specs = (
        P(None, None, "space", "basis", None),
        P("basis", None, "space", None, None),
        P("space", "basis", None),
        P(),
        P(),
        P(),
        P(),
        P(),
        P(),
        P(),
    )
    out_specs = (P(None, None, "space", "basis", None), P("basis", None), P())
    return jax.shard_map(shards, mesh=mesh, in_specs=in_specs, out_specs=out_specs, check_vma=False)
```

```python
import functools

import jax
import jax.numpy as jnp
from jax import lax
from jax.experimental import pallas as pl
from jax.experimental.pallas import tpu as pltpu
from jax.sharding import PartitionSpec as P

exact_precision = lax.Precision.HIGHEST
VMEM = pl.BlockSpec(memory_space=pltpu.VMEM)
SMEM = pl.BlockSpec(memory_space=pltpu.SMEM)
HBM = pl.BlockSpec(memory_space=pltpu.HBM)
LOSS = 256.0
EARLY = pl.CostEstimate(flops=10**9, bytes_accessed=10**6, transcendentals=0)
NEXT = pl.CostEstimate(flops=3 * 10**8, bytes_accessed=10**6, transcendentals=0)
SCRATCH = pltpu.CompilerParams(vmem_limit_bytes=8 * 2**20)


def f32(*shape):
    return jax.ShapeDtypeStruct(shape, jnp.float32)


def near(*shape, dtype=jnp.float32):
    return pltpu.VMEM(shape, dtype)


def kept(*arrays):
    return [pltpu.with_memory_space_constraint(array, pltpu.VMEM) for array in arrays]


def far(*arrays):
    return [pltpu.with_memory_space_constraint(array, pltpu.HBM) for array in arrays]


def swap(values, axis, first):
    pairs = [(i, i + 1) for i in range(first, lax.axis_size(axis) - 1, 2)]
    return lax.ppermute(values, axis, pairs + [(j, i) for i, j in pairs])


def partners(count):
    return range(1, count), [k for k in range(1, count) if k & (k + 1) == 0]


def pack_kernel(comps, ks, edge_ks, place_ref, basis_ref, rider_ref, *refs):
    x_refs, refs = refs[: len(refs) - len(ks) - 2], refs[len(refs) - len(ks) - 2 :]
    *piece_refs, rider_out_ref, sems = refs
    x_ref = x_refs[0] if x_refs else rider_out_ref
    tiles, _, rows, lanes = basis_ref.shape
    block_cols = x_ref.shape[0] // (comps * rows)
    place = place_ref[0]
    rider = pltpu.make_async_copy(rider_ref, rider_out_ref, sems.at[len(ks)])
    rider.start()
    copies = [
        pltpu.make_async_copy(
            basis_ref.at[:, place ^ k], piece_ref.at[pl.ds(0, tiles)], sems.at[index]
        )
        for index, (k, piece_ref) in enumerate(zip(ks, piece_refs))
    ]
    for copy in copies:
        copy.start()
    rider.wait()
    for comp in range(comps):
        first, last = (
            x_ref[pl.ds(comp * rows + row, block_cols, stride=comps * rows), :]
            for row in (0, rows - 1)
        )
        for k, piece_ref in zip(ks, piece_refs):
            if k in edge_ks:
                edge = jnp.where((place ^ k) > place, last, first)
                for part in range(block_cols // rows):
                    piece_ref[tiles + comp * (block_cols // rows) + part] = edge[
                        part * rows : (part + 1) * rows
                    ]
    for copy in copies:
        copy.wait()


def pack(place, basis, rider, block_cols, ks, *x_rows):
    group_cols, comps, _, full_y, lanes = basis.shape
    count = lax.axis_size("basis")
    rows = full_y // count
    tiles = group_cols * comps
    edge_tiles = block_cols * comps // rows
    edge_ks = partners(count)[1]
    pieces = [near(tiles + (edge_tiles if k in edge_ks else 0), rows, lanes) for k in ks]
    return pl.pallas_call(
        functools.partial(pack_kernel, comps, tuple(ks), tuple(edge_ks)),
        out_shape=(*pieces, near(*rider.shape, dtype=rider.dtype)),
        in_specs=[SMEM, HBM, HBM] + [VMEM] * len(x_rows),
        out_specs=(VMEM,) * (len(ks) + 1),
        scratch_shapes=[pltpu.SemaphoreType.DMA((len(ks) + 1,))],
        compiler_params=SCRATCH,
        name="pack",
    )(place, *far(basis.reshape(tiles, count, rows, lanes), rider), *kept(*x_rows))


def three_parts(values):
    high = values.astype(jnp.bfloat16)
    rest = values - high.astype(jnp.float32)
    middle = rest.astype(jnp.bfloat16)
    low = (rest - middle.astype(jnp.float32)).astype(jnp.bfloat16)
    return high, middle, low


def line_of(ref, comp, row, comps, rows, block_cols):
    return ref[pl.ds(comp * rows + row, block_cols, stride=comps * rows), :]


def ahead_kernel(
    sample_ref, *refs
):
    far_refs, refs = refs[:6], refs[6:]
    material_ref, x_ref, own_ref, fields_ref, applied_ref, stack_ref, *near_refs, sems = refs
    velocities_ref, shifts_ref, k0_ref, ke_ref, diag_ref, mass_ref = near_refs
    copies = [
        pltpu.make_async_copy(source, target, sems.at[index])
        for index, (source, target) in enumerate(zip(far_refs, near_refs))
    ]
    for copy in copies:
        copy.start()
    group_cols = stack_ref.shape[0] // 3
    split_lines(
        own_ref, stack_ref, applied_ref.shape[0], group_cols, [i * group_cols for i in range(3)]
    )
    for copy in copies:
        copy.wait()
    comps, _, levels, offsets = k0_ref.shape
    rows, lanes = material_ref.shape
    lines = comps * rows
    block_cols = x_ref.shape[0] // lines
    velocity = velocities_ref[sample_ref[0]]
    sigma = shifts_ref[sample_ref[0]]
    entry_rows = fields_ref.shape[1]
    stride = entry_rows // (comps * comps)
    gap = jnp.zeros((levels, stride - offsets), jnp.float32)
    wide = []
    for out in range(comps):
        for comp in range(comps):
            wide += [k0_ref[out, comp] - velocity * velocity * ke_ref[out, comp], gap]
    wide.append(jnp.zeros((levels, lanes - entry_rows), jnp.float32))
    table = jnp.concatenate(wide, axis=1).T[:entry_rows]
    entry = lax.broadcasted_iota(jnp.int32, table.shape, 0)
    for comp in range(comps):
        centre = diag_ref[comp : comp + 1, :] - sigma * mass_ref[comp : comp + 1, :]
        table = table + jnp.where(entry == comp * (comps + 1) * stride, centre, 0.0)

    lane = lax.broadcasted_iota(jnp.int32, (block_cols, lanes), 1)
    level = lax.broadcasted_iota(jnp.int32, (levels, lanes), 0)
    for row in range(rows):
        chosen = jnp.broadcast_to(material_ref[row : row + 1, :], (levels, lanes)) == level
        fields = jnp.dot(
            table, chosen.astype(jnp.float32),
            precision=exact_precision, preferred_element_type=jnp.float32,
        )
        fields_ref[row] = fields
        sums = [None] * comps
        for comp in range(comps):
            centre = line_of(x_ref, comp, row, comps, rows, block_cols)
            views = {
                0: centre,
                5: jnp.where(lane == 0, 0.0, pltpu.roll(centre, 1, 1)),
                6: jnp.where(lane == lanes - 1, 0.0, pltpu.roll(centre, lanes - 1, 1)),
            }
            if row > 0:
                views[3] = line_of(x_ref, comp, row - 1, comps, rows, block_cols)
            if row < rows - 1:
                views[4] = line_of(x_ref, comp, row + 1, comps, rows, block_cols)
            for offset, view in views.items():
                for out in range(comps):
                    place = (out * comps + comp) * stride + offset
                    term = fields[place : place + 1, :] * view
                    sums[out] = term if sums[out] is None else sums[out] + term
        for out in range(comps):
            applied_ref[out * rows + row] = sums[out]


def ahead(sample, velocities, shifts, k0, ke, diag, mass, material, x_rows, own, comps):
    rows, lanes = material.shape
    lines = comps * rows
    stride = -(-k0.shape[1] // 8) * 8
    k0, ke = (jnp.transpose(blocks, (2, 3, 0, 1)) for blocks in (k0, ke))
    tables = far(velocities, shifts, k0, ke, diag.T, mass.T)
    return pl.pallas_call(
        ahead_kernel,
        out_shape=(
            near(rows, comps * comps * stride, lanes),
            near(lines, x_rows.shape[0] // lines, lanes),
            near(3 * own.shape[0] // lines, lines * lanes, dtype=jnp.bfloat16),
        ),
        in_specs=[SMEM] + [HBM] * 6 + [VMEM] * 3,
        out_specs=(VMEM,) * 3,
        scratch_shapes=[
            (pltpu.SMEM if array.ndim == 1 else pltpu.VMEM)(array.shape, jnp.float32)
            for array in tables
        ] + [pltpu.SemaphoreType.DMA((len(tables),))],
        compiler_params=SCRATCH,
        name="ahead",
    )(sample, *tables, *kept(material, x_rows, own))


def side_terms(field_row, swapped, side, out, comp, comps):
    stride = field_row.shape[0] // (comps * comps)
    begin = (out * comps + comp) * stride
    below, above = field_row[begin + 1 : begin + 2], field_row[begin + 2 : begin + 3]
    other = (below, above) if side == "even" else (above, below)
    return jnp.where(swapped, *other)


def side_kernel(comps, side, slab_ref, fields_ref, applied_ref, halo_ref, out_ref):
    lines, block_cols, _ = applied_ref.shape
    rows = lines // comps
    swapped = slab_ref[0] % 2 == 1
    for row in range(rows):
        field_row = fields_ref[row]
        views = [line_of(halo_ref, comp, row, comps, rows, block_cols) for comp in range(comps)]
        for out in range(comps):
            total = applied_ref[out * rows + row]
            for comp, view in enumerate(views):
                total = total + side_terms(field_row, swapped, side, out, comp, comps) * view
            out_ref[out * rows + row] = total


def add_side(slab, fields, applied, halo, comps, side):
    return pl.pallas_call(
        functools.partial(side_kernel, comps, side),
        out_shape=near(*applied.shape),
        in_specs=[SMEM] + [VMEM] * 3,
        out_specs=VMEM,
        compiler_params=SCRATCH,
        cost_estimate=NEXT,
        name="side",
    )(slab, *kept(fields, applied, halo))


def split_lines(piece_ref, stack_ref, lines, group_cols, begins):
    lanes = piece_ref.shape[1]
    for line in range(lines):
        values = piece_ref[pl.ds(line, group_cols, stride=lines), :]
        for begin, part in zip(begins, three_parts(values)):
            stack_ref[pl.ds(begin, group_cols), pl.ds(line * lanes, lanes)] = part


def edges_kernel(comps, ks, group_cols, place_ref, fields_ref, applied_ref, *refs):
    piece_refs, out_ref, parts_refs = refs[: len(ks)], refs[len(ks)], refs[len(ks) + 1 :]
    lines, block_cols, lanes = applied_ref.shape
    rows = lines // comps
    stride = fields_ref.shape[1] // (comps * comps)
    place = place_ref[0]

    def edge(comp, step):
        result = jnp.zeros((block_cols, lanes), jnp.float32)
        for k, ref in zip(ks, piece_refs):
            begin = ref.shape[0] - (comps - comp) * block_cols
            here = (place ^ k) == place + step
            result = jnp.where(here, ref[pl.ds(begin, block_cols), :], result)
        return result

    out_ref[...] = applied_ref[...]
    for row, offset, step in ((0, 3, -1), (rows - 1, 4, 1)):
        field_row = fields_ref[row]
        views = [edge(comp, step) for comp in range(comps)]
        for out in range(comps):
            total = out_ref[out * rows + row]
            for comp, view in enumerate(views):
                entry = (out * comps + comp) * stride + offset
                total = total + field_row[entry : entry + 1] * view
            out_ref[out * rows + row] = total
    for piece_ref, parts_ref in zip(piece_refs, parts_refs):
        split_lines(piece_ref, parts_ref, lines, group_cols, [i * group_cols for i in range(3)])


def add_edges(place, fields, applied, pieces, comps, group_cols, weight):
    lines, _, lanes = applied.shape
    parts = near(3 * group_cols, lines * lanes, dtype=jnp.bfloat16)
    return pl.pallas_call(
        functools.partial(edges_kernel, comps, tuple(pieces), group_cols),
        out_shape=(near(*applied.shape),) + (parts,) * len(pieces),
        in_specs=[SMEM] + [VMEM] * (2 + len(pieces)),
        out_specs=(VMEM,) * (1 + len(pieces)),
        compiler_params=SCRATCH,
        cost_estimate=weight,
        name="edges",
    )(place, *kept(fields, applied, *pieces.values()))


def fold(total, basis_cols, block_cols, lanes):
    half = basis_cols // 2
    row = lax.broadcasted_iota(jnp.int32, (half, half), 0)
    column = lax.broadcasted_iota(jnp.int32, (half, half), 1)
    last = total[half:basis_cols, half:basis_cols]
    shared = jnp.where(row >= column, total[:half, :half], last)
    diagonal = jnp.sum(jnp.where(row == column, last, 0.0), axis=1, keepdims=True)
    below = total[basis_cols:]
    first = jnp.concatenate((below[:, :half], below[:, half:basis_cols]), axis=0)
    rest = jnp.zeros((half - block_cols, block_cols), jnp.float32)
    block = jnp.concatenate((below[:, basis_cols:], rest), axis=0)
    pad = jnp.zeros((half, lanes - 3 * half - block_cols - 1), jnp.float32)
    return jnp.concatenate(
        (shared, total[:half, half:basis_cols], first, block, diagonal, pad), axis=1
    )


def unfold(folded, block_cols):
    half = folded.shape[0]
    row = lax.broadcasted_iota(jnp.int32, (half, half), 0)
    column = lax.broadcasted_iota(jnp.int32, (half, half), 1)
    shared, across = folded[:, :half], folded[:, half : 2 * half]
    turned = shared.T
    start = jnp.where(row >= column, shared, turned)
    end = jnp.where(row < column, shared, turned)
    diagonal = folded[:, 3 * half + block_cols : 3 * half + block_cols + 1]
    end = jnp.where(row == column, diagonal, end)
    gram = jnp.concatenate(
        (jnp.concatenate((start, across), axis=1), jnp.concatenate((across.T, end), axis=1)), axis=0
    )
    first = folded[:, 2 * half : 3 * half]
    first = jnp.concatenate((first[:block_cols], first[block_cols : 2 * block_cols]), axis=1)
    return gram, first, folded[:block_cols, 3 * half : 3 * half + block_cols]


def sums_kernel(
    comps, split, raw, place_ref, slab_ref, fields_ref, applied_ref, *refs
):
    *refs, halo_ref, stack_ref, keep_ref, give_ref = refs
    lines, block_cols, lanes = applied_ref.shape
    rows = lines // comps
    group_cols = refs[0].shape[0] // 3
    basis_cols = (len(split) + len(raw)) * group_cols
    joined = basis_cols + block_cols
    place = place_ref[0]
    swapped = slab_ref[0] % 2 == 1
    for k, ref in zip(split + raw, refs):
        begin = pl.multiple_of((place ^ k) * group_cols, group_cols)
        begins = [index * joined + begin for index in range(3)]
        if k in split:
            for index in range(3):
                stack_ref[pl.ds(begins[index], group_cols), :] = ref[
                    pl.ds(index * group_cols, group_cols), :
                ]
        else:
            split_lines(ref, stack_ref, lines, group_cols, begins)
    for row in range(rows):
        field_row = fields_ref[row]
        views = [line_of(halo_ref, comp, row, comps, rows, block_cols) for comp in range(comps)]
        for out in range(comps):
            line = out * rows + row
            total = applied_ref[line]
            for comp, view in enumerate(views):
                total = total + side_terms(field_row, swapped, "odd", out, comp, comps) * view
            for index, part in enumerate(three_parts(total)):
                there = pl.ds(index * joined + basis_cols, block_cols)
                stack_ref[there, pl.ds(line * lanes, lanes)] = part

    stack = stack_ref[...]
    products = lax.dot_general(
        stack, stack, (((1,), (1,)), ((), ())), preferred_element_type=jnp.float32
    )
    wide = products[:joined] + products[joined : 2 * joined] + products[2 * joined :]
    total = wide[:, :joined] + wide[:, joined : 2 * joined] + wide[:, 2 * joined :]
    folded = fold(total, basis_cols, block_cols, keep_ref.shape[1])
    half = keep_ref.shape[0]
    odd = place % 2 == 1
    keep_ref[...] = jnp.where(odd, folded[half:], folded[:half])
    give_ref[...] = jnp.where(odd, folded[:half], folded[half:])


def sums(place, slab, fields, applied, halo, split, raw, comps):
    lines, block_cols, lanes = applied.shape
    basis_cols = (len(split) + len(raw)) * (split[0].shape[0] // 3)
    joined = basis_cols + block_cols
    return pl.pallas_call(
        functools.partial(sums_kernel, comps, tuple(split), tuple(raw)),
        out_shape=(
            near(3 * joined, lines * lanes, dtype=jnp.bfloat16),
            near(basis_cols // 4, 2 * basis_cols),
            near(basis_cols // 4, 2 * basis_cols),
        ),
        in_specs=[SMEM] * 2 + [VMEM] * (3 + len(split) + len(raw)),
        out_specs=(VMEM,) * 3,
        compiler_params=SCRATCH,
        name="sums",
    )(place, slab, *kept(fields, applied, *split.values(), *raw.values(), halo))


def exchange_all(keep, give):
    sizes = [lax.axis_size(axis) for axis in ("space", "basis")]
    pairs = [(i, i ^ 1) for i in range(sizes[1])]
    part = keep + lax.ppermute(give, "basis", pairs)
    groups = [
        [i * sizes[1] + j for i in range(sizes[0]) for j in range(first, sizes[1], 2)]
        for first in range(2)
    ]
    copies = jnp.broadcast_to(part[None], (len(groups[0]),) + part.shape)
    parts = lax.all_to_all(copies, ("space", "basis"), 0, 0, axis_index_groups=groups)
    own = jnp.sum(parts, axis=0)
    return own, lax.ppermute(own, "basis", pairs)


def finish_kernel(
    row_count, comps, place_ref, own_ref, given_ref, stack_ref, block_ref, coeffs_ref, upper_ref, bad_ref,
    coeffs_scratch, upper_scratch, bad_scratch, block_scratch, sems,
):
    block_cols = upper_ref.shape[0]
    basis_cols = own_ref.shape[1] // 2
    joined = basis_cols + block_cols
    lines, lanes = block_ref.shape[1:]
    odd = place_ref[0] % 2 == 1
    own, given = own_ref[...], given_ref[...]
    total = jnp.concatenate((jnp.where(odd, given, own), jnp.where(odd, own, given)), axis=0)
    total = total / row_count
    gram, first, block_gram = unfold(total, block_cols)

    def times(left, right, right_dim=0):
        return lax.dot_general(
            left, right, (((1,), (right_dim,)), ((), ())),
            precision=exact_precision, preferred_element_type=jnp.float32,
        )

    coeffs = first + (first - times(first, gram))
    image = times(coeffs, gram)
    matrix = block_gram - times(
        jnp.concatenate((coeffs, first - image), axis=1), jnp.concatenate((first, coeffs), axis=1), 1
    )
    coeffs_scratch[...] = coeffs.T
    group_cols = coeffs_ref.shape[0]
    start = pl.multiple_of(place_ref[0] * group_cols, group_cols)
    copies = [
        pltpu.make_async_copy(
            coeffs_scratch.at[pl.ds(start, group_cols)], coeffs_ref, sems.at[comps]
        )
    ]
    copies[0].start()

    row = lax.broadcasted_iota(jnp.int32, (block_cols, block_cols), 0)
    column = lax.broadcasted_iota(jnp.int32, (block_cols, block_cols), 1)
    unit = jnp.where(row == column, 1.0, 0.0)
    pad = jnp.zeros((block_cols, 2 * basis_cols - joined - block_cols), jnp.float32)
    work = jnp.concatenate((-coeffs, unit, matrix, pad), axis=1)
    height = lax.broadcasted_iota(jnp.int32, work.shape, 0)
    width = 4
    for begin in range(0, block_cols, width):
        done, new_rows = [], []
        for step in range(begin, begin + width):
            column_here = jnp.broadcast_to(work[:, joined + step : joined + step + 1], work.shape)
            pivot_row = work[step : step + 1]
            for other_column, other_row, inverse in done:
                entry = other_column[step : step + 1]
                pivot_row = pivot_row - entry * other_row
                column_here = column_here - other_column * (entry * inverse)
            pivot = column_here[step : step + 1]
            inverse = 1.0 / pivot
            done.append((column_here, pivot_row * inverse, inverse))
            new_rows.append(pivot_row * lax.rsqrt(pivot))
        rest = work
        for column_here, scaled, _ in done:
            rest = rest - column_here * scaled
        work = jnp.where(height >= begin + width, rest, work)
        for step, new_row in enumerate(new_rows, begin):
            work = jnp.where(height == step, new_row, work)
    upper = jnp.where(row <= column, work[:, joined : joined + block_cols], 0.0)
    upper_scratch[...] = upper
    kept_enough = jnp.where(row == column, upper * upper * LOSS, block_gram) >= block_gram
    kept_enough = jnp.min(jnp.where(kept_enough, 1.0, 0.0), axis=0, keepdims=True)
    kept_enough = jnp.min(kept_enough, axis=1, keepdims=True)
    bad_scratch[...] = jnp.where(kept_enough > 0.0, 0, 1)
    copies.append(pltpu.make_async_copy(bad_scratch, bad_ref, sems.at[comps + 2]))
    copies[-1].start()
    copies.append(pltpu.make_async_copy(upper_scratch, upper_ref, sems.at[comps + 1]))
    copies[-1].start()
    weights = three_parts(work[:, :joined])
    wide = jnp.concatenate(
        [jnp.concatenate((part, part, part), axis=1) for part in weights], axis=0
    )
    rows = lines // comps
    for comp in range(comps):
        there = pl.ds(comp * rows * lanes, rows * lanes)
        result = jnp.dot(wide, stack_ref[:, there], preferred_element_type=jnp.float32)
        result = result[:block_cols] + result[block_cols : 2 * block_cols] + result[2 * block_cols :]
        for index in range(rows):
            block_scratch[pl.ds(comp * rows + index, block_cols, stride=lines), :] = result[
                :, index * lanes : (index + 1) * lanes
            ]
        part = pl.ds(comp * rows, rows)
        copies.append(
            pltpu.make_async_copy(
                block_scratch.reshape(block_cols, lines, lanes).at[:, part, :],
                block_ref.at[:, part, :],
                sems.at[comp],
            )
        )
        copies[-1].start()
    for copy in copies:
        copy.wait()


def finish(place, halves, stack, row_count, block_cols, group_cols, lines, comps):
    lanes = stack.shape[1] // lines
    basis_cols = halves[0].shape[1] // 2
    return pl.pallas_call(
        functools.partial(finish_kernel, row_count, comps),
        out_shape=(
            f32(block_cols, lines, lanes), f32(group_cols, block_cols), f32(block_cols, block_cols),
            jax.ShapeDtypeStruct((1, 1), jnp.int32),
        ),
        in_specs=[SMEM] + [VMEM] * 3,
        out_specs=(HBM,) * 4,
        scratch_shapes=[
            pltpu.VMEM((basis_cols, block_cols), jnp.float32),
            pltpu.VMEM((block_cols, block_cols), jnp.float32),
            pltpu.VMEM((1, 1), jnp.int32),
            pltpu.VMEM((block_cols * lines, lanes), jnp.float32),
            pltpu.SemaphoreType.DMA((comps + 3,)),
        ],
        compiler_params=SCRATCH,
        name="finish",
    )(place, *kept(*halves, stack))


def stencil_tables(k0_blocks, k0_diag, ke_blocks, mass, velocities, shifts, sample):
    velocity = jnp.take(velocities, sample, axis=0)[0]
    sigma_value = jnp.take(shifts, sample, axis=0)[0]
    center = (k0_diag - sigma_value * mass)[:, :, None] * jnp.eye(3, dtype=jnp.float32)
    tables = k0_blocks - velocity * velocity * ke_blocks
    return tables.at[:, 0].add(center)


def shifted(cells, dim, axis, up):
    extent = cells.shape[dim]
    edge = lax.slice_in_dim(cells, 0, 1, axis=dim) if up else (
        lax.slice_in_dim(cells, extent - 1, extent, axis=dim)
    )
    if axis is None:
        edge = jnp.zeros_like(edge)
    else:
        ends = [(i, i + 1) for i in range(lax.axis_size(axis) - 1)]
        edge = lax.ppermute(edge, axis, [(j, i) for i, j in ends] if up else ends)
    if up:
        return jnp.concatenate((lax.slice_in_dim(cells, 1, extent, axis=dim), edge), axis=dim)
    return jnp.concatenate((edge, lax.slice_in_dim(cells, 0, extent - 1, axis=dim)), axis=dim)


def hold_kernel(*refs):
    *refs, sems = refs
    half = len(refs) // 2
    copies = [
        pltpu.make_async_copy(source, target, sems.at[index])
        for index, (source, target) in enumerate(zip(refs[:half], refs[half:]))
    ]
    for copy in copies:
        copy.start()
    for copy in copies:
        copy.wait()


def hold(*arrays):
    return pl.pallas_call(
        hold_kernel,
        out_shape=[jax.ShapeDtypeStruct(array.shape, array.dtype) for array in arrays],
        in_specs=[HBM] * len(arrays),
        out_specs=[HBM] * len(arrays),
        scratch_shapes=[pltpu.SemaphoreType.DMA((len(arrays),))],
        compiler_params=SCRATCH,
        name="hold",
    )(*far(*arrays))


def careful(arguments):
    x_block, basis, material, k0_blocks, k0_diag, ke_blocks, mass, velocities, shifts, sample = arguments
    x_block, basis, material, k0_blocks, k0_diag, ke_blocks, mass, velocities, shifts = hold(
        x_block, basis, material, jnp.transpose(k0_blocks, (2, 3, 0, 1)), k0_diag.T,
        jnp.transpose(ke_blocks, (2, 3, 0, 1)), mass.T, velocities, shifts,
    )
    k0_blocks, ke_blocks = (jnp.transpose(blocks, (2, 3, 0, 1)) for blocks in (k0_blocks, ke_blocks))
    k0_diag, mass = k0_diag.T, mass.T
    tables = stencil_tables(k0_blocks, k0_diag, ke_blocks, mass, velocities, shifts, sample)
    block_cols, comps, extent_x, _, lanes = x_block.shape
    group_cols = basis.shape[0]
    row_count = float(comps * extent_x * lax.axis_size("space") * basis.shape[3] * lanes)
    fields = jnp.zeros((7, comps, comps) + material.shape, jnp.float32)
    for level in range(tables.shape[0]):
        chosen = (material == level).astype(jnp.float32)
        fields = fields + tables[level][:, :, :, None, None, None] * chosen
    views = [x_block]
    for dim, axis in ((2, "space"), (3, "basis"), (4, None)):
        views += [shifted(x_block, dim, axis, False), shifted(x_block, dim, axis, True)]
    applied = jnp.zeros_like(x_block)
    for offset, view in enumerate(views):
        for comp in range(comps):
            applied = applied + fields[offset, :, comp][None] * view[:, comp : comp + 1]

    count = lax.axis_size("basis")
    place = lax.axis_index("basis")
    pieces = jnp.moveaxis(basis.reshape(basis.shape[:3] + (count, -1, lanes)), 3, 0)
    rows = jnp.zeros((count,) + pieces.shape[1:], jnp.float32)
    for k in range(count):
        piece = lax.dynamic_index_in_dim(pieces, place ^ k, 0, keepdims=False)
        if k:
            piece = lax.ppermute(piece, "basis", [(i, i ^ k) for i in range(count)])
        rows = lax.dynamic_update_index_in_dim(rows, piece, place ^ k, 0)
    rows = rows.reshape((count * group_cols,) + pieces.shape[2:])

    def total(part):
        for axis in ("basis", "space"):
            mask = 1
            while mask < lax.axis_size(axis):
                pairs = [(i, i ^ mask) for i in range(lax.axis_size(axis))]
                part = part + lax.ppermute(part, axis, pairs)
                mask *= 2
        return part / row_count

    running = jnp.zeros((count * group_cols, block_cols), jnp.float32)
    for repeat in range(2):
        coeffs = total(
            jnp.einsum("kcxyz,ncxyz->kn", rows, applied, precision=exact_precision)
        )
        applied = applied - jnp.einsum("kcxyz,kn->ncxyz", rows, coeffs, precision=exact_precision)
        running = running + coeffs
    gram = total(jnp.einsum("ncxyz,mcxyz->nm", applied, applied, precision=exact_precision))
    lower = jnp.linalg.cholesky(gram)
    inverse = lax.linalg.triangular_solve(
        lower, jnp.eye(block_cols, dtype=jnp.float32), left_side=True, lower=True
    )
    block = jnp.einsum("mcxyz,nm->ncxyz", applied, inverse, precision=exact_precision)
    own = lax.dynamic_slice_in_dim(running, place * group_cols, group_cols, axis=0)
    return tuple(hold(block.reshape(block_cols, -1, lanes), own, lower.T))


def shards(
    x_block, basis, material, k0_blocks, k0_diag, ke_blocks, mass, velocities, shifts, sample
):
    arguments = (
        x_block, basis, material, k0_blocks, k0_diag, ke_blocks, mass, velocities, shifts, sample
    )
    block_cols, comps, extent_x, rows, lanes = x_block.shape
    group_cols = basis.shape[0]
    lines = comps * rows
    row_count = float(comps * extent_x * lax.axis_size("space") * basis.shape[3] * lanes)

    place = lax.axis_index("basis").astype(jnp.int32).reshape(1)
    slab = lax.axis_index("space").astype(jnp.int32).reshape(1)
    count = lax.axis_size("basis")
    x_far = x_block.reshape(block_cols * lines, lanes)
    first = partners(count)[1][-1]
    rest = [k for k in range(count) if k != first]
    piece, x_rows = pack(place, basis, x_far, block_cols, [first])
    pieces = {first: piece}
    *packed, material = pack(
        place, basis, material.reshape(rows, lanes), block_cols, rest, x_rows
    )
    pieces.update(zip(rest, packed))
    own = pieces.pop(0)
    got = {}
    for name in ("even", *reversed(partners(count)[0]), "odd"):
        if name == "even":
            got[name] = swap(x_far, "space", 0)
        elif name == "odd":
            got[name] = swap(x_far, "space", 1)
        else:
            piece = lax.ppermute(pieces[name], "basis", [(i, i ^ name) for i in range(count)])
            got[name] = piece.reshape(-1, lanes)
    fields, applied, own = ahead(
        sample, velocities, shifts, k0_blocks, ke_blocks, k0_diag, mass, material, x_rows,
        own.reshape(-1, lanes), comps,
    )
    split = {0: own}
    first, *rest = reversed(partners(count)[1])
    applied, split[first] = add_edges(
        place, fields, applied, {first: got.pop(first)}, comps, group_cols, EARLY
    )
    applied = add_side(slab, fields, applied, got.pop("even"), comps, "even")
    for k in rest:
        applied, split[k] = add_edges(
            place, fields, applied, {k: got.pop(k)}, comps, group_cols, None
        )
    stack, keep, give = sums(place, slab, fields, applied, got.pop("odd"), split, got, comps)
    halves = exchange_all(keep, give)
    block, coeffs, upper, bad = finish(
        place, halves, stack, row_count, block_cols, group_cols, lines, comps
    )
    block, coeffs, upper = lax.while_loop(
        lambda state: state[0] > 0,
        lambda state: (jnp.zeros_like(state[0]), careful(arguments)),
        (bad[0, 0], (block, coeffs, upper)),
    )[1]
    return block.reshape(x_block.shape), coeffs, upper


def solution(mesh):
    in_specs = (
        P(None, None, "space", "basis", None),
        P("basis", None, "space", None, None),
        P("space", "basis", None),
        P(),
        P(),
        P(),
        P(),
        P(),
        P(),
        P(),
    )
    out_specs = (P(None, None, "space", "basis", None), P("basis", None), P())
    return jax.shard_map(shards, mesh=mesh, in_specs=in_specs, out_specs=out_specs, check_vma=False)
```

```python
import functools

import jax
import jax.numpy as jnp
from jax import lax
from jax.experimental import pallas as pl
from jax.experimental.pallas import tpu as pltpu
from jax.sharding import PartitionSpec as P

exact_precision = lax.Precision.HIGHEST
VMEM = pl.BlockSpec(memory_space=pltpu.VMEM)
SMEM = pl.BlockSpec(memory_space=pltpu.SMEM)
HBM = pl.BlockSpec(memory_space=pltpu.HBM)
LOSS = 256.0
EARLY = pl.CostEstimate(flops=10**9, bytes_accessed=10**6, transcendentals=0)
NEXT = pl.CostEstimate(flops=3 * 10**8, bytes_accessed=10**6, transcendentals=0)
LATE = pl.CostEstimate(flops=10**6, bytes_accessed=10**6, transcendentals=0)
SCRATCH = pltpu.CompilerParams(vmem_limit_bytes=8 * 2**20)


def f32(*shape):
    return jax.ShapeDtypeStruct(shape, jnp.float32)


def near(*shape, dtype=jnp.float32):
    return pltpu.VMEM(shape, dtype)


def kept(*arrays):
    return [pltpu.with_memory_space_constraint(array, pltpu.VMEM) for array in arrays]


def far(*arrays):
    return [pltpu.with_memory_space_constraint(array, pltpu.HBM) for array in arrays]


def swap(values, axis, first):
    pairs = [(i, i + 1) for i in range(first, lax.axis_size(axis) - 1, 2)]
    return lax.ppermute(values, axis, pairs + [(j, i) for i, j in pairs])


def partners(count):
    return range(1, count), [k for k in range(1, count) if k & (k + 1) == 0]


def pack_kernel(comps, place_ref, basis_ref, x_ref, material_ref, *refs):
    *piece_refs, x_out_ref, material_out_ref, sems = refs
    count = len(piece_refs)
    tiles, _, rows, lanes = basis_ref.shape
    block_cols = x_ref.shape[0] // (comps * rows)
    place = place_ref[0]
    x_copy = pltpu.make_async_copy(x_ref, x_out_ref, sems.at[count])
    x_copy.start()
    copies = [pltpu.make_async_copy(material_ref, material_out_ref, sems.at[count + 1])]
    for k in reversed(range(count)):
        copies.append(
            pltpu.make_async_copy(
                basis_ref.at[:, place ^ k], piece_refs[k].at[pl.ds(0, tiles)], sems.at[k]
            )
        )
    for copy in copies:
        copy.start()
    x_copy.wait()
    for comp in range(comps):
        first, last = (
            x_out_ref[pl.ds(comp * rows + row, block_cols, stride=comps * rows), :]
            for row in (0, rows - 1)
        )
        for k in partners(count)[1]:
            edge = jnp.where((place ^ k) > place, last, first)
            for part in range(block_cols // rows):
                piece_refs[k][tiles + comp * (block_cols // rows) + part] = edge[
                    part * rows : (part + 1) * rows
                ]
    for copy in copies:
        copy.wait()


def pack(place, basis, x_rows, material, block_cols):
    group_cols, comps, _, full_y, lanes = basis.shape
    count = lax.axis_size("basis")
    rows = full_y // count
    tiles = group_cols * comps
    edge_tiles = block_cols * comps // rows
    pieces = [
        near(tiles + (edge_tiles if k in partners(count)[1] else 0), rows, lanes)
        for k in range(count)
    ]
    return pl.pallas_call(
        functools.partial(pack_kernel, comps),
        out_shape=(*pieces, near(*x_rows.shape), near(*material.shape, dtype=jnp.int32)),
        in_specs=[SMEM, HBM, HBM, HBM],
        out_specs=(VMEM,) * (count + 2),
        scratch_shapes=[pltpu.SemaphoreType.DMA((count + 2,))],
        compiler_params=SCRATCH,
        name="pack",
    )(place, *far(basis.reshape(tiles, count, rows, lanes), x_rows, material))


def three_parts(values):
    high = values.astype(jnp.bfloat16)
    rest = values - high.astype(jnp.float32)
    middle = rest.astype(jnp.bfloat16)
    low = (rest - middle.astype(jnp.float32)).astype(jnp.bfloat16)
    return high, middle, low


def line_of(ref, comp, row, comps, rows, block_cols):
    return ref[pl.ds(comp * rows + row, block_cols, stride=comps * rows), :]


def ahead_kernel(
    sample_ref, *refs
):
    far_refs, refs = refs[:6], refs[6:]
    material_ref, x_ref, own_ref, fields_ref, applied_ref, stack_ref, *near_refs, sems = refs
    velocities_ref, shifts_ref, k0_ref, ke_ref, diag_ref, mass_ref = near_refs
    copies = [
        pltpu.make_async_copy(source, target, sems.at[index])
        for index, (source, target) in enumerate(zip(far_refs, near_refs))
    ]
    for copy in copies:
        copy.start()
    group_cols = stack_ref.shape[0] // 3
    split_lines(
        own_ref, stack_ref, applied_ref.shape[0], group_cols, [i * group_cols for i in range(3)]
    )
    for copy in copies:
        copy.wait()
    comps, _, levels, offsets = k0_ref.shape
    rows, lanes = material_ref.shape
    lines = comps * rows
    block_cols = x_ref.shape[0] // lines
    velocity = velocities_ref[sample_ref[0]]
    sigma = shifts_ref[sample_ref[0]]
    entry_rows = fields_ref.shape[1]
    stride = entry_rows // (comps * comps)
    gap = jnp.zeros((levels, stride - offsets), jnp.float32)
    wide = []
    for out in range(comps):
        for comp in range(comps):
            wide += [k0_ref[out, comp] - velocity * velocity * ke_ref[out, comp], gap]
    wide.append(jnp.zeros((levels, lanes - entry_rows), jnp.float32))
    table = jnp.concatenate(wide, axis=1).T[:entry_rows]
    entry = lax.broadcasted_iota(jnp.int32, table.shape, 0)
    for comp in range(comps):
        centre = diag_ref[comp : comp + 1, :] - sigma * mass_ref[comp : comp + 1, :]
        table = table + jnp.where(entry == comp * (comps + 1) * stride, centre, 0.0)

    lane = lax.broadcasted_iota(jnp.int32, (block_cols, lanes), 1)
    level = lax.broadcasted_iota(jnp.int32, (levels, lanes), 0)
    for row in range(rows):
        chosen = jnp.broadcast_to(material_ref[row : row + 1, :], (levels, lanes)) == level
        fields = jnp.dot(
            table, chosen.astype(jnp.float32),
            precision=exact_precision, preferred_element_type=jnp.float32,
        )
        fields_ref[row] = fields
        sums = [None] * comps
        for comp in range(comps):
            centre = line_of(x_ref, comp, row, comps, rows, block_cols)
            views = {
                0: centre,
                5: jnp.where(lane == 0, 0.0, pltpu.roll(centre, 1, 1)),
                6: jnp.where(lane == lanes - 1, 0.0, pltpu.roll(centre, lanes - 1, 1)),
            }
            if row > 0:
                views[3] = line_of(x_ref, comp, row - 1, comps, rows, block_cols)
            if row < rows - 1:
                views[4] = line_of(x_ref, comp, row + 1, comps, rows, block_cols)
            for offset, view in views.items():
                for out in range(comps):
                    place = (out * comps + comp) * stride + offset
                    term = fields[place : place + 1, :] * view
                    sums[out] = term if sums[out] is None else sums[out] + term
        for out in range(comps):
            applied_ref[out * rows + row] = sums[out]


def ahead(sample, velocities, shifts, k0, ke, diag, mass, material, x_rows, own, comps):
    rows, lanes = material.shape
    lines = comps * rows
    stride = -(-k0.shape[1] // 8) * 8
    k0, ke = (jnp.transpose(blocks, (2, 3, 0, 1)) for blocks in (k0, ke))
    tables = far(velocities, shifts, k0, ke, diag.T, mass.T)
    return pl.pallas_call(
        ahead_kernel,
        out_shape=(
            near(rows, comps * comps * stride, lanes),
            near(lines, x_rows.shape[0] // lines, lanes),
            near(3 * own.shape[0] // lines, lines * lanes, dtype=jnp.bfloat16),
        ),
        in_specs=[SMEM] + [HBM] * 6 + [VMEM] * 3,
        out_specs=(VMEM,) * 3,
        scratch_shapes=[
            (pltpu.SMEM if array.ndim == 1 else pltpu.VMEM)(array.shape, jnp.float32)
            for array in tables
        ] + [pltpu.SemaphoreType.DMA((len(tables),))],
        compiler_params=SCRATCH,
        name="ahead",
    )(sample, *tables, *kept(material, x_rows, own))


def side_terms(field_row, swapped, side, out, comp, comps):
    stride = field_row.shape[0] // (comps * comps)
    begin = (out * comps + comp) * stride
    below, above = field_row[begin + 1 : begin + 2], field_row[begin + 2 : begin + 3]
    other = (below, above) if side == "even" else (above, below)
    return jnp.where(swapped, *other)


def side_kernel(comps, side, slab_ref, fields_ref, applied_ref, halo_ref, out_ref):
    lines, block_cols, _ = applied_ref.shape
    rows = lines // comps
    swapped = slab_ref[0] % 2 == 1
    for row in range(rows):
        field_row = fields_ref[row]
        views = [line_of(halo_ref, comp, row, comps, rows, block_cols) for comp in range(comps)]
        for out in range(comps):
            total = applied_ref[out * rows + row]
            for comp, view in enumerate(views):
                total = total + side_terms(field_row, swapped, side, out, comp, comps) * view
            out_ref[out * rows + row] = total


def add_side(slab, fields, applied, halo, comps, side, weight):
    return pl.pallas_call(
        functools.partial(side_kernel, comps, side),
        out_shape=near(*applied.shape),
        in_specs=[SMEM] + [VMEM] * 3,
        out_specs=VMEM,
        compiler_params=SCRATCH,
        cost_estimate=weight,
        name="side",
    )(slab, *kept(fields, applied, halo))


def split_lines(piece_ref, stack_ref, lines, group_cols, begins):
    lanes = piece_ref.shape[1]
    for line in range(lines):
        values = piece_ref[pl.ds(line, group_cols, stride=lines), :]
        for begin, part in zip(begins, three_parts(values)):
            stack_ref[pl.ds(begin, group_cols), pl.ds(line * lanes, lanes)] = part


def edges_kernel(comps, ks, group_cols, place_ref, fields_ref, applied_ref, *refs):
    piece_refs, out_ref, parts_refs = refs[: len(ks)], refs[len(ks)], refs[len(ks) + 1 :]
    lines, block_cols, lanes = applied_ref.shape
    rows = lines // comps
    stride = fields_ref.shape[1] // (comps * comps)
    place = place_ref[0]

    def edge(comp, step):
        result = jnp.zeros((block_cols, lanes), jnp.float32)
        for k, ref in zip(ks, piece_refs):
            begin = ref.shape[0] - (comps - comp) * block_cols
            here = (place ^ k) == place + step
            result = jnp.where(here, ref[pl.ds(begin, block_cols), :], result)
        return result

    out_ref[...] = applied_ref[...]
    for row, offset, step in ((0, 3, -1), (rows - 1, 4, 1)):
        field_row = fields_ref[row]
        views = [edge(comp, step) for comp in range(comps)]
        for out in range(comps):
            total = out_ref[out * rows + row]
            for comp, view in enumerate(views):
                entry = (out * comps + comp) * stride + offset
                total = total + field_row[entry : entry + 1] * view
            out_ref[out * rows + row] = total
    for piece_ref, parts_ref in zip(piece_refs, parts_refs):
        split_lines(piece_ref, parts_ref, lines, group_cols, [i * group_cols for i in range(3)])


def add_edges(place, fields, applied, pieces, comps, group_cols, weight):
    lines, _, lanes = applied.shape
    parts = near(3 * group_cols, lines * lanes, dtype=jnp.bfloat16)
    return pl.pallas_call(
        functools.partial(edges_kernel, comps, tuple(pieces), group_cols),
        out_shape=(near(*applied.shape),) + (parts,) * len(pieces),
        in_specs=[SMEM] + [VMEM] * (2 + len(pieces)),
        out_specs=(VMEM,) * (1 + len(pieces)),
        compiler_params=SCRATCH,
        cost_estimate=weight,
        name="edges",
    )(place, *kept(fields, applied, *pieces.values()))


def fold(total, basis_cols, block_cols, lanes):
    half = basis_cols // 2
    row = lax.broadcasted_iota(jnp.int32, (half, half), 0)
    column = lax.broadcasted_iota(jnp.int32, (half, half), 1)
    last = total[half:basis_cols, half:basis_cols]
    shared = jnp.where(row >= column, total[:half, :half], last)
    diagonal = jnp.sum(jnp.where(row == column, last, 0.0), axis=1, keepdims=True)
    below = total[basis_cols:]
    first = jnp.concatenate((below[:, :half], below[:, half:basis_cols]), axis=0)
    rest = jnp.zeros((half - block_cols, block_cols), jnp.float32)
    block = jnp.concatenate((below[:, basis_cols:], rest), axis=0)
    pad = jnp.zeros((half, lanes - 3 * half - block_cols - 1), jnp.float32)
    return jnp.concatenate(
        (shared, total[:half, half:basis_cols], first, block, diagonal, pad), axis=1
    )


def unfold(folded, block_cols):
    half = folded.shape[0]
    row = lax.broadcasted_iota(jnp.int32, (half, half), 0)
    column = lax.broadcasted_iota(jnp.int32, (half, half), 1)
    shared, across = folded[:, :half], folded[:, half : 2 * half]
    turned = shared.T
    start = jnp.where(row >= column, shared, turned)
    end = jnp.where(row < column, shared, turned)
    diagonal = folded[:, 3 * half + block_cols : 3 * half + block_cols + 1]
    end = jnp.where(row == column, diagonal, end)
    gram = jnp.concatenate(
        (jnp.concatenate((start, across), axis=1), jnp.concatenate((across.T, end), axis=1)), axis=0
    )
    first = folded[:, 2 * half : 3 * half]
    first = jnp.concatenate((first[:block_cols], first[block_cols : 2 * block_cols]), axis=1)
    return gram, first, folded[:block_cols, 3 * half : 3 * half + block_cols]


def sums_kernel(
    split, raw, place_ref, applied_ref, *refs
):
    *refs, stack_ref, keep_ref, give_ref = refs
    lines, block_cols, lanes = applied_ref.shape
    group_cols = refs[0].shape[0] // 3
    basis_cols = (len(split) + len(raw)) * group_cols
    joined = basis_cols + block_cols
    place = place_ref[0]
    for k, ref in zip(split + raw, refs):
        begin = pl.multiple_of((place ^ k) * group_cols, group_cols)
        begins = [index * joined + begin for index in range(3)]
        if k in split:
            for index in range(3):
                stack_ref[pl.ds(begins[index], group_cols), :] = ref[
                    pl.ds(index * group_cols, group_cols), :
                ]
        else:
            split_lines(ref, stack_ref, lines, group_cols, begins)
    for line in range(lines):
        for index, part in enumerate(three_parts(applied_ref[line])):
            there = pl.ds(index * joined + basis_cols, block_cols)
            stack_ref[there, pl.ds(line * lanes, lanes)] = part

    stack = stack_ref[...]
    products = lax.dot_general(
        stack, stack, (((1,), (1,)), ((), ())), preferred_element_type=jnp.float32
    )
    wide = products[:joined] + products[joined : 2 * joined] + products[2 * joined :]
    total = wide[:, :joined] + wide[:, joined : 2 * joined] + wide[:, 2 * joined :]
    folded = fold(total, basis_cols, block_cols, keep_ref.shape[1])
    half = keep_ref.shape[0]
    odd = place % 2 == 1
    keep_ref[...] = jnp.where(odd, folded[half:], folded[:half])
    give_ref[...] = jnp.where(odd, folded[:half], folded[half:])


def sums(place, applied, split, raw):
    lines, block_cols, lanes = applied.shape
    basis_cols = (len(split) + len(raw)) * (split[0].shape[0] // 3)
    joined = basis_cols + block_cols
    return pl.pallas_call(
        functools.partial(sums_kernel, tuple(split), tuple(raw)),
        out_shape=(
            near(3 * joined, lines * lanes, dtype=jnp.bfloat16),
            near(basis_cols // 4, 2 * basis_cols),
            near(basis_cols // 4, 2 * basis_cols),
        ),
        in_specs=[SMEM] + [VMEM] * (1 + len(split) + len(raw)),
        out_specs=(VMEM,) * 3,
        compiler_params=SCRATCH,
        name="sums",
    )(place, *kept(applied, *split.values(), *raw.values()))


def exchange_all(keep, give):
    sizes = [lax.axis_size(axis) for axis in ("space", "basis")]
    pairs = [(i, i ^ 1) for i in range(sizes[1])]
    part = keep + lax.ppermute(give, "basis", pairs)
    groups = [
        [i * sizes[1] + j for i in range(sizes[0]) for j in range(first, sizes[1], 2)]
        for first in range(2)
    ]
    copies = jnp.broadcast_to(part[None], (len(groups[0]),) + part.shape)
    parts = lax.all_to_all(copies, ("space", "basis"), 0, 0, axis_index_groups=groups)
    own = jnp.sum(parts, axis=0)
    return own, lax.ppermute(own, "basis", pairs)


def finish_kernel(
    row_count, comps, place_ref, own_ref, given_ref, stack_ref, block_ref, coeffs_ref, upper_ref, bad_ref,
    coeffs_scratch, upper_scratch, bad_scratch, block_scratch, sems,
):
    block_cols = upper_ref.shape[0]
    basis_cols = own_ref.shape[1] // 2
    joined = basis_cols + block_cols
    lines, lanes = block_ref.shape[1:]
    odd = place_ref[0] % 2 == 1
    own, given = own_ref[...], given_ref[...]
    total = jnp.concatenate((jnp.where(odd, given, own), jnp.where(odd, own, given)), axis=0)
    total = total / row_count
    gram, first, block_gram = unfold(total, block_cols)

    def times(left, right, right_dim=0):
        return lax.dot_general(
            left, right, (((1,), (right_dim,)), ((), ())),
            precision=exact_precision, preferred_element_type=jnp.float32,
        )

    coeffs = first + (first - times(first, gram))
    image = times(coeffs, gram)
    matrix = block_gram - times(
        jnp.concatenate((coeffs, first - image), axis=1), jnp.concatenate((first, coeffs), axis=1), 1
    )
    coeffs_scratch[...] = coeffs.T
    group_cols = coeffs_ref.shape[0]
    start = pl.multiple_of(place_ref[0] * group_cols, group_cols)
    copies = [
        pltpu.make_async_copy(
            coeffs_scratch.at[pl.ds(start, group_cols)], coeffs_ref, sems.at[comps]
        )
    ]
    copies[0].start()

    row = lax.broadcasted_iota(jnp.int32, (block_cols, block_cols), 0)
    column = lax.broadcasted_iota(jnp.int32, (block_cols, block_cols), 1)
    unit = jnp.where(row == column, 1.0, 0.0)
    pad = jnp.zeros((block_cols, 2 * basis_cols - joined - block_cols), jnp.float32)
    work = jnp.concatenate((-coeffs, unit, matrix, pad), axis=1)
    height = lax.broadcasted_iota(jnp.int32, work.shape, 0)
    width = 4
    for begin in range(0, block_cols, width):
        done, new_rows = [], []
        for step in range(begin, begin + width):
            column_here = jnp.broadcast_to(work[:, joined + step : joined + step + 1], work.shape)
            pivot_row = work[step : step + 1]
            for other_column, other_row, inverse in done:
                entry = other_column[step : step + 1]
                pivot_row = pivot_row - entry * other_row
                column_here = column_here - other_column * (entry * inverse)
            pivot = column_here[step : step + 1]
            inverse = 1.0 / pivot
            done.append((column_here, pivot_row * inverse, inverse))
            new_rows.append(pivot_row * lax.rsqrt(pivot))
        rest = work
        for column_here, scaled, _ in done:
            rest = rest - column_here * scaled
        work = jnp.where(height >= begin + width, rest, work)
        for step, new_row in enumerate(new_rows, begin):
            work = jnp.where(height == step, new_row, work)
    upper = jnp.where(row <= column, work[:, joined : joined + block_cols], 0.0)
    upper_scratch[...] = upper
    kept_enough = jnp.where(row == column, upper * upper * LOSS, block_gram) >= block_gram
    kept_enough = jnp.min(jnp.where(kept_enough, 1.0, 0.0), axis=0, keepdims=True)
    kept_enough = jnp.min(kept_enough, axis=1, keepdims=True)
    bad_scratch[...] = jnp.where(kept_enough > 0.0, 0, 1)
    copies.append(pltpu.make_async_copy(bad_scratch, bad_ref, sems.at[comps + 2]))
    copies[-1].start()
    copies.append(pltpu.make_async_copy(upper_scratch, upper_ref, sems.at[comps + 1]))
    copies[-1].start()
    weights = three_parts(work[:, :joined])
    wide = jnp.concatenate(
        [jnp.concatenate((part, part, part), axis=1) for part in weights], axis=0
    )
    rows = lines // comps
    for comp in range(comps):
        there = pl.ds(comp * rows * lanes, rows * lanes)
        result = jnp.dot(wide, stack_ref[:, there], preferred_element_type=jnp.float32)
        result = result[:block_cols] + result[block_cols : 2 * block_cols] + result[2 * block_cols :]
        for index in range(rows):
            block_scratch[pl.ds(comp * rows + index, block_cols, stride=lines), :] = result[
                :, index * lanes : (index + 1) * lanes
            ]
        part = pl.ds(comp * rows, rows)
        copies.append(
            pltpu.make_async_copy(
                block_scratch.reshape(block_cols, lines, lanes).at[:, part, :],
                block_ref.at[:, part, :],
                sems.at[comp],
            )
        )
        copies[-1].start()
    for copy in copies:
        copy.wait()


def finish(place, halves, stack, row_count, block_cols, group_cols, lines, comps):
    lanes = stack.shape[1] // lines
    basis_cols = halves[0].shape[1] // 2
    return pl.pallas_call(
        functools.partial(finish_kernel, row_count, comps),
        out_shape=(
            f32(block_cols, lines, lanes), f32(group_cols, block_cols), f32(block_cols, block_cols),
            jax.ShapeDtypeStruct((1, 1), jnp.int32),
        ),
        in_specs=[SMEM] + [VMEM] * 3,
        out_specs=(HBM,) * 4,
        scratch_shapes=[
            pltpu.VMEM((basis_cols, block_cols), jnp.float32),
            pltpu.VMEM((block_cols, block_cols), jnp.float32),
            pltpu.VMEM((1, 1), jnp.int32),
            pltpu.VMEM((block_cols * lines, lanes), jnp.float32),
            pltpu.SemaphoreType.DMA((comps + 3,)),
        ],
        compiler_params=SCRATCH,
        name="finish",
    )(place, *kept(*halves, stack))


def stencil_tables(k0_blocks, k0_diag, ke_blocks, mass, velocities, shifts, sample):
    velocity = jnp.take(velocities, sample, axis=0)[0]
    sigma_value = jnp.take(shifts, sample, axis=0)[0]
    center = (k0_diag - sigma_value * mass)[:, :, None] * jnp.eye(3, dtype=jnp.float32)
    tables = k0_blocks - velocity * velocity * ke_blocks
    return tables.at[:, 0].add(center)


def shifted(cells, dim, axis, up):
    extent = cells.shape[dim]
    edge = lax.slice_in_dim(cells, 0, 1, axis=dim) if up else (
        lax.slice_in_dim(cells, extent - 1, extent, axis=dim)
    )
    if axis is None:
        edge = jnp.zeros_like(edge)
    else:
        ends = [(i, i + 1) for i in range(lax.axis_size(axis) - 1)]
        edge = lax.ppermute(edge, axis, [(j, i) for i, j in ends] if up else ends)
    if up:
        return jnp.concatenate((lax.slice_in_dim(cells, 1, extent, axis=dim), edge), axis=dim)
    return jnp.concatenate((edge, lax.slice_in_dim(cells, 0, extent - 1, axis=dim)), axis=dim)


def hold_kernel(*refs):
    *refs, sems = refs
    half = len(refs) // 2
    copies = [
        pltpu.make_async_copy(source, target, sems.at[index])
        for index, (source, target) in enumerate(zip(refs[:half], refs[half:]))
    ]
    for copy in copies:
        copy.start()
    for copy in copies:
        copy.wait()


def hold(*arrays):
    return pl.pallas_call(
        hold_kernel,
        out_shape=[jax.ShapeDtypeStruct(array.shape, array.dtype) for array in arrays],
        in_specs=[HBM] * len(arrays),
        out_specs=[HBM] * len(arrays),
        scratch_shapes=[pltpu.SemaphoreType.DMA((len(arrays),))],
        compiler_params=SCRATCH,
        name="hold",
    )(*far(*arrays))


def careful(arguments):
    x_block, basis, material, k0_blocks, k0_diag, ke_blocks, mass, velocities, shifts, sample = arguments
    x_block, basis, material, k0_blocks, k0_diag, ke_blocks, mass, velocities, shifts = hold(
        x_block, basis, material, jnp.transpose(k0_blocks, (2, 3, 0, 1)), k0_diag.T,
        jnp.transpose(ke_blocks, (2, 3, 0, 1)), mass.T, velocities, shifts,
    )
    k0_blocks, ke_blocks = (jnp.transpose(blocks, (2, 3, 0, 1)) for blocks in (k0_blocks, ke_blocks))
    k0_diag, mass = k0_diag.T, mass.T
    tables = stencil_tables(k0_blocks, k0_diag, ke_blocks, mass, velocities, shifts, sample)
    block_cols, comps, extent_x, _, lanes = x_block.shape
    group_cols = basis.shape[0]
    row_count = float(comps * extent_x * lax.axis_size("space") * basis.shape[3] * lanes)
    fields = jnp.zeros((7, comps, comps) + material.shape, jnp.float32)
    for level in range(tables.shape[0]):
        chosen = (material == level).astype(jnp.float32)
        fields = fields + tables[level][:, :, :, None, None, None] * chosen
    views = [x_block]
    for dim, axis in ((2, "space"), (3, "basis"), (4, None)):
        views += [shifted(x_block, dim, axis, False), shifted(x_block, dim, axis, True)]
    applied = jnp.zeros_like(x_block)
    for offset, view in enumerate(views):
        for comp in range(comps):
            applied = applied + fields[offset, :, comp][None] * view[:, comp : comp + 1]

    count = lax.axis_size("basis")
    place = lax.axis_index("basis")
    pieces = jnp.moveaxis(basis.reshape(basis.shape[:3] + (count, -1, lanes)), 3, 0)
    rows = jnp.zeros((count,) + pieces.shape[1:], jnp.float32)
    for k in range(count):
        piece = lax.dynamic_index_in_dim(pieces, place ^ k, 0, keepdims=False)
        if k:
            piece = lax.ppermute(piece, "basis", [(i, i ^ k) for i in range(count)])
        rows = lax.dynamic_update_index_in_dim(rows, piece, place ^ k, 0)
    rows = rows.reshape((count * group_cols,) + pieces.shape[2:])

    def total(part):
        for axis in ("basis", "space"):
            mask = 1
            while mask < lax.axis_size(axis):
                pairs = [(i, i ^ mask) for i in range(lax.axis_size(axis))]
                part = part + lax.ppermute(part, axis, pairs)
                mask *= 2
        return part / row_count

    running = jnp.zeros((count * group_cols, block_cols), jnp.float32)
    for repeat in range(2):
        coeffs = total(
            jnp.einsum("kcxyz,ncxyz->kn", rows, applied, precision=exact_precision)
        )
        applied = applied - jnp.einsum("kcxyz,kn->ncxyz", rows, coeffs, precision=exact_precision)
        running = running + coeffs
    gram = total(jnp.einsum("ncxyz,mcxyz->nm", applied, applied, precision=exact_precision))
    lower = jnp.linalg.cholesky(gram)
    inverse = lax.linalg.triangular_solve(
        lower, jnp.eye(block_cols, dtype=jnp.float32), left_side=True, lower=True
    )
    block = jnp.einsum("mcxyz,nm->ncxyz", applied, inverse, precision=exact_precision)
    own = lax.dynamic_slice_in_dim(running, place * group_cols, group_cols, axis=0)
    return tuple(hold(block.reshape(block_cols, -1, lanes), own, lower.T))


def shards(
    x_block, basis, material, k0_blocks, k0_diag, ke_blocks, mass, velocities, shifts, sample
):
    arguments = (
        x_block, basis, material, k0_blocks, k0_diag, ke_blocks, mass, velocities, shifts, sample
    )
    block_cols, comps, extent_x, rows, lanes = x_block.shape
    group_cols = basis.shape[0]
    lines = comps * rows
    row_count = float(comps * extent_x * lax.axis_size("space") * basis.shape[3] * lanes)

    place = lax.axis_index("basis").astype(jnp.int32).reshape(1)
    slab = lax.axis_index("space").astype(jnp.int32).reshape(1)
    count = lax.axis_size("basis")
    x_far = x_block.reshape(block_cols * lines, lanes)
    own, *pieces, x_rows, material = pack(place, basis, x_far, material.reshape(rows, lanes), block_cols)
    got = {}
    for name in ("even", *reversed(partners(count)[0]), "odd"):
        if name == "even":
            got[name] = swap(x_far, "space", 0)
        elif name == "odd":
            got[name] = swap(x_far, "space", 1)
        else:
            piece = lax.ppermute(pieces[name - 1], "basis", [(i, i ^ name) for i in range(count)])
            got[name] = piece.reshape(-1, lanes)
    fields, applied, own = ahead(
        sample, velocities, shifts, k0_blocks, ke_blocks, k0_diag, mass, material, x_rows,
        own.reshape(-1, lanes), comps,
    )
    split = {0: own}
    first, *rest = reversed(partners(count)[1])
    applied, split[first] = add_edges(
        place, fields, applied, {first: got.pop(first)}, comps, group_cols, EARLY
    )
    applied = add_side(slab, fields, applied, got.pop("even"), comps, "even", NEXT)
    for k in rest:
        applied, split[k] = add_edges(
            place, fields, applied, {k: got.pop(k)}, comps, group_cols, None
        )
    applied = add_side(slab, fields, applied, got.pop("odd"), comps, "odd", LATE)
    stack, keep, give = sums(place, applied, split, got)
    halves = exchange_all(keep, give)
    block, coeffs, upper, bad = finish(
        place, halves, stack, row_count, block_cols, group_cols, lines, comps
    )
    block, coeffs, upper = lax.while_loop(
        lambda state: state[0] > 0,
        lambda state: (jnp.zeros_like(state[0]), careful(arguments)),
        (bad[0, 0], (block, coeffs, upper)),
    )[1]
    return block.reshape(x_block.shape), coeffs, upper


def solution(mesh):
    in_specs = (
        P(None, None, "space", "basis", None),
        P("basis", None, "space", None, None),
        P("space", "basis", None),
        P(),
        P(),
        P(),
        P(),
        P(),
        P(),
        P(),
    )
    out_specs = (P(None, None, "space", "basis", None), P("basis", None), P())
    return jax.shard_map(shards, mesh=mesh, in_specs=in_specs, out_specs=out_specs, check_vma=False)
```

```python
import functools

import jax
import jax.numpy as jnp
from jax import lax
from jax.experimental import pallas as pl
from jax.experimental.pallas import tpu as pltpu
from jax.sharding import PartitionSpec as P

exact_precision = lax.Precision.HIGHEST
VMEM = pl.BlockSpec(memory_space=pltpu.VMEM)
SMEM = pl.BlockSpec(memory_space=pltpu.SMEM)
HBM = pl.BlockSpec(memory_space=pltpu.HBM)
LOSS = 256.0
EARLY = pl.CostEstimate(flops=10**9, bytes_accessed=10**6, transcendentals=0)
NEXT = pl.CostEstimate(flops=3 * 10**8, bytes_accessed=10**6, transcendentals=0)
LATE = pl.CostEstimate(flops=10**6, bytes_accessed=10**6, transcendentals=0)
SCRATCH = pltpu.CompilerParams(vmem_limit_bytes=8 * 2**20)


def f32(*shape):
    return jax.ShapeDtypeStruct(shape, jnp.float32)


def near(*shape, dtype=jnp.float32):
    return pltpu.VMEM(shape, dtype)


def kept(*arrays):
    return [pltpu.with_memory_space_constraint(array, pltpu.VMEM) for array in arrays]


def far(*arrays):
    return [pltpu.with_memory_space_constraint(array, pltpu.HBM) for array in arrays]


def swap(values, axis, first):
    pairs = [(i, i + 1) for i in range(first, lax.axis_size(axis) - 1, 2)]
    return lax.ppermute(values, axis, pairs + [(j, i) for i, j in pairs])


def partners(count):
    return range(1, count), [k for k in range(1, count) if k & (k + 1) == 0]


def pack_kernel(comps, place_ref, basis_ref, x_ref, material_ref, *refs):
    *piece_refs, x_out_ref, material_out_ref, sems = refs
    count = len(piece_refs)
    tiles, _, rows, lanes = basis_ref.shape
    block_cols = x_ref.shape[0] // (comps * rows)
    place = place_ref[0]
    x_copy = pltpu.make_async_copy(x_ref, x_out_ref, sems.at[count])
    x_copy.start()
    copies = [pltpu.make_async_copy(material_ref, material_out_ref, sems.at[count + 1])]
    for k in reversed(range(count)):
        copies.append(
            pltpu.make_async_copy(
                basis_ref.at[:, place ^ k], piece_refs[k].at[pl.ds(0, tiles)], sems.at[k]
            )
        )
    for copy in copies:
        copy.start()
    x_copy.wait()
    for comp in range(comps):
        first, last = (
            x_out_ref[pl.ds(comp * rows + row, block_cols, stride=comps * rows), :]
            for row in (0, rows - 1)
        )
        for k in partners(count)[1]:
            edge = jnp.where((place ^ k) > place, last, first)
            for part in range(block_cols // rows):
                piece_refs[k][tiles + comp * (block_cols // rows) + part] = edge[
                    part * rows : (part + 1) * rows
                ]
    for copy in copies:
        copy.wait()


def pack(place, basis, x_rows, material, block_cols):
    group_cols, comps, _, full_y, lanes = basis.shape
    count = lax.axis_size("basis")
    rows = full_y // count
    tiles = group_cols * comps
    edge_tiles = block_cols * comps // rows
    pieces = [
        near(tiles + (edge_tiles if k in partners(count)[1] else 0), rows, lanes)
        for k in range(count)
    ]
    return pl.pallas_call(
        functools.partial(pack_kernel, comps),
        out_shape=(*pieces, near(*x_rows.shape), near(*material.shape, dtype=jnp.int32)),
        in_specs=[SMEM, HBM, HBM, HBM],
        out_specs=(VMEM,) * (count + 2),
        scratch_shapes=[pltpu.SemaphoreType.DMA((count + 2,))],
        compiler_params=SCRATCH,
        name="pack",
    )(place, *far(basis.reshape(tiles, count, rows, lanes), x_rows, material))


def three_parts(values):
    high = values.astype(jnp.bfloat16)
    rest = values - high.astype(jnp.float32)
    middle = rest.astype(jnp.bfloat16)
    low = (rest - middle.astype(jnp.float32)).astype(jnp.bfloat16)
    return high, middle, low


def line_of(ref, comp, row, comps, rows, block_cols):
    return ref[pl.ds(comp * rows + row, block_cols, stride=comps * rows), :]


def ahead_kernel(
    sample_ref, *refs
):
    far_refs, refs = refs[:6], refs[6:]
    material_ref, x_ref, own_ref, fields_ref, applied_ref, stack_ref, *near_refs, sems = refs
    velocities_ref, shifts_ref, k0_ref, ke_ref, diag_ref, mass_ref = near_refs
    copies = [
        pltpu.make_async_copy(source, target, sems.at[index])
        for index, (source, target) in enumerate(zip(far_refs, near_refs))
    ]
    for copy in copies:
        copy.start()
    group_cols = stack_ref.shape[0] // 3
    split_lines(
        own_ref, stack_ref, applied_ref.shape[0], group_cols, [i * group_cols for i in range(3)]
    )
    for copy in copies:
        copy.wait()
    comps, _, levels, offsets = k0_ref.shape
    rows, lanes = material_ref.shape
    lines = comps * rows
    block_cols = x_ref.shape[0] // lines
    velocity = velocities_ref[sample_ref[0]]
    sigma = shifts_ref[sample_ref[0]]
    entry_rows = fields_ref.shape[1]
    stride = entry_rows // (comps * comps)
    gap = jnp.zeros((levels, stride - offsets), jnp.float32)
    wide = []
    for out in range(comps):
        for comp in range(comps):
            wide += [k0_ref[out, comp] - velocity * velocity * ke_ref[out, comp], gap]
    wide.append(jnp.zeros((levels, lanes - entry_rows), jnp.float32))
    table = jnp.concatenate(wide, axis=1).T[:entry_rows]
    entry = lax.broadcasted_iota(jnp.int32, table.shape, 0)
    for comp in range(comps):
        centre = diag_ref[comp : comp + 1, :] - sigma * mass_ref[comp : comp + 1, :]
        table = table + jnp.where(entry == comp * (comps + 1) * stride, centre, 0.0)

    lane = lax.broadcasted_iota(jnp.int32, (block_cols, lanes), 1)
    level = lax.broadcasted_iota(jnp.int32, (levels, lanes), 0)
    for row in range(rows):
        chosen = jnp.broadcast_to(material_ref[row : row + 1, :], (levels, lanes)) == level
        fields = jnp.dot(
            table, chosen.astype(jnp.float32),
            precision=exact_precision, preferred_element_type=jnp.float32,
        )
        fields_ref[row] = fields
        sums = [None] * comps
        for comp in range(comps):
            centre = line_of(x_ref, comp, row, comps, rows, block_cols)
            views = {
                0: centre,
                5: jnp.where(lane == 0, 0.0, pltpu.roll(centre, 1, 1)),
                6: jnp.where(lane == lanes - 1, 0.0, pltpu.roll(centre, lanes - 1, 1)),
            }
            if row > 0:
                views[3] = line_of(x_ref, comp, row - 1, comps, rows, block_cols)
            if row < rows - 1:
                views[4] = line_of(x_ref, comp, row + 1, comps, rows, block_cols)
            for offset, view in views.items():
                for out in range(comps):
                    place = (out * comps + comp) * stride + offset
                    term = fields[place : place + 1, :] * view
                    sums[out] = term if sums[out] is None else sums[out] + term
        for out in range(comps):
            applied_ref[out * rows + row] = sums[out]


def ahead(sample, velocities, shifts, k0, ke, diag, mass, material, x_rows, own, comps):
    rows, lanes = material.shape
    lines = comps * rows
    stride = -(-k0.shape[1] // 8) * 8
    k0, ke = (jnp.transpose(blocks, (2, 3, 0, 1)) for blocks in (k0, ke))
    tables = far(velocities, shifts, k0, ke, diag.T, mass.T)
    return pl.pallas_call(
        ahead_kernel,
        out_shape=(
            near(rows, comps * comps * stride, lanes),
            near(lines, x_rows.shape[0] // lines, lanes),
            near(3 * own.shape[0] // lines, lines * lanes, dtype=jnp.bfloat16),
        ),
        in_specs=[SMEM] + [HBM] * 6 + [VMEM] * 3,
        out_specs=(VMEM,) * 3,
        scratch_shapes=[
            (pltpu.SMEM if array.ndim == 1 else pltpu.VMEM)(array.shape, jnp.float32)
            for array in tables
        ] + [pltpu.SemaphoreType.DMA((len(tables),))],
        compiler_params=SCRATCH,
        name="ahead",
    )(sample, *tables, *kept(material, x_rows, own))


def side_terms(field_row, swapped, side, out, comp, comps):
    stride = field_row.shape[0] // (comps * comps)
    begin = (out * comps + comp) * stride
    below, above = field_row[begin + 1 : begin + 2], field_row[begin + 2 : begin + 3]
    other = (below, above) if side == "even" else (above, below)
    return jnp.where(swapped, *other)


def side_kernel(comps, side, slab_ref, fields_ref, applied_ref, halo_ref, out_ref):
    lines, block_cols, _ = applied_ref.shape
    rows = lines // comps
    swapped = slab_ref[0] % 2 == 1
    for row in range(rows):
        field_row = fields_ref[row]
        views = [line_of(halo_ref, comp, row, comps, rows, block_cols) for comp in range(comps)]
        for out in range(comps):
            total = applied_ref[out * rows + row]
            for comp, view in enumerate(views):
                total = total + side_terms(field_row, swapped, side, out, comp, comps) * view
            out_ref[out * rows + row] = total


def add_side(slab, fields, applied, halo, comps, side, weight):
    return pl.pallas_call(
        functools.partial(side_kernel, comps, side),
        out_shape=near(*applied.shape),
        in_specs=[SMEM] + [VMEM] * 3,
        out_specs=VMEM,
        compiler_params=SCRATCH,
        cost_estimate=weight,
        name="side",
    )(slab, *kept(fields, applied, halo))


def split_lines(piece_ref, stack_ref, lines, group_cols, begins):
    lanes = piece_ref.shape[1]
    for line in range(lines):
        values = piece_ref[pl.ds(line, group_cols, stride=lines), :]
        for begin, part in zip(begins, three_parts(values)):
            stack_ref[pl.ds(begin, group_cols), pl.ds(line * lanes, lanes)] = part


def edges_kernel(comps, ks, group_cols, place_ref, fields_ref, applied_ref, *refs):
    piece_refs, out_ref, parts_refs = refs[: len(ks)], refs[len(ks)], refs[len(ks) + 1 :]
    lines, block_cols, lanes = applied_ref.shape
    rows = lines // comps
    stride = fields_ref.shape[1] // (comps * comps)
    place = place_ref[0]

    def edge(comp, step):
        result = jnp.zeros((block_cols, lanes), jnp.float32)
        for k, ref in zip(ks, piece_refs):
            begin = ref.shape[0] - (comps - comp) * block_cols
            here = (place ^ k) == place + step
            result = jnp.where(here, ref[pl.ds(begin, block_cols), :], result)
        return result

    out_ref[...] = applied_ref[...]
    for row, offset, step in ((0, 3, -1), (rows - 1, 4, 1)):
        field_row = fields_ref[row]
        views = [edge(comp, step) for comp in range(comps)]
        for out in range(comps):
            total = out_ref[out * rows + row]
            for comp, view in enumerate(views):
                entry = (out * comps + comp) * stride + offset
                total = total + field_row[entry : entry + 1] * view
            out_ref[out * rows + row] = total
    for piece_ref, parts_ref in zip(piece_refs, parts_refs):
        split_lines(piece_ref, parts_ref, lines, group_cols, [i * group_cols for i in range(3)])


def add_edges(place, fields, applied, pieces, comps, group_cols, weight):
    lines, _, lanes = applied.shape
    parts = near(3 * group_cols, lines * lanes, dtype=jnp.bfloat16)
    return pl.pallas_call(
        functools.partial(edges_kernel, comps, tuple(pieces), group_cols),
        out_shape=(near(*applied.shape),) + (parts,) * len(pieces),
        in_specs=[SMEM] + [VMEM] * (2 + len(pieces)),
        out_specs=(VMEM,) * (1 + len(pieces)),
        compiler_params=SCRATCH,
        cost_estimate=weight,
        name="edges",
    )(place, *kept(fields, applied, *pieces.values()))


def fold(total, basis_cols, block_cols, lanes):
    half = basis_cols // 2
    row = lax.broadcasted_iota(jnp.int32, (half, half), 0)
    column = lax.broadcasted_iota(jnp.int32, (half, half), 1)
    last = total[half:basis_cols, half:basis_cols]
    shared = jnp.where(row >= column, total[:half, :half], last)
    diagonal = jnp.sum(jnp.where(row == column, last, 0.0), axis=1, keepdims=True)
    below = total[basis_cols:]
    first = jnp.concatenate((below[:, :half], below[:, half:basis_cols]), axis=0)
    rest = jnp.zeros((half - block_cols, block_cols), jnp.float32)
    block = jnp.concatenate((below[:, basis_cols:], rest), axis=0)
    pad = jnp.zeros((half, lanes - 3 * half - block_cols - 1), jnp.float32)
    return jnp.concatenate(
        (shared, total[:half, half:basis_cols], first, block, diagonal, pad), axis=1
    )


def unfold(folded, block_cols):
    half = folded.shape[0]
    row = lax.broadcasted_iota(jnp.int32, (half, half), 0)
    column = lax.broadcasted_iota(jnp.int32, (half, half), 1)
    shared, across = folded[:, :half], folded[:, half : 2 * half]
    turned = shared.T
    start = jnp.where(row >= column, shared, turned)
    end = jnp.where(row < column, shared, turned)
    diagonal = folded[:, 3 * half + block_cols : 3 * half + block_cols + 1]
    end = jnp.where(row == column, diagonal, end)
    gram = jnp.concatenate(
        (jnp.concatenate((start, across), axis=1), jnp.concatenate((across.T, end), axis=1)), axis=0
    )
    first = folded[:, 2 * half : 3 * half]
    first = jnp.concatenate((first[:block_cols], first[block_cols : 2 * block_cols]), axis=1)
    return gram, first, folded[:block_cols, 3 * half : 3 * half + block_cols]


def sums_kernel(
    split, raw, place_ref, applied_ref, *refs
):
    *refs, stack_ref, keep_ref, give_ref = refs
    lines, block_cols, lanes = applied_ref.shape
    group_cols = refs[0].shape[0] // 3
    basis_cols = (len(split) + len(raw)) * group_cols
    joined = basis_cols + block_cols
    place = place_ref[0]
    for k, ref in zip(split + raw, refs):
        begin = pl.multiple_of((place ^ k) * group_cols, group_cols)
        begins = [index * joined + begin for index in range(3)]
        if k in split:
            for index in range(3):
                stack_ref[pl.ds(begins[index], group_cols), :] = ref[
                    pl.ds(index * group_cols, group_cols), :
                ]
        else:
            split_lines(ref, stack_ref, lines, group_cols, begins)
    for line in range(lines):
        for index, part in enumerate(three_parts(applied_ref[line])):
            there = pl.ds(index * joined + basis_cols, block_cols)
            stack_ref[there, pl.ds(line * lanes, lanes)] = part

    stack = stack_ref[...]
    products = lax.dot_general(
        stack, stack, (((1,), (1,)), ((), ())), preferred_element_type=jnp.float32
    )
    wide = products[:joined] + products[joined : 2 * joined] + products[2 * joined :]
    total = wide[:, :joined] + wide[:, joined : 2 * joined] + wide[:, 2 * joined :]
    folded = fold(total, basis_cols, block_cols, keep_ref.shape[1])
    half = keep_ref.shape[0]
    odd = place % 2 == 1
    keep_ref[...] = jnp.where(odd, folded[half:], folded[:half])
    give_ref[...] = jnp.where(odd, folded[:half], folded[half:])


def sums(place, applied, split, raw):
    lines, block_cols, lanes = applied.shape
    basis_cols = (len(split) + len(raw)) * (split[0].shape[0] // 3)
    joined = basis_cols + block_cols
    return pl.pallas_call(
        functools.partial(sums_kernel, tuple(split), tuple(raw)),
        out_shape=(
            near(3 * joined, lines * lanes, dtype=jnp.bfloat16),
            near(basis_cols // 4, 2 * basis_cols),
            near(basis_cols // 4, 2 * basis_cols),
        ),
        in_specs=[SMEM] + [VMEM] * (1 + len(split) + len(raw)),
        out_specs=(VMEM,) * 3,
        compiler_params=SCRATCH,
        name="sums",
    )(place, *kept(applied, *split.values(), *raw.values()))


def exchange_all(keep, give):
    sizes = [lax.axis_size(axis) for axis in ("space", "basis")]
    pairs = [(i, i ^ 1) for i in range(sizes[1])]
    part = keep + lax.ppermute(give, "basis", pairs)
    groups = [
        [
            i * sizes[1] + j
            for side in range(2)
            for j in range(first, sizes[1], 2)
            for i in range(side, sizes[0], 2)
        ]
        for first in range(2)
    ]
    copies = jnp.broadcast_to(part[None], (len(groups[0]),) + part.shape)
    parts = lax.all_to_all(copies, ("space", "basis"), 0, 0, axis_index_groups=groups)
    own = jnp.sum(parts, axis=0)
    return own, lax.ppermute(own, "basis", pairs)


def finish_kernel(
    row_count, comps, place_ref, own_ref, given_ref, stack_ref, block_ref, coeffs_ref, upper_ref, bad_ref,
    coeffs_scratch, upper_scratch, bad_scratch, block_scratch, sems,
):
    block_cols = upper_ref.shape[0]
    basis_cols = own_ref.shape[1] // 2
    joined = basis_cols + block_cols
    lines, lanes = block_ref.shape[1:]
    odd = place_ref[0] % 2 == 1
    own, given = own_ref[...], given_ref[...]
    total = jnp.concatenate((jnp.where(odd, given, own), jnp.where(odd, own, given)), axis=0)
    total = total / row_count
    gram, first, block_gram = unfold(total, block_cols)

    def times(left, right, right_dim=0):
        return lax.dot_general(
            left, right, (((1,), (right_dim,)), ((), ())),
            precision=exact_precision, preferred_element_type=jnp.float32,
        )

    coeffs = first + (first - times(first, gram))
    image = times(coeffs, gram)
    matrix = block_gram - times(
        jnp.concatenate((coeffs, first - image), axis=1), jnp.concatenate((first, coeffs), axis=1), 1
    )
    coeffs_scratch[...] = coeffs.T
    group_cols = coeffs_ref.shape[0]
    start = pl.multiple_of(place_ref[0] * group_cols, group_cols)
    copies = [
        pltpu.make_async_copy(
            coeffs_scratch.at[pl.ds(start, group_cols)], coeffs_ref, sems.at[comps]
        )
    ]
    copies[0].start()

    row = lax.broadcasted_iota(jnp.int32, (block_cols, block_cols), 0)
    column = lax.broadcasted_iota(jnp.int32, (block_cols, block_cols), 1)
    unit = jnp.where(row == column, 1.0, 0.0)
    pad = jnp.zeros((block_cols, 2 * basis_cols - joined - block_cols), jnp.float32)
    work = jnp.concatenate((-coeffs, unit, matrix, pad), axis=1)
    height = lax.broadcasted_iota(jnp.int32, work.shape, 0)
    width = 4
    for begin in range(0, block_cols, width):
        done, new_rows = [], []
        for step in range(begin, begin + width):
            column_here = jnp.broadcast_to(work[:, joined + step : joined + step + 1], work.shape)
            pivot_row = work[step : step + 1]
            for other_column, other_row, inverse in done:
                entry = other_column[step : step + 1]
                pivot_row = pivot_row - entry * other_row
                column_here = column_here - other_column * (entry * inverse)
            pivot = column_here[step : step + 1]
            inverse = 1.0 / pivot
            done.append((column_here, pivot_row * inverse, inverse))
            new_rows.append(pivot_row * lax.rsqrt(pivot))
        rest = work
        for column_here, scaled, _ in done:
            rest = rest - column_here * scaled
        work = jnp.where(height >= begin + width, rest, work)
        for step, new_row in enumerate(new_rows, begin):
            work = jnp.where(height == step, new_row, work)
    upper = jnp.where(row <= column, work[:, joined : joined + block_cols], 0.0)
    upper_scratch[...] = upper
    kept_enough = jnp.where(row == column, upper * upper * LOSS, block_gram) >= block_gram
    kept_enough = jnp.min(jnp.where(kept_enough, 1.0, 0.0), axis=0, keepdims=True)
    kept_enough = jnp.min(kept_enough, axis=1, keepdims=True)
    bad_scratch[...] = jnp.where(kept_enough > 0.0, 0, 1)
    copies.append(pltpu.make_async_copy(bad_scratch, bad_ref, sems.at[comps + 2]))
    copies[-1].start()
    copies.append(pltpu.make_async_copy(upper_scratch, upper_ref, sems.at[comps + 1]))
    copies[-1].start()
    weights = three_parts(work[:, :joined])
    wide = jnp.concatenate(
        [jnp.concatenate((part, part, part), axis=1) for part in weights], axis=0
    )
    rows = lines // comps
    for comp in range(comps):
        there = pl.ds(comp * rows * lanes, rows * lanes)
        result = jnp.dot(wide, stack_ref[:, there], preferred_element_type=jnp.float32)
        result = result[:block_cols] + result[block_cols : 2 * block_cols] + result[2 * block_cols :]
        for index in range(rows):
            block_scratch[pl.ds(comp * rows + index, block_cols, stride=lines), :] = result[
                :, index * lanes : (index + 1) * lanes
            ]
        part = pl.ds(comp * rows, rows)
        copies.append(
            pltpu.make_async_copy(
                block_scratch.reshape(block_cols, lines, lanes).at[:, part, :],
                block_ref.at[:, part, :],
                sems.at[comp],
            )
        )
        copies[-1].start()
    for copy in copies:
        copy.wait()


def finish(place, halves, stack, row_count, block_cols, group_cols, lines, comps):
    lanes = stack.shape[1] // lines
    basis_cols = halves[0].shape[1] // 2
    return pl.pallas_call(
        functools.partial(finish_kernel, row_count, comps),
        out_shape=(
            f32(block_cols, lines, lanes), f32(group_cols, block_cols), f32(block_cols, block_cols),
            jax.ShapeDtypeStruct((1, 1), jnp.int32),
        ),
        in_specs=[SMEM] + [VMEM] * 3,
        out_specs=(HBM,) * 4,
        scratch_shapes=[
            pltpu.VMEM((basis_cols, block_cols), jnp.float32),
            pltpu.VMEM((block_cols, block_cols), jnp.float32),
            pltpu.VMEM((1, 1), jnp.int32),
            pltpu.VMEM((block_cols * lines, lanes), jnp.float32),
            pltpu.SemaphoreType.DMA((comps + 3,)),
        ],
        compiler_params=SCRATCH,
        name="finish",
    )(place, *kept(*halves, stack))


def stencil_tables(k0_blocks, k0_diag, ke_blocks, mass, velocities, shifts, sample):
    velocity = jnp.take(velocities, sample, axis=0)[0]
    sigma_value = jnp.take(shifts, sample, axis=0)[0]
    center = (k0_diag - sigma_value * mass)[:, :, None] * jnp.eye(3, dtype=jnp.float32)
    tables = k0_blocks - velocity * velocity * ke_blocks
    return tables.at[:, 0].add(center)


def shifted(cells, dim, axis, up):
    extent = cells.shape[dim]
    edge = lax.slice_in_dim(cells, 0, 1, axis=dim) if up else (
        lax.slice_in_dim(cells, extent - 1, extent, axis=dim)
    )
    if axis is None:
        edge = jnp.zeros_like(edge)
    else:
        ends = [(i, i + 1) for i in range(lax.axis_size(axis) - 1)]
        edge = lax.ppermute(edge, axis, [(j, i) for i, j in ends] if up else ends)
    if up:
        return jnp.concatenate((lax.slice_in_dim(cells, 1, extent, axis=dim), edge), axis=dim)
    return jnp.concatenate((edge, lax.slice_in_dim(cells, 0, extent - 1, axis=dim)), axis=dim)


def hold_kernel(*refs):
    *refs, sems = refs
    half = len(refs) // 2
    copies = [
        pltpu.make_async_copy(source, target, sems.at[index])
        for index, (source, target) in enumerate(zip(refs[:half], refs[half:]))
    ]
    for copy in copies:
        copy.start()
    for copy in copies:
        copy.wait()


def hold(*arrays):
    return pl.pallas_call(
        hold_kernel,
        out_shape=[jax.ShapeDtypeStruct(array.shape, array.dtype) for array in arrays],
        in_specs=[HBM] * len(arrays),
        out_specs=[HBM] * len(arrays),
        scratch_shapes=[pltpu.SemaphoreType.DMA((len(arrays),))],
        compiler_params=SCRATCH,
        name="hold",
    )(*far(*arrays))


def careful(arguments):
    x_block, basis, material, k0_blocks, k0_diag, ke_blocks, mass, velocities, shifts, sample = arguments
    x_block, basis, material, k0_blocks, k0_diag, ke_blocks, mass, velocities, shifts = hold(
        x_block, basis, material, jnp.transpose(k0_blocks, (2, 3, 0, 1)), k0_diag.T,
        jnp.transpose(ke_blocks, (2, 3, 0, 1)), mass.T, velocities, shifts,
    )
    k0_blocks, ke_blocks = (jnp.transpose(blocks, (2, 3, 0, 1)) for blocks in (k0_blocks, ke_blocks))
    k0_diag, mass = k0_diag.T, mass.T
    tables = stencil_tables(k0_blocks, k0_diag, ke_blocks, mass, velocities, shifts, sample)
    block_cols, comps, extent_x, _, lanes = x_block.shape
    group_cols = basis.shape[0]
    row_count = float(comps * extent_x * lax.axis_size("space") * basis.shape[3] * lanes)
    fields = jnp.zeros((7, comps, comps) + material.shape, jnp.float32)
    for level in range(tables.shape[0]):
        chosen = (material == level).astype(jnp.float32)
        fields = fields + tables[level][:, :, :, None, None, None] * chosen
    views = [x_block]
    for dim, axis in ((2, "space"), (3, "basis"), (4, None)):
        views += [shifted(x_block, dim, axis, False), shifted(x_block, dim, axis, True)]
    applied = jnp.zeros_like(x_block)
    for offset, view in enumerate(views):
        for comp in range(comps):
            applied = applied + fields[offset, :, comp][None] * view[:, comp : comp + 1]

    count = lax.axis_size("basis")
    place = lax.axis_index("basis")
    pieces = jnp.moveaxis(basis.reshape(basis.shape[:3] + (count, -1, lanes)), 3, 0)
    rows = jnp.zeros((count,) + pieces.shape[1:], jnp.float32)
    for k in range(count):
        piece = lax.dynamic_index_in_dim(pieces, place ^ k, 0, keepdims=False)
        if k:
            piece = lax.ppermute(piece, "basis", [(i, i ^ k) for i in range(count)])
        rows = lax.dynamic_update_index_in_dim(rows, piece, place ^ k, 0)
    rows = rows.reshape((count * group_cols,) + pieces.shape[2:])

    def total(part):
        for axis in ("basis", "space"):
            mask = 1
            while mask < lax.axis_size(axis):
                pairs = [(i, i ^ mask) for i in range(lax.axis_size(axis))]
                part = part + lax.ppermute(part, axis, pairs)
                mask *= 2
        return part / row_count

    running = jnp.zeros((count * group_cols, block_cols), jnp.float32)
    for repeat in range(2):
        coeffs = total(
            jnp.einsum("kcxyz,ncxyz->kn", rows, applied, precision=exact_precision)
        )
        applied = applied - jnp.einsum("kcxyz,kn->ncxyz", rows, coeffs, precision=exact_precision)
        running = running + coeffs
    gram = total(jnp.einsum("ncxyz,mcxyz->nm", applied, applied, precision=exact_precision))
    lower = jnp.linalg.cholesky(gram)
    inverse = lax.linalg.triangular_solve(
        lower, jnp.eye(block_cols, dtype=jnp.float32), left_side=True, lower=True
    )
    block = jnp.einsum("mcxyz,nm->ncxyz", applied, inverse, precision=exact_precision)
    own = lax.dynamic_slice_in_dim(running, place * group_cols, group_cols, axis=0)
    return tuple(hold(block.reshape(block_cols, -1, lanes), own, lower.T))


def shards(
    x_block, basis, material, k0_blocks, k0_diag, ke_blocks, mass, velocities, shifts, sample
):
    arguments = (
        x_block, basis, material, k0_blocks, k0_diag, ke_blocks, mass, velocities, shifts, sample
    )
    block_cols, comps, extent_x, rows, lanes = x_block.shape
    group_cols = basis.shape[0]
    lines = comps * rows
    row_count = float(comps * extent_x * lax.axis_size("space") * basis.shape[3] * lanes)

    place = lax.axis_index("basis").astype(jnp.int32).reshape(1)
    slab = lax.axis_index("space").astype(jnp.int32).reshape(1)
    count = lax.axis_size("basis")
    x_far = x_block.reshape(block_cols * lines, lanes)
    own, *pieces, x_rows, material = pack(place, basis, x_far, material.reshape(rows, lanes), block_cols)
    got = {}
    for name in ("even", *reversed(partners(count)[0]), "odd"):
        if name == "even":
            got[name] = swap(x_far, "space", 0)
        elif name == "odd":
            got[name] = swap(x_far, "space", 1)
        else:
            piece = lax.ppermute(pieces[name - 1], "basis", [(i, i ^ name) for i in range(count)])
            got[name] = piece.reshape(-1, lanes)
    fields, applied, own = ahead(
        sample, velocities, shifts, k0_blocks, ke_blocks, k0_diag, mass, material, x_rows,
        own.reshape(-1, lanes), comps,
    )
    split = {0: own}
    first, *rest = reversed(partners(count)[1])
    applied, split[first] = add_edges(
        place, fields, applied, {first: got.pop(first)}, comps, group_cols, EARLY
    )
    applied = add_side(slab, fields, applied, got.pop("even"), comps, "even", NEXT)
    for k in rest:
        applied, split[k] = add_edges(
            place, fields, applied, {k: got.pop(k)}, comps, group_cols, None
        )
    applied = add_side(slab, fields, applied, got.pop("odd"), comps, "odd", LATE)
    stack, keep, give = sums(place, applied, split, got)
    halves = exchange_all(keep, give)
    block, coeffs, upper, bad = finish(
        place, halves, stack, row_count, block_cols, group_cols, lines, comps
    )
    block, coeffs, upper = lax.while_loop(
        lambda state: state[0] > 0,
        lambda state: (jnp.zeros_like(state[0]), careful(arguments)),
        (bad[0, 0], (block, coeffs, upper)),
    )[1]
    return block.reshape(x_block.shape), coeffs, upper


def solution(mesh):
    in_specs = (
        P(None, None, "space", "basis", None),
        P("basis", None, "space", None, None),
        P("space", "basis", None),
        P(),
        P(),
        P(),
        P(),
        P(),
        P(),
        P(),
    )
    out_specs = (P(None, None, "space", "basis", None), P("basis", None), P())
    return jax.shard_map(shards, mesh=mesh, in_specs=in_specs, out_specs=out_specs, check_vma=False)
```

```python
import functools

import jax
import jax.numpy as jnp
from jax import lax
from jax.experimental import pallas as pl
from jax.experimental.pallas import tpu as pltpu
from jax.sharding import PartitionSpec as P

exact_precision = lax.Precision.HIGHEST
VMEM = pl.BlockSpec(memory_space=pltpu.VMEM)
SMEM = pl.BlockSpec(memory_space=pltpu.SMEM)
HBM = pl.BlockSpec(memory_space=pltpu.HBM)
LOSS = 256.0
EARLY = pl.CostEstimate(flops=10**9, bytes_accessed=10**6, transcendentals=0)
NEXT = pl.CostEstimate(flops=3 * 10**8, bytes_accessed=10**6, transcendentals=0)
LATE = pl.CostEstimate(flops=10**6, bytes_accessed=10**6, transcendentals=0)
SCRATCH = pltpu.CompilerParams(vmem_limit_bytes=8 * 2**20)


def f32(*shape):
    return jax.ShapeDtypeStruct(shape, jnp.float32)


def near(*shape, dtype=jnp.float32):
    return pltpu.VMEM(shape, dtype)


def kept(*arrays):
    return [pltpu.with_memory_space_constraint(array, pltpu.VMEM) for array in arrays]


def far(*arrays):
    return [pltpu.with_memory_space_constraint(array, pltpu.HBM) for array in arrays]


def swap(values, axis, first):
    pairs = [(i, i + 1) for i in range(first, lax.axis_size(axis) - 1, 2)]
    return lax.ppermute(values, axis, pairs + [(j, i) for i, j in pairs])


def partners(count):
    return range(1, count), [k for k in range(1, count) if k & (k + 1) == 0]


def pack_kernel(comps, place_ref, basis_ref, x_ref, *refs):
    *piece_refs, x_out_ref, sems = refs
    piece_refs = dict(enumerate(piece_refs, 1))
    count = 1 + len(piece_refs)
    tiles, _, rows, lanes = basis_ref.shape
    block_cols = x_ref.shape[0] // (comps * rows)
    place = place_ref[0]
    x_copy = pltpu.make_async_copy(x_ref, x_out_ref, sems.at[0])
    x_copy.start()
    copies = []
    for k in reversed(range(1, count)):
        copies.append(
            pltpu.make_async_copy(
                basis_ref.at[:, place ^ k], piece_refs[k].at[pl.ds(0, tiles)], sems.at[k]
            )
        )
    for copy in copies:
        copy.start()
    x_copy.wait()
    for comp in range(comps):
        first, last = (
            x_out_ref[pl.ds(comp * rows + row, block_cols, stride=comps * rows), :]
            for row in (0, rows - 1)
        )
        for k in partners(count)[1]:
            edge = jnp.where((place ^ k) > place, last, first)
            for part in range(block_cols // rows):
                piece_refs[k][tiles + comp * (block_cols // rows) + part] = edge[
                    part * rows : (part + 1) * rows
                ]
    for copy in copies:
        copy.wait()


def pack(place, basis, x_rows, block_cols):
    group_cols, comps, _, full_y, lanes = basis.shape
    count = lax.axis_size("basis")
    rows = full_y // count
    tiles = group_cols * comps
    edge_tiles = block_cols * comps // rows
    pieces = [
        near(tiles + (edge_tiles if k in partners(count)[1] else 0), rows, lanes)
        for k in range(1, count)
    ]
    return pl.pallas_call(
        functools.partial(pack_kernel, comps),
        out_shape=(*pieces, near(*x_rows.shape)),
        in_specs=[SMEM, HBM, HBM],
        out_specs=(VMEM,) * count,
        scratch_shapes=[pltpu.SemaphoreType.DMA((count,))],
        compiler_params=SCRATCH,
        name="pack",
    )(place, *far(basis.reshape(tiles, count, rows, lanes), x_rows))


def three_parts(values):
    high = values.astype(jnp.bfloat16)
    rest = values - high.astype(jnp.float32)
    middle = rest.astype(jnp.bfloat16)
    low = (rest - middle.astype(jnp.float32)).astype(jnp.bfloat16)
    return high, middle, low


def line_of(ref, comp, row, comps, rows, block_cols):
    return ref[pl.ds(comp * rows + row, block_cols, stride=comps * rows), :]


def ahead_kernel(
    sample_ref, place_ref, basis_ref, *refs
):
    far_refs, refs = refs[:7], refs[7:]
    x_ref, fields_ref, applied_ref, stack_ref, *near_refs, piece_ref, sems = refs
    velocities_ref, shifts_ref, k0_ref, ke_ref, diag_ref, mass_ref, material_ref = near_refs
    own = pltpu.make_async_copy(basis_ref.at[:, place_ref[0]], piece_ref, sems.at[len(near_refs)])
    own.start()
    copies = [
        pltpu.make_async_copy(source, target, sems.at[index])
        for index, (source, target) in enumerate(zip(far_refs, near_refs))
    ]
    for copy in copies:
        copy.start()
    group_cols = stack_ref.shape[0] // 3
    own.wait()
    own_ref = piece_ref.reshape(piece_ref.shape[0] * piece_ref.shape[1], piece_ref.shape[2])
    split_lines(
        own_ref, stack_ref, applied_ref.shape[0], group_cols, [i * group_cols for i in range(3)]
    )
    for copy in copies:
        copy.wait()
    comps, _, levels, offsets = k0_ref.shape
    rows, lanes = material_ref.shape
    lines = comps * rows
    block_cols = x_ref.shape[0] // lines
    velocity = velocities_ref[sample_ref[0]]
    sigma = shifts_ref[sample_ref[0]]
    entry_rows = fields_ref.shape[1]
    stride = entry_rows // (comps * comps)
    gap = jnp.zeros((levels, stride - offsets), jnp.float32)
    wide = []
    for out in range(comps):
        for comp in range(comps):
            wide += [k0_ref[out, comp] - velocity * velocity * ke_ref[out, comp], gap]
    wide.append(jnp.zeros((levels, lanes - entry_rows), jnp.float32))
    table = jnp.concatenate(wide, axis=1).T[:entry_rows]
    entry = lax.broadcasted_iota(jnp.int32, table.shape, 0)
    for comp in range(comps):
        centre = diag_ref[comp : comp + 1, :] - sigma * mass_ref[comp : comp + 1, :]
        table = table + jnp.where(entry == comp * (comps + 1) * stride, centre, 0.0)

    lane = lax.broadcasted_iota(jnp.int32, (block_cols, lanes), 1)
    level = lax.broadcasted_iota(jnp.int32, (levels, lanes), 0)
    for row in range(rows):
        chosen = jnp.broadcast_to(material_ref[row : row + 1, :], (levels, lanes)) == level
        fields = jnp.dot(
            table, chosen.astype(jnp.float32),
            precision=exact_precision, preferred_element_type=jnp.float32,
        )
        fields_ref[row] = fields
        sums = [None] * comps
        for comp in range(comps):
            centre = line_of(x_ref, comp, row, comps, rows, block_cols)
            views = {
                0: centre,
                5: jnp.where(lane == 0, 0.0, pltpu.roll(centre, 1, 1)),
                6: jnp.where(lane == lanes - 1, 0.0, pltpu.roll(centre, lanes - 1, 1)),
            }
            if row > 0:
                views[3] = line_of(x_ref, comp, row - 1, comps, rows, block_cols)
            if row < rows - 1:
                views[4] = line_of(x_ref, comp, row + 1, comps, rows, block_cols)
            for offset, view in views.items():
                for out in range(comps):
                    place = (out * comps + comp) * stride + offset
                    term = fields[place : place + 1, :] * view
                    sums[out] = term if sums[out] is None else sums[out] + term
        for out in range(comps):
            applied_ref[out * rows + row] = sums[out]


def ahead(sample, place, basis, velocities, shifts, k0, ke, diag, mass, material, x_rows, comps):
    rows, lanes = material.shape
    lines = comps * rows
    stride = -(-k0.shape[1] // 8) * 8
    k0, ke = (jnp.transpose(blocks, (2, 3, 0, 1)) for blocks in (k0, ke))
    tables = far(velocities, shifts, k0, ke, diag.T, mass.T, material)
    group_cols, _, _, full_y, _ = basis.shape
    tiles = group_cols * comps
    basis = basis.reshape(tiles, full_y // rows, rows, lanes)
    return pl.pallas_call(
        ahead_kernel,
        out_shape=(
            near(rows, comps * comps * stride, lanes),
            near(lines, x_rows.shape[0] // lines, lanes),
            near(3 * group_cols, lines * lanes, dtype=jnp.bfloat16),
        ),
        in_specs=[SMEM] * 2 + [HBM] * (1 + len(tables)) + [VMEM],
        out_specs=(VMEM,) * 3,
        scratch_shapes=[
            (pltpu.SMEM if array.ndim == 1 else pltpu.VMEM)(array.shape, array.dtype)
            for array in tables
        ] + [
            pltpu.VMEM((tiles, rows, lanes), jnp.float32),
            pltpu.SemaphoreType.DMA((len(tables) + 1,)),
        ],
        compiler_params=SCRATCH,
        name="ahead",
    )(sample, place, *far(basis), *tables, *kept(x_rows))


def side_terms(field_row, swapped, side, out, comp, comps):
    stride = field_row.shape[0] // (comps * comps)
    begin = (out * comps + comp) * stride
    below, above = field_row[begin + 1 : begin + 2], field_row[begin + 2 : begin + 3]
    other = (below, above) if side == "even" else (above, below)
    return jnp.where(swapped, *other)


def side_kernel(comps, side, slab_ref, fields_ref, applied_ref, halo_ref, out_ref):
    lines, block_cols, _ = applied_ref.shape
    rows = lines // comps
    swapped = slab_ref[0] % 2 == 1
    for row in range(rows):
        field_row = fields_ref[row]
        views = [line_of(halo_ref, comp, row, comps, rows, block_cols) for comp in range(comps)]
        for out in range(comps):
            total = applied_ref[out * rows + row]
            for comp, view in enumerate(views):
                total = total + side_terms(field_row, swapped, side, out, comp, comps) * view
            out_ref[out * rows + row] = total


def add_side(slab, fields, applied, halo, comps, side, weight):
    return pl.pallas_call(
        functools.partial(side_kernel, comps, side),
        out_shape=near(*applied.shape),
        in_specs=[SMEM] + [VMEM] * 3,
        out_specs=VMEM,
        compiler_params=SCRATCH,
        cost_estimate=weight,
        name="side",
    )(slab, *kept(fields, applied, halo))


def split_lines(piece_ref, stack_ref, lines, group_cols, begins):
    lanes = piece_ref.shape[1]
    for line in range(lines):
        values = piece_ref[pl.ds(line, group_cols, stride=lines), :]
        for begin, part in zip(begins, three_parts(values)):
            stack_ref[pl.ds(begin, group_cols), pl.ds(line * lanes, lanes)] = part


def edges_kernel(comps, ks, group_cols, place_ref, fields_ref, applied_ref, *refs):
    piece_refs, out_ref, parts_refs = refs[: len(ks)], refs[len(ks)], refs[len(ks) + 1 :]
    lines, block_cols, lanes = applied_ref.shape
    rows = lines // comps
    stride = fields_ref.shape[1] // (comps * comps)
    place = place_ref[0]

    def edge(comp, step):
        result = jnp.zeros((block_cols, lanes), jnp.float32)
        for k, ref in zip(ks, piece_refs):
            begin = ref.shape[0] - (comps - comp) * block_cols
            here = (place ^ k) == place + step
            result = jnp.where(here, ref[pl.ds(begin, block_cols), :], result)
        return result

    out_ref[...] = applied_ref[...]
    for row, offset, step in ((0, 3, -1), (rows - 1, 4, 1)):
        field_row = fields_ref[row]
        views = [edge(comp, step) for comp in range(comps)]
        for out in range(comps):
            total = out_ref[out * rows + row]
            for comp, view in enumerate(views):
                entry = (out * comps + comp) * stride + offset
                total = total + field_row[entry : entry + 1] * view
            out_ref[out * rows + row] = total
    for piece_ref, parts_ref in zip(piece_refs, parts_refs):
        split_lines(piece_ref, parts_ref, lines, group_cols, [i * group_cols for i in range(3)])


def add_edges(place, fields, applied, pieces, comps, group_cols, weight):
    lines, _, lanes = applied.shape
    parts = near(3 * group_cols, lines * lanes, dtype=jnp.bfloat16)
    return pl.pallas_call(
        functools.partial(edges_kernel, comps, tuple(pieces), group_cols),
        out_shape=(near(*applied.shape),) + (parts,) * len(pieces),
        in_specs=[SMEM] + [VMEM] * (2 + len(pieces)),
        out_specs=(VMEM,) * (1 + len(pieces)),
        compiler_params=SCRATCH,
        cost_estimate=weight,
        name="edges",
    )(place, *kept(fields, applied, *pieces.values()))


def fold(total, basis_cols, block_cols, lanes):
    half = basis_cols // 2
    row = lax.broadcasted_iota(jnp.int32, (half, half), 0)
    column = lax.broadcasted_iota(jnp.int32, (half, half), 1)
    last = total[half:basis_cols, half:basis_cols]
    shared = jnp.where(row >= column, total[:half, :half], last)
    diagonal = jnp.sum(jnp.where(row == column, last, 0.0), axis=1, keepdims=True)
    below = total[basis_cols:]
    first = jnp.concatenate((below[:, :half], below[:, half:basis_cols]), axis=0)
    rest = jnp.zeros((half - block_cols, block_cols), jnp.float32)
    block = jnp.concatenate((below[:, basis_cols:], rest), axis=0)
    pad = jnp.zeros((half, lanes - 3 * half - block_cols - 1), jnp.float32)
    return jnp.concatenate(
        (shared, total[:half, half:basis_cols], first, block, diagonal, pad), axis=1
    )


def unfold(folded, block_cols):
    half = folded.shape[0]
    row = lax.broadcasted_iota(jnp.int32, (half, half), 0)
    column = lax.broadcasted_iota(jnp.int32, (half, half), 1)
    shared, across = folded[:, :half], folded[:, half : 2 * half]
    turned = shared.T
    start = jnp.where(row >= column, shared, turned)
    end = jnp.where(row < column, shared, turned)
    diagonal = folded[:, 3 * half + block_cols : 3 * half + block_cols + 1]
    end = jnp.where(row == column, diagonal, end)
    gram = jnp.concatenate(
        (jnp.concatenate((start, across), axis=1), jnp.concatenate((across.T, end), axis=1)), axis=0
    )
    first = folded[:, 2 * half : 3 * half]
    first = jnp.concatenate((first[:block_cols], first[block_cols : 2 * block_cols]), axis=1)
    return gram, first, folded[:block_cols, 3 * half : 3 * half + block_cols]


def sums_kernel(
    split, raw, place_ref, applied_ref, *refs
):
    *refs, stack_ref, keep_ref, give_ref = refs
    lines, block_cols, lanes = applied_ref.shape
    group_cols = refs[0].shape[0] // 3
    basis_cols = (len(split) + len(raw)) * group_cols
    joined = basis_cols + block_cols
    place = place_ref[0]
    for k, ref in zip(split + raw, refs):
        begin = pl.multiple_of((place ^ k) * group_cols, group_cols)
        begins = [index * joined + begin for index in range(3)]
        if k in split:
            for index in range(3):
                stack_ref[pl.ds(begins[index], group_cols), :] = ref[
                    pl.ds(index * group_cols, group_cols), :
                ]
        else:
            split_lines(ref, stack_ref, lines, group_cols, begins)
    for line in range(lines):
        for index, part in enumerate(three_parts(applied_ref[line])):
            there = pl.ds(index * joined + basis_cols, block_cols)
            stack_ref[there, pl.ds(line * lanes, lanes)] = part

    stack = stack_ref[...]
    products = lax.dot_general(
        stack, stack, (((1,), (1,)), ((), ())), preferred_element_type=jnp.float32
    )
    wide = products[:joined] + products[joined : 2 * joined] + products[2 * joined :]
    total = wide[:, :joined] + wide[:, joined : 2 * joined] + wide[:, 2 * joined :]
    folded = fold(total, basis_cols, block_cols, keep_ref.shape[1])
    half = keep_ref.shape[0]
    odd = place % 2 == 1
    keep_ref[...] = jnp.where(odd, folded[half:], folded[:half])
    give_ref[...] = jnp.where(odd, folded[:half], folded[half:])


def sums(place, applied, split, raw):
    lines, block_cols, lanes = applied.shape
    basis_cols = (len(split) + len(raw)) * (split[0].shape[0] // 3)
    joined = basis_cols + block_cols
    return pl.pallas_call(
        functools.partial(sums_kernel, tuple(split), tuple(raw)),
        out_shape=(
            near(3 * joined, lines * lanes, dtype=jnp.bfloat16),
            near(basis_cols // 4, 2 * basis_cols),
            near(basis_cols // 4, 2 * basis_cols),
        ),
        in_specs=[SMEM] + [VMEM] * (1 + len(split) + len(raw)),
        out_specs=(VMEM,) * 3,
        compiler_params=SCRATCH,
        name="sums",
    )(place, *kept(applied, *split.values(), *raw.values()))


def exchange_all(keep, give):
    sizes = [lax.axis_size(axis) for axis in ("space", "basis")]
    pairs = [(i, i ^ 1) for i in range(sizes[1])]
    part = keep + lax.ppermute(give, "basis", pairs)
    groups = [
        [i * sizes[1] + j for i in range(sizes[0]) for j in range(first, sizes[1], 2)]
        for first in range(2)
    ]
    copies = jnp.broadcast_to(part[None], (len(groups[0]),) + part.shape)
    parts = lax.all_to_all(copies, ("space", "basis"), 0, 0, axis_index_groups=groups)
    own = jnp.sum(parts, axis=0)
    return own, lax.ppermute(own, "basis", pairs)


def finish_kernel(
    row_count, comps, place_ref, own_ref, given_ref, stack_ref, block_ref, coeffs_ref, upper_ref, bad_ref,
    coeffs_scratch, upper_scratch, bad_scratch, block_scratch, sems,
):
    block_cols = upper_ref.shape[0]
    basis_cols = own_ref.shape[1] // 2
    joined = basis_cols + block_cols
    lines, lanes = block_ref.shape[1:]
    odd = place_ref[0] % 2 == 1
    own, given = own_ref[...], given_ref[...]
    total = jnp.concatenate((jnp.where(odd, given, own), jnp.where(odd, own, given)), axis=0)
    total = total / row_count
    gram, first, block_gram = unfold(total, block_cols)

    def times(left, right, right_dim=0):
        return lax.dot_general(
            left, right, (((1,), (right_dim,)), ((), ())),
            precision=exact_precision, preferred_element_type=jnp.float32,
        )

    coeffs = first + (first - times(first, gram))
    image = times(coeffs, gram)
    matrix = block_gram - times(
        jnp.concatenate((coeffs, first - image), axis=1), jnp.concatenate((first, coeffs), axis=1), 1
    )
    coeffs_scratch[...] = coeffs.T
    group_cols = coeffs_ref.shape[0]
    start = pl.multiple_of(place_ref[0] * group_cols, group_cols)
    copies = [
        pltpu.make_async_copy(
            coeffs_scratch.at[pl.ds(start, group_cols)], coeffs_ref, sems.at[comps]
        )
    ]
    copies[0].start()

    row = lax.broadcasted_iota(jnp.int32, (block_cols, block_cols), 0)
    column = lax.broadcasted_iota(jnp.int32, (block_cols, block_cols), 1)
    unit = jnp.where(row == column, 1.0, 0.0)
    pad = jnp.zeros((block_cols, 2 * basis_cols - joined - block_cols), jnp.float32)
    work = jnp.concatenate((-coeffs, unit, matrix, pad), axis=1)
    height = lax.broadcasted_iota(jnp.int32, work.shape, 0)
    width = 4
    for begin in range(0, block_cols, width):
        done, new_rows = [], []
        for step in range(begin, begin + width):
            column_here = jnp.broadcast_to(work[:, joined + step : joined + step + 1], work.shape)
            pivot_row = work[step : step + 1]
            for other_column, other_row, inverse in done:
                entry = other_column[step : step + 1]
                pivot_row = pivot_row - entry * other_row
                column_here = column_here - other_column * (entry * inverse)
            pivot = column_here[step : step + 1]
            inverse = 1.0 / pivot
            done.append((column_here, pivot_row * inverse, inverse))
            new_rows.append(pivot_row * lax.rsqrt(pivot))
        rest = work
        for column_here, scaled, _ in done:
            rest = rest - column_here * scaled
        work = jnp.where(height >= begin + width, rest, work)
        for step, new_row in enumerate(new_rows, begin):
            work = jnp.where(height == step, new_row, work)
    upper = jnp.where(row <= column, work[:, joined : joined + block_cols], 0.0)
    upper_scratch[...] = upper
    kept_enough = jnp.where(row == column, upper * upper * LOSS, block_gram) >= block_gram
    kept_enough = jnp.min(jnp.where(kept_enough, 1.0, 0.0), axis=0, keepdims=True)
    kept_enough = jnp.min(kept_enough, axis=1, keepdims=True)
    bad_scratch[...] = jnp.where(kept_enough > 0.0, 0, 1)
    copies.append(pltpu.make_async_copy(bad_scratch, bad_ref, sems.at[comps + 2]))
    copies[-1].start()
    copies.append(pltpu.make_async_copy(upper_scratch, upper_ref, sems.at[comps + 1]))
    copies[-1].start()
    weights = three_parts(work[:, :joined])
    wide = jnp.concatenate(
        [jnp.concatenate((part, part, part), axis=1) for part in weights], axis=0
    )
    rows = lines // comps
    for comp in range(comps):
        there = pl.ds(comp * rows * lanes, rows * lanes)
        result = jnp.dot(wide, stack_ref[:, there], preferred_element_type=jnp.float32)
        result = result[:block_cols] + result[block_cols : 2 * block_cols] + result[2 * block_cols :]
        for index in range(rows):
            block_scratch[pl.ds(comp * rows + index, block_cols, stride=lines), :] = result[
                :, index * lanes : (index + 1) * lanes
            ]
        part = pl.ds(comp * rows, rows)
        copies.append(
            pltpu.make_async_copy(
                block_scratch.reshape(block_cols, lines, lanes).at[:, part, :],
                block_ref.at[:, part, :],
                sems.at[comp],
            )
        )
        copies[-1].start()
    for copy in copies:
        copy.wait()


def finish(place, halves, stack, row_count, block_cols, group_cols, lines, comps):
    lanes = stack.shape[1] // lines
    basis_cols = halves[0].shape[1] // 2
    return pl.pallas_call(
        functools.partial(finish_kernel, row_count, comps),
        out_shape=(
            f32(block_cols, lines, lanes), f32(group_cols, block_cols), f32(block_cols, block_cols),
            jax.ShapeDtypeStruct((1, 1), jnp.int32),
        ),
        in_specs=[SMEM] + [VMEM] * 3,
        out_specs=(HBM,) * 4,
        scratch_shapes=[
            pltpu.VMEM((basis_cols, block_cols), jnp.float32),
            pltpu.VMEM((block_cols, block_cols), jnp.float32),
            pltpu.VMEM((1, 1), jnp.int32),
            pltpu.VMEM((block_cols * lines, lanes), jnp.float32),
            pltpu.SemaphoreType.DMA((comps + 3,)),
        ],
        compiler_params=SCRATCH,
        name="finish",
    )(place, *kept(*halves, stack))


def stencil_tables(k0_blocks, k0_diag, ke_blocks, mass, velocities, shifts, sample):
    velocity = jnp.take(velocities, sample, axis=0)[0]
    sigma_value = jnp.take(shifts, sample, axis=0)[0]
    center = (k0_diag - sigma_value * mass)[:, :, None] * jnp.eye(3, dtype=jnp.float32)
    tables = k0_blocks - velocity * velocity * ke_blocks
    return tables.at[:, 0].add(center)


def shifted(cells, dim, axis, up):
    extent = cells.shape[dim]
    edge = lax.slice_in_dim(cells, 0, 1, axis=dim) if up else (
        lax.slice_in_dim(cells, extent - 1, extent, axis=dim)
    )
    if axis is None:
        edge = jnp.zeros_like(edge)
    else:
        ends = [(i, i + 1) for i in range(lax.axis_size(axis) - 1)]
        edge = lax.ppermute(edge, axis, [(j, i) for i, j in ends] if up else ends)
    if up:
        return jnp.concatenate((lax.slice_in_dim(cells, 1, extent, axis=dim), edge), axis=dim)
    return jnp.concatenate((edge, lax.slice_in_dim(cells, 0, extent - 1, axis=dim)), axis=dim)


def hold_kernel(*refs):
    *refs, sems = refs
    half = len(refs) // 2
    copies = [
        pltpu.make_async_copy(source, target, sems.at[index])
        for index, (source, target) in enumerate(zip(refs[:half], refs[half:]))
    ]
    for copy in copies:
        copy.start()
    for copy in copies:
        copy.wait()


def hold(*arrays):
    return pl.pallas_call(
        hold_kernel,
        out_shape=[jax.ShapeDtypeStruct(array.shape, array.dtype) for array in arrays],
        in_specs=[HBM] * len(arrays),
        out_specs=[HBM] * len(arrays),
        scratch_shapes=[pltpu.SemaphoreType.DMA((len(arrays),))],
        compiler_params=SCRATCH,
        name="hold",
    )(*far(*arrays))


def careful(arguments):
    x_block, basis, material, k0_blocks, k0_diag, ke_blocks, mass, velocities, shifts, sample = arguments
    x_block, basis, material, k0_blocks, k0_diag, ke_blocks, mass, velocities, shifts = hold(
        x_block, basis, material, jnp.transpose(k0_blocks, (2, 3, 0, 1)), k0_diag.T,
        jnp.transpose(ke_blocks, (2, 3, 0, 1)), mass.T, velocities, shifts,
    )
    k0_blocks, ke_blocks = (jnp.transpose(blocks, (2, 3, 0, 1)) for blocks in (k0_blocks, ke_blocks))
    k0_diag, mass = k0_diag.T, mass.T
    tables = stencil_tables(k0_blocks, k0_diag, ke_blocks, mass, velocities, shifts, sample)
    block_cols, comps, extent_x, _, lanes = x_block.shape
    group_cols = basis.shape[0]
    row_count = float(comps * extent_x * lax.axis_size("space") * basis.shape[3] * lanes)
    fields = jnp.zeros((7, comps, comps) + material.shape, jnp.float32)
    for level in range(tables.shape[0]):
        chosen = (material == level).astype(jnp.float32)
        fields = fields + tables[level][:, :, :, None, None, None] * chosen
    views = [x_block]
    for dim, axis in ((2, "space"), (3, "basis"), (4, None)):
        views += [shifted(x_block, dim, axis, False), shifted(x_block, dim, axis, True)]
    applied = jnp.zeros_like(x_block)
    for offset, view in enumerate(views):
        for comp in range(comps):
            applied = applied + fields[offset, :, comp][None] * view[:, comp : comp + 1]

    count = lax.axis_size("basis")
    place = lax.axis_index("basis")
    pieces = jnp.moveaxis(basis.reshape(basis.shape[:3] + (count, -1, lanes)), 3, 0)
    rows = jnp.zeros((count,) + pieces.shape[1:], jnp.float32)
    for k in range(count):
        piece = lax.dynamic_index_in_dim(pieces, place ^ k, 0, keepdims=False)
        if k:
            piece = lax.ppermute(piece, "basis", [(i, i ^ k) for i in range(count)])
        rows = lax.dynamic_update_index_in_dim(rows, piece, place ^ k, 0)
    rows = rows.reshape((count * group_cols,) + pieces.shape[2:])

    def total(part):
        for axis in ("basis", "space"):
            mask = 1
            while mask < lax.axis_size(axis):
                pairs = [(i, i ^ mask) for i in range(lax.axis_size(axis))]
                part = part + lax.ppermute(part, axis, pairs)
                mask *= 2
        return part / row_count

    running = jnp.zeros((count * group_cols, block_cols), jnp.float32)
    for repeat in range(2):
        coeffs = total(
            jnp.einsum("kcxyz,ncxyz->kn", rows, applied, precision=exact_precision)
        )
        applied = applied - jnp.einsum("kcxyz,kn->ncxyz", rows, coeffs, precision=exact_precision)
        running = running + coeffs
    gram = total(jnp.einsum("ncxyz,mcxyz->nm", applied, applied, precision=exact_precision))
    lower = jnp.linalg.cholesky(gram)
    inverse = lax.linalg.triangular_solve(
        lower, jnp.eye(block_cols, dtype=jnp.float32), left_side=True, lower=True
    )
    block = jnp.einsum("mcxyz,nm->ncxyz", applied, inverse, precision=exact_precision)
    own = lax.dynamic_slice_in_dim(running, place * group_cols, group_cols, axis=0)
    return tuple(hold(block.reshape(block_cols, -1, lanes), own, lower.T))


def shards(
    x_block, basis, material, k0_blocks, k0_diag, ke_blocks, mass, velocities, shifts, sample
):
    arguments = (
        x_block, basis, material, k0_blocks, k0_diag, ke_blocks, mass, velocities, shifts, sample
    )
    block_cols, comps, extent_x, rows, lanes = x_block.shape
    group_cols = basis.shape[0]
    lines = comps * rows
    row_count = float(comps * extent_x * lax.axis_size("space") * basis.shape[3] * lanes)

    place = lax.axis_index("basis").astype(jnp.int32).reshape(1)
    slab = lax.axis_index("space").astype(jnp.int32).reshape(1)
    count = lax.axis_size("basis")
    x_far = x_block.reshape(block_cols * lines, lanes)
    *pieces, x_rows = pack(place, basis, x_far, block_cols)
    got = {}
    for name in ("even", *reversed(partners(count)[0]), "odd"):
        if name == "even":
            got[name] = swap(x_far, "space", 0)
        elif name == "odd":
            got[name] = swap(x_far, "space", 1)
        else:
            piece = lax.ppermute(pieces[name - 1], "basis", [(i, i ^ name) for i in range(count)])
            got[name] = piece.reshape(-1, lanes)
    fields, applied, own = ahead(
        sample, place, basis, velocities, shifts, k0_blocks, ke_blocks, k0_diag, mass,
        material.reshape(rows, lanes), x_rows, comps,
    )
    split = {0: own}
    first, *rest = reversed(partners(count)[1])
    applied, split[first] = add_edges(
        place, fields, applied, {first: got.pop(first)}, comps, group_cols, EARLY
    )
    applied = add_side(slab, fields, applied, got.pop("even"), comps, "even", NEXT)
    for k in rest:
        applied, split[k] = add_edges(
            place, fields, applied, {k: got.pop(k)}, comps, group_cols, None
        )
    applied = add_side(slab, fields, applied, got.pop("odd"), comps, "odd", LATE)
    stack, keep, give = sums(place, applied, split, got)
    halves = exchange_all(keep, give)
    block, coeffs, upper, bad = finish(
        place, halves, stack, row_count, block_cols, group_cols, lines, comps
    )
    block, coeffs, upper = lax.while_loop(
        lambda state: state[0] > 0,
        lambda state: (jnp.zeros_like(state[0]), careful(arguments)),
        (bad[0, 0], (block, coeffs, upper)),
    )[1]
    return block.reshape(x_block.shape), coeffs, upper


def solution(mesh):
    in_specs = (
        P(None, None, "space", "basis", None),
        P("basis", None, "space", None, None),
        P("space", "basis", None),
        P(),
        P(),
        P(),
        P(),
        P(),
        P(),
        P(),
    )
    out_specs = (P(None, None, "space", "basis", None), P("basis", None), P())
    return jax.shard_map(shards, mesh=mesh, in_specs=in_specs, out_specs=out_specs, check_vma=False)
```

```python
import functools

import jax
import jax.numpy as jnp
from jax import lax
from jax.experimental import pallas as pl
from jax.experimental.pallas import tpu as pltpu
from jax.sharding import PartitionSpec as P

exact_precision = lax.Precision.HIGHEST
VMEM = pl.BlockSpec(memory_space=pltpu.VMEM)
SMEM = pl.BlockSpec(memory_space=pltpu.SMEM)
HBM = pl.BlockSpec(memory_space=pltpu.HBM)
LOSS = 256.0
EARLY = pl.CostEstimate(flops=10**9, bytes_accessed=10**6, transcendentals=0)
NEXT = pl.CostEstimate(flops=3 * 10**8, bytes_accessed=10**6, transcendentals=0)
LATE = pl.CostEstimate(flops=10**6, bytes_accessed=10**6, transcendentals=0)
SCRATCH = pltpu.CompilerParams(vmem_limit_bytes=8 * 2**20)


def f32(*shape):
    return jax.ShapeDtypeStruct(shape, jnp.float32)


def near(*shape, dtype=jnp.float32):
    return pltpu.VMEM(shape, dtype)


def kept(*arrays):
    return [pltpu.with_memory_space_constraint(array, pltpu.VMEM) for array in arrays]


def far(*arrays):
    return [pltpu.with_memory_space_constraint(array, pltpu.HBM) for array in arrays]


def swap(values, axis, first):
    pairs = [(i, i + 1) for i in range(first, lax.axis_size(axis) - 1, 2)]
    return lax.ppermute(values, axis, pairs + [(j, i) for i, j in pairs])


def partners(count):
    return range(1, count), [k for k in range(1, count) if k & (k + 1) == 0]


def pack_kernel(comps, place_ref, basis_ref, x_ref, *refs):
    *piece_refs, x_out_ref, sems = refs
    piece_refs = dict(enumerate(piece_refs, 1))
    count = 1 + len(piece_refs)
    tiles, _, rows, lanes = basis_ref.shape
    block_cols = x_ref.shape[0] // (comps * rows)
    place = place_ref[0]
    x_copy = pltpu.make_async_copy(x_ref, x_out_ref, sems.at[0])
    x_copy.start()
    copies = []
    for k in reversed(range(1, count)):
        copies.append(
            pltpu.make_async_copy(
                basis_ref.at[:, place ^ k], piece_refs[k].at[pl.ds(0, tiles)], sems.at[k]
            )
        )
    for copy in copies:
        copy.start()
    x_copy.wait()
    for comp in range(comps):
        first, last = (
            x_out_ref[pl.ds(comp * rows + row, block_cols, stride=comps * rows), :]
            for row in (0, rows - 1)
        )
        for k in partners(count)[1]:
            edge = jnp.where((place ^ k) > place, last, first)
            for part in range(block_cols // rows):
                piece_refs[k][tiles + comp * (block_cols // rows) + part] = edge[
                    part * rows : (part + 1) * rows
                ]
    for copy in copies:
        copy.wait()


def pack(place, basis, x_rows, block_cols):
    group_cols, comps, _, full_y, lanes = basis.shape
    count = lax.axis_size("basis")
    rows = full_y // count
    tiles = group_cols * comps
    edge_tiles = block_cols * comps // rows
    pieces = [
        near(tiles + (edge_tiles if k in partners(count)[1] else 0), rows, lanes)
        for k in range(1, count)
    ]
    return pl.pallas_call(
        functools.partial(pack_kernel, comps),
        out_shape=(*pieces, near(*x_rows.shape)),
        in_specs=[SMEM, HBM, HBM],
        out_specs=(VMEM,) * count,
        scratch_shapes=[pltpu.SemaphoreType.DMA((count,))],
        compiler_params=SCRATCH,
        name="pack",
    )(place, *far(basis.reshape(tiles, count, rows, lanes), x_rows))


def three_parts(values):
    high = values.astype(jnp.bfloat16)
    rest = values - high.astype(jnp.float32)
    middle = rest.astype(jnp.bfloat16)
    low = (rest - middle.astype(jnp.float32)).astype(jnp.bfloat16)
    return high, middle, low


def line_of(ref, comp, row, comps, rows, block_cols):
    return ref[pl.ds(comp * rows + row, block_cols, stride=comps * rows), :]


def ahead_kernel(
    sample_ref, place_ref, basis_ref, *refs
):
    far_refs, refs = refs[:7], refs[7:]
    x_ref, fields_ref, applied_ref, stack_ref, *near_refs, piece_ref, sems = refs
    velocities_ref, shifts_ref, k0_ref, ke_ref, diag_ref, mass_ref, material_ref = near_refs
    own = pltpu.make_async_copy(basis_ref.at[:, place_ref[0]], piece_ref, sems.at[len(near_refs)])
    own.start()
    copies = [
        pltpu.make_async_copy(source, target, sems.at[index])
        for index, (source, target) in enumerate(zip(far_refs, near_refs))
    ]
    for copy in copies:
        copy.start()
    group_cols = stack_ref.shape[0] // 3
    own.wait()
    own_ref = piece_ref.reshape(piece_ref.shape[0] * piece_ref.shape[1], piece_ref.shape[2])
    split_lines(
        own_ref, stack_ref, applied_ref.shape[0], group_cols, [i * group_cols for i in range(3)]
    )
    for copy in copies:
        copy.wait()
    comps, _, levels, offsets = k0_ref.shape
    rows, lanes = material_ref.shape
    lines = comps * rows
    block_cols = x_ref.shape[0] // lines
    velocity = velocities_ref[sample_ref[0]]
    sigma = shifts_ref[sample_ref[0]]
    entry_rows = fields_ref.shape[1]
    stride = entry_rows // (comps * comps)
    gap = jnp.zeros((levels, stride - offsets), jnp.float32)
    wide = []
    for out in range(comps):
        for comp in range(comps):
            wide += [k0_ref[out, comp] - velocity * velocity * ke_ref[out, comp], gap]
    wide.append(jnp.zeros((levels, lanes - entry_rows), jnp.float32))
    table = jnp.concatenate(wide, axis=1).T[:entry_rows]
    entry = lax.broadcasted_iota(jnp.int32, table.shape, 0)
    for comp in range(comps):
        centre = diag_ref[comp : comp + 1, :] - sigma * mass_ref[comp : comp + 1, :]
        table = table + jnp.where(entry == comp * (comps + 1) * stride, centre, 0.0)

    lane = lax.broadcasted_iota(jnp.int32, (block_cols, lanes), 1)
    level = lax.broadcasted_iota(jnp.int32, (levels, lanes), 0)
    for row in range(rows):
        chosen = jnp.broadcast_to(material_ref[row : row + 1, :], (levels, lanes)) == level
        fields = jnp.dot(
            table, chosen.astype(jnp.float32),
            precision=exact_precision, preferred_element_type=jnp.float32,
        )
        fields_ref[row] = fields
        sums = [None] * comps
        for comp in range(comps):
            centre = line_of(x_ref, comp, row, comps, rows, block_cols)
            views = {
                0: centre,
                5: jnp.where(lane == 0, 0.0, pltpu.roll(centre, 1, 1)),
                6: jnp.where(lane == lanes - 1, 0.0, pltpu.roll(centre, lanes - 1, 1)),
            }
            if row > 0:
                views[3] = line_of(x_ref, comp, row - 1, comps, rows, block_cols)
            if row < rows - 1:
                views[4] = line_of(x_ref, comp, row + 1, comps, rows, block_cols)
            for offset, view in views.items():
                for out in range(comps):
                    place = (out * comps + comp) * stride + offset
                    term = fields[place : place + 1, :] * view
                    sums[out] = term if sums[out] is None else sums[out] + term
        for out in range(comps):
            applied_ref[out * rows + row] = sums[out]


def ahead(sample, place, basis, velocities, shifts, k0, ke, diag, mass, material, x_rows, comps):
    rows, lanes = material.shape
    lines = comps * rows
    stride = -(-k0.shape[1] // 8) * 8
    k0, ke = (jnp.transpose(blocks, (2, 3, 0, 1)) for blocks in (k0, ke))
    tables = far(velocities, shifts, k0, ke, diag.T, mass.T, material)
    group_cols, _, _, full_y, _ = basis.shape
    tiles = group_cols * comps
    basis = basis.reshape(tiles, full_y // rows, rows, lanes)
    return pl.pallas_call(
        ahead_kernel,
        out_shape=(
            near(rows, comps * comps * stride, lanes),
            near(lines, x_rows.shape[0] // lines, lanes),
            near(3 * group_cols, lines * lanes, dtype=jnp.bfloat16),
        ),
        in_specs=[SMEM] * 2 + [HBM] * (1 + len(tables)) + [VMEM],
        out_specs=(VMEM,) * 3,
        scratch_shapes=[
            (pltpu.SMEM if array.ndim == 1 else pltpu.VMEM)(array.shape, array.dtype)
            for array in tables
        ] + [
            pltpu.VMEM((tiles, rows, lanes), jnp.float32),
            pltpu.SemaphoreType.DMA((len(tables) + 1,)),
        ],
        compiler_params=SCRATCH,
        name="ahead",
    )(sample, place, *far(basis), *tables, *kept(x_rows))


def side_terms(field_row, swapped, side, out, comp, comps):
    stride = field_row.shape[0] // (comps * comps)
    begin = (out * comps + comp) * stride
    below, above = field_row[begin + 1 : begin + 2], field_row[begin + 2 : begin + 3]
    other = (below, above) if side == "even" else (above, below)
    return jnp.where(swapped, *other)


def side_kernel(comps, side, slab_ref, fields_ref, applied_ref, halo_ref, out_ref):
    lines, block_cols, _ = applied_ref.shape
    rows = lines // comps
    swapped = slab_ref[0] % 2 == 1
    for row in range(rows):
        field_row = fields_ref[row]
        views = [line_of(halo_ref, comp, row, comps, rows, block_cols) for comp in range(comps)]
        for out in range(comps):
            total = applied_ref[out * rows + row]
            for comp, view in enumerate(views):
                total = total + side_terms(field_row, swapped, side, out, comp, comps) * view
            out_ref[out * rows + row] = total


def add_side(slab, fields, applied, halo, comps, side, weight):
    return pl.pallas_call(
        functools.partial(side_kernel, comps, side),
        out_shape=near(*applied.shape),
        in_specs=[SMEM] + [VMEM] * 3,
        out_specs=VMEM,
        compiler_params=SCRATCH,
        cost_estimate=weight,
        name="side",
    )(slab, *kept(fields, applied, halo))


def split_lines(piece_ref, stack_ref, lines, group_cols, begins):
    lanes = piece_ref.shape[1]
    for line in range(lines):
        values = piece_ref[pl.ds(line, group_cols, stride=lines), :]
        for begin, part in zip(begins, three_parts(values)):
            stack_ref[pl.ds(begin, group_cols), pl.ds(line * lanes, lanes)] = part


def edges_kernel(comps, ks, group_cols, place_ref, fields_ref, applied_ref, *refs):
    piece_refs, out_ref, parts_refs = refs[: len(ks)], refs[len(ks)], refs[len(ks) + 1 :]
    lines, block_cols, lanes = applied_ref.shape
    rows = lines // comps
    stride = fields_ref.shape[1] // (comps * comps)
    place = place_ref[0]

    def edge(comp, step):
        result = jnp.zeros((block_cols, lanes), jnp.float32)
        for k, ref in zip(ks, piece_refs):
            begin = ref.shape[0] - (comps - comp) * block_cols
            here = (place ^ k) == place + step
            result = jnp.where(here, ref[pl.ds(begin, block_cols), :], result)
        return result

    out_ref[...] = applied_ref[...]
    for row, offset, step in ((0, 3, -1), (rows - 1, 4, 1)):
        field_row = fields_ref[row]
        views = [edge(comp, step) for comp in range(comps)]
        for out in range(comps):
            total = out_ref[out * rows + row]
            for comp, view in enumerate(views):
                entry = (out * comps + comp) * stride + offset
                total = total + field_row[entry : entry + 1] * view
            out_ref[out * rows + row] = total
    for piece_ref, parts_ref in zip(piece_refs, parts_refs):
        split_lines(piece_ref, parts_ref, lines, group_cols, [i * group_cols for i in range(3)])


def add_edges(place, fields, applied, pieces, comps, group_cols, weight):
    lines, _, lanes = applied.shape
    parts = near(3 * group_cols, lines * lanes, dtype=jnp.bfloat16)
    return pl.pallas_call(
        functools.partial(edges_kernel, comps, tuple(pieces), group_cols),
        out_shape=(near(*applied.shape),) + (parts,) * len(pieces),
        in_specs=[SMEM] + [VMEM] * (2 + len(pieces)),
        out_specs=(VMEM,) * (1 + len(pieces)),
        compiler_params=SCRATCH,
        cost_estimate=weight,
        name="edges",
    )(place, *kept(fields, applied, *pieces.values()))


def fold(total, basis_cols, block_cols, lanes):
    half = basis_cols // 2
    row = lax.broadcasted_iota(jnp.int32, (half, half), 0)
    column = lax.broadcasted_iota(jnp.int32, (half, half), 1)
    last = total[half:basis_cols, half:basis_cols]
    shared = jnp.where(row >= column, total[:half, :half], last)
    diagonal = jnp.sum(jnp.where(row == column, last, 0.0), axis=1, keepdims=True)
    below = total[basis_cols:]
    first = jnp.concatenate((below[:, :half], below[:, half:basis_cols]), axis=0)
    rest = jnp.zeros((half - block_cols, block_cols), jnp.float32)
    block = jnp.concatenate((below[:, basis_cols:], rest), axis=0)
    pad = jnp.zeros((half, lanes - 3 * half - block_cols - 1), jnp.float32)
    return jnp.concatenate(
        (shared, total[:half, half:basis_cols], first, block, diagonal, pad), axis=1
    )


def unfold(folded, block_cols):
    half = folded.shape[0]
    row = lax.broadcasted_iota(jnp.int32, (half, half), 0)
    column = lax.broadcasted_iota(jnp.int32, (half, half), 1)
    shared, across = folded[:, :half], folded[:, half : 2 * half]
    turned = shared.T
    start = jnp.where(row >= column, shared, turned)
    end = jnp.where(row < column, shared, turned)
    diagonal = folded[:, 3 * half + block_cols : 3 * half + block_cols + 1]
    end = jnp.where(row == column, diagonal, end)
    gram = jnp.concatenate(
        (jnp.concatenate((start, across), axis=1), jnp.concatenate((across.T, end), axis=1)), axis=0
    )
    first = folded[:, 2 * half : 3 * half]
    first = jnp.concatenate((first[:block_cols], first[block_cols : 2 * block_cols]), axis=1)
    return gram, first, folded[:block_cols, 3 * half : 3 * half + block_cols]


def sums_kernel(
    split, raw, place_ref, applied_ref, *refs
):
    *refs, stack_ref, keep_ref, give_ref = refs
    lines, block_cols, lanes = applied_ref.shape
    group_cols = refs[0].shape[0] // 3
    basis_cols = (len(split) + len(raw)) * group_cols
    joined = basis_cols + block_cols
    place = place_ref[0]
    for k, ref in zip(split + raw, refs):
        begin = pl.multiple_of((place ^ k) * group_cols, group_cols)
        begins = [index * joined + begin for index in range(3)]
        if k in split:
            for index in range(3):
                stack_ref[pl.ds(begins[index], group_cols), :] = ref[
                    pl.ds(index * group_cols, group_cols), :
                ]
        else:
            split_lines(ref, stack_ref, lines, group_cols, begins)
    for line in range(lines):
        for index, part in enumerate(three_parts(applied_ref[line])):
            there = pl.ds(index * joined + basis_cols, block_cols)
            stack_ref[there, pl.ds(line * lanes, lanes)] = part

    stack = stack_ref[...]
    products = lax.dot_general(
        stack, stack, (((1,), (1,)), ((), ())), preferred_element_type=jnp.float32
    )
    wide = products[:joined] + products[joined : 2 * joined] + products[2 * joined :]
    total = wide[:, :joined] + wide[:, joined : 2 * joined] + wide[:, 2 * joined :]
    folded = fold(total, basis_cols, block_cols, keep_ref.shape[1])
    half = keep_ref.shape[0]
    odd = place % 2 == 1
    keep_ref[...] = jnp.where(odd, folded[half:], folded[:half])
    give_ref[...] = jnp.where(odd, folded[:half], folded[half:])


def sums(place, applied, split, raw):
    lines, block_cols, lanes = applied.shape
    basis_cols = (len(split) + len(raw)) * (split[0].shape[0] // 3)
    joined = basis_cols + block_cols
    return pl.pallas_call(
        functools.partial(sums_kernel, tuple(split), tuple(raw)),
        out_shape=(
            near(3 * joined, lines * lanes, dtype=jnp.bfloat16),
            near(basis_cols // 4, 2 * basis_cols),
            near(basis_cols // 4, 2 * basis_cols),
        ),
        in_specs=[SMEM] + [VMEM] * (1 + len(split) + len(raw)),
        out_specs=(VMEM,) * 3,
        compiler_params=SCRATCH,
        name="sums",
    )(place, *kept(applied, *split.values(), *raw.values()))


def exchange_all(keep, give):
    sizes = [lax.axis_size(axis) for axis in ("space", "basis")]
    pairs = [(i, i ^ 1) for i in range(sizes[1])]
    part = keep + lax.ppermute(give, "basis", pairs)
    groups = [
        [i * sizes[1] + j for i in range(sizes[0]) for j in range(first, sizes[1], 2)][::-1]
        for first in range(2)
    ]
    copies = jnp.broadcast_to(part[None], (len(groups[0]),) + part.shape)
    parts = lax.all_to_all(copies, ("space", "basis"), 0, 0, axis_index_groups=groups)
    own = jnp.sum(parts, axis=0)
    return own, lax.ppermute(own, "basis", pairs)


def finish_kernel(
    row_count, comps, place_ref, own_ref, given_ref, stack_ref, block_ref, coeffs_ref, upper_ref, bad_ref,
    coeffs_scratch, upper_scratch, bad_scratch, block_scratch, sems,
):
    block_cols = upper_ref.shape[0]
    basis_cols = own_ref.shape[1] // 2
    joined = basis_cols + block_cols
    lines, lanes = block_ref.shape[1:]
    odd = place_ref[0] % 2 == 1
    own, given = own_ref[...], given_ref[...]
    total = jnp.concatenate((jnp.where(odd, given, own), jnp.where(odd, own, given)), axis=0)
    total = total / row_count
    gram, first, block_gram = unfold(total, block_cols)

    def times(left, right, right_dim=0):
        return lax.dot_general(
            left, right, (((1,), (right_dim,)), ((), ())),
            precision=exact_precision, preferred_element_type=jnp.float32,
        )

    coeffs = first + (first - times(first, gram))
    image = times(coeffs, gram)
    matrix = block_gram - times(
        jnp.concatenate((coeffs, first - image), axis=1), jnp.concatenate((first, coeffs), axis=1), 1
    )
    coeffs_scratch[...] = coeffs.T
    group_cols = coeffs_ref.shape[0]
    start = pl.multiple_of(place_ref[0] * group_cols, group_cols)
    copies = [
        pltpu.make_async_copy(
            coeffs_scratch.at[pl.ds(start, group_cols)], coeffs_ref, sems.at[comps]
        )
    ]
    copies[0].start()

    row = lax.broadcasted_iota(jnp.int32, (block_cols, block_cols), 0)
    column = lax.broadcasted_iota(jnp.int32, (block_cols, block_cols), 1)
    unit = jnp.where(row == column, 1.0, 0.0)
    pad = jnp.zeros((block_cols, 2 * basis_cols - joined - block_cols), jnp.float32)
    work = jnp.concatenate((-coeffs, unit, matrix, pad), axis=1)
    height = lax.broadcasted_iota(jnp.int32, work.shape, 0)
    width = 4
    for begin in range(0, block_cols, width):
        done, new_rows = [], []
        for step in range(begin, begin + width):
            column_here = jnp.broadcast_to(work[:, joined + step : joined + step + 1], work.shape)
            pivot_row = work[step : step + 1]
            for other_column, other_row, inverse in done:
                entry = other_column[step : step + 1]
                pivot_row = pivot_row - entry * other_row
                column_here = column_here - other_column * (entry * inverse)
            pivot = column_here[step : step + 1]
            inverse = 1.0 / pivot
            done.append((column_here, pivot_row * inverse, inverse))
            new_rows.append(pivot_row * lax.rsqrt(pivot))
        rest = work
        for column_here, scaled, _ in done:
            rest = rest - column_here * scaled
        work = jnp.where(height >= begin + width, rest, work)
        for step, new_row in enumerate(new_rows, begin):
            work = jnp.where(height == step, new_row, work)
    upper = jnp.where(row <= column, work[:, joined : joined + block_cols], 0.0)
    upper_scratch[...] = upper
    kept_enough = jnp.where(row == column, upper * upper * LOSS, block_gram) >= block_gram
    kept_enough = jnp.min(jnp.where(kept_enough, 1.0, 0.0), axis=0, keepdims=True)
    kept_enough = jnp.min(kept_enough, axis=1, keepdims=True)
    bad_scratch[...] = jnp.where(kept_enough > 0.0, 0, 1)
    copies.append(pltpu.make_async_copy(bad_scratch, bad_ref, sems.at[comps + 2]))
    copies[-1].start()
    copies.append(pltpu.make_async_copy(upper_scratch, upper_ref, sems.at[comps + 1]))
    copies[-1].start()
    weights = three_parts(work[:, :joined])
    wide = jnp.concatenate(
        [jnp.concatenate((part, part, part), axis=1) for part in weights], axis=0
    )
    rows = lines // comps
    for comp in range(comps):
        there = pl.ds(comp * rows * lanes, rows * lanes)
        result = jnp.dot(wide, stack_ref[:, there], preferred_element_type=jnp.float32)
        result = result[:block_cols] + result[block_cols : 2 * block_cols] + result[2 * block_cols :]
        for index in range(rows):
            block_scratch[pl.ds(comp * rows + index, block_cols, stride=lines), :] = result[
                :, index * lanes : (index + 1) * lanes
            ]
        part = pl.ds(comp * rows, rows)
        copies.append(
            pltpu.make_async_copy(
                block_scratch.reshape(block_cols, lines, lanes).at[:, part, :],
                block_ref.at[:, part, :],
                sems.at[comp],
            )
        )
        copies[-1].start()
    for copy in copies:
        copy.wait()


def finish(place, halves, stack, row_count, block_cols, group_cols, lines, comps):
    lanes = stack.shape[1] // lines
    basis_cols = halves[0].shape[1] // 2
    return pl.pallas_call(
        functools.partial(finish_kernel, row_count, comps),
        out_shape=(
            f32(block_cols, lines, lanes), f32(group_cols, block_cols), f32(block_cols, block_cols),
            jax.ShapeDtypeStruct((1, 1), jnp.int32),
        ),
        in_specs=[SMEM] + [VMEM] * 3,
        out_specs=(HBM,) * 4,
        scratch_shapes=[
            pltpu.VMEM((basis_cols, block_cols), jnp.float32),
            pltpu.VMEM((block_cols, block_cols), jnp.float32),
            pltpu.VMEM((1, 1), jnp.int32),
            pltpu.VMEM((block_cols * lines, lanes), jnp.float32),
            pltpu.SemaphoreType.DMA((comps + 3,)),
        ],
        compiler_params=SCRATCH,
        name="finish",
    )(place, *kept(*halves, stack))


def stencil_tables(k0_blocks, k0_diag, ke_blocks, mass, velocities, shifts, sample):
    velocity = jnp.take(velocities, sample, axis=0)[0]
    sigma_value = jnp.take(shifts, sample, axis=0)[0]
    center = (k0_diag - sigma_value * mass)[:, :, None] * jnp.eye(3, dtype=jnp.float32)
    tables = k0_blocks - velocity * velocity * ke_blocks
    return tables.at[:, 0].add(center)


def shifted(cells, dim, axis, up):
    extent = cells.shape[dim]
    edge = lax.slice_in_dim(cells, 0, 1, axis=dim) if up else (
        lax.slice_in_dim(cells, extent - 1, extent, axis=dim)
    )
    if axis is None:
        edge = jnp.zeros_like(edge)
    else:
        ends = [(i, i + 1) for i in range(lax.axis_size(axis) - 1)]
        edge = lax.ppermute(edge, axis, [(j, i) for i, j in ends] if up else ends)
    if up:
        return jnp.concatenate((lax.slice_in_dim(cells, 1, extent, axis=dim), edge), axis=dim)
    return jnp.concatenate((edge, lax.slice_in_dim(cells, 0, extent - 1, axis=dim)), axis=dim)


def hold_kernel(*refs):
    *refs, sems = refs
    half = len(refs) // 2
    copies = [
        pltpu.make_async_copy(source, target, sems.at[index])
        for index, (source, target) in enumerate(zip(refs[:half], refs[half:]))
    ]
    for copy in copies:
        copy.start()
    for copy in copies:
        copy.wait()


def hold(*arrays):
    return pl.pallas_call(
        hold_kernel,
        out_shape=[jax.ShapeDtypeStruct(array.shape, array.dtype) for array in arrays],
        in_specs=[HBM] * len(arrays),
        out_specs=[HBM] * len(arrays),
        scratch_shapes=[pltpu.SemaphoreType.DMA((len(arrays),))],
        compiler_params=SCRATCH,
        name="hold",
    )(*far(*arrays))


def careful(arguments):
    x_block, basis, material, k0_blocks, k0_diag, ke_blocks, mass, velocities, shifts, sample = arguments
    x_block, basis, material, k0_blocks, k0_diag, ke_blocks, mass, velocities, shifts = hold(
        x_block, basis, material, jnp.transpose(k0_blocks, (2, 3, 0, 1)), k0_diag.T,
        jnp.transpose(ke_blocks, (2, 3, 0, 1)), mass.T, velocities, shifts,
    )
    k0_blocks, ke_blocks = (jnp.transpose(blocks, (2, 3, 0, 1)) for blocks in (k0_blocks, ke_blocks))
    k0_diag, mass = k0_diag.T, mass.T
    tables = stencil_tables(k0_blocks, k0_diag, ke_blocks, mass, velocities, shifts, sample)
    block_cols, comps, extent_x, _, lanes = x_block.shape
    group_cols = basis.shape[0]
    row_count = float(comps * extent_x * lax.axis_size("space") * basis.shape[3] * lanes)
    fields = jnp.zeros((7, comps, comps) + material.shape, jnp.float32)
    for level in range(tables.shape[0]):
        chosen = (material == level).astype(jnp.float32)
        fields = fields + tables[level][:, :, :, None, None, None] * chosen
    views = [x_block]
    for dim, axis in ((2, "space"), (3, "basis"), (4, None)):
        views += [shifted(x_block, dim, axis, False), shifted(x_block, dim, axis, True)]
    applied = jnp.zeros_like(x_block)
    for offset, view in enumerate(views):
        for comp in range(comps):
            applied = applied + fields[offset, :, comp][None] * view[:, comp : comp + 1]

    count = lax.axis_size("basis")
    place = lax.axis_index("basis")
    pieces = jnp.moveaxis(basis.reshape(basis.shape[:3] + (count, -1, lanes)), 3, 0)
    rows = jnp.zeros((count,) + pieces.shape[1:], jnp.float32)
    for k in range(count):
        piece = lax.dynamic_index_in_dim(pieces, place ^ k, 0, keepdims=False)
        if k:
            piece = lax.ppermute(piece, "basis", [(i, i ^ k) for i in range(count)])
        rows = lax.dynamic_update_index_in_dim(rows, piece, place ^ k, 0)
    rows = rows.reshape((count * group_cols,) + pieces.shape[2:])

    def total(part):
        for axis in ("basis", "space"):
            mask = 1
            while mask < lax.axis_size(axis):
                pairs = [(i, i ^ mask) for i in range(lax.axis_size(axis))]
                part = part + lax.ppermute(part, axis, pairs)
                mask *= 2
        return part / row_count

    running = jnp.zeros((count * group_cols, block_cols), jnp.float32)
    for repeat in range(2):
        coeffs = total(
            jnp.einsum("kcxyz,ncxyz->kn", rows, applied, precision=exact_precision)
        )
        applied = applied - jnp.einsum("kcxyz,kn->ncxyz", rows, coeffs, precision=exact_precision)
        running = running + coeffs
    gram = total(jnp.einsum("ncxyz,mcxyz->nm", applied, applied, precision=exact_precision))
    lower = jnp.linalg.cholesky(gram)
    inverse = lax.linalg.triangular_solve(
        lower, jnp.eye(block_cols, dtype=jnp.float32), left_side=True, lower=True
    )
    block = jnp.einsum("mcxyz,nm->ncxyz", applied, inverse, precision=exact_precision)
    own = lax.dynamic_slice_in_dim(running, place * group_cols, group_cols, axis=0)
    return tuple(hold(block.reshape(block_cols, -1, lanes), own, lower.T))


def shards(
    x_block, basis, material, k0_blocks, k0_diag, ke_blocks, mass, velocities, shifts, sample
):
    arguments = (
        x_block, basis, material, k0_blocks, k0_diag, ke_blocks, mass, velocities, shifts, sample
    )
    block_cols, comps, extent_x, rows, lanes = x_block.shape
    group_cols = basis.shape[0]
    lines = comps * rows
    row_count = float(comps * extent_x * lax.axis_size("space") * basis.shape[3] * lanes)

    place = lax.axis_index("basis").astype(jnp.int32).reshape(1)
    slab = lax.axis_index("space").astype(jnp.int32).reshape(1)
    count = lax.axis_size("basis")
    x_far = x_block.reshape(block_cols * lines, lanes)
    *pieces, x_rows = pack(place, basis, x_far, block_cols)
    got = {}
    for name in ("even", *reversed(partners(count)[0]), "odd"):
        if name == "even":
            got[name] = swap(x_far, "space", 0)
        elif name == "odd":
            got[name] = swap(x_far, "space", 1)
        else:
            piece = lax.ppermute(pieces[name - 1], "basis", [(i, i ^ name) for i in range(count)])
            got[name] = piece.reshape(-1, lanes)
    fields, applied, own = ahead(
        sample, place, basis, velocities, shifts, k0_blocks, ke_blocks, k0_diag, mass,
        material.reshape(rows, lanes), x_rows, comps,
    )
    split = {0: own}
    first, *rest = reversed(partners(count)[1])
    applied, split[first] = add_edges(
        place, fields, applied, {first: got.pop(first)}, comps, group_cols, EARLY
    )
    applied = add_side(slab, fields, applied, got.pop("even"), comps, "even", NEXT)
    for k in rest:
        applied, split[k] = add_edges(
            place, fields, applied, {k: got.pop(k)}, comps, group_cols, None
        )
    applied = add_side(slab, fields, applied, got.pop("odd"), comps, "odd", LATE)
    stack, keep, give = sums(place, applied, split, got)
    halves = exchange_all(keep, give)
    block, coeffs, upper, bad = finish(
        place, halves, stack, row_count, block_cols, group_cols, lines, comps
    )
    block, coeffs, upper = lax.while_loop(
        lambda state: state[0] > 0,
        lambda state: (jnp.zeros_like(state[0]), careful(arguments)),
        (bad[0, 0], (block, coeffs, upper)),
    )[1]
    return block.reshape(x_block.shape), coeffs, upper


def solution(mesh):
    in_specs = (
        P(None, None, "space", "basis", None),
        P("basis", None, "space", None, None),
        P("space", "basis", None),
        P(),
        P(),
        P(),
        P(),
        P(),
        P(),
        P(),
    )
    out_specs = (P(None, None, "space", "basis", None), P("basis", None), P())
    return jax.shard_map(shards, mesh=mesh, in_specs=in_specs, out_specs=out_specs, check_vma=False)
```
